32 devices in a mesh: dp: 8 (over y, x, core), tensor: 4 (over z).
Axes of the slice: x: 2, y: 2, z: 4, core: 2. Of those that a mesh axis runs over, the one named last changes fastest.
Arguments:
- tokens: bfloat16 [8, 512, 1024], P('dp'), may hold values from -6 to 6
- segment_ids: int32 [8, 512], P('dp'), may hold values from 0 to 9, never falling along the last dimension, each value on 1 to 200 neighbouring positions
- cotangent: bfloat16 [8, 512, 1024], P('dp'), may hold values from -6 to 6
- qkv_weight: bfloat16 [2, 1024, 3, 1024], P(None, None, None, 'tensor'), may hold values from -0.1875 to 0.1875
- qv_bias: bfloat16 [2, 2, 1024], P(None, None, 'tensor'), may hold values from -3 to 3
- proj_weight: bfloat16 [2, 1024, 1024], P(None, 'tensor'), may hold values from -1 to 1
- proj_bias: bfloat16 [2, 1024], replicated, may hold values from -2 to 2
- first_gain: bfloat16 [2, 1024], replicated, may hold values from 0.099609375 to 1.8984375
- first_shift: bfloat16 [2, 1024], replicated, may hold values from -2 to 2
- up_weight: bfloat16 [2, 1024, 4096], P(None, None, 'tensor'), may hold values from -0.1875 to 0.1875
- up_bias: bfloat16 [2, 4096], P(None, 'tensor'), may hold values from -3 to 3
- down_weight: bfloat16 [2, 4096, 1024], P(None, 'tensor'), may hold values from -0.09375 to 0.09375
- down_bias: bfloat16 [2, 1024], replicated, may hold values from -2 to 2
- second_gain: bfloat16 [2, 1024], replicated, may hold values from 0.099609375 to 1.8984375
- second_shift: bfloat16 [2, 1024], replicated, may hold values from -2 to 2
Outputs:
- mixed: float32 [8, 512, 1024], P('dp')
- input_grad: float32 [8, 512, 1024], P('dp')
- qkv_weight_grad: float32 [2, 1024, 3, 1024], P(None, None, None, 'tensor')
- qv_bias_grad: float32 [2, 2, 1024], P(None, None, 'tensor')
- proj_weight_grad: float32 [2, 1024, 1024], P(None, 'tensor')
- proj_bias_grad: float32 [2, 1024], replicated
- first_gain_grad: float32 [2, 1024], replicated
- first_shift_grad: float32 [2, 1024], replicated
- up_weight_grad: float32 [2, 1024, 4096], P(None, None, 'tensor')
- up_bias_grad: float32 [2, 4096], P(None, 'tensor')
- down_weight_grad: float32 [2, 4096, 1024], P(None, 'tensor')
- down_bias_grad: float32 [2, 1024], replicated
- second_gain_grad: float32 [2, 1024], replicated
- second_shift_grad: float32 [2, 1024], replicated
The draws below stay inside these ranges and needn't reach their ends.
Inputs may be any that keep to these rules, and one draw needn't show every extreme that they name: `segment_ids`: within a sequence the document number never falls; every document holds 1 to 200 tokens, and tokens attend only within their document.
All inputs are finite; a program needn't handle non-finite values.
Results may differ from the reference program's by a relative error of at most 0.034.
Values may be sent and summed in bfloat16 or wider, within the bound.
A program may use at most 192 MiB of HBM per device.

```python
import math
import jax
import jax.numpy as jnp
import numpy as np
from jax import lax

D = 1024
HEADS = 16
HEAD = 64
FF = 4096
LEN = 512
LAYERS = 2
SEQS = 8


def with_spikes(entries, key, source, target, blocks, factor):
    def block_of(position):
        return (jnp.arange(entries.shape[position]) // (entries.shape[position] // blocks)).reshape((-1,) + (1,) * (entries.ndim - 1 - position))

    near = jax.random.permutation(key, blocks)[block_of(target)]
    far = (block_of(target) + blocks // 2) % blocks
    return jnp.where((block_of(source) == near) | (block_of(source) == far), factor * entries, entries)


def block_scale(rng, dims, cuts, low, largest):
    def one(dim, shards_of):
        heights = jax.random.uniform(jax.random.fold_in(jax.random.fold_in(rng, 6), dim), (shards_of,), jnp.float32, low / len(cuts), largest / len(cuts))
        return jnp.repeat(jnp.exp(heights), dims[dim] // shards_of).reshape((-1,) + (1,) * (len(dims) - dim - 1))

    level = one(*cuts[0])
    for cut in cuts[1:]:
        level = level * one(*cut)
    return level


def profile(count, total, reach, slope):
    weights = [(1 << 20) // math.isqrt(standing ** slope) + 1 for standing in range(2, count + 1)]
    spare, holding = total - reach - (count - 1), [1] * (count - 1)
    while spare > 0:
        free = [i for i in range(count - 1) if holding[i] < reach]
        pool, remaining = sum([weights[i] for i in free]), spare
        for i in free:
            addition = min(reach - holding[i], max(1, remaining * weights[i] // pool), spare)
            holding[i] = holding[i] + addition
            spare = spare - addition
    return np.array([reach] + holding)


def ragged(stream_key, count, total, bound, slope):
    if count == 2:
        one = jax.random.randint(stream_key, (), max(1, total - bound), min(bound, total - 1) + 1)
        return jnp.stack([one, total - one])
    sizes = jnp.asarray(profile(count, total, bound, slope), jnp.int32)
    couples = (count - 1) // 2
    donor, taker = sizes[1:1 + 2 * couples:2], sizes[2:2 + 2 * couples:2]
    room = jnp.minimum(donor - 1, bound - taker)
    passed = jax.random.randint(jax.random.fold_in(stream_key, 1), (couples,), 0, 1 << 20) % (room + 1)
    sizes = sizes.at[1:1 + 2 * couples:2].set(donor - passed).at[2:2 + 2 * couples:2].set(taker + passed)
    return sizes[jax.random.permutation(jax.random.fold_in(stream_key, 2), count)]


def bell_draw(stream_key, extent, scale, limit, cuts=(), kind=jnp.bfloat16):
    level = block_scale(stream_key, extent, cuts, -0.22, 0.18) if cuts else 1.0
    drawn = jax.random.normal(stream_key, extent, jnp.float32) * scale * level
    return jnp.minimum(jnp.maximum(drawn, -limit), limit).astype(kind)


def bell_draw_with(stream_key, shape, scale, limit, cuts, heavy, kind=jnp.bfloat16):
    array = scale * jax.random.normal(stream_key, shape, jnp.float32)
    if cuts:
        array = array * block_scale(stream_key, shape, cuts, -0.22, 0.18)
    return jnp.clip(with_spikes(array, jax.random.fold_in(stream_key, 3), *heavy), -limit, limit).astype(kind)


def setup_inputs(seed: int = 0) -> dict:
    seeds = jax.random.split(jax.random.key(seed), 16)
    return {
        "tokens": bell_draw(seeds[0], (SEQS, LEN, D), 1.0, 6.0, ((0, 8),)),
        "segment_ids": jax.vmap(lambda own: jnp.searchsorted(jnp.cumsum(ragged(own, LEN // 64 + 2, LEN, min(200, 3 * LEN // 4), 0)), jnp.arange(LEN), side="right"))(jax.random.split(seeds[1], SEQS)).reshape((SEQS, LEN)).astype(jnp.int32),
        "cotangent": bell_draw_with(seeds[2], (SEQS, LEN, D), 1.0, 6.0, ((0, 8),), (0, 2, 8, 2.0)),
        "qkv_weight": bell_draw(seeds[3], (LAYERS, D, 3, D), D ** -0.5, 0.1875, ((3, 4),)),
        "qv_bias": bell_draw(seeds[4], (LAYERS, 2, D), 0.5, 3.0, ((2, 4),)),
        "proj_weight": bell_draw(seeds[5], (LAYERS, D, D), (D // 32) ** -0.5, 1.0, ((1, 4),)),
        "proj_bias": bell_draw(seeds[6], (LAYERS, D), 0.3, 2.0),
        "first_gain": jnp.clip(1.0 + 0.18 * jax.random.normal(seeds[7], (LAYERS, D), jnp.float32), 0.099609375, 1.8984375).astype(jnp.bfloat16),
        "first_shift": bell_draw(seeds[8], (LAYERS, D), 0.3, 2.0),
        "up_weight": bell_draw(seeds[9], (LAYERS, D, FF), D ** -0.5, 0.1875, ((2, 4),)),
        "up_bias": bell_draw(seeds[10], (LAYERS, FF), 0.5, 3.0, ((1, 4),)),
        "down_weight": bell_draw(seeds[11], (LAYERS, FF, D), FF ** -0.5, 0.09375, ((1, 4),)),
        "down_bias": bell_draw(seeds[12], (LAYERS, D), 0.3, 2.0),
        "second_gain": jnp.clip(1.0 + 0.18 * jax.random.normal(seeds[13], (LAYERS, D), jnp.float32), 0.099609375, 1.8984375).astype(jnp.bfloat16),
        "second_shift": bell_draw(seeds[14], (LAYERS, D), 0.3, 2.0),
    }


@jax.custom_vjp
def low(v):
    return lax.optimization_barrier(v.astype(jnp.bfloat16)).astype(jnp.float32)

@jax.custom_vjp
def low_back(v):
    return v

def low_keep(v):
    return (low(v), None)

def low_pass(kept, grad):
    return (grad,)

def back_keep(v):
    return (v, None)

def back_low(kept, grad):
    return (low(grad),)
low.defvjp(low_keep, low_pass)
low_back.defvjp(back_keep, back_low)
norm_eps = 1e-12
masked_value = -1000000000.0
highest = lax.Precision.HIGHEST

def layer_norm(residual, norm_gain, norm_shift):
    centred = residual - lax.optimization_barrier(jnp.mean(residual, axis=-1, keepdims=True))
    spread = lax.optimization_barrier(jnp.mean(centred * centred, axis=-1, keepdims=True))
    return centred * lax.rsqrt(spread + norm_eps) * norm_gain + norm_shift

def attend_block(block_items):
    query_rows, key_rows, value_rows, seg_row = block_items
    score_scale = HEAD ** (-0.5)
    raw_scores = jnp.einsum('qhd,khd->hqk', query_rows, key_rows, precision=highest) * score_scale
    same_doc = seg_row[:, None] == seg_row[None, :]
    scores = low_back(jnp.where(same_doc[None], raw_scores, masked_value))
    probability = jax.nn.softmax(scores, axis=-1)
    return jnp.einsum('hqk,khd->qhd', low(probability), value_rows, precision=highest)

def layer_forward(hidden, seg_ids, params):
    qkv_w, qv_b, proj_w, proj_b, gain_one, shift_one, up_w, up_b, down_w, down_b, gain_two, shift_two = params
    row_count = hidden.shape[0]
    seq_count = seg_ids.shape[0]
    projected = jnp.dot(low(hidden), qkv_w.reshape(D, 3 * D), precision=highest).reshape(row_count, 3, D)
    zero_row = jnp.zeros_like(qv_b[0])
    projected = low(low_back(projected + jnp.stack([qv_b[0], zero_row, qv_b[1]])))
    split_heads = projected.reshape(seq_count, LEN, 3, HEADS, HEAD)
    context = lax.map(jax.checkpoint(attend_block), (split_heads[:, :, 0], split_heads[:, :, 1], split_heads[:, :, 2], seg_ids))
    context = low(low_back(context.reshape(row_count, D)))
    attn_out = low_back(jnp.dot(context, proj_w, precision=highest) + proj_b)
    normed = layer_norm(hidden + attn_out, gain_one, shift_one)
    pre_act = low_back(jnp.dot(low(normed), up_w, precision=highest) + up_b)
    act_low = low(jax.nn.gelu(pre_act, approximate=False))
    ffn_out = low_back(jnp.dot(act_low, down_w, precision=highest) + down_b)
    return layer_norm(normed + ffn_out, gain_two, shift_two)

def network(rows_in, seg_ids, params):
    hidden = rows_in
    for layer_idx in range(LAYERS):
        hidden = layer_forward(hidden, seg_ids, tuple((stacked[layer_idx] for stacked in params)))
    return hidden

def reference(tokens, segment_ids, cotangent, qkv_weight, qv_bias, proj_weight, proj_bias, first_gain, first_shift, up_weight, up_bias, down_weight, down_bias, second_gain, second_shift):
    params = tuple((stacked.astype(jnp.float32) for stacked in (qkv_weight, qv_bias, proj_weight, proj_bias, first_gain, first_shift, up_weight, up_bias, down_weight, down_bias, second_gain, second_shift)))
    seq_count = tokens.shape[0]
    group_size = math.gcd(seq_count, max(1, 4096 // LEN))
    group_count = seq_count // group_size
    token_groups = tokens.astype(jnp.float32).reshape(group_count, group_size * LEN, D)
    seg_groups = segment_ids.reshape(group_count, group_size, LEN)
    cot_groups = cotangent.astype(jnp.float32).reshape(group_count, group_size * LEN, D)

    def one_group(totals, group_items):
        rows_in, seg_ids, cot_rows = group_items

        def forward(hidden_in, weights):
            return network(hidden_in, seg_ids, weights)
        output, pullback = jax.vjp(forward, rows_in, params)
        grad_rows, grad_params = pullback(cot_rows)
        return (jax.tree.map(jnp.add, totals, grad_params), (output, grad_rows))
    zero_grads = jax.tree.map(jnp.zeros_like, params)
    totals, (outputs, grad_inputs) = lax.scan(one_group, zero_grads, (token_groups, seg_groups, cot_groups))
    return (outputs.reshape(seq_count, LEN, D), grad_inputs.reshape(seq_count, LEN, D), totals[0], totals[1], totals[2], totals[3], totals[4], totals[5], totals[6], totals[7], totals[8], totals[9], totals[10], totals[11])
```

```python
import jax
import jax.numpy as jnp
from jax import lax
from jax.sharding import PartitionSpec as P

HEAD = 64


norm_eps = 1e-12
masked_value = -1000000000.0


def layer_norm(residual, norm_gain, norm_shift):
    centred = residual - jnp.mean(residual, axis=-1, keepdims=True)
    spread = jnp.mean(centred * centred, axis=-1, keepdims=True)
    return centred * lax.rsqrt(spread + norm_eps) * norm_gain + norm_shift


def gelu_exact(pre_act):
    return jax.nn.gelu(pre_act, approximate=False)


def masked_scores(query_rows, key_rows, seg_row):
    score_scale = query_rows.shape[-1] ** (-0.5)
    raw_scores = (
        jnp.einsum("qhd,khd->hqk", query_rows, key_rows, preferred_element_type=jnp.float32)
        * score_scale
    )
    same_doc = seg_row[:, None] == seg_row[None, :]
    return jnp.where(same_doc[None], raw_scores, masked_value)


def attend_forward(block_items):
    query_rows, key_rows, value_rows, seg_row = block_items
    scores = masked_scores(query_rows, key_rows, seg_row)
    row_max = jnp.max(scores, axis=-1, keepdims=True)
    exponent = jnp.exp(scores - row_max)
    row_total = jnp.sum(exponent, axis=-1, keepdims=True)
    probs_low = (exponent / row_total).astype(jnp.bfloat16)
    context = jnp.einsum("hqk,khd->qhd", probs_low, value_rows, preferred_element_type=jnp.float32)
    return (context.astype(jnp.bfloat16), row_max + jnp.log(row_total))


def attend_backward(block_items):
    query_rows, key_rows, value_rows, seg_row, log_total, grad_context = block_items
    score_scale = query_rows.shape[-1] ** (-0.5)
    scores = masked_scores(query_rows, key_rows, seg_row)
    probability = jnp.exp(scores - log_total)
    grad_probs = jnp.einsum(
        "qhd,khd->hqk", grad_context, value_rows, preferred_element_type=jnp.float32
    )
    row_inner = jnp.sum(probability * grad_probs, axis=-1, keepdims=True)
    grad_scores = (probability * (grad_probs - row_inner)).astype(jnp.bfloat16)
    grad_query = (
        jnp.einsum("hqk,khd->qhd", grad_scores, key_rows, preferred_element_type=jnp.float32)
        * score_scale
    )
    grad_key = (
        jnp.einsum("hqk,qhd->khd", grad_scores, query_rows, preferred_element_type=jnp.float32)
        * score_scale
    )
    grad_value = jnp.einsum(
        "hqk,qhd->khd",
        probability.astype(jnp.bfloat16),
        grad_context,
        preferred_element_type=jnp.float32,
    )
    return jnp.stack([grad_query, grad_key, grad_value], axis=1).astype(jnp.bfloat16)


def layer_forward(own_rows, full_low, params, seg_ids, reduce_rows, widen_rows):
    (
        qkv_w,
        qv_b,
        proj_w,
        proj_b,
        gain_one,
        shift_one,
        up_w,
        up_b,
        down_w,
        down_b,
        gain_two,
        shift_two,
    ) = params
    row_count, model_width = full_low.shape
    local_width = qkv_w.shape[-1]
    seq_count, length = seg_ids.shape
    projected = jnp.dot(
        full_low, qkv_w.reshape(model_width, 3 * local_width), preferred_element_type=jnp.float32
    )
    projected = projected.reshape(row_count, 3, local_width)
    zero_row = jnp.zeros_like(qv_b[0])
    projected = (projected + jnp.stack([qv_b[0], zero_row, qv_b[1]]).astype(jnp.float32)).astype(
        jnp.bfloat16
    )
    split_heads = projected.reshape(seq_count, length, 3, local_width // HEAD, HEAD)
    context, log_total = lax.map(
        attend_forward, (split_heads[:, :, 0], split_heads[:, :, 1], split_heads[:, :, 2], seg_ids)
    )
    context = context.reshape(row_count, local_width)
    attn_out = reduce_rows(
        jnp.dot(context, proj_w, preferred_element_type=jnp.float32)
    ) + proj_b.astype(jnp.float32)
    first_sum = own_rows + attn_out
    normed = layer_norm(first_sum, gain_one.astype(jnp.float32), shift_one.astype(jnp.float32))
    normed_low = widen_rows(normed.astype(jnp.bfloat16))
    pre_act = jnp.dot(normed_low, up_w, preferred_element_type=jnp.float32) + up_b.astype(
        jnp.float32
    )
    act_low = gelu_exact(pre_act).astype(jnp.bfloat16)
    ffn_out = reduce_rows(
        jnp.dot(act_low, down_w, preferred_element_type=jnp.float32)
    ) + down_b.astype(jnp.float32)
    second_sum = normed + ffn_out
    output = layer_norm(second_sum, gain_two.astype(jnp.float32), shift_two.astype(jnp.float32))
    kept_values = (
        full_low,
        projected,
        log_total,
        context,
        first_sum,
        normed_low,
        pre_act,
        second_sum,
    )
    return (output, kept_values)


def layer_backward(grad_own, kept_values, params, seg_ids, reduce_rows, widen_rows):
    (
        qkv_w,
        qv_b,
        proj_w,
        proj_b,
        gain_one,
        shift_one,
        up_w,
        up_b,
        down_w,
        down_b,
        gain_two,
        shift_two,
    ) = params
    full_low, projected, log_total, context, first_sum, normed_low, pre_act, second_sum = (
        kept_values
    )
    row_count, model_width = full_low.shape
    local_width = qkv_w.shape[-1]
    seq_count, length = seg_ids.shape
    unused, norm_pull = jax.vjp(
        layer_norm, second_sum, gain_two.astype(jnp.float32), shift_two.astype(jnp.float32)
    )
    grad_second, grad_gain_two, grad_shift_two = norm_pull(grad_own)
    branch_low = grad_second.astype(jnp.bfloat16)
    grad_down_b = jnp.sum(branch_low.astype(jnp.float32), axis=0)
    branch_full = widen_rows(branch_low)
    act_value, gelu_pull = jax.vjp(gelu_exact, pre_act)
    act_low = act_value.astype(jnp.bfloat16)
    grad_down_w = jnp.einsum("rf,rd->fd", act_low, branch_full, preferred_element_type=jnp.float32)
    grad_act = jnp.einsum("rd,fd->rf", branch_full, down_w, preferred_element_type=jnp.float32)
    (grad_pre,) = gelu_pull(grad_act)
    pre_low = grad_pre.astype(jnp.bfloat16)
    grad_up_b = jnp.sum(pre_low.astype(jnp.float32), axis=0)
    grad_up_w = jnp.einsum("rd,rf->df", normed_low, pre_low, preferred_element_type=jnp.float32)
    grad_normed = grad_second + reduce_rows(
        jnp.einsum("rf,df->rd", pre_low, up_w, preferred_element_type=jnp.float32)
    )
    unused, norm_pull = jax.vjp(
        layer_norm, first_sum, gain_one.astype(jnp.float32), shift_one.astype(jnp.float32)
    )
    grad_first, grad_gain_one, grad_shift_one = norm_pull(grad_normed)
    attn_low = grad_first.astype(jnp.bfloat16)
    grad_proj_b = jnp.sum(attn_low.astype(jnp.float32), axis=0)
    attn_full = widen_rows(attn_low)
    grad_proj_w = jnp.einsum("rc,rd->cd", context, attn_full, preferred_element_type=jnp.float32)
    grad_context = jnp.einsum(
        "rd,cd->rc", attn_full, proj_w, preferred_element_type=jnp.float32
    ).astype(jnp.bfloat16)
    head_count = local_width // HEAD
    split_heads = projected.reshape(seq_count, length, 3, head_count, HEAD)
    grad_heads = lax.map(
        attend_backward,
        (
            split_heads[:, :, 0],
            split_heads[:, :, 1],
            split_heads[:, :, 2],
            seg_ids,
            log_total,
            grad_context.reshape(seq_count, length, head_count, HEAD),
        ),
    )
    grad_proj = grad_heads.reshape(row_count, 3 * local_width)
    grad_qkv_w = jnp.einsum(
        "rd,rc->dc", full_low, grad_proj, preferred_element_type=jnp.float32
    ).reshape(model_width, 3, local_width)
    grad_sums = jnp.sum(grad_proj.astype(jnp.float32).reshape(row_count, 3, local_width), axis=0)
    grad_qv_b = jnp.stack([grad_sums[0], grad_sums[2]])
    flat_weight = qkv_w.reshape(model_width, 3 * local_width)
    grad_input = grad_first + reduce_rows(
        jnp.einsum("rc,dc->rd", grad_proj, flat_weight, preferred_element_type=jnp.float32)
    )
    big_layer = (grad_qkv_w, grad_proj_w, grad_up_w, grad_down_w)
    sharded_layer = (grad_qv_b, grad_up_b)
    shared_layer = (
        grad_proj_b,
        grad_gain_one,
        grad_shift_one,
        grad_down_b,
        grad_gain_two,
        grad_shift_two,
    )
    return (grad_input, big_layer, sharded_layer, shared_layer)


def local(
    tokens,
    segment_ids,
    cotangent,
    qkv_weight,
    qv_bias,
    proj_weight,
    proj_bias,
    first_gain,
    first_shift,
    up_weight,
    up_bias,
    down_weight,
    down_bias,
    second_gain,
    second_shift,
):
    seq_count, length, model_width = tokens.shape
    row_count = seq_count * length
    layers = qkv_weight.shape[0]
    tensor_size = lax.axis_size("tensor")
    share_rows = row_count // tensor_size
    tensor_pos = lax.axis_index("tensor")
    row_start = tensor_pos * share_rows

    def reduce_rows(partial_sum):
        return lax.psum_scatter(
            partial_sum.astype(jnp.bfloat16), "tensor", scatter_dimension=0, tiled=True
        ).astype(jnp.float32)

    def widen_rows(low_rows):
        return lax.all_gather(low_rows, "tensor", axis=0, tiled=True)

    def own_part(full_rows):
        return lax.dynamic_slice_in_dim(full_rows, row_start, share_rows, 0)

    def whole_rows(part_rows):
        return lax.all_gather(part_rows.astype(jnp.bfloat16), "tensor", axis=0, tiled=True).astype(
            part_rows.dtype
        )

    def whole_grads(grads):
        low = [g.astype(jnp.bfloat16).reshape(-1, model_width) for g in grads]
        rows = [g.shape[0] for g in low]
        share = lax.psum_scatter(
            jnp.concatenate(low), "dp", scatter_dimension=0, tiled=True
        )
        whole = lax.all_gather(share, "dp", axis=0, tiled=True)
        parts, at = [], 0
        for g, count in zip(grads, rows):
            parts.append(whole[at : at + count].reshape(g.shape))
            at += count
        return parts

    all_params = (
        qkv_weight,
        qv_bias,
        proj_weight,
        proj_bias,
        first_gain,
        first_shift,
        up_weight,
        up_bias,
        down_weight,
        down_bias,
        second_gain,
        second_shift,
    )
    flat_rows = tokens.reshape(row_count, model_width)
    own_rows = own_part(flat_rows.astype(jnp.float32))
    full_low = flat_rows
    kept_layers = []
    for layer_idx in range(layers):
        params = tuple((stacked[layer_idx] for stacked in all_params))
        output, kept_values = layer_forward(
            own_rows, full_low, params, segment_ids, reduce_rows, widen_rows
        )
        kept_layers.append(kept_values)
        own_rows = output
        if layer_idx + 1 < layers:
            full_low = widen_rows(output.astype(jnp.bfloat16))
    final_out = whole_rows(own_rows).reshape(seq_count, length, model_width)
    grad_own = own_part(cotangent.reshape(row_count, model_width).astype(jnp.float32))
    big_grads = [None] * layers
    sharded_grads = [None] * layers
    shared_grads = [None] * layers
    for layer_idx in range(layers - 1, -1, -1):
        params = tuple((stacked[layer_idx] for stacked in all_params))
        grad_own, big_layer, sharded_layer, shared_layer = layer_backward(
            grad_own, kept_layers[layer_idx], params, segment_ids, reduce_rows, widen_rows
        )
        big_grads[layer_idx] = big_layer
        sharded_grads[layer_idx] = sharded_layer
        shared_grads[layer_idx] = shared_layer
    input_grad = whole_rows(grad_own).reshape(seq_count, length, model_width)
    layer_big = [whole_grads(big_grads[layer_pos]) for layer_pos in range(layers)]
    whole_big = tuple(
        jnp.stack([layer_big[layer_pos][member].astype(jnp.float32) for layer_pos in range(layers)])
        for member in range(4)
    )
    sharded = jnp.concatenate(
        [
            jnp.stack([sharded_grads[p][0] for p in range(layers)]).reshape(-1),
            jnp.stack([sharded_grads[p][1] for p in range(layers)]).reshape(-1),
        ]
    )
    shared = jnp.concatenate(
        [
            jnp.stack([shared_grads[p][member] for p in range(layers)]).reshape(-1)
            for member in range(6)
        ]
    )
    tensor_sums = lax.all_gather(shared, "tensor").sum(axis=0)
    totals = lax.all_gather(jnp.concatenate([sharded, tensor_sums]), "dp").sum(axis=0)
    local_width = qv_bias.shape[-1]
    local_hidden = up_bias.shape[-1]
    at = layers * 2 * local_width
    qv_total = totals[:at].reshape(layers, 2, local_width)
    up_total = totals[at : at + layers * local_hidden].reshape(layers, local_hidden)
    rest = totals[at + layers * local_hidden :].reshape(6, layers, model_width)
    return (
        final_out,
        input_grad,
        whole_big[0],
        qv_total,
        whole_big[1],
        rest[0],
        rest[1],
        rest[2],
        whole_big[2],
        up_total,
        whole_big[3],
        rest[3],
        rest[4],
        rest[5],
    )


def solution(mesh):
    return jax.shard_map(
        local,
        mesh=mesh,
        in_specs=(
            P("dp", None, None),
            P("dp", None),
            P("dp", None, None),
            P(None, None, None, "tensor"),
            P(None, None, "tensor"),
            P(None, "tensor", None),
            P(),
            P(),
            P(),
            P(None, None, "tensor"),
            P(None, "tensor"),
            P(None, "tensor", None),
            P(),
            P(),
            P(),
        ),
        out_specs=(
            P("dp", None, None),
            P("dp", None, None),
            P(None, None, None, "tensor"),
            P(None, None, "tensor"),
            P(None, "tensor", None),
            P(),
            P(),
            P(),
            P(None, None, "tensor"),
            P(None, "tensor"),
            P(None, "tensor", None),
            P(),
            P(),
            P(),
        ),
        check_vma=False,
    )
```

```python
import functools
import math

import jax
import jax.numpy as jnp
from jax import lax
from jax.experimental import pallas as pl
from jax.experimental.pallas import tpu as pltpu
from jax.sharding import PartitionSpec as P

HEAD = 64


norm_eps = 1e-12
masked_value = -1000000000.0


def masked_scores(query_rows, key_rows, seg_row):
    score_scale = query_rows.shape[-1] ** (-0.5)
    raw_scores = (
        jnp.einsum("qhd,khd->hqk", query_rows, key_rows, preferred_element_type=jnp.float32)
        * score_scale
    )
    same_doc = seg_row[:, None] == seg_row[None, :]
    return jnp.where(same_doc[None], raw_scores, masked_value)


def attend_forward(block_items):
    query_rows, key_rows, value_rows, seg_row = block_items
    scores = masked_scores(query_rows, key_rows, seg_row)
    row_max = jnp.max(scores, axis=-1, keepdims=True)
    exponent = jnp.exp(scores - row_max)
    row_total = jnp.sum(exponent, axis=-1, keepdims=True)
    probs_low = (exponent / row_total).astype(jnp.bfloat16)
    context = jnp.einsum("hqk,khd->qhd", probs_low, value_rows, preferred_element_type=jnp.float32)
    return (context.astype(jnp.bfloat16), row_max + jnp.log(row_total))


def attend_backward(block_items):
    query_rows, key_rows, value_rows, seg_row, log_total, grad_context = block_items
    score_scale = query_rows.shape[-1] ** (-0.5)
    scores = masked_scores(query_rows, key_rows, seg_row)
    probability = jnp.exp(scores - log_total)
    grad_probs = jnp.einsum(
        "qhd,khd->hqk", grad_context, value_rows, preferred_element_type=jnp.float32
    )
    row_inner = jnp.sum(probability * grad_probs, axis=-1, keepdims=True)
    grad_scores = (probability * (grad_probs - row_inner)).astype(jnp.bfloat16)
    grad_query = (
        jnp.einsum("hqk,khd->qhd", grad_scores, key_rows, preferred_element_type=jnp.float32)
        * score_scale
    )
    grad_key = (
        jnp.einsum("hqk,qhd->khd", grad_scores, query_rows, preferred_element_type=jnp.float32)
        * score_scale
    )
    grad_value = jnp.einsum(
        "hqk,qhd->khd",
        probability.astype(jnp.bfloat16),
        grad_context,
        preferred_element_type=jnp.float32,
    )
    return jnp.stack([grad_query, grad_key, grad_value], axis=1).astype(jnp.bfloat16)


MESH = pl.DeviceIdType.MESH
F32 = jnp.float32
LOW = jnp.bfloat16
CHUNK = 32
LAG = 2
BLOCK = 64


def dot(a, b):
    return jnp.dot(a, b, preferred_element_type=F32)


def dot_t(a, b):
    return lax.dot_general(a, b, (((1,), (1,)), ((), ())), preferred_element_type=F32)


def dot_tn(a, b):
    return lax.dot_general(a, b, (((0,), (0,)), ((), ())), preferred_element_type=F32)


def greet(size):
    row, place = lax.axis_index("dp"), lax.axis_index("tensor")
    barrier = pltpu.get_barrier_semaphore()
    left, right = place > 0, place < size - 1

    @pl.when(left)
    def _():
        pl.semaphore_signal(barrier, inc=1, device_id=(row, place - 1), device_id_type=MESH)

    @pl.when(right)
    def _():
        pl.semaphore_signal(barrier, inc=1, device_id=(row, place + 1), device_id_type=MESH)

    @pl.when(left & right)
    def _():
        pl.semaphore_wait(barrier, 2)

    @pl.when(jnp.logical_not(left & right))
    def _():
        pl.semaphore_wait(barrier, 1)


def line_reduce(size, produce, finish, part, recv, outs, sems):
    sum_sent, sum_got, row_sent, row_got = sems
    row, place = lax.axis_index("dp"), lax.axis_index("tensor")
    half = part.shape[0] // 2
    chunks = half // CHUNK
    end = size - 1

    def rows_of(side, chunk):
        return pl.ds(pl.multiple_of(side * half + chunk * CHUNK, CHUNK), CHUNK)

    def sum_copy(side, chunk, target):
        rows = rows_of(side, chunk)
        return pltpu.make_async_remote_copy(
            src_ref=part.at[rows],
            dst_ref=recv.at[rows],
            send_sem=sum_sent.at[side, chunk],
            recv_sem=sum_got.at[side, chunk],
            device_id=(row, target),
            device_id_type=MESH,
        )

    def row_copy(which, side, chunk, target):
        rows = rows_of(side, chunk)
        return pltpu.make_async_remote_copy(
            src_ref=outs[which].at[rows],
            dst_ref=outs[which].at[rows],
            send_sem=row_sent.at[which, side, chunk],
            recv_sem=row_got.at[which, side, chunk],
            device_id=(row, target),
            device_id_type=MESH,
        )

    def side_facts(side):
        if side == 0:
            return place, place + 1, place - 1
        return end - place, place - 1, place + 1

    per_block = BLOCK // CHUNK

    def step(now, carry):
        @pl.when((now < chunks) & (lax.rem(now, per_block) == 0))
        def _():
            for side in range(2):
                produce(pl.ds(pl.multiple_of(side * half + now * CHUNK, CHUNK), BLOCK))

        for side in range(2):
            at, onward, back = side_facts(side)
            chunk = now - LAG * at

            @pl.when((chunk >= 0) & (chunk < chunks))
            def _():
                @pl.when(at > 0)
                def _():
                    sum_copy(side, chunk, onward).wait_recv()

                @pl.when(at < end)
                def _():
                    @pl.when(at > 0)
                    def _():
                        rows = rows_of(side, chunk)
                        part[rows] = (part[rows].astype(F32) + recv[rows].astype(F32)).astype(LOW)

                    sum_copy(side, chunk, onward).start()

                @pl.when(at == end)
                def _():
                    rows = rows_of(side, chunk)
                    own = pl.ds(pl.multiple_of(chunk * CHUNK, CHUNK), CHUNK)
                    finish(rows, own, part[rows].astype(F32) + recv[rows].astype(F32))
                    for which in range(len(outs)):
                        row_copy(which, side, chunk, back).start()

        for side in range(2):
            at, onward, back = side_facts(side)
            chunk = now - LAG * end - LAG * (end - at)

            @pl.when((at < end) & (chunk >= 0) & (chunk < chunks))
            def _():
                for which in range(len(outs)):
                    row_copy(which, side, chunk, back).wait_recv()

                    @pl.when(at > 0)
                    def _():
                        row_copy(which, side, chunk, back).start()

        return carry

    lax.fori_loop(0, chunks + 2 * LAG * end, step, 0)

    def drain(chunk, carry):
        for side in range(2):
            at, onward, back = side_facts(side)

            @pl.when(at < end)
            def _():
                sum_copy(side, chunk, onward).wait_send()

            @pl.when(at > 0)
            def _():
                for which in range(len(outs)):
                    row_copy(which, side, chunk, back).wait_send()

        return carry

    lax.fori_loop(0, chunks, drain, 0)


def normalize(residual):
    centred = residual - jnp.mean(residual, axis=-1, keepdims=True)
    inverse = lax.rsqrt(jnp.mean(centred * centred, axis=-1, keepdims=True) + norm_eps)
    return centred * inverse, inverse


def norm_back(grad, gain, unit, inverse):
    scaled = grad * gain
    return (
        scaled
        - jnp.mean(scaled, axis=-1, keepdims=True)
        - unit * jnp.mean(scaled * unit, axis=-1, keepdims=True)
    ) * inverse


def tally(total, values):
    total[...] += jnp.sum(values.reshape(-1, 8, values.shape[-1]), axis=0)


def line_call(size, collective, body, ins, out_shapes, rows, width, out_count, scratch=()):
    chunks = rows // 2 // CHUNK
    vmem = pl.BlockSpec(memory_space=pltpu.VMEM)
    return pl.pallas_call(
        body,
        out_shape=out_shapes,
        in_specs=[vmem] * len(ins),
        out_specs=[vmem] * len(out_shapes),
        scratch_shapes=[
            pltpu.VMEM((rows, width), LOW),
            pltpu.VMEM((rows, width), LOW),
            pltpu.SemaphoreType.DMA((2, chunks)),
            pltpu.SemaphoreType.DMA((2, chunks)),
            pltpu.SemaphoreType.DMA((out_count, 2, chunks)),
            pltpu.SemaphoreType.DMA((out_count, 2, chunks)),
            *scratch,
        ],
        compiler_params=pltpu.CompilerParams(
            collective_id=collective, has_side_effects=True, vmem_limit_bytes=56 << 20
        ),
    )(*ins)


def shape(*dims, kind=F32):
    return jax.ShapeDtypeStruct(dims, kind)


def attn_forward(size, collective, context, proj_w, proj_b, residual, gain, shift):
    rows, width = context.shape[0], proj_w.shape[1]
    half = rows // 2
    whole = residual.shape[0] == rows

    def body(context, proj_w, proj_b, residual, gain, shift, unit, inverse, normed, low, part, recv, *sems):
        greet(size)

        def produce(block):
            part[block] = dot(context[block], proj_w[...]).astype(LOW)

        def finish(at, own, total):
            came = residual[at if whole else own].astype(F32)
            unit_now, inverse_now = normalize(came + total + proj_b[...])
            unit[own] = unit_now
            inverse[own] = inverse_now
            result = unit_now * gain[...] + shift[...]
            normed[own] = result
            low[at] = result.astype(LOW)

        line_reduce(size, produce, finish, part, recv, [low], sems)

    return line_call(
        size,
        collective,
        body,
        (context, proj_w, proj_b, residual, gain, shift),
        (shape(half, width), shape(half, 1), shape(half, width), shape(rows, width, kind=LOW)),
        rows,
        width,
        1,
    )


def ffn_forward(size, collective, normed_low, normed, up_w, up_b, down_w, down_b, gain, shift, cotangent=None):
    rows, width = normed_low.shape
    hidden = up_w.shape[1]
    half = rows // 2
    last = cotangent is not None

    def body(*refs):
        normed_low, normed, up_w, up_b, down_w, down_b, gain, shift = refs[:8]
        rest = refs[8:]
        if last:
            cotangent, *rest = rest
            act, slope, grad, low, mixed, gain_sum, shift_sum, bias_sum, part, recv, *sems = rest
            outs = [low, mixed]
            for total in (gain_sum, shift_sum, bias_sum):
                total[...] = jnp.zeros_like(total)
        else:
            act, slope, unit, inverse, out, low, part, recv, *sems = rest
            outs = [low]
        greet(size)

        def produce(block):
            pre = dot(normed_low[block], up_w[...]) + up_b[...]
            cdf = 0.5 * lax.erf(pre * math.sqrt(0.5)) + 0.5
            act_now = (pre * cdf).astype(LOW)
            slope[block] = (
                cdf + pre * jnp.exp(-0.5 * pre * pre) * (1.0 / math.sqrt(2 * math.pi))
            ).astype(LOW)
            act[block] = act_now
            part[block] = dot(act_now, down_w[...]).astype(LOW)

        def finish(at, own, total):
            unit_now, inverse_now = normalize(normed[own] + total + down_b[...])
            result = unit_now * gain[...] + shift[...]
            if last:
                mixed[at] = result.astype(LOW)
                grad_in = cotangent[at].astype(F32)
                grad_now = norm_back(grad_in, gain[...], unit_now, inverse_now)
                grad[own] = grad_now
                grad_low = grad_now.astype(LOW)
                low[at] = grad_low
                tally(gain_sum, grad_in * unit_now)
                tally(shift_sum, grad_in)
                tally(bias_sum, grad_low.astype(F32))
            else:
                unit[own] = unit_now
                inverse[own] = inverse_now
                out[own] = result
                low[at] = result.astype(LOW)

        line_reduce(size, produce, finish, part, recv, outs, sems)

    ins = [normed_low, normed, up_w, up_b, down_w, down_b, gain, shift]
    outs = [shape(rows, hidden, kind=LOW), shape(rows, hidden, kind=LOW)]
    if last:
        ins += [cotangent]
        outs += [shape(half, width), shape(rows, width, kind=LOW), shape(rows, width, kind=LOW)]
        outs += [shape(8, width)] * 3
    else:
        outs += [shape(half, width), shape(half, 1), shape(half, width), shape(rows, width, kind=LOW)]
    return line_call(size, collective, body, ins, outs, rows, width, 2 if last else 1)


def ffn_backward(size, collective, branch_low, grad_second, slope, up_w, down_w, unit, inverse, gain):
    rows, width = branch_low.shape
    hidden = up_w.shape[1]
    half = rows // 2

    def body(branch_low, grad_second, slope, up_w, down_w, unit, inverse, gain, pre, grad, low, gain_sum, shift_sum, bias_sum, part, recv, *sems):
        for total in (gain_sum, shift_sum, bias_sum):
            total[...] = jnp.zeros_like(total)
        greet(size)

        def produce(block):
            pre_now = (dot_t(branch_low[block], down_w[...]) * slope[block].astype(F32)).astype(LOW)
            pre[block] = pre_now
            part[block] = dot_t(pre_now, up_w[...]).astype(LOW)

        def finish(at, own, total):
            grad_in = grad_second[own] + total
            unit_now = unit[own]
            grad_now = norm_back(grad_in, gain[...], unit_now, inverse[own])
            grad[own] = grad_now
            grad_low = grad_now.astype(LOW)
            low[at] = grad_low
            tally(gain_sum, grad_in * unit_now)
            tally(shift_sum, grad_in)
            tally(bias_sum, grad_low.astype(F32))

        line_reduce(size, produce, finish, part, recv, [low], sems)

    return line_call(
        size,
        collective,
        body,
        (branch_low, grad_second, slope, up_w, down_w, unit, inverse, gain),
        [shape(rows, hidden, kind=LOW), shape(half, width), shape(rows, width, kind=LOW)]
        + [shape(8, width)] * 3,
        rows,
        width,
        1,
    )


def attn_backward(size, collective, grad_proj, grad_first, qkv_w, below=None):
    rows, width = grad_proj.shape[0], qkv_w.shape[0]
    half = rows // 2
    inner = below is not None

    def body(grad_proj, grad_first, qkv_w, *rest):
        if inner:
            unit, inverse, gain, grad, low, gain_sum, shift_sum, bias_sum, part, recv, *sems = rest
            for total in (gain_sum, shift_sum, bias_sum):
                total[...] = jnp.zeros_like(total)
        else:
            low, part, recv, *sems = rest
        greet(size)

        def produce(block):
            part[block] = dot_t(grad_proj[block], qkv_w[...]).astype(LOW)

        def finish(at, own, total):
            grad_in = grad_first[own] + total
            if not inner:
                low[at] = grad_in.astype(LOW)
                return
            unit_now = unit[own]
            grad_now = norm_back(grad_in, gain[...], unit_now, inverse[own])
            grad[own] = grad_now
            grad_low = grad_now.astype(LOW)
            low[at] = grad_low
            tally(gain_sum, grad_in * unit_now)
            tally(shift_sum, grad_in)
            tally(bias_sum, grad_low.astype(F32))

        line_reduce(size, produce, finish, part, recv, [low], sems)

    ins = [grad_proj, grad_first, qkv_w]
    outs = [shape(rows, width, kind=LOW)]
    if inner:
        ins += list(below)
        outs = [shape(half, width), *outs] + [shape(8, width)] * 3
    return line_call(size, collective, body, ins, outs, rows, width, 1)


def local(
    tokens,
    segment_ids,
    cotangent,
    qkv_weight,
    qv_bias,
    proj_weight,
    proj_bias,
    first_gain,
    first_shift,
    up_weight,
    up_bias,
    down_weight,
    down_bias,
    second_gain,
    second_shift,
):
    seq_count, length, width = tokens.shape
    rows = seq_count * length
    layers = qkv_weight.shape[0]
    size = lax.axis_size("tensor")
    part_width = qkv_weight.shape[-1]
    heads = part_width // HEAD
    seg_row = segment_ids.reshape(length)

    def row_of(stacked, layer):
        return stacked[layer].astype(F32).reshape(1, -1)

    low = tokens.reshape(rows, width)
    residual = low
    cot = cotangent.reshape(rows, width)
    kept = []
    for layer in range(layers):
        qkv = qkv_weight[layer].reshape(width, 3 * part_width)
        bias = jnp.concatenate([qv_bias[layer, 0], jnp.zeros_like(qv_bias[layer, 0]), qv_bias[layer, 1]])
        projected = (dot(low, qkv) + bias.astype(F32)).astype(LOW)
        split = projected.reshape(length, 3, heads, HEAD)
        context, log_total = attend_forward((split[:, 0], split[:, 1], split[:, 2], seg_row))
        context = context.reshape(rows, part_width)
        unit_one, inverse_one, normed, normed_low = attn_forward(
            size,
            2 * layer,
            context,
            proj_weight[layer],
            row_of(proj_bias, layer),
            residual,
            row_of(first_gain, layer),
            row_of(first_shift, layer),
        )
        ffn_in = (
            normed_low,
            normed,
            up_weight[layer],
            row_of(up_bias, layer),
            down_weight[layer],
            row_of(down_bias, layer),
            row_of(second_gain, layer),
            row_of(second_shift, layer),
        )
        keep = (low, qkv, split, log_total, context, unit_one, inverse_one, normed_low)
        if layer + 1 < layers:
            act, slope, unit_two, inverse_two, residual, low = ffn_forward(size, 2 * layer + 1, *ffn_in)
            kept.append((*keep, act, slope, unit_two, inverse_two))
        else:
            act, slope, grad, branch_low, mixed, *two_sums = ffn_forward(size, 2 * layer + 1, *ffn_in, cot)
            kept.append((*keep, act, slope, None, None))

    def whole_grads(grads):
        low_grads = [g.astype(LOW).reshape(-1, width) for g in grads]
        counts = [g.shape[0] for g in low_grads]
        share = lax.psum_scatter(jnp.concatenate(low_grads), "dp", scatter_dimension=0, tiled=True)
        whole = lax.all_gather(share, "dp", axis=0, tiled=True)
        parts, at = [], 0
        for g, count in zip(grads, counts):
            parts.append(whole[at : at + count].reshape(g.shape))
            at += count
        return parts

    big = [None] * layers
    sharded = [None] * layers
    shared = [None] * layers
    for layer in range(layers - 1, -1, -1):
        (low, qkv, split, log_total, context, unit_one, inverse_one, normed_low, act, slope, _, _) = kept[layer]
        pre, grad_first, attn_low, *one_sums = ffn_backward(
            size,
            2 * layers + 2 * layer,
            branch_low,
            grad,
            slope,
            up_weight[layer],
            down_weight[layer],
            unit_one,
            inverse_one,
            row_of(first_gain, layer),
        )
        grad_context = dot_t(attn_low, proj_weight[layer]).astype(LOW)
        grad_heads = attend_backward(
            (
                split[:, 0],
                split[:, 1],
                split[:, 2],
                seg_row,
                log_total,
                grad_context.reshape(length, heads, HEAD),
            )
        )
        grad_proj = grad_heads.reshape(rows, 3 * part_width)
        grad_down = dot_tn(act, branch_low)
        grad_up = dot_tn(normed_low, pre)
        layer_sums = (one_sums, two_sums)
        if layer > 0:
            unit_two, inverse_two = kept[layer - 1][-2:]
            grad, branch_low, *two_sums = attn_backward(
                size,
                2 * layers + 2 * layer + 1,
                grad_proj,
                grad_first,
                qkv,
                (unit_two, inverse_two, row_of(second_gain, layer - 1)),
            )
        else:
            (input_grad,) = attn_backward(size, 2 * layers + 1, grad_proj, grad_first, qkv)
        grad_proj_w = dot_tn(context, attn_low)
        grad_qkv = dot_tn(low, grad_proj).reshape(width, 3, part_width)
        big[layer] = whole_grads([grad_qkv, grad_proj_w, grad_up, grad_down])
        sums = jnp.sum(grad_proj.astype(F32).reshape(rows, 3, part_width), axis=0)
        sharded[layer] = (jnp.stack([sums[0], sums[2]]), jnp.sum(pre.astype(F32), axis=0))
        (gain_one, shift_one, proj_b), (gain_two, shift_two, down_b) = layer_sums
        shared[layer] = (proj_b, gain_one, shift_one, down_b, gain_two, shift_two)

    whole_big = [
        jnp.stack([big[layer][member].astype(F32) for layer in range(layers)]) for member in range(4)
    ]
    sharded_flat = jnp.concatenate(
        [jnp.stack([sharded[p][member] for p in range(layers)]).reshape(-1) for member in range(2)]
    )
    shared_flat = jnp.concatenate(
        [jnp.sum(shared[p][member], axis=0) for member in range(6) for p in range(layers)]
    )
    tensor_sums = lax.all_gather(shared_flat, "tensor").sum(axis=0)
    totals = lax.all_gather(jnp.concatenate([sharded_flat, tensor_sums]), "dp").sum(axis=0)
    at = layers * 2 * part_width
    qv_total = totals[:at].reshape(layers, 2, part_width)
    to = at + layers * up_bias.shape[-1]
    up_total = totals[at:to].reshape(layers, -1)
    rest = totals[to:].reshape(6, layers, width)
    return (
        mixed.astype(F32).reshape(tokens.shape),
        input_grad.astype(F32).reshape(tokens.shape),
        whole_big[0],
        qv_total,
        whole_big[1],
        rest[0],
        rest[1],
        rest[2],
        whole_big[2],
        up_total,
        whole_big[3],
        rest[3],
        rest[4],
        rest[5],
    )


def solution(mesh):
    return jax.shard_map(
        local,
        mesh=mesh,
        in_specs=(
            P("dp", None, None),
            P("dp", None),
            P("dp", None, None),
            P(None, None, None, "tensor"),
            P(None, None, "tensor"),
            P(None, "tensor", None),
            P(),
            P(),
            P(),
            P(None, None, "tensor"),
            P(None, "tensor"),
            P(None, "tensor", None),
            P(),
            P(),
            P(),
        ),
        out_specs=(
            P("dp", None, None),
            P("dp", None, None),
            P(None, None, None, "tensor"),
            P(None, None, "tensor"),
            P(None, "tensor", None),
            P(),
            P(),
            P(),
            P(None, None, "tensor"),
            P(None, "tensor"),
            P(None, "tensor", None),
            P(),
            P(),
            P(),
        ),
        check_vma=False,
    )
```

```python
import math
import types

import jax
import jax.numpy as jnp
from jax import lax
from jax.experimental import pallas as pl
from jax.experimental.pallas import tpu as pltpu
from jax.sharding import PartitionSpec as P

HEAD = 64


norm_eps = 1e-12
masked_value = -1000000000.0


def masked_scores(query_rows, key_rows, seg_row):
    score_scale = query_rows.shape[-1] ** (-0.5)
    raw_scores = (
        jnp.einsum("qhd,khd->hqk", query_rows, key_rows, preferred_element_type=jnp.float32)
        * score_scale
    )
    same_doc = seg_row[:, None] == seg_row[None, :]
    return jnp.where(same_doc[None], raw_scores, masked_value)


def attend_forward(block_items):
    query_rows, key_rows, value_rows, seg_row = block_items
    scores = masked_scores(query_rows, key_rows, seg_row)
    row_max = jnp.max(scores, axis=-1, keepdims=True)
    exponent = jnp.exp(scores - row_max)
    row_total = jnp.sum(exponent, axis=-1, keepdims=True)
    probs_low = (exponent / row_total).astype(jnp.bfloat16)
    context = jnp.einsum("hqk,khd->qhd", probs_low, value_rows, preferred_element_type=jnp.float32)
    return (context.astype(jnp.bfloat16), row_max + jnp.log(row_total))


def attend_backward(block_items):
    query_rows, key_rows, value_rows, seg_row, log_total, grad_context = block_items
    score_scale = query_rows.shape[-1] ** (-0.5)
    scores = masked_scores(query_rows, key_rows, seg_row)
    probability = jnp.exp(scores - log_total)
    grad_probs = jnp.einsum(
        "qhd,khd->hqk", grad_context, value_rows, preferred_element_type=jnp.float32
    )
    row_inner = jnp.sum(probability * grad_probs, axis=-1, keepdims=True)
    grad_scores = (probability * (grad_probs - row_inner)).astype(jnp.bfloat16)
    grad_query = (
        jnp.einsum("hqk,khd->qhd", grad_scores, key_rows, preferred_element_type=jnp.float32)
        * score_scale
    )
    grad_key = (
        jnp.einsum("hqk,qhd->khd", grad_scores, query_rows, preferred_element_type=jnp.float32)
        * score_scale
    )
    grad_value = jnp.einsum(
        "hqk,qhd->khd",
        probability.astype(jnp.bfloat16),
        grad_context,
        preferred_element_type=jnp.float32,
    )
    return jnp.stack([grad_query, grad_key, grad_value], axis=1).astype(jnp.bfloat16)


MESH = pl.DeviceIdType.MESH
F32 = jnp.float32
LOW = jnp.bfloat16
CHUNK = 32
LAG = 2
PIECE = 256


def dot(a, b):
    return jnp.dot(a, b, preferred_element_type=F32)


def dot_t(a, b):
    return lax.dot_general(a, b, (((1,), (1,)), ((), ())), preferred_element_type=F32)


def dot_tn(a, b):
    return lax.dot_general(a, b, (((0,), (0,)), ((), ())), preferred_element_type=F32)


def here():
    return lax.axis_index("dp"), lax.axis_index("tensor")


def greet(size, line=True, targets=()):
    row, place = here()
    barrier = pltpu.get_barrier_semaphore()
    for count, target in targets:

        def signal(index, carry):
            pl.semaphore_signal(barrier, inc=1, device_id=target(index), device_id_type=MESH)
            return carry

        lax.fori_loop(0, count, signal, 0)
    expected = sum(count for count, _ in targets)
    if not line:
        pl.semaphore_wait(barrier, expected)
        return
    left, right = place > 0, place < size - 1

    @pl.when(left)
    def _():
        pl.semaphore_signal(barrier, inc=1, device_id=(row, place - 1), device_id_type=MESH)

    @pl.when(right)
    def _():
        pl.semaphore_signal(barrier, inc=1, device_id=(row, place + 1), device_id_type=MESH)

    @pl.when(left & right)
    def _():
        pl.semaphore_wait(barrier, expected + 2)

    @pl.when(jnp.logical_not(left & right))
    def _():
        pl.semaphore_wait(barrier, expected + 1)


def partner():
    row, place = here()
    return (row + 1 - 2 * lax.rem(row, 2), place)


def plane_peer(chips, index):
    row, place = here()
    return (lax.rem(row // 2 + index + 1, chips) * 2 + lax.rem(row, 2), place)


def line_loop(size, stages, extras=()):
    row, place = here()
    half = stages[0].part.shape[0] // 2
    chunks = half // CHUNK
    end = size - 1
    span = 2 * LAG * end

    def rows_of(side, chunk):
        return pl.ds(pl.multiple_of(side * half + chunk * CHUNK, CHUNK), CHUNK)

    def sum_copy(stage, side, chunk, target):
        rows = rows_of(side, chunk)
        return pltpu.make_async_remote_copy(
            src_ref=stage.part.at[rows],
            dst_ref=stage.recv.at[rows],
            send_sem=stage.sems[0].at[side, chunk],
            recv_sem=stage.sems[1].at[side, chunk],
            device_id=(row, target),
            device_id_type=MESH,
        )

    def row_copy(stage, which, side, chunk, target):
        rows = rows_of(side, chunk)
        return pltpu.make_async_remote_copy(
            src_ref=stage.outs[which].at[rows],
            dst_ref=stage.outs[which].at[rows],
            send_sem=stage.sems[2].at[which, side, chunk],
            recv_sem=stage.sems[3].at[which, side, chunk],
            device_id=(row, target),
            device_id_type=MESH,
        )

    def side_facts(side):
        if side == 0:
            return place, place + 1, place - 1
        return end - place, place - 1, place + 1

    def bring_back(stage, since):
        for side in range(2):
            at, onward, back = side_facts(side)
            chunk = since - LAG * end - LAG * (end - at)

            @pl.when((at < end) & (chunk >= 0) & (chunk < chunks))
            def _():
                for which in range(len(stage.outs)):
                    row_copy(stage, which, side, chunk, back).wait_recv()

                    @pl.when(at > 0)
                    def _():
                        row_copy(stage, which, side, chunk, back).start()

    def sum_up(stage, since):
        for side in range(2):
            at, onward, back = side_facts(side)
            chunk = since - LAG * at

            @pl.when((chunk >= 0) & (chunk < chunks))
            def _():
                @pl.when(at > 0)
                def _():
                    sum_copy(stage, side, chunk, onward).wait_recv()

                @pl.when(at < end)
                def _():
                    @pl.when(at > 0)
                    def _():
                        rows = rows_of(side, chunk)
                        total = stage.part[rows].astype(F32) + stage.recv[rows].astype(F32)
                        stage.part[rows] = total.astype(LOW)

                    sum_copy(stage, side, chunk, onward).start()

                @pl.when(at == end)
                def _():
                    rows = rows_of(side, chunk)
                    own = pl.ds(pl.multiple_of(chunk * CHUNK, CHUNK), CHUNK)
                    stage.finish(rows, own, stage.part[rows].astype(F32) + stage.recv[rows].astype(F32))
                    for which in range(len(stage.outs)):
                        row_copy(stage, which, side, chunk, back).start()

    def step(now, carry):
        for number, stage in enumerate(stages):
            bring_back(stage, now - number * span)
        for number, stage in enumerate(stages):
            since = now - number * span

            @pl.when((since >= 0) & (since < chunks))
            def _():
                for side in range(2):
                    stage.produce(rows_of(side, since))

            sum_up(stage, since)
        for first, count, work in extras:

            @pl.when((now >= first) & (now < first + count))
            def _():
                work(now - first)

        return carry

    lax.fori_loop(0, chunks + span * len(stages), step, 0)

    def drain(chunk, carry):
        for stage in stages:
            for side in range(2):
                at, onward, back = side_facts(side)

                @pl.when(at < end)
                def _():
                    sum_copy(stage, side, chunk, onward).wait_send()

                @pl.when(at > 0)
                def _():
                    for which in range(len(stage.outs)):
                        row_copy(stage, which, side, chunk, back).wait_send()

        return carry

    lax.fori_loop(0, chunks, drain, 0)


def by_rows(count, work, block=32):
    def one(index, carry):
        work(pl.ds(pl.multiple_of(index * block, block), block), index * block)
        return carry

    block = min(block, count)
    lax.fori_loop(0, count // block, one, 0)


class Spread:
    def __init__(self, chips, rows, width, grads, near, far, share, whole, sems):
        self.chips, self.half = chips, rows // 2
        self.count = self.half // chips
        self.grads, self.near, self.far, self.share, self.whole = grads, near, far, share, whole
        self.near_sems, self.far_sems, self.back_sems, self.last_sems = sems
        row, _ = here()
        self.core, self.chip = lax.rem(row, 2), row // 2

    @staticmethod
    def scratch(chips, rows, width):
        half = rows // 2
        pair = pltpu.SemaphoreType.DMA((2,))
        many = pltpu.SemaphoreType.DMA((2, chips - 1))
        return [
            pltpu.VMEM((half, width), LOW),
            pltpu.VMEM((chips - 1, half // chips, width), LOW),
            pair,
            many,
            many,
            pair,
        ]

    def half_rows(self, core):
        return pl.ds(pl.multiple_of(core * self.half, 16), self.half)

    def near_copy(self):
        return pltpu.make_async_remote_copy(
            src_ref=self.grads.at[self.half_rows(1 - self.core)],
            dst_ref=self.near,
            send_sem=self.near_sems.at[0],
            recv_sem=self.near_sems.at[1],
            device_id=partner(),
            device_id_type=MESH,
        )

    def far_copy(self, index):
        chip = lax.rem(self.chip + index + 1, self.chips)
        return pltpu.make_async_remote_copy(
            src_ref=self.near.at[pl.ds(pl.multiple_of(chip * self.count, 16), self.count)],
            dst_ref=self.far.at[index],
            send_sem=self.far_sems.at[0, index],
            recv_sem=self.far_sems.at[1, index],
            device_id=plane_peer(self.chips, index),
            device_id_type=MESH,
        )

    def back_copy(self, index):
        to = pl.multiple_of(self.core * self.half + self.chip * self.count, 16)
        return pltpu.make_async_remote_copy(
            src_ref=self.share,
            dst_ref=self.whole.at[pl.ds(to, self.count)],
            send_sem=self.back_sems.at[0, index],
            recv_sem=self.back_sems.at[1, index],
            device_id=plane_peer(self.chips, index),
            device_id_type=MESH,
        )

    def last_copy(self):
        rows = self.half_rows(self.core)
        return pltpu.make_async_remote_copy(
            src_ref=self.whole.at[rows],
            dst_ref=self.whole.at[rows],
            send_sem=self.last_sems.at[0],
            recv_sem=self.last_sems.at[1],
            device_id=partner(),
            device_id_type=MESH,
        )

    def each(self, work):
        def one(index, carry):
            work(index)
            return carry

        lax.fori_loop(0, self.chips - 1, one, 0)

    def to_partner(self):
        self.near_copy().start()

    def to_chips(self):
        self.near_copy().wait_recv()
        base = self.core * self.half

        def add(rows, first):
            own = self.grads[pl.ds(pl.multiple_of(base + first, 16), rows.size)]
            self.near[rows] = (self.near[rows].astype(F32) + own.astype(F32)).astype(LOW)

        by_rows(self.half, add)
        self.each(lambda index: self.far_copy(index).start())

    def sum_share(self):
        self.each(lambda index: self.far_copy(index).wait_recv())
        base = self.chip * self.count

        def add(rows, first):
            total = self.near[pl.ds(pl.multiple_of(base + first, 16), rows.size)].astype(F32)
            if self.chips <= 4:
                for index in range(self.chips - 1):
                    total += self.far[index, rows].astype(F32)
            else:
                total = lax.fori_loop(
                    0, self.chips - 1, lambda index, so_far: so_far + self.far[index, rows].astype(F32), total
                )
            self.share[rows] = total.astype(LOW)

        by_rows(self.count, add)

    def settle_sum(self):
        self.near_copy().wait_send()
        self.each(lambda index: self.far_copy(index).wait_send())

    def give_share(self):
        self.each(lambda index: self.back_copy(index).start())
        base = self.core * self.half + self.chip * self.count

        def keep(rows, first):
            self.whole[pl.ds(pl.multiple_of(base + first, 16), rows.size)] = self.share[rows]

        by_rows(self.count, keep)

    def to_other_core(self):
        self.each(lambda index: self.back_copy(index).wait_recv())
        self.last_copy().start()

    def settle_whole(self):
        self.last_copy().wait_recv()
        self.last_copy().wait_send()
        self.each(lambda index: self.back_copy(index).wait_send())


def normalize(residual):
    centred = residual - jnp.mean(residual, axis=-1, keepdims=True)
    inverse = lax.rsqrt(jnp.mean(centred * centred, axis=-1, keepdims=True) + norm_eps)
    return centred * inverse, inverse


def norm_back(grad, gain, unit, inverse):
    scaled = grad * gain
    return (
        scaled
        - jnp.mean(scaled, axis=-1, keepdims=True)
        - unit * jnp.mean(scaled * unit, axis=-1, keepdims=True)
    ) * inverse


def tally(total, values):
    total[...] += jnp.sum(values.reshape(-1, 8, values.shape[-1]), axis=0)


def call(collective, body, ins, outs, scratch):
    vmem = pl.BlockSpec(memory_space=pltpu.VMEM)
    names = [*ins, *outs]
    extra = {name: spec if isinstance(spec, list) else [spec] for name, spec in scratch.items()}

    def run(*refs):
        named = dict(zip(names, refs))
        rest = list(refs[len(names) :])
        for name, specs in extra.items():
            taken = [rest.pop(0) for _ in specs]
            named[name] = taken if isinstance(scratch[name], list) else taken[0]
        body(types.SimpleNamespace(**named))

    results = pl.pallas_call(
        run,
        out_shape=list(outs.values()),
        in_specs=[vmem] * len(ins),
        out_specs=[vmem] * len(outs),
        scratch_shapes=[spec for specs in extra.values() for spec in specs],
        compiler_params=pltpu.CompilerParams(
            collective_id=collective, has_side_effects=True, vmem_limit_bytes=60 << 20
        ),
    )(*ins.values())
    return types.SimpleNamespace(**dict(zip(outs, results)))


def shape(*dims, kind=F32):
    return jax.ShapeDtypeStruct(dims, kind)


def line_scratch(rows, width, outs=1):
    chunks = rows // 2 // CHUNK
    return [
        pltpu.VMEM((rows, width), LOW),
        pltpu.VMEM((rows, width), LOW),
        pltpu.SemaphoreType.DMA((2, chunks)),
        pltpu.SemaphoreType.DMA((2, chunks)),
        pltpu.SemaphoreType.DMA((outs, 2, chunks)),
        pltpu.SemaphoreType.DMA((outs, 2, chunks)),
    ]


def stage_of(produce, finish, outs, scratch):
    part, recv, *sems = scratch
    return types.SimpleNamespace(
        produce=produce, finish=finish, outs=outs, part=part, recv=recv, sems=sems
    )


def clear(*refs):
    for ref in refs:
        ref[...] = jnp.zeros_like(ref)


def proj_stage(r, whole):
    def produce(block):
        r.proj_line[0][block] = dot(r.context[block], r.proj_w[...]).astype(LOW)

    def finish(at, own, total):
        came = r.residual[at if whole else own].astype(F32)
        unit, inverse = normalize(came + total + r.proj_b[...])
        r.unit_one[own] = unit
        r.inverse_one[own] = inverse
        result = unit * r.gain_one[...] + r.shift_one[...]
        r.normed[own] = result
        r.normed_low[at] = result.astype(LOW)

    return stage_of(produce, finish, [r.normed_low], r.proj_line)


def ffn_stage(r, last):
    def produce(block):
        pre = dot(r.normed_low[block], r.up_w[...]) + r.up_b[...]
        cdf = 0.5 * lax.erf(pre * math.sqrt(0.5)) + 0.5
        act = (pre * cdf).astype(LOW)
        slope = cdf + pre * jnp.exp(-0.5 * pre * pre) * (1.0 / math.sqrt(2 * math.pi))
        r.slope[block] = slope.astype(LOW)
        r.act[block] = act
        r.ffn_line[0][block] = dot(act, r.down_w[...]).astype(LOW)

    def finish(at, own, total):
        unit, inverse = normalize(r.normed[own] + total + r.down_b[...])
        result = unit * r.gain_two[...] + r.shift_two[...]
        if last:
            r.mixed_own[own] = result.astype(LOW)
            grad_in = r.cotangent[at].astype(F32)
            grad = norm_back(grad_in, r.gain_two[...], unit, inverse)
            r.grad_second[own] = grad
            r.branch[at] = grad.astype(LOW)
            tally(r.sums.at[0], grad_in * unit)
            tally(r.sums.at[1], grad_in)
            tally(r.sums.at[2], grad.astype(LOW).astype(F32))
        else:
            r.unit_two[own] = unit
            r.inverse_two[own] = inverse
            r.hidden[own] = result
            r.low[at] = result.astype(LOW)

    return stage_of(produce, finish, [r.branch if last else r.low], r.ffn_line)


def ffn_back_stage(r):
    def produce(block):
        pre = (dot_t(r.branch[block], r.down_w[...]) * r.slope[block].astype(F32)).astype(LOW)
        r.pre[block] = pre
        tally(r.up_sum, pre.astype(F32))
        r.back_line[0][block] = dot_t(pre, r.up_w[...]).astype(LOW)

    def finish(at, own, total):
        grad_in = r.grad_second[own] + total
        unit = r.unit_one[own]
        grad = norm_back(grad_in, r.gain_one[...], unit, r.inverse_one[own])
        r.grad_first[own] = grad
        r.attn_low[at] = grad.astype(LOW)
        tally(r.sums.at[3], grad_in * unit)
        tally(r.sums.at[4], grad_in)
        tally(r.sums.at[5], grad.astype(LOW).astype(F32))

    return stage_of(produce, finish, [r.attn_low], r.back_line)


def columns(piece):
    return pl.ds(pl.multiple_of(piece * PIECE, PIECE), PIECE)


def ffn_grads(r, out, first):
    width, hidden = r.up_w.shape

    def up(piece):
        rows = pl.ds(pl.multiple_of(piece * PIECE, PIECE), PIECE)
        out[rows] = dot_tn(r.normed_low[:, columns(piece)], r.pre[...]).astype(LOW)

    def down(piece):
        rows = pl.ds(pl.multiple_of(width + piece * PIECE, PIECE), PIECE)
        out[rows] = dot_tn(r.act[:, columns(piece)], r.branch[...]).astype(LOW)

    return [(first, width // PIECE, up), (first + width // PIECE, hidden // PIECE, down)]


def attn_grads(r, out, first):
    split = r.grad_proj.shape[1]

    def piece_of(piece):
        rows = pl.ds(pl.multiple_of(piece * PIECE, PIECE), PIECE)
        out[rows, :split] = dot_tn(r.low_in[:, columns(piece)], r.grad_proj[...]).astype(LOW)
        out[rows, split:] = dot_tn(r.attn_low_in[:, columns(piece)], r.context_in[...]).astype(LOW)

    return [(first, r.low_in.shape[1] // PIECE, piece_of)]


def at_step(step, work):
    return (step, 1, lambda index: work())


def forward_kernel(size, collective, context, proj, residual, ffn):
    rows, width = context.shape[0], proj[0].shape[1]
    half, hidden = rows // 2, ffn[0].shape[1]
    whole = residual.shape[0] == rows

    def body(r):
        greet(size)
        line_loop(size, [proj_stage(r, whole), ffn_stage(r, False)])

    ins = dict(context=context, residual=residual)
    ins.update(zip(("proj_w", "proj_b", "gain_one", "shift_one"), proj))
    ins.update(zip(("up_w", "up_b", "down_w", "down_b", "gain_two", "shift_two"), ffn))
    outs = dict(
        unit_one=shape(half, width),
        inverse_one=shape(half, 1),
        normed_low=shape(rows, width, kind=LOW),
        act=shape(rows, hidden, kind=LOW),
        slope=shape(rows, hidden, kind=LOW),
        unit_two=shape(half, width),
        inverse_two=shape(half, 1),
        hidden=shape(half, width),
        low=shape(rows, width, kind=LOW),
    )
    scratch = dict(
        normed=pltpu.VMEM((half, width), F32),
        proj_line=line_scratch(rows, width),
        ffn_line=line_scratch(rows, width),
    )
    return call(collective, body, ins, outs, scratch)


def turn_kernel(size, collective, context, proj, residual, ffn, cotangent):
    rows, width = context.shape[0], proj[0].shape[1]
    half, hidden = rows // 2, ffn[0].shape[1]
    chunks = half // CHUNK
    whole = residual.shape[0] == rows

    def body(r):
        clear(r.sums, r.up_sum)
        greet(size)
        stages = [proj_stage(r, whole), ffn_stage(r, True), ffn_back_stage(r)]
        first = 4 * LAG * (size - 1) + chunks
        line_loop(size, stages, ffn_grads(r, r.ffn_grad, first))

    ins = dict(context=context, residual=residual, cotangent=cotangent)
    ins.update(zip(("proj_w", "proj_b", "gain_one", "shift_one"), proj))
    ins.update(zip(("up_w", "up_b", "down_w", "down_b", "gain_two", "shift_two"), ffn))
    outs = dict(
        mixed_own=shape(half, width, kind=LOW),
        grad_first=shape(half, width),
        attn_low=shape(rows, width, kind=LOW),
        ffn_grad=shape(width + hidden, width, kind=LOW),
        up_sum=shape(8, hidden),
        sums=shape(6, 8, width),
    )
    scratch = dict(
        normed=pltpu.VMEM((half, width), F32),
        unit_one=pltpu.VMEM((half, width), F32),
        inverse_one=pltpu.VMEM((half, 1), F32),
        normed_low=pltpu.VMEM((rows, width), LOW),
        act=pltpu.VMEM((rows, hidden), LOW),
        slope=pltpu.VMEM((rows, hidden), LOW),
        pre=pltpu.VMEM((rows, hidden), LOW),
        branch=pltpu.VMEM((rows, width), LOW),
        grad_second=pltpu.VMEM((half, width), F32),
        proj_line=line_scratch(rows, width),
        ffn_line=line_scratch(rows, width),
        back_line=line_scratch(rows, width),
    )
    return call(collective, body, ins, outs, scratch)


def qkv_back_stage(r, inner):
    def produce(block):
        r.qkv_line[0][block] = dot_t(r.grad_proj[block], r.qkv_w[...]).astype(LOW)

    def finish(at, own, total):
        grad_in = r.grad_first_in[own] + total
        if not inner:
            r.grad_low[at] = grad_in.astype(LOW)
            r.mixed[at] = r.mixed_own[own]
            return
        unit = r.unit_two[own]
        grad = norm_back(grad_in, r.gain_two[...], unit, r.inverse_two[own])
        r.grad_second[own] = grad
        r.branch[at] = grad.astype(LOW)
        tally(r.sums.at[0], grad_in * unit)
        tally(r.sums.at[1], grad_in)
        tally(r.sums.at[2], grad.astype(LOW).astype(F32))

    return stage_of(produce, finish, [r.branch] if inner else [r.grad_low, r.mixed], r.qkv_line)


def spread_targets(chips):
    return [(1, lambda index: partner()), (chips - 1, lambda index: plane_peer(chips, index))]


def backward_kernel(size, chips, collective, attn, below, ffn, ffn_grad):
    rows, width = attn["grad_proj"].shape[0], attn["low_in"].shape[1]
    half, hidden = rows // 2, ffn["up_w"].shape[1]
    chunks = half // CHUNK
    span = 2 * LAG * (size - 1)
    ffn_rows = width + hidden

    def body(r):
        clear(r.sums, r.up_sum)
        greet(size, targets=spread_targets(chips))
        near, far, *sems = r.ffn_spread
        ffn_sum = Spread(chips, ffn_rows, width, r.ffn_grad_in, near, far, r.ffn_share, r.ffn_whole, sems)
        near, far, *sems = r.attn_spread
        attn_sum = Spread(chips, width, width, r.attn_grad, near, far, r.attn_share, None, sems)
        ffn_sum.to_partner()
        extras = [
            at_step(2, ffn_sum.to_chips),
            *attn_grads(r, r.attn_grad, 3),
            at_step(8, attn_sum.to_partner),
            at_step(span + 3, lambda: (ffn_sum.sum_share(), ffn_sum.give_share())),
            at_step(span + 4, attn_sum.to_chips),
            *ffn_grads(r, r.ffn_grad, span + chunks),
            at_step(2 * span + 3, ffn_sum.to_other_core),
        ]
        line_loop(size, [qkv_back_stage(r, True), ffn_back_stage(r)], extras)
        attn_sum.sum_share()
        attn_sum.settle_sum()
        ffn_sum.settle_sum()
        ffn_sum.settle_whole()

    ins = dict(**attn, **below, **ffn, ffn_grad_in=ffn_grad)
    outs = dict(
        grad_first=shape(half, width),
        attn_low=shape(rows, width, kind=LOW),
        ffn_grad=shape(ffn_rows, width, kind=LOW),
        up_sum=shape(8, hidden),
        sums=shape(6, 8, width),
        attn_share=shape(width // 2 // chips, width, kind=LOW),
        ffn_whole=shape(ffn_rows, width, kind=LOW),
    )
    scratch = dict(
        pre=pltpu.VMEM((rows, hidden), LOW),
        branch=pltpu.VMEM((rows, width), LOW),
        grad_second=pltpu.VMEM((half, width), F32),
        attn_grad=pltpu.VMEM((width, width), LOW),
        ffn_share=pltpu.VMEM((ffn_rows // 2 // chips, width), LOW),
        qkv_line=line_scratch(rows, width),
        back_line=line_scratch(rows, width),
        ffn_spread=Spread.scratch(chips, ffn_rows, width),
        attn_spread=Spread.scratch(chips, width, width),
    )
    return call(collective, body, ins, outs, scratch)


def last_kernel(size, chips, collective, attn, mixed_own, ffn_grad, attn_share, small, own_rows):
    rows, width = attn["grad_proj"].shape[0], attn["low_in"].shape[1]
    chunks = rows // 2 // CHUNK
    span = 2 * LAG * (size - 1)
    ffn_rows = ffn_grad.shape[0]
    count = small.shape[0]
    teams = 2 * chips

    def row_peer(index):
        row, place = here()
        return (lax.rem(row + index + 1, teams), place)

    def line_peer(index):
        row, place = here()
        return (row, lax.rem(place + index + 1, size))

    def body(r):
        row, place = here()
        clear(r.ends)
        greet(size, line=False, targets=[(teams - 1, row_peer), (size - 1, line_peer)])
        near, far, *sems = r.ffn_spread
        ffn_sum = Spread(chips, ffn_rows, width, r.ffn_grad_in, near, far, r.ffn_share, r.ffn_whole, sems)
        near, far, *sems = r.attn_spread
        attn_sum = Spread(chips, width, width, r.attn_grad, near, far, r.attn_share, r.attn_whole, sems)
        near, far, *sems = r.above_spread
        above_sum = Spread(chips, width, width, None, near, far, r.above_share, r.above_whole, sems)

        def end_copy(slot, index):
            return pltpu.make_async_remote_copy(
                src_ref=r.small,
                dst_ref=r.ends.at[slot],
                send_sem=r.end_sent.at[slot, index],
                recv_sem=r.end_got.at[slot],
                device_id=line_peer(index),
                device_id_type=MESH,
            )

        def team_copy(index, slot):
            return pltpu.make_async_remote_copy(
                src_ref=r.mine,
                dst_ref=r.others.at[slot],
                send_sem=r.team_sent.at[index],
                recv_sem=r.team_got.at[slot],
                device_id=row_peer(index),
                device_id_type=MESH,
            )

        def each(number, work):
            def one(index, carry):
                work(index)
                return carry

            lax.fori_loop(0, number, one, 0)

        end_places = ((0, 0), (1, size - 1))

        def small_to_line():
            for slot, end in end_places:

                @pl.when(place == end)
                def _():
                    each(size - 1, lambda index: end_copy(slot, index).start())

        def small_to_teams():
            for slot, end in end_places:

                @pl.when(place != end)
                def _():
                    end_copy(slot, 0).wait_recv()

            line_total = r.small[...] + r.ends[0] + r.ends[1]
            number = lax.broadcasted_iota(jnp.int32, (count, width), 0)
            r.mine[...] = jnp.where(number < own_rows, r.small[...], line_total)
            each(teams - 1, lambda index: team_copy(index, row).start())
            r.others[row] = r.mine[...]

        def small_finish():
            each(teams - 1, lambda index: team_copy(index, row_peer(index)[0]).wait_recv())
            r.small_total[...] = lax.fori_loop(
                1, teams, lambda index, total: total + r.others[index], r.others[0]
            )
            each(teams - 1, lambda index: team_copy(index, row).wait_send())
            for slot, end in end_places:

                @pl.when(place == end)
                def _():
                    each(size - 1, lambda index: end_copy(slot, index).wait_send())

        ffn_sum.to_partner()
        above_sum.give_share()
        small_to_line()
        extras = [
            *attn_grads(r, r.attn_grad, 0),
            at_step(1, ffn_sum.to_chips),
            at_step(4, attn_sum.to_partner),
            at_step(5, small_to_teams),
            at_step(6, attn_sum.to_chips),
            at_step(span, above_sum.to_other_core),
        ]
        line_loop(size, [qkv_back_stage(r, False)], extras)
        ffn_sum.sum_share()
        ffn_sum.give_share()
        attn_sum.sum_share()
        attn_sum.give_share()
        small_finish()
        above_sum.settle_whole()
        ffn_sum.settle_sum()
        attn_sum.settle_sum()
        ffn_sum.to_other_core()
        attn_sum.to_other_core()
        ffn_sum.settle_whole()
        attn_sum.settle_whole()

    ins = dict(**attn, mixed_own=mixed_own, ffn_grad_in=ffn_grad, above_share=attn_share, small=small)
    outs = dict(
        grad_low=shape(rows, width, kind=LOW),
        mixed=shape(rows, width, kind=LOW),
        ffn_whole=shape(ffn_rows, width, kind=LOW),
        attn_whole=shape(width, width, kind=LOW),
        above_whole=shape(width, width, kind=LOW),
        small_total=shape(count, width),
    )
    scratch = dict(
        attn_grad=pltpu.VMEM((width, width), LOW),
        ffn_share=pltpu.VMEM((ffn_rows // 2 // chips, width), LOW),
        attn_share=pltpu.VMEM((width // 2 // chips, width), LOW),
        ends=pltpu.VMEM((2, count, width), F32),
        mine=pltpu.VMEM((count, width), F32),
        others=pltpu.VMEM((teams, count, width), F32),
        end_sent=pltpu.SemaphoreType.DMA((2, size - 1)),
        end_got=pltpu.SemaphoreType.DMA((2,)),
        team_sent=pltpu.SemaphoreType.DMA((teams - 1,)),
        team_got=pltpu.SemaphoreType.DMA((teams,)),
        qkv_line=line_scratch(rows, width, 2),
        ffn_spread=Spread.scratch(chips, ffn_rows, width),
        attn_spread=Spread.scratch(chips, width, width),
        above_spread=Spread.scratch(chips, width, width),
    )
    return call(collective, body, ins, outs, scratch)


def local(
    tokens,
    segment_ids,
    cotangent,
    qkv_weight,
    qv_bias,
    proj_weight,
    proj_bias,
    first_gain,
    first_shift,
    up_weight,
    up_bias,
    down_weight,
    down_bias,
    second_gain,
    second_shift,
):
    seq_count, length, width = tokens.shape
    rows = seq_count * length
    layers = qkv_weight.shape[0]
    size = lax.axis_size("tensor")
    chips = lax.axis_size("dp") // 2
    part_width = qkv_weight.shape[-1]
    hidden = up_weight.shape[-1]
    heads = part_width // HEAD
    seg_row = segment_ids.reshape(length)

    def row_of(stacked, layer):
        return stacked[layer].astype(F32).reshape(1, -1)

    low = tokens.reshape(rows, width)
    residual = low
    cot = cotangent.reshape(rows, width)
    kept = []
    for layer in range(layers):
        qkv = qkv_weight[layer].reshape(width, 3 * part_width)
        bias = jnp.concatenate([qv_bias[layer, 0], jnp.zeros_like(qv_bias[layer, 0]), qv_bias[layer, 1]])
        projected = (dot(low, qkv) + bias.astype(F32)).astype(LOW)
        split = projected.reshape(length, 3, heads, HEAD)
        context, log_total = attend_forward((split[:, 0], split[:, 1], split[:, 2], seg_row))
        context = context.reshape(rows, part_width)
        proj = (
            proj_weight[layer],
            row_of(proj_bias, layer),
            row_of(first_gain, layer),
            row_of(first_shift, layer),
        )
        ffn = (
            up_weight[layer],
            row_of(up_bias, layer),
            down_weight[layer],
            row_of(down_bias, layer),
            row_of(second_gain, layer),
            row_of(second_shift, layer),
        )
        keep = types.SimpleNamespace(low=low, qkv=qkv, split=split, log_total=log_total, context=context)
        if layer + 1 < layers:
            keep.done = forward_kernel(size, layer, context, proj, residual, ffn)
            residual, low = keep.done.hidden, keep.done.low
        else:
            above = turn_kernel(size, layer, context, proj, residual, ffn, cot)
            mixed_own = above.mixed_own
        kept.append(keep)

    sums = [None] * layers
    norm_sums = [None] * layers
    up_sums = [None] * layers
    qv_sums = [None] * layers
    ffn_whole = [None] * layers
    attn_whole = [None] * layers
    norm_sums[layers - 1] = above.sums.sum(axis=1)
    up_sums[layers - 1] = above.up_sum.sum(axis=0)
    attn_share = None
    for layer in range(layers - 1, -1, -1):
        keep = kept[layer]
        split = keep.split
        grad_context = dot_t(above.attn_low, proj_weight[layer]).astype(LOW)
        grad_heads = attend_backward(
            (
                split[:, 0],
                split[:, 1],
                split[:, 2],
                seg_row,
                keep.log_total,
                grad_context.reshape(length, heads, HEAD),
            )
        )
        grad_proj = grad_heads.reshape(rows, 3 * part_width)
        qkv_sums = jnp.sum(grad_proj.astype(F32).reshape(rows, 3, part_width), axis=0)
        qv_sums[layer] = jnp.concatenate([qkv_sums[0], qkv_sums[2]])
        attn = dict(
            grad_proj=grad_proj,
            grad_first_in=above.grad_first,
            qkv_w=keep.qkv,
            low_in=keep.low,
            attn_low_in=above.attn_low,
            context_in=keep.context,
        )
        if layer > 0:
            done = kept[layer - 1].done
            below = dict(
                unit_two=done.unit_two,
                inverse_two=done.inverse_two,
                gain_two=row_of(second_gain, layer - 1),
            )
            ffn = dict(
                act=done.act,
                slope=done.slope,
                normed_low=done.normed_low,
                unit_one=done.unit_one,
                inverse_one=done.inverse_one,
                gain_one=row_of(first_gain, layer - 1),
                up_w=up_weight[layer - 1],
                down_w=down_weight[layer - 1],
            )
            above = backward_kernel(
                size, chips, 2 * layers - layer, attn, below, ffn, above.ffn_grad
            )
            norm_sums[layer - 1] = above.sums.sum(axis=1)
            up_sums[layer - 1] = above.up_sum.sum(axis=0)
            ffn_whole[layer] = above.ffn_whole
            attn_share = above.attn_share
        else:
            norm_rows = jnp.stack(norm_sums, axis=1).reshape(6 * layers, width)
            own = jnp.concatenate([*qv_sums, *up_sums]).reshape(-1, width)
            used = own.shape[0] + norm_rows.shape[0]
            small = jnp.concatenate([own, norm_rows, jnp.zeros((-used % 8, width), F32)])
            last = last_kernel(
                size, chips, 2 * layers, attn, mixed_own, above.ffn_grad, attn_share, small, own.shape[0]
            )
            ffn_whole[0] = last.ffn_whole
            attn_whole[0] = last.attn_whole
            attn_whole[1] = last.above_whole

    totals = last.small_total
    flat = totals[: own.shape[0]].reshape(-1)
    at = layers * 2 * part_width
    qv_total = flat[:at].reshape(layers, 2, part_width)
    up_total = flat[at:].reshape(layers, hidden)
    rest = totals[own.shape[0] : used].reshape(6, layers, width)
    split_at = 3 * part_width

    def stack(parts):
        return jnp.stack([part.astype(F32) for part in parts])

    return (
        last.mixed.astype(F32).reshape(tokens.shape),
        last.grad_low.astype(F32).reshape(tokens.shape),
        stack([part[:, :split_at].reshape(width, 3, part_width) for part in attn_whole]),
        qv_total,
        stack([part[:, split_at:].T for part in attn_whole]),
        rest[5],
        rest[3],
        rest[4],
        stack([part[:width] for part in ffn_whole]),
        up_total,
        stack([part[width:] for part in ffn_whole]),
        rest[2],
        rest[0],
        rest[1],
    )


def solution(mesh):
    return jax.shard_map(
        local,
        mesh=mesh,
        in_specs=(
            P("dp", None, None),
            P("dp", None),
            P("dp", None, None),
            P(None, None, None, "tensor"),
            P(None, None, "tensor"),
            P(None, "tensor", None),
            P(),
            P(),
            P(),
            P(None, None, "tensor"),
            P(None, "tensor"),
            P(None, "tensor", None),
            P(),
            P(),
            P(),
        ),
        out_specs=(
            P("dp", None, None),
            P("dp", None, None),
            P(None, None, None, "tensor"),
            P(None, None, "tensor"),
            P(None, "tensor", None),
            P(),
            P(),
            P(),
            P(None, None, "tensor"),
            P(None, "tensor"),
            P(None, "tensor", None),
            P(),
            P(),
            P(),
        ),
        check_vma=False,
    )
```

```python
import math
import types

import jax
import jax.numpy as jnp
from jax import lax
from jax.experimental import pallas as pl
from jax.experimental.pallas import tpu as pltpu
from jax.sharding import PartitionSpec as P

HEAD = 64


norm_eps = 1e-12
masked_value = -1000000000.0


MESH = pl.DeviceIdType.MESH
F32 = jnp.float32
LOW = jnp.bfloat16
CHUNK = 32
LAG = 2
PIECE = 256
QUERIES = 128


def dot(a, b):
    return jnp.dot(a, b, preferred_element_type=F32)


def dot_t(a, b):
    return lax.dot_general(a, b, (((1,), (1,)), ((), ())), preferred_element_type=F32)


def dot_tn(a, b):
    return lax.dot_general(a, b, (((0,), (0,)), ((), ())), preferred_element_type=F32)


def here():
    return lax.axis_index("dp"), lax.axis_index("tensor")


def greet(size, line=True, targets=()):
    row, place = here()
    barrier = pltpu.get_barrier_semaphore()
    for count, target in targets:

        def signal(index, carry):
            pl.semaphore_signal(barrier, inc=1, device_id=target(index), device_id_type=MESH)
            return carry

        lax.fori_loop(0, count, signal, 0)
    expected = sum(count for count, _ in targets)
    left, right = place > 0, place < size - 1
    if line:

        @pl.when(left)
        def _():
            pl.semaphore_signal(barrier, inc=1, device_id=(row, place - 1), device_id_type=MESH)

        @pl.when(right)
        def _():
            pl.semaphore_signal(barrier, inc=1, device_id=(row, place + 1), device_id_type=MESH)

    def wait():
        if not line:
            pl.semaphore_wait(barrier, expected)
            return

        @pl.when(left & right)
        def _():
            pl.semaphore_wait(barrier, expected + 2)

        @pl.when(jnp.logical_not(left & right))
        def _():
            pl.semaphore_wait(barrier, expected + 1)

    return wait


def partner():
    row, place = here()
    return (row + 1 - 2 * lax.rem(row, 2), place)


def plane_peer(chips, index):
    row, place = here()
    return (lax.rem(row // 2 + index + 1, chips) * 2 + lax.rem(row, 2), place)


def line_loop(size, stages, extras=()):
    row, place = here()
    half = stages[0].part.shape[0] // 2
    chunks = half // CHUNK
    end = size - 1
    span = 2 * LAG * end

    def rows_of(side, chunk):
        return pl.ds(pl.multiple_of(side * half + chunk * CHUNK, CHUNK), CHUNK)

    def sum_copy(stage, side, chunk, target):
        rows = rows_of(side, chunk)
        return pltpu.make_async_remote_copy(
            src_ref=stage.part.at[rows],
            dst_ref=stage.recv.at[rows],
            send_sem=stage.sems[0].at[side, chunk],
            recv_sem=stage.sems[1].at[side, chunk],
            device_id=(row, target),
            device_id_type=MESH,
        )

    def row_copy(stage, which, side, chunk, target):
        rows = rows_of(side, chunk)
        return pltpu.make_async_remote_copy(
            src_ref=stage.outs[which].at[rows],
            dst_ref=stage.outs[which].at[rows],
            send_sem=stage.sems[2].at[which, side, chunk],
            recv_sem=stage.sems[3].at[which, side, chunk],
            device_id=(row, target),
            device_id_type=MESH,
        )

    def side_facts(side):
        if side == 0:
            return place, place + 1, place - 1
        return end - place, place - 1, place + 1

    def bring_back(stage, since):
        for side in range(2):
            at, onward, back = side_facts(side)
            chunk = since - LAG * end - LAG * (end - at)

            @pl.when((at < end) & (chunk >= 0) & (chunk < chunks))
            def _():
                for which in range(len(stage.outs)):
                    row_copy(stage, which, side, chunk, back).wait_recv()

                    @pl.when(at > 0)
                    def _():
                        row_copy(stage, which, side, chunk, back).start()

    def sum_up(stage, since):
        for side in range(2):
            at, onward, back = side_facts(side)
            chunk = since - LAG * at

            @pl.when((chunk >= 0) & (chunk < chunks))
            def _():
                @pl.when(at > 0)
                def _():
                    sum_copy(stage, side, chunk, onward).wait_recv()

                @pl.when(at < end)
                def _():
                    @pl.when(at > 0)
                    def _():
                        rows = rows_of(side, chunk)
                        total = stage.part[rows].astype(F32) + stage.recv[rows].astype(F32)
                        stage.part[rows] = total.astype(LOW)

                    sum_copy(stage, side, chunk, onward).start()

                @pl.when(at == end)
                def _():
                    rows = rows_of(side, chunk)
                    own = pl.ds(pl.multiple_of(chunk * CHUNK, CHUNK), CHUNK)
                    stage.finish(rows, own, stage.part[rows].astype(F32) + stage.recv[rows].astype(F32))
                    for which in range(len(stage.outs)):
                        row_copy(stage, which, side, chunk, back).start()

    def step(now, carry):
        for number, stage in enumerate(stages):
            bring_back(stage, now - number * span)
        for number, stage in enumerate(stages):
            since = now - number * span

            @pl.when((since >= 0) & (since < chunks))
            def _():
                for side in range(2):
                    stage.produce(rows_of(side, since))

            sum_up(stage, since)
        for first, count, work in extras:

            @pl.when((now >= first) & (now < first + count))
            def _():
                work(now - first)

        return carry

    lax.fori_loop(0, chunks + span * len(stages), step, 0)

    def drain(chunk, carry):
        for stage in stages:
            for side in range(2):
                at, onward, back = side_facts(side)

                @pl.when(at < end)
                def _():
                    sum_copy(stage, side, chunk, onward).wait_send()

                @pl.when(at > 0)
                def _():
                    for which in range(len(stage.outs)):
                        row_copy(stage, which, side, chunk, back).wait_send()

        return carry

    lax.fori_loop(0, chunks, drain, 0)


def by_rows(count, work, block=32):
    def one(index, carry):
        work(pl.ds(pl.multiple_of(index * block, block), block), index * block)
        return carry

    block = min(block, count)
    lax.fori_loop(0, count // block, one, 0)


class Spread:
    def __init__(self, chips, rows, width, grads, near, far, share, whole, sems):
        self.chips, self.half = chips, rows // 2
        self.count = self.half // chips
        self.grads, self.near, self.far, self.share, self.whole = grads, near, far, share, whole
        self.near_sems, self.far_sems, self.back_sems, self.last_sems = sems
        row, _ = here()
        self.core, self.chip = lax.rem(row, 2), row // 2

    @staticmethod
    def scratch(chips, rows, width):
        half = rows // 2
        pair = pltpu.SemaphoreType.DMA((2,))
        many = pltpu.SemaphoreType.DMA((2, chips - 1))
        return [
            pltpu.VMEM((half, width), LOW),
            pltpu.VMEM((chips - 1, half // chips, width), LOW),
            pair,
            many,
            many,
            pair,
        ]

    def half_rows(self, core):
        return pl.ds(pl.multiple_of(core * self.half, 16), self.half)

    def near_copy(self):
        return pltpu.make_async_remote_copy(
            src_ref=self.grads.at[self.half_rows(1 - self.core)],
            dst_ref=self.near,
            send_sem=self.near_sems.at[0],
            recv_sem=self.near_sems.at[1],
            device_id=partner(),
            device_id_type=MESH,
        )

    def far_copy(self, index):
        chip = lax.rem(self.chip + index + 1, self.chips)
        return pltpu.make_async_remote_copy(
            src_ref=self.near.at[pl.ds(pl.multiple_of(chip * self.count, 16), self.count)],
            dst_ref=self.far.at[index],
            send_sem=self.far_sems.at[0, index],
            recv_sem=self.far_sems.at[1, index],
            device_id=plane_peer(self.chips, index),
            device_id_type=MESH,
        )

    def back_copy(self, index):
        to = pl.multiple_of(self.core * self.half + self.chip * self.count, 16)
        return pltpu.make_async_remote_copy(
            src_ref=self.share,
            dst_ref=self.whole.at[pl.ds(to, self.count)],
            send_sem=self.back_sems.at[0, index],
            recv_sem=self.back_sems.at[1, index],
            device_id=plane_peer(self.chips, index),
            device_id_type=MESH,
        )

    def last_copy(self):
        rows = self.half_rows(self.core)
        return pltpu.make_async_remote_copy(
            src_ref=self.whole.at[rows],
            dst_ref=self.whole.at[rows],
            send_sem=self.last_sems.at[0],
            recv_sem=self.last_sems.at[1],
            device_id=partner(),
            device_id_type=MESH,
        )

    def each(self, work):
        def one(index, carry):
            work(index)
            return carry

        lax.fori_loop(0, self.chips - 1, one, 0)

    def to_partner(self):
        self.near_copy().start()

    def to_chips(self):
        self.near_copy().wait_recv()
        base = self.core * self.half

        def add(rows, first):
            own = self.grads[pl.ds(pl.multiple_of(base + first, 16), rows.size)]
            self.near[rows] = (self.near[rows].astype(F32) + own.astype(F32)).astype(LOW)

        by_rows(self.half, add)
        self.each(lambda index: self.far_copy(index).start())

    def sum_share(self):
        self.each(lambda index: self.far_copy(index).wait_recv())
        base = self.chip * self.count

        def add(rows, first):
            total = self.near[pl.ds(pl.multiple_of(base + first, 16), rows.size)].astype(F32)
            if self.chips <= 4:
                for index in range(self.chips - 1):
                    total += self.far[index, rows].astype(F32)
            else:
                total = lax.fori_loop(
                    0, self.chips - 1, lambda index, so_far: so_far + self.far[index, rows].astype(F32), total
                )
            self.share[rows] = total.astype(LOW)

        by_rows(self.count, add)

    def settle_sum(self):
        self.near_copy().wait_send()
        self.each(lambda index: self.far_copy(index).wait_send())

    def give_share(self):
        self.each(lambda index: self.back_copy(index).start())
        base = self.core * self.half + self.chip * self.count

        def keep(rows, first):
            self.whole[pl.ds(pl.multiple_of(base + first, 16), rows.size)] = self.share[rows]

        by_rows(self.count, keep)

    def to_other_core(self):
        self.each(lambda index: self.back_copy(index).wait_recv())
        self.last_copy().start()

    def settle_whole(self):
        self.last_copy().wait_recv()
        self.last_copy().wait_send()
        self.each(lambda index: self.back_copy(index).wait_send())


def normalize(residual):
    centred = residual - jnp.mean(residual, axis=-1, keepdims=True)
    inverse = lax.rsqrt(jnp.mean(centred * centred, axis=-1, keepdims=True) + norm_eps)
    return centred * inverse, inverse


def norm_back(grad, gain, unit, inverse):
    scaled = grad * gain
    return (
        scaled
        - jnp.mean(scaled, axis=-1, keepdims=True)
        - unit * jnp.mean(scaled * unit, axis=-1, keepdims=True)
    ) * inverse


def tally(total, values):
    total[...] += jnp.sum(values.reshape(-1, 8, values.shape[-1]), axis=0)


class Layer:
    def __init__(self, array, layer):
        self.array, self.layer = array, layer


def call(collective, body, ins, outs, scratch):
    vmem = pl.BlockSpec(memory_space=pltpu.VMEM)
    names = [*ins, *outs]
    fetched = {name: value for name, value in ins.items() if isinstance(value, Layer)}
    extra = {name: spec if isinstance(spec, list) else [spec] for name, spec in scratch.items()}

    def run(*refs):
        named = dict(zip(names, refs))
        rest = list(refs[len(names) :])
        copies = {}
        arrivals = rest.pop(0)
        for number, (name, value) in enumerate(fetched.items()):
            room = rest.pop(0)
            copies[name] = pltpu.make_async_copy(named[name].at[value.layer], room, arrivals.at[number])
            copies[name].start()
            named[name] = room
        for name, specs in extra.items():
            taken = [rest.pop(0) for _ in specs]
            named[name] = taken if isinstance(scratch[name], list) else taken[0]

        def need(*wanted):
            for name in wanted:
                copies[name].wait()

        body(types.SimpleNamespace(**named, need=need))

    results = pl.pallas_call(
        run,
        out_shape=list(outs.values()),
        in_specs=[pl.BlockSpec(memory_space=pl.ANY) if name in fetched else vmem for name in ins],
        out_specs=[vmem] * len(outs),
        scratch_shapes=[
            pltpu.SemaphoreType.DMA((len(fetched),)),
            *(pltpu.VMEM(value.array.shape[1:], value.array.dtype) for value in fetched.values()),
            *(spec for specs in extra.values() for spec in specs),
        ],
        compiler_params=pltpu.CompilerParams(
            collective_id=collective, has_side_effects=True, vmem_limit_bytes=60 << 20
        ),
    )(*(value.array if isinstance(value, Layer) else value for value in ins.values()))
    return types.SimpleNamespace(**dict(zip(outs, results)))


def shape(*dims, kind=F32):
    return jax.ShapeDtypeStruct(dims, kind)


def line_scratch(rows, width, outs=1):
    chunks = rows // 2 // CHUNK
    return [
        pltpu.VMEM((rows, width), LOW),
        pltpu.VMEM((rows, width), LOW),
        pltpu.SemaphoreType.DMA((2, chunks)),
        pltpu.SemaphoreType.DMA((2, chunks)),
        pltpu.SemaphoreType.DMA((outs, 2, chunks)),
        pltpu.SemaphoreType.DMA((outs, 2, chunks)),
    ]


def stage_of(produce, finish, outs, scratch):
    part, recv, *sems = scratch
    return types.SimpleNamespace(
        produce=produce, finish=finish, outs=outs, part=part, recv=recv, sems=sems
    )


def clear(*refs):
    for ref in refs:
        ref[...] = jnp.zeros_like(ref)


def vector(ref, layer):
    return ref[...].astype(F32)[layer : layer + 1]


def head_lanes(values, head):
    lane = lax.broadcasted_iota(jnp.int32, values.shape, 1)
    return jnp.where(lane // HEAD == head, values, jnp.zeros_like(values))


def turned(values):
    return jnp.transpose(values.astype(F32)).astype(LOW)


def mark_segments(r):
    length = r.seg_row.shape[1]
    wide = jnp.broadcast_to(r.seg_row[...].astype(F32), (QUERIES, length))
    r.seg_cols[...] = jnp.transpose(wide)


def masked_block(r, keys, queries, at):
    same = r.seg_cols[...] == r.seg_row[:, at].astype(F32)
    return jnp.where(same, dot_t(keys, queries) * HEAD ** (-0.5), masked_value)


def project(r, layer):
    bias = r.qv_bias[layer].astype(F32)
    for member in range(3):
        rows = dot(r.low_in[...], r.qkv_w[member])
        if member != 1:
            rows += bias[member // 2 : member // 2 + 1]
        r.projected[member] = rows.astype(LOW)
    r.turned_rows[...] = turned(r.projected[2])
    mark_segments(r)


def attend(r, block):
    at = pl.ds(pl.multiple_of(block * QUERIES, QUERIES), QUERIES)
    queries = r.projected[0, at]
    heads = queries.shape[1] // HEAD
    parts = []
    for head in range(heads):
        scores = masked_block(r, r.projected[1], head_lanes(queries, head), at)
        row_max = jnp.max(scores, axis=0, keepdims=True)
        exponent = jnp.exp(scores - row_max)
        row_total = jnp.sum(exponent, axis=0, keepdims=True)
        r.log_total[head : head + 1, at] = row_max + jnp.log(row_total)
        probs = (exponent * (1.0 / row_total)).astype(LOW)
        parts.append(dot(r.turned_rows[head * HEAD : (head + 1) * HEAD], probs))
    r.context[at] = jnp.transpose(jnp.concatenate(parts, axis=0)).astype(LOW)


def attend_first(r, half):
    per_side = half // QUERIES
    for side in range(2):
        attend(r, side * per_side)
    extras = []
    for block in range(1, per_side):
        for side in range(2):
            step = max(0, block * QUERIES // CHUNK - 2 + side)
            extras.append(at_step(step, lambda block=side * per_side + block: attend(r, block)))
    return extras


def attend_back(r, between=()):
    rows = r.attn_low_in.shape[0]
    heads = r.qkv_w.shape[2] // HEAD
    scale = HEAD ** (-0.5)
    mark_segments(r)
    r.grad_context[...] = dot_t(r.attn_low_in[...], r.proj_w[...]).astype(LOW)
    r.turned_rows[...] = turned(r.projected[1])
    clear(r.grad_key, r.grad_value)
    for number in range(rows // QUERIES):
        at = slice(number * QUERIES, (number + 1) * QUERIES)
        queries, context_rows = r.projected[0, at], r.grad_context[at]
        parts = []
        for head in range(heads):
            to = slice(head * QUERIES, (head + 1) * QUERIES)
            r.head_queries[to] = head_lanes(queries, head)
            r.head_context[to] = head_lanes(context_rows, head)
            scores = masked_block(r, r.projected[1], r.head_queries[to], at)
            probability = jnp.exp(scores - r.log_total[head : head + 1, at])
            grad_probs = dot_t(r.projected[2], r.head_context[to])
            inner = jnp.sum(probability * grad_probs, axis=0, keepdims=True)
            grad_scores = (probability * (grad_probs - inner)).astype(LOW)
            r.score_rows[:, to] = grad_scores
            r.prob_rows[:, to] = probability.astype(LOW)
            parts.append(dot(r.turned_rows[head * HEAD : (head + 1) * HEAD], grad_scores))
        r.grad_key[...] += dot(r.score_rows[...], r.head_queries[...])
        r.grad_value[...] += dot(r.prob_rows[...], r.head_context[...])
        r.grad_proj[0, at] = (jnp.transpose(jnp.concatenate(parts, axis=0)) * scale).astype(LOW)
        if number < len(between):
            between[number]()
    r.grad_proj[1] = (r.grad_key[...] * scale).astype(LOW)
    r.grad_proj[2] = r.grad_value[...].astype(LOW)
    for slot, member in ((0, 0), (1, 2)):
        r.qv_sum[slot] = jnp.sum(r.grad_proj[member].astype(F32).reshape(-1, 8, r.qv_sum.shape[2]), axis=0)


def proj_stage(r, layer, whole):
    def produce(block):
        r.proj_line[0][block] = dot(r.context[block], r.proj_w[...]).astype(LOW)

    def finish(at, own, total):
        came = r.residual[at if whole else own].astype(F32)
        unit, inverse = normalize(came + total + vector(r.proj_b, layer))
        r.unit_one[own] = unit
        r.inverse_one[own] = inverse
        result = unit * vector(r.first_gain, layer) + vector(r.first_shift, layer)
        r.normed[own] = result
        r.normed_low[at] = result.astype(LOW)

    return stage_of(produce, finish, [r.normed_low], r.proj_line)


def ffn_stage(r, layer, last):
    def produce(block):
        pre = dot(r.normed_low[block], r.up_w[...]) + vector(r.up_b, layer)
        cdf = 0.5 * lax.erf(pre * math.sqrt(0.5)) + 0.5
        act = (pre * cdf).astype(LOW)
        slope = cdf + pre * jnp.exp(-0.5 * pre * pre) * (1.0 / math.sqrt(2 * math.pi))
        r.slope[block] = slope.astype(LOW)
        r.act[block] = act
        r.ffn_line[0][block] = dot(act, r.down_w[...]).astype(LOW)

    def finish(at, own, total):
        unit, inverse = normalize(r.normed[own] + total + vector(r.down_b, layer))
        gain = vector(r.second_gain, layer)
        result = unit * gain + vector(r.second_shift, layer)
        if last:
            r.mixed_own[own] = result.astype(LOW)
            grad_in = r.cotangent[at].astype(F32)
            grad = norm_back(grad_in, gain, unit, inverse)
            r.grad_second[own] = grad
            r.branch[at] = grad.astype(LOW)
            tally(r.sums.at[0], grad_in * unit)
            tally(r.sums.at[1], grad_in)
            tally(r.sums.at[2], grad.astype(LOW).astype(F32))
        else:
            r.unit_two[own] = unit
            r.inverse_two[own] = inverse
            r.hidden[own] = result
            r.low[at] = result.astype(LOW)

    return stage_of(produce, finish, [r.branch if last else r.low], r.ffn_line)


def ffn_back_stage(r, layer):
    def produce(block):
        pre = (dot_t(r.branch[block], r.down_w[...]) * r.slope[block].astype(F32)).astype(LOW)
        r.pre[block] = pre
        tally(r.up_sum, pre.astype(F32))
        r.back_line[0][block] = dot_t(pre, r.up_w[...]).astype(LOW)

    def finish(at, own, total):
        grad_in = r.grad_second[own] + total
        unit = r.unit_one[own]
        grad = norm_back(grad_in, vector(r.first_gain, layer), unit, r.inverse_one[own])
        r.grad_first[own] = grad
        r.attn_low[at] = grad.astype(LOW)
        tally(r.sums.at[3], grad_in * unit)
        tally(r.sums.at[4], grad_in)
        tally(r.sums.at[5], grad.astype(LOW).astype(F32))

    return stage_of(produce, finish, [r.attn_low], r.back_line)


def qkv_back_stage(r, layer, inner):
    def produce(block):
        total = sum(dot_t(r.grad_proj[member, block], r.qkv_w[member]) for member in range(3))
        r.qkv_line[0][block] = total.astype(LOW)

    def finish(at, own, total):
        grad_in = r.grad_first_in[own] + total
        if not inner:
            r.grad_low[at] = grad_in.astype(LOW)
            r.mixed[at] = r.mixed_own[own]
            return
        unit = r.unit_two[own]
        grad = norm_back(grad_in, vector(r.second_gain, layer), unit, r.inverse_two[own])
        r.grad_second[own] = grad
        r.branch[at] = grad.astype(LOW)
        tally(r.sums.at[0], grad_in * unit)
        tally(r.sums.at[1], grad_in)
        tally(r.sums.at[2], grad.astype(LOW).astype(F32))

    return stage_of(produce, finish, [r.branch] if inner else [r.grad_low, r.mixed], r.qkv_line)


def columns(piece):
    return pl.ds(pl.multiple_of(piece * PIECE, PIECE), PIECE)


def ffn_grads(r, out, first):
    width, hidden = r.up_w.shape

    def up(piece):
        rows = pl.ds(pl.multiple_of(piece * PIECE, PIECE), PIECE)
        out[rows] = dot_tn(r.normed_low[:, columns(piece)], r.pre[...]).astype(LOW)

    def down(piece):
        rows = pl.ds(pl.multiple_of(width + piece * PIECE, PIECE), PIECE)
        out[rows] = dot_tn(r.act[:, columns(piece)], r.branch[...]).astype(LOW)

    return [(first, width // PIECE, up), (first + width // PIECE, hidden // PIECE, down)]


def attn_grads(r, out, first):
    width, part = r.low_in.shape[1], r.context_in.shape[1]

    def piece_of(piece):
        for member in range(3):
            rows = pl.ds(pl.multiple_of(member * width + piece * part, part), part)
            taken = r.low_in[:, pl.ds(pl.multiple_of(piece * part, part), part)]
            out[rows] = dot_tn(taken, r.grad_proj[member]).astype(LOW)
        rows = pl.ds(pl.multiple_of(3 * width + piece * part, part), part)
        taken = r.attn_low_in[:, pl.ds(pl.multiple_of(piece * part, part), part)]
        out[rows] = dot_tn(r.context_in[...], taken).astype(LOW)

    return [(first, width // part, piece_of)]


def at_step(step, work):
    return (step, 1, lambda index: work())


def forward_scratch(rows, width, part):
    return dict(
        normed=pltpu.VMEM((rows // 2, width), F32),
        turned_rows=pltpu.VMEM((part, rows), LOW),
        seg_cols=pltpu.VMEM((rows, QUERIES), F32),
        proj_line=line_scratch(rows, width),
        ffn_line=line_scratch(rows, width),
    )


def kept_attention(rows, part):
    return dict(
        projected=shape(3, rows, part, kind=LOW),
        log_total=shape(part // HEAD, rows),
        context=shape(rows, part, kind=LOW),
    )


def forward_kernel(size, collective, layer, ins):
    rows, width = ins["low_in"].shape
    part, hidden = ins["proj_w"].array.shape[1], ins["up_w"].array.shape[2]
    half = rows // 2
    whole = ins["residual"].shape[0] == rows

    def body(r):
        wait = greet(size)
        r.need("qkv_w")
        project(r, layer)
        extras = attend_first(r, half)
        r.need("proj_w", "up_w", "down_w")
        wait()
        line_loop(size, [proj_stage(r, layer, whole), ffn_stage(r, layer, False)], extras)

    outs = dict(
        **kept_attention(rows, part),
        unit_one=shape(half, width),
        inverse_one=shape(half, 1),
        normed_low=shape(rows, width, kind=LOW),
        act=shape(rows, hidden, kind=LOW),
        slope=shape(rows, hidden, kind=LOW),
        unit_two=shape(half, width),
        inverse_two=shape(half, 1),
        hidden=shape(half, width),
        low=shape(rows, width, kind=LOW),
    )
    return call(collective, body, ins, outs, forward_scratch(rows, width, part))


def turn_kernel(size, collective, layer, ins):
    rows, width = ins["low_in"].shape
    part, hidden = ins["proj_w"].array.shape[1], ins["up_w"].array.shape[2]
    half = rows // 2
    chunks = half // CHUNK
    whole = ins["residual"].shape[0] == rows

    def body(r):
        wait = greet(size)
        clear(r.sums, r.up_sum)
        r.need("qkv_w")
        project(r, layer)
        extras = attend_first(r, half)
        r.need("proj_w", "up_w", "down_w")
        wait()
        stages = [proj_stage(r, layer, whole), ffn_stage(r, layer, True), ffn_back_stage(r, layer)]
        first = 4 * LAG * (size - 1) + chunks
        line_loop(size, stages, [*extras, *ffn_grads(r, r.ffn_grad, first)])

    outs = dict(
        **kept_attention(rows, part),
        mixed_own=shape(half, width, kind=LOW),
        grad_first=shape(half, width),
        attn_low=shape(rows, width, kind=LOW),
        ffn_grad=shape(width + hidden, width, kind=LOW),
        up_sum=shape(8, hidden),
        sums=shape(6, 8, width),
    )
    scratch = dict(
        **forward_scratch(rows, width, part),
        unit_one=pltpu.VMEM((half, width), F32),
        inverse_one=pltpu.VMEM((half, 1), F32),
        normed_low=pltpu.VMEM((rows, width), LOW),
        act=pltpu.VMEM((rows, hidden), LOW),
        slope=pltpu.VMEM((rows, hidden), LOW),
        pre=pltpu.VMEM((rows, hidden), LOW),
        branch=pltpu.VMEM((rows, width), LOW),
        grad_second=pltpu.VMEM((half, width), F32),
        back_line=line_scratch(rows, width),
    )
    return call(collective, body, ins, outs, scratch)


def back_scratch(rows, part):
    heads = part // HEAD
    return dict(
        seg_cols=pltpu.VMEM((rows, QUERIES), F32),
        turned_rows=pltpu.VMEM((part, rows), LOW),
        grad_context=pltpu.VMEM((rows, part), LOW),
        grad_key=pltpu.VMEM((rows, part), F32),
        grad_value=pltpu.VMEM((rows, part), F32),
        grad_proj=pltpu.VMEM((3, rows, part), LOW),
        head_queries=pltpu.VMEM((heads * QUERIES, part), LOW),
        head_context=pltpu.VMEM((heads * QUERIES, part), LOW),
        score_rows=pltpu.VMEM((rows, heads * QUERIES), LOW),
        prob_rows=pltpu.VMEM((rows, heads * QUERIES), LOW),
    )


def spread_targets(chips):
    return [(1, lambda index: partner()), (chips - 1, lambda index: plane_peer(chips, index))]


def backward_kernel(size, chips, collective, layer, ins):
    rows, width = ins["low_in"].shape
    part, hidden = ins["proj_w"].array.shape[1], ins["up_w"].array.shape[2]
    half = rows // 2
    chunks = half // CHUNK
    span = 2 * LAG * (size - 1)
    ffn_rows, attn_rows = width + hidden, 4 * width

    def body(r):
        wait = greet(size, targets=spread_targets(chips))
        clear(r.sums, r.up_sum)
        near, far, *sems = r.ffn_spread
        ffn_sum = Spread(chips, ffn_rows, width, r.ffn_grad_in, near, far, r.ffn_share, r.ffn_whole, sems)
        near, far, *sems = r.attn_spread
        attn_sum = Spread(chips, attn_rows, part, r.attn_grad, near, far, r.attn_share, None, sems)
        wait()
        ffn_sum.to_partner()
        r.need("proj_w")
        attend_back(r, [lambda: None, ffn_sum.to_chips])
        r.need("qkv_w", "up_w", "down_w")
        extras = [
            *attn_grads(r, r.attn_grad, 1),
            at_step(8, attn_sum.to_partner),
            at_step(span, lambda: (ffn_sum.sum_share(), ffn_sum.give_share())),
            at_step(span + 1, attn_sum.to_chips),
            *ffn_grads(r, r.ffn_grad, span + chunks),
            at_step(2 * span + 2, ffn_sum.to_other_core),
        ]
        stages = [qkv_back_stage(r, layer - 1, True), ffn_back_stage(r, layer - 1)]
        line_loop(size, stages, extras)
        attn_sum.sum_share()
        attn_sum.settle_sum()
        ffn_sum.settle_sum()
        ffn_sum.settle_whole()

    outs = dict(
        grad_first=shape(half, width),
        attn_low=shape(rows, width, kind=LOW),
        ffn_grad=shape(ffn_rows, width, kind=LOW),
        up_sum=shape(8, hidden),
        sums=shape(6, 8, width),
        qv_sum=shape(2, 8, part),
        attn_share=shape(attn_rows // 2 // chips, part, kind=LOW),
        ffn_whole=shape(ffn_rows, width, kind=LOW),
    )
    scratch = dict(
        **back_scratch(rows, part),
        pre=pltpu.VMEM((rows, hidden), LOW),
        branch=pltpu.VMEM((rows, width), LOW),
        grad_second=pltpu.VMEM((half, width), F32),
        attn_grad=pltpu.VMEM((attn_rows, part), LOW),
        ffn_share=pltpu.VMEM((ffn_rows // 2 // chips, width), LOW),
        qkv_line=line_scratch(rows, width),
        back_line=line_scratch(rows, width),
        ffn_spread=Spread.scratch(chips, ffn_rows, width),
        attn_spread=Spread.scratch(chips, attn_rows, part),
    )
    return call(collective, body, ins, outs, scratch)


def last_kernel(size, chips, collective, layers, ins):
    rows, width = ins["low_in"].shape
    part, hidden = ins["proj_w"].array.shape[1], ins["up_sums"][0].shape[1]
    span = 2 * LAG * (size - 1)
    ffn_rows, attn_rows = width + hidden, 4 * width
    own_rows = layers * (2 * part + hidden) // width
    count = -(-(own_rows + 6 * layers) // 8) * 8
    teams = 2 * chips
    up_sums, all_sums, qv_sums = ins.pop("up_sums"), ins.pop("all_sums"), ins.pop("qv_sums")
    ins = dict(
        **ins,
        **{"up_sum_%d" % n: value for n, value in enumerate(up_sums)},
        **{"sums_%d" % n: value for n, value in enumerate(all_sums)},
        **{"qv_sum_%d" % (n + 1): value for n, value in enumerate(qv_sums)},
    )

    def row_peer(index):
        row, place = here()
        return (lax.rem(row + index + 1, teams), place)

    def line_peer(index):
        row, place = here()
        return (row, lax.rem(place + index + 1, size))

    def each(number, work):
        def one(index, carry):
            work(index)
            return carry

        lax.fori_loop(0, number, one, 0)

    def body(r):
        row, place = here()
        clear(r.ends)
        wait = greet(size, line=False, targets=[(teams - 1, row_peer), (size - 1, line_peer)])
        near, far, *sems = r.ffn_spread
        ffn_sum = Spread(chips, ffn_rows, width, r.ffn_grad_in, near, far, r.ffn_share, r.ffn_whole, sems)
        near, far, *sems = r.attn_spread
        attn_sum = Spread(chips, attn_rows, part, r.attn_grad, near, far, r.attn_share, r.attn_whole, sems)
        near, far, *sems = r.above_spread
        above_sum = Spread(chips, attn_rows, part, None, near, far, r.above_share, r.above_whole, sems)

        def end_copy(slot, index):
            return pltpu.make_async_remote_copy(
                src_ref=r.small,
                dst_ref=r.ends.at[slot],
                send_sem=r.end_sent.at[slot, index],
                recv_sem=r.end_got.at[slot],
                device_id=line_peer(index),
                device_id_type=MESH,
            )

        def team_copy(index, slot):
            return pltpu.make_async_remote_copy(
                src_ref=r.mine,
                dst_ref=r.others.at[slot],
                send_sem=r.team_sent.at[index],
                recv_sem=r.team_got.at[slot],
                device_id=row_peer(index),
                device_id_type=MESH,
            )

        end_places = ((0, 0), (1, size - 1))

        def small_to_line():
            named = vars(r)
            clear(r.small)
            lines = []
            for layer in range(layers):
                sums = jnp.sum(named["qv_sum_%d" % layer if layer else "qv_sum"][...], axis=1)
                lines += [sums[0:1], sums[1:2]]
            flat = jnp.concatenate(lines, axis=1)
            for layer in range(layers):
                flat = jnp.concatenate(
                    [flat, jnp.sum(named["up_sum_%d" % layer][...], axis=0, keepdims=True)], axis=1
                )
            for number in range(own_rows):
                r.small[number : number + 1] = flat[:, number * width : (number + 1) * width]
            for layer in range(layers):
                sums = jnp.sum(named["sums_%d" % layer][...], axis=1)
                for member in range(6):
                    to = own_rows + member * layers + layer
                    r.small[to : to + 1] = sums[member : member + 1]
            for slot, end in end_places:

                @pl.when(place == end)
                def _():
                    each(size - 1, lambda index: end_copy(slot, index).start())

        def small_to_teams():
            for slot, end in end_places:

                @pl.when(place != end)
                def _():
                    end_copy(slot, 0).wait_recv()

            line_total = r.small[...] + r.ends[0] + r.ends[1]
            number = lax.broadcasted_iota(jnp.int32, (count, width), 0)
            r.mine[...] = jnp.where(number < own_rows, r.small[...], line_total)
            each(teams - 1, lambda index: team_copy(index, row).start())
            r.others[row] = r.mine[...]

        def small_finish():
            each(teams - 1, lambda index: team_copy(index, row_peer(index)[0]).wait_recv())
            r.small_total[...] = lax.fori_loop(
                1, teams, lambda index, total: total + r.others[index], r.others[0]
            )
            each(teams - 1, lambda index: team_copy(index, row).wait_send())
            for slot, end in end_places:

                @pl.when(place == end)
                def _():
                    each(size - 1, lambda index: end_copy(slot, index).wait_send())

        wait()
        ffn_sum.to_partner()
        above_sum.give_share()
        r.need("proj_w")
        attend_back(r, [lambda: None, ffn_sum.to_chips])
        r.need("qkv_w")
        small_to_line()
        extras = [
            *attn_grads(r, r.attn_grad, 0),
            at_step(4, attn_sum.to_partner),
            at_step(5, small_to_teams),
            at_step(6, attn_sum.to_chips),
            at_step(span, above_sum.to_other_core),
        ]
        line_loop(size, [qkv_back_stage(r, 0, False)], extras)
        ffn_sum.sum_share()
        ffn_sum.give_share()
        attn_sum.sum_share()
        attn_sum.give_share()
        small_finish()
        above_sum.settle_whole()
        ffn_sum.settle_sum()
        attn_sum.settle_sum()
        ffn_sum.to_other_core()
        attn_sum.to_other_core()
        ffn_sum.settle_whole()
        attn_sum.settle_whole()

    outs = dict(
        grad_low=shape(rows, width, kind=LOW),
        mixed=shape(rows, width, kind=LOW),
        ffn_whole=shape(ffn_rows, width, kind=LOW),
        attn_whole=shape(attn_rows, part, kind=LOW),
        above_whole=shape(attn_rows, part, kind=LOW),
        small_total=shape(count, width),
    )
    scratch = dict(
        **back_scratch(rows, part),
        qv_sum=pltpu.VMEM((2, 8, part), F32),
        small=pltpu.VMEM((count, width), F32),
        attn_grad=pltpu.VMEM((attn_rows, part), LOW),
        ffn_share=pltpu.VMEM((ffn_rows // 2 // chips, width), LOW),
        attn_share=pltpu.VMEM((attn_rows // 2 // chips, part), LOW),
        ends=pltpu.VMEM((2, count, width), F32),
        mine=pltpu.VMEM((count, width), F32),
        others=pltpu.VMEM((teams, count, width), F32),
        end_sent=pltpu.SemaphoreType.DMA((2, size - 1)),
        end_got=pltpu.SemaphoreType.DMA((2,)),
        team_sent=pltpu.SemaphoreType.DMA((teams - 1,)),
        team_got=pltpu.SemaphoreType.DMA((teams,)),
        qkv_line=line_scratch(rows, width, 2),
        ffn_spread=Spread.scratch(chips, ffn_rows, width),
        attn_spread=Spread.scratch(chips, attn_rows, part),
        above_spread=Spread.scratch(chips, attn_rows, part),
    )
    return call(collective, body, ins, outs, scratch), own_rows


def assemble(attn_wholes, ffn_wholes, mixed, grad_low, small, own_rows, part):
    layers = len(attn_wholes)
    rows, width = mixed.shape
    hidden = ffn_wholes[0].shape[0] - width
    steps = 8
    cut = width // steps

    def for_layer(number, spec_of):
        def index(layer, step):
            return spec_of(jnp.where(layer == number, step, jnp.where(layer < number, 0, steps - 1)))

        return index

    ins, in_specs = [], []
    for number in range(layers):
        ins += [
            attn_wholes[number].reshape(4, width, part),
            attn_wholes[number].reshape(-1, part, part),
            ffn_wholes[number].reshape(-1, width, width),
        ]
        in_specs += [
            pl.BlockSpec((3, cut, part), for_layer(number, lambda step: (0, step, 0))),
            pl.BlockSpec((width // part, part // steps, part), for_layer(number, lambda step: (3, step, 0))),
            pl.BlockSpec((1 + hidden // width, cut, width), for_layer(number, lambda step: (0, step, 0))),
        ]
    slab = rows // (layers * steps)
    ins += [mixed, grad_low, small]
    row_spec = pl.BlockSpec((slab, width), lambda layer, step: (layer * steps + step, 0))
    in_specs += [row_spec, row_spec, pl.BlockSpec(small.shape, lambda layer, step: (0, 0))]
    def all_of(*dims):
        return pl.BlockSpec(dims, lambda layer, step: (0,) * len(dims))

    out_shape = [
        shape(rows, width),
        shape(rows, width),
        shape(layers, 3, width, part),
        shape(layers, part, width),
        shape(layers, width, hidden),
        shape(layers, hidden, width),
        shape(layers, 2, part),
        shape(layers, hidden),
    ] + [shape(layers, width)] * 6
    out_specs = [
        row_spec,
        row_spec,
        pl.BlockSpec((1, 3, cut, part), lambda layer, step: (layer, 0, step, 0)),
        pl.BlockSpec((1, part // steps, width), lambda layer, step: (layer, step, 0)),
        pl.BlockSpec((1, cut, hidden), lambda layer, step: (layer, step, 0)),
        pl.BlockSpec((1, cut, width), lambda layer, step: (layer, step, 0)),
        all_of(layers, 2, part),
        all_of(layers, hidden),
    ] + [all_of(layers, width)] * 6

    def body(*refs):
        sources = refs[: 3 * layers]
        mixed_in, grad_in, small_in = refs[3 * layers : 3 * layers + 3]
        mixed_out, grad_out, qkv, proj, up, down, qv, up_b, *norms = refs[3 * layers + 3 :]
        mixed_out[...] = mixed_in[...].astype(F32)
        grad_out[...] = grad_in[...].astype(F32)
        for number in range(layers):
            attn_in, proj_in, ffn_in = sources[3 * number : 3 * number + 3]

            @pl.when(pl.program_id(0) == number)
            def _():
                qkv[0] = attn_in[...].astype(F32)
                for block in range(width // part):
                    proj[0, :, block * part : (block + 1) * part] = proj_in[block].astype(F32)
                up[0] = ffn_in[0].astype(F32)
                down[0] = ffn_in[1].astype(F32)

        @pl.when((pl.program_id(0) == 0) & (pl.program_id(1) == 0))
        def _():
            values = small_in[...]
            flat = jnp.concatenate([values[n : n + 1] for n in range(own_rows)], axis=1)
            for layer in range(layers):
                for member in range(2):
                    at = (2 * layer + member) * part
                    qv[layer, member : member + 1] = flat[:, at : at + part]
                at = 2 * layers * part + layer * hidden
                up_b[layer : layer + 1] = flat[:, at : at + hidden]
            for member, norm in enumerate(norms):
                norm[...] = values[own_rows + member * layers : own_rows + (member + 1) * layers]

    return pl.pallas_call(
        body,
        grid=(layers, steps),
        out_shape=out_shape,
        in_specs=in_specs,
        out_specs=out_specs,
        compiler_params=pltpu.CompilerParams(vmem_limit_bytes=48 << 20),
    )(*ins)


def local(
    tokens,
    segment_ids,
    cotangent,
    qkv_weight,
    qv_bias,
    proj_weight,
    proj_bias,
    first_gain,
    first_shift,
    up_weight,
    up_bias,
    down_weight,
    down_bias,
    second_gain,
    second_shift,
):
    seq_count, length, width = tokens.shape
    rows = seq_count * length
    layers = qkv_weight.shape[0]
    size = lax.axis_size("tensor")
    chips = lax.axis_size("dp") // 2
    part = qkv_weight.shape[-1]
    qkv_stack = jnp.transpose(qkv_weight, (0, 2, 1, 3))
    low = tokens.reshape(rows, width)
    residual = low
    kept = []
    for layer in range(layers):
        ins = dict(
            low_in=low,
            residual=residual,
            seg_row=segment_ids,
            qkv_w=Layer(qkv_stack, layer),
            qv_bias=qv_bias,
            proj_w=Layer(proj_weight, layer),
            proj_b=proj_bias,
            first_gain=first_gain,
            first_shift=first_shift,
            up_w=Layer(up_weight, layer),
            up_b=up_bias,
            down_w=Layer(down_weight, layer),
            down_b=down_bias,
            second_gain=second_gain,
            second_shift=second_shift,
        )
        if layer + 1 < layers:
            done = forward_kernel(size, layer, layer, ins)
            kept.append((low, done))
            residual, low = done.hidden, done.low
        else:
            done = turn_kernel(size, layer, layer, dict(**ins, cotangent=cotangent.reshape(rows, width)))
            kept.append((low, done))

    above = done
    mixed_own = done.mixed_own
    all_sums, up_sums, qv_sums = [done.sums], [done.up_sum], []
    ffn_wholes, attn_wholes = [], []
    for layer in range(layers - 1, -1, -1):
        low, done = kept[layer]
        ins = dict(
            low_in=low,
            seg_row=segment_ids,
            projected=done.projected,
            log_total=done.log_total,
            context_in=done.context,
            attn_low_in=above.attn_low,
            grad_first_in=above.grad_first,
            qkv_w=Layer(qkv_stack, layer),
            proj_w=Layer(proj_weight, layer),
            ffn_grad_in=above.ffn_grad,
        )
        if layer > 0:
            _, below = kept[layer - 1]
            above = backward_kernel(
                size,
                chips,
                2 * layers - layer,
                layer,
                dict(
                    **ins,
                    unit_two=below.unit_two,
                    inverse_two=below.inverse_two,
                    second_gain=second_gain,
                    act=below.act,
                    slope=below.slope,
                    normed_low=below.normed_low,
                    unit_one=below.unit_one,
                    inverse_one=below.inverse_one,
                    first_gain=first_gain,
                    up_w=Layer(up_weight, layer - 1),
                    down_w=Layer(down_weight, layer - 1),
                ),
            )
            all_sums.insert(0, above.sums)
            up_sums.insert(0, above.up_sum)
            qv_sums.insert(0, above.qv_sum)
            ffn_wholes.insert(0, above.ffn_whole)
        else:
            last, own_rows = last_kernel(
                size,
                chips,
                2 * layers,
                layers,
                dict(
                    **ins,
                    mixed_own=mixed_own,
                    above_share=above.attn_share,
                    up_sums=up_sums,
                    all_sums=all_sums,
                    qv_sums=qv_sums,
                ),
            )
            ffn_wholes.insert(0, last.ffn_whole)
            attn_wholes = [last.attn_whole, last.above_whole]

    mixed, input_grad, qkv, proj, up, down, qv, up_b, *norms = assemble(
        attn_wholes, ffn_wholes, last.mixed, last.grad_low, last.small_total, own_rows, part
    )
    return (
        mixed.reshape(tokens.shape),
        input_grad.reshape(tokens.shape),
        jnp.transpose(qkv, (0, 2, 1, 3)),
        qv,
        proj,
        norms[5],
        norms[3],
        norms[4],
        up,
        up_b,
        down,
        norms[2],
        norms[0],
        norms[1],
    )


def solution(mesh):
    return jax.shard_map(
        local,
        mesh=mesh,
        in_specs=(
            P("dp", None, None),
            P("dp", None),
            P("dp", None, None),
            P(None, None, None, "tensor"),
            P(None, None, "tensor"),
            P(None, "tensor", None),
            P(),
            P(),
            P(),
            P(None, None, "tensor"),
            P(None, "tensor"),
            P(None, "tensor", None),
            P(),
            P(),
            P(),
        ),
        out_specs=(
            P("dp", None, None),
            P("dp", None, None),
            P(None, None, None, "tensor"),
            P(None, None, "tensor"),
            P(None, "tensor", None),
            P(),
            P(),
            P(),
            P(None, None, "tensor"),
            P(None, "tensor"),
            P(None, "tensor", None),
            P(),
            P(),
            P(),
        ),
        check_vma=False,
    )
```

```python
import math
import types

import jax
import jax.numpy as jnp
from jax import lax
from jax.experimental import pallas as pl
from jax.experimental.pallas import tpu as pltpu
from jax.sharding import PartitionSpec as P

HEAD = 64


norm_eps = 1e-12
masked_value = -1000000000.0


MESH = pl.DeviceIdType.MESH
F32 = jnp.float32
LOW = jnp.bfloat16
CHUNK = 32
LAG = 2
PIECE = 256
QUERIES = 128


def dot(a, b):
    return jnp.dot(a, b, preferred_element_type=F32)


def dot_t(a, b):
    return lax.dot_general(a, b, (((1,), (1,)), ((), ())), preferred_element_type=F32)


def dot_tn(a, b):
    return lax.dot_general(a, b, (((0,), (0,)), ((), ())), preferred_element_type=F32)


def here():
    return lax.axis_index("dp"), lax.axis_index("tensor")


def greet(size, line=True, targets=()):
    row, place = here()
    barrier = pltpu.get_barrier_semaphore()
    for count, target in targets:

        def signal(index, carry):
            pl.semaphore_signal(barrier, inc=1, device_id=target(index), device_id_type=MESH)
            return carry

        lax.fori_loop(0, count, signal, 0)
    expected = sum(count for count, _ in targets)
    left, right = place > 0, place < size - 1
    if line:

        @pl.when(left)
        def _():
            pl.semaphore_signal(barrier, inc=1, device_id=(row, place - 1), device_id_type=MESH)

        @pl.when(right)
        def _():
            pl.semaphore_signal(barrier, inc=1, device_id=(row, place + 1), device_id_type=MESH)

    def wait():
        if not line:
            pl.semaphore_wait(barrier, expected)
            return

        @pl.when(left & right)
        def _():
            pl.semaphore_wait(barrier, expected + 2)

        @pl.when(jnp.logical_not(left & right))
        def _():
            pl.semaphore_wait(barrier, expected + 1)

    return wait


def partner():
    row, place = here()
    return (row + 1 - 2 * lax.rem(row, 2), place)


def line_loop(size, stages, extras=()):
    row, place = here()
    half = stages[0].part.shape[0] // 2
    chunks = half // CHUNK
    end = size - 1
    span = 2 * LAG * end

    def rows_of(side, chunk):
        return pl.ds(pl.multiple_of(side * half + chunk * CHUNK, CHUNK), CHUNK)

    def sum_copy(stage, side, chunk, target):
        rows = rows_of(side, chunk)
        return pltpu.make_async_remote_copy(
            src_ref=stage.part.at[rows],
            dst_ref=stage.recv.at[rows],
            send_sem=stage.sems[0].at[side, chunk],
            recv_sem=stage.sems[1].at[side, chunk],
            device_id=(row, target),
            device_id_type=MESH,
        )

    def row_copy(stage, which, side, chunk, target):
        rows = rows_of(side, chunk)
        return pltpu.make_async_remote_copy(
            src_ref=stage.outs[which].at[rows],
            dst_ref=stage.outs[which].at[rows],
            send_sem=stage.sems[2].at[which, side, chunk],
            recv_sem=stage.sems[3].at[which, side, chunk],
            device_id=(row, target),
            device_id_type=MESH,
        )

    def side_facts(side):
        if side == 0:
            return place, place + 1, place - 1
        return end - place, place - 1, place + 1

    def bring_back(stage, since):
        for side in range(2):
            at, onward, back = side_facts(side)
            chunk = since - LAG * end - LAG * (end - at)

            @pl.when((at < end) & (chunk >= 0) & (chunk < chunks))
            def _():
                for which in range(len(stage.outs)):
                    row_copy(stage, which, side, chunk, back).wait_recv()

                    @pl.when(at > 0)
                    def _():
                        row_copy(stage, which, side, chunk, back).start()

    def sum_up(stage, since):
        for side in range(2):
            at, onward, back = side_facts(side)
            chunk = since - LAG * at

            @pl.when((chunk >= 0) & (chunk < chunks))
            def _():
                @pl.when(at > 0)
                def _():
                    sum_copy(stage, side, chunk, onward).wait_recv()

                @pl.when(at < end)
                def _():
                    @pl.when(at > 0)
                    def _():
                        rows = rows_of(side, chunk)
                        total = stage.part[rows].astype(F32) + stage.recv[rows].astype(F32)
                        stage.part[rows] = total.astype(LOW)

                    sum_copy(stage, side, chunk, onward).start()

                @pl.when(at == end)
                def _():
                    rows = rows_of(side, chunk)
                    own = pl.ds(pl.multiple_of(chunk * CHUNK, CHUNK), CHUNK)
                    stage.finish(rows, own, stage.part[rows].astype(F32) + stage.recv[rows].astype(F32))
                    for which in range(len(stage.outs)):
                        row_copy(stage, which, side, chunk, back).start()

    def step(now, carry):
        for number, stage in enumerate(stages):
            bring_back(stage, now - number * span)
        for number, stage in enumerate(stages):
            since = now - number * span

            @pl.when((since >= 0) & (since < chunks))
            def _():
                for side in range(2):
                    stage.produce(rows_of(side, since))

            sum_up(stage, since)
        for first, count, work in extras:

            @pl.when((now >= first) & (now < first + count))
            def _():
                work(now - first)

        return carry

    lax.fori_loop(0, chunks + span * len(stages), step, 0)

    def drain(chunk, carry):
        for stage in stages:
            for side in range(2):
                at, onward, back = side_facts(side)

                @pl.when(at < end)
                def _():
                    sum_copy(stage, side, chunk, onward).wait_send()

                @pl.when(at > 0)
                def _():
                    for which in range(len(stage.outs)):
                        row_copy(stage, which, side, chunk, back).wait_send()

        return carry

    lax.fori_loop(0, chunks, drain, 0)


def by_rows(count, work, block=32):
    def one(index, carry):
        work(pl.ds(pl.multiple_of(index * block, block), block), index * block)
        return carry

    block = min(block, count)
    lax.fori_loop(0, count // block, one, 0)


class Spread:
    def __init__(self, chips, grads, scratch):
        self.chips, self.grads = chips, grads
        self.half = grads.shape[0] // 2
        self.near, self.far, self.near_sems, self.far_sems, self.free = scratch
        row, place = here()
        self.core, self.chip, self.place = lax.rem(row, 2), row // 2, place

    @staticmethod
    def scratch(chips, rows, width):
        half = rows // 2
        far = half * 3 // 4 if chips == 4 else half // chips * (chips - 1)
        copies = 8 if chips == 4 else 2 * (chips - 1)
        sems = [
            pltpu.SemaphoreType.DMA((4,)),
            pltpu.SemaphoreType.DMA((2, copies)),
            pltpu.SemaphoreType.REGULAR,
        ]
        return [pltpu.VMEM((half, width), LOW), pltpu.VMEM((far, width), LOW), *sems, *sems]

    def rows(self, first, count):
        return pl.ds(pl.multiple_of(first, 16), count)

    def core_copy(self, source, target, number):
        return pltpu.make_async_remote_copy(
            src_ref=source,
            dst_ref=target,
            send_sem=self.near_sems.at[2 * number],
            recv_sem=self.near_sems.at[2 * number + 1],
            device_id=partner(),
            device_id_type=MESH,
        )

    def near_copy(self):
        other = self.rows((1 - self.core) * self.half, self.half)
        return self.core_copy(self.grads.at[other], self.near, 0)

    def last_copy(self):
        own = self.grads.at[self.rows(self.core * self.half, self.half)]
        return self.core_copy(own, own, 1)

    def chip_copy(self, source, target, number, chip):
        return pltpu.make_async_remote_copy(
            src_ref=source,
            dst_ref=target,
            send_sem=self.far_sems.at[0, number],
            recv_sem=self.far_sems.at[1, number],
            device_id=(chip * 2 + self.core, self.place),
            device_id_type=MESH,
        )

    def to_partner(self):
        self.near_copy().start()

    def add_partner(self):
        self.near_copy().wait_send()
        pl.semaphore_signal(self.free, inc=1, device_id=partner(), device_id_type=MESH)
        self.near_copy().wait_recv()
        base = self.core * self.half

        def add(rows, first):
            own = self.grads[self.rows(base + first, rows.size)]
            self.near[rows] = (self.near[rows].astype(F32) + own.astype(F32)).astype(LOW)

        by_rows(self.half, add)

    def to_other_core(self):
        self.take_back()
        self.settle_chips()
        pl.semaphore_wait(self.free, 1)
        self.last_copy().start()

    def settle(self):
        self.last_copy().wait_recv()
        self.last_copy().wait_send()


class DirectSpread(Spread):
    def each(self, work):
        def one(index, carry):
            work(index)
            return carry

        lax.fori_loop(0, self.chips - 1, one, 0)

    def peer(self, index):
        return lax.rem(self.chip + index + 1, self.chips)

    def far_copy(self, index):
        count = self.half // self.chips
        chip = self.peer(index)
        source = self.near.at[self.rows(chip * count, count)]
        return self.chip_copy(source, self.far.at[self.rows(index * count, count)], index, chip)

    def back_copy(self, index):
        count = self.half // self.chips
        share = self.grads.at[self.rows(self.core * self.half + self.chip * count, count)]
        return self.chip_copy(share, share, self.chips - 1 + index, self.peer(index))

    def to_chips(self):
        self.add_partner()
        self.each(lambda index: self.far_copy(index).start())

    def onward(self):
        pass

    def give_share(self):
        self.each(lambda index: self.far_copy(index).wait_recv())
        count = self.half // self.chips
        base = self.chip * count

        def add(rows, first):
            def one(index, total):
                return total + self.far[self.rows(index * count + first, rows.size)].astype(F32)

            own = self.near[self.rows(base + first, rows.size)].astype(F32)
            total = lax.fori_loop(0, self.chips - 1, one, own)
            self.grads[self.rows(self.core * self.half + base + first, rows.size)] = total.astype(LOW)

        by_rows(count, add)
        self.each(lambda index: self.back_copy(index).start())

    def pass_on(self):
        pass

    def take_back(self):
        self.each(lambda index: self.back_copy(index).wait_recv())

    def settle_chips(self):
        self.each(lambda index: self.far_copy(index).wait_send())
        self.each(lambda index: self.back_copy(index).wait_send())


class SquareSpread(Spread):
    def __init__(self, chips, grads, scratch):
        super().__init__(chips, grads, scratch)
        quarter = self.half // 4
        eighth = self.half // 8
        first, second = lax.rem(self.chip, 2), self.chip // 2
        along = self.chip + 1 - 2 * first
        across = self.chip + 2 - 4 * second
        self.quarter, self.eighth = quarter, eighth
        self.chips_of = ((along, across), (across, along))
        self.bits = ((first, second), (second, first))
        self.part = [side * 2 * quarter for side in range(2)]
        self.kept = [self.part[side] + self.bits[side][0] * quarter for side in range(2)]
        self.own = [self.kept[side] + self.bits[side][1] * eighth for side in range(2)]

    def first_copy(self, side):
        sent = self.part[side] + (1 - self.bits[side][0]) * self.quarter
        room = self.far.at[pl.ds(side * self.quarter, self.quarter)]
        source = self.near.at[self.rows(sent, self.quarter)]
        return self.chip_copy(source, room, side, self.chips_of[side][0])

    def second_copy(self, side):
        sent = self.kept[side] + (1 - self.bits[side][1]) * self.eighth
        room = self.far.at[pl.ds(2 * self.quarter + side * self.eighth, self.eighth)]
        source = self.near.at[self.rows(sent, self.eighth)]
        return self.chip_copy(source, room, 2 + side, self.chips_of[side][1])

    def share_copy(self, side):
        share = self.grads.at[self.rows(self.core * self.half + self.own[side], self.eighth)]
        return self.chip_copy(share, share, 4 + side, self.chips_of[side][1])

    def pass_copy(self, side):
        share = self.grads.at[self.rows(self.core * self.half + self.kept[side], self.quarter)]
        return self.chip_copy(share, share, 6 + side, self.chips_of[side][0])

    def to_chips(self):
        self.add_partner()
        for side in range(2):
            self.first_copy(side).start()

    def onward(self):
        for side in range(2):
            self.first_copy(side).wait_recv()
            base = self.kept[side]

            def add(rows, first, side=side, base=base):
                at = self.rows(base + first, rows.size)
                came = self.far[self.rows(side * self.quarter + first, rows.size)]
                self.near[at] = (self.near[at].astype(F32) + came.astype(F32)).astype(LOW)

            by_rows(self.quarter, add)
            self.second_copy(side).start()

    def give_share(self):
        for side in range(2):
            self.second_copy(side).wait_recv()
            base = self.own[side]

            def add(rows, first, side=side, base=base):
                came = self.far[self.rows(2 * self.quarter + side * self.eighth + first, rows.size)]
                total = self.near[self.rows(base + first, rows.size)].astype(F32) + came.astype(F32)
                to = self.rows(self.core * self.half + base + first, rows.size)
                self.grads[to] = total.astype(LOW)

            by_rows(self.eighth, add)
            self.share_copy(side).start()

    def pass_on(self):
        for side in range(2):
            self.share_copy(side).wait_recv()
            self.pass_copy(side).start()

    def take_back(self):
        for side in range(2):
            self.pass_copy(side).wait_recv()

    def settle_chips(self):
        for side in range(2):
            self.first_copy(side).wait_send()
            self.second_copy(side).wait_send()
            self.share_copy(side).wait_send()
            self.pass_copy(side).wait_send()


def spread_of(chips, grads, scratch):
    return (SquareSpread if chips == 4 else DirectSpread)(chips, grads, scratch)


def normalize(residual):
    centred = residual - jnp.mean(residual, axis=-1, keepdims=True)
    inverse = lax.rsqrt(jnp.mean(centred * centred, axis=-1, keepdims=True) + norm_eps)
    return centred * inverse, inverse


def norm_back(grad, gain, unit, inverse):
    scaled = grad * gain
    return (
        scaled
        - jnp.mean(scaled, axis=-1, keepdims=True)
        - unit * jnp.mean(scaled * unit, axis=-1, keepdims=True)
    ) * inverse


def tally(total, values):
    total[...] += jnp.sum(values.reshape(-1, 8, values.shape[-1]), axis=0)


class Layer:
    def __init__(self, array, layer):
        self.array, self.layer = array, layer


def view(refs, suffix):
    named = dict(vars(refs))
    for name, ref in vars(refs).items():
        if name.endswith(suffix):
            named[name[: -len(suffix)]] = ref
    return types.SimpleNamespace(**named)


def call(collective, body, ins, outs, scratch, into=types.MappingProxyType({}), later=()):
    vmem = pl.BlockSpec(memory_space=pltpu.VMEM)
    names = [*ins, *outs]
    fetched = {name: value for name, value in ins.items() if isinstance(value, Layer)}
    inside = {name: value for name, value in fetched.items() if name not in into}
    extra = {name: spec if isinstance(spec, list) else [spec] for name, spec in scratch.items()}

    def run(*refs):
        named = dict(zip(names, refs))
        rest = list(refs[len(names) :])
        copies = {}
        arrivals = rest.pop(0)
        for number, (name, value) in enumerate(fetched.items()):
            room = named[into[name]] if name in into else rest.pop(0)
            source = named[name] if value.layer is None else named[name].at[value.layer]
            copies[name] = pltpu.make_async_copy(source, room, arrivals.at[number])
            if name not in later:
                copies[name].start()
            named[name] = room
        for name, specs in extra.items():
            taken = [rest.pop(0) for _ in specs]
            named[name] = taken if isinstance(scratch[name], list) else taken[0]

        def need(*wanted):
            for name in wanted:
                copies[name].wait()

        def fetch(*wanted):
            for name in wanted:
                copies[name].start()

        body(types.SimpleNamespace(**named, need=need, fetch=fetch))

    results = pl.pallas_call(
        run,
        out_shape=list(outs.values()),
        in_specs=[pl.BlockSpec(memory_space=pl.ANY) if name in fetched else vmem for name in ins],
        out_specs=[vmem] * len(outs),
        scratch_shapes=[
            pltpu.SemaphoreType.DMA((len(fetched),)),
            *(pltpu.VMEM(value.array.shape[1:], value.array.dtype) for value in inside.values()),
            *(spec for specs in extra.values() for spec in specs),
        ],
        compiler_params=pltpu.CompilerParams(
            collective_id=collective, has_side_effects=True, vmem_limit_bytes=60 << 20
        ),
    )(*(value.array if isinstance(value, Layer) else value for value in ins.values()))
    return types.SimpleNamespace(**dict(zip(outs, results)))


def shape(*dims, kind=F32):
    return jax.ShapeDtypeStruct(dims, kind)


def line_scratch(rows, width, outs=1):
    chunks = rows // 2 // CHUNK
    return [
        pltpu.VMEM((rows, width), LOW),
        pltpu.VMEM((rows, width), LOW),
        pltpu.SemaphoreType.DMA((2, chunks)),
        pltpu.SemaphoreType.DMA((2, chunks)),
        pltpu.SemaphoreType.DMA((outs, 2, chunks)),
        pltpu.SemaphoreType.DMA((outs, 2, chunks)),
    ]


def stage_of(produce, finish, outs, scratch):
    part, recv, *sems = scratch
    return types.SimpleNamespace(
        produce=produce, finish=finish, outs=outs, part=part, recv=recv, sems=sems
    )


def clear(*refs):
    for ref in refs:
        ref[...] = jnp.zeros_like(ref)


def vector(ref, layer):
    return ref[...].astype(F32)[layer : layer + 1]


def head_lanes(values, head):
    lane = lax.broadcasted_iota(jnp.int32, values.shape, 1)
    return jnp.where(lane // HEAD == head, values, jnp.zeros_like(values))


def turned(values):
    return jnp.transpose(values.astype(F32)).astype(LOW)


def mark_segments(r):
    length = r.seg_row.shape[1]
    wide = jnp.broadcast_to(r.seg_row[...].astype(F32), (QUERIES, length))
    r.seg_cols[...] = jnp.transpose(wide)


def masked_block(r, keys, queries, at):
    same = r.seg_cols[...] == r.seg_row[:, at].astype(F32)
    return jnp.where(same, dot_t(keys, queries) * HEAD ** (-0.5), masked_value)


def project(r, layer):
    bias = r.qv_bias[layer].astype(F32)
    for member in range(3):
        rows = dot(r.low_in[...], r.qkv_w[member])
        if member != 1:
            rows += bias[member // 2 : member // 2 + 1]
        r.projected[member] = rows.astype(LOW)
    r.turned_rows[...] = turned(r.projected[2])


def attend(r, block):
    at = pl.ds(pl.multiple_of(block * QUERIES, QUERIES), QUERIES)
    queries = r.projected[0, at]
    heads = queries.shape[1] // HEAD
    parts = []
    for head in range(heads):
        scores = masked_block(r, r.projected[1], head_lanes(queries, head), at)
        row_max = jnp.max(scores, axis=0, keepdims=True)
        exponent = jnp.exp(scores - row_max)
        row_total = jnp.sum(exponent, axis=0, keepdims=True)
        r.log_total[head : head + 1, at] = row_max + jnp.log(row_total)
        probs = (exponent * (1.0 / row_total)).astype(LOW)
        parts.append(dot(r.turned_rows[head * HEAD : (head + 1) * HEAD], probs))
    r.context[at] = jnp.transpose(jnp.concatenate(parts, axis=0)).astype(LOW)


def attend_first(r, half):
    per_side = half // QUERIES
    for side in range(2):
        attend(r, side * per_side)
    extras = []
    for block in range(1, per_side):
        for side in range(2):
            step = max(0, block * QUERIES // CHUNK - 2 + side)
            extras.append(at_step(step, lambda block=side * per_side + block: attend(r, block)))
    return extras


def attend_back(r, between=()):
    rows = r.attn_low_in.shape[0]
    heads = r.qkv_w.shape[2] // HEAD
    scale = HEAD ** (-0.5)
    r.grad_context[...] = dot_t(r.attn_low_in[...], r.proj_w[...]).astype(LOW)
    r.turned_rows[...] = turned(r.projected[1])
    clear(r.grad_key, r.grad_value)
    for number in range(rows // QUERIES):
        at = slice(number * QUERIES, (number + 1) * QUERIES)
        queries, context_rows = r.projected[0, at], r.grad_context[at]
        parts = []
        for head in range(heads):
            to = slice(head * QUERIES, (head + 1) * QUERIES)
            r.head_queries[to] = head_lanes(queries, head)
            r.head_context[to] = head_lanes(context_rows, head)
            scores = masked_block(r, r.projected[1], r.head_queries[to], at)
            probability = jnp.exp(scores - r.log_total[head : head + 1, at])
            grad_probs = dot_t(r.projected[2], r.head_context[to])
            inner = jnp.sum(probability * grad_probs, axis=0, keepdims=True)
            grad_scores = (probability * (grad_probs - inner)).astype(LOW)
            r.score_rows[:, to] = grad_scores
            r.prob_rows[:, to] = probability.astype(LOW)
            parts.append(dot(r.turned_rows[head * HEAD : (head + 1) * HEAD], grad_scores))
        r.grad_key[...] += dot(r.score_rows[...], r.head_queries[...])
        r.grad_value[...] += dot(r.prob_rows[...], r.head_context[...])
        r.grad_proj[0, at] = (jnp.transpose(jnp.concatenate(parts, axis=0)) * scale).astype(LOW)
        if number < len(between):
            between[number]()
    r.grad_proj[1] = (r.grad_key[...] * scale).astype(LOW)
    r.grad_proj[2] = r.grad_value[...].astype(LOW)
    for slot, member in ((0, 0), (1, 2)):
        r.qv_sum[slot] = jnp.sum(r.grad_proj[member].astype(F32).reshape(-1, 8, r.qv_sum.shape[2]), axis=0)


def proj_stage(r, layer, whole):
    def produce(block):
        r.proj_line[0][block] = dot(r.context[block], r.proj_w[...]).astype(LOW)

    def finish(at, own, total):
        came = r.residual[at if whole else own].astype(F32)
        unit, inverse = normalize(came + total + vector(r.proj_b, layer))
        r.unit_one[own] = unit
        r.inverse_one[own] = inverse
        result = unit * vector(r.first_gain, layer) + vector(r.first_shift, layer)
        r.normed[own] = result
        r.normed_low[at] = result.astype(LOW)

    return stage_of(produce, finish, [r.normed_low], r.proj_line)


def ffn_stage(r, layer, last):
    def produce(block):
        pre = dot(r.normed_low[block], r.up_w[...]) + vector(r.up_b, layer)
        cdf = 0.5 * lax.erf(pre * math.sqrt(0.5)) + 0.5
        act = (pre * cdf).astype(LOW)
        slope = cdf + pre * jnp.exp(-0.5 * pre * pre) * (1.0 / math.sqrt(2 * math.pi))
        r.slope[block] = slope.astype(LOW)
        r.act[block] = act
        r.ffn_line[0][block] = dot(act, r.down_w[...]).astype(LOW)

    def finish(at, own, total):
        unit, inverse = normalize(r.normed[own] + total + vector(r.down_b, layer))
        gain = vector(r.second_gain, layer)
        result = unit * gain + vector(r.second_shift, layer)
        if last:
            r.mixed_own[own] = result.astype(LOW)
            grad_in = r.cotangent[at].astype(F32)
            grad = norm_back(grad_in, gain, unit, inverse)
            r.grad_second[own] = grad
            r.branch[at] = grad.astype(LOW)
            tally(r.sums.at[0], grad_in * unit)
            tally(r.sums.at[1], grad_in)
            tally(r.sums.at[2], grad.astype(LOW).astype(F32))
        else:
            r.unit_two[own] = unit
            r.inverse_two[own] = inverse
            r.hidden[own] = result
            r.low[at] = result.astype(LOW)

    return stage_of(produce, finish, [r.branch if last else r.low], r.ffn_line)


def ffn_back_stage(r, layer):
    def produce(block):
        pre = (dot_t(r.branch[block], r.down_w[...]) * r.slope[block].astype(F32)).astype(LOW)
        r.pre[block] = pre
        tally(r.up_sum, pre.astype(F32))
        r.back_line[0][block] = dot_t(pre, r.up_w[...]).astype(LOW)

    def finish(at, own, total):
        grad_in = r.grad_second[own] + total
        unit = r.unit_one[own]
        grad = norm_back(grad_in, vector(r.first_gain, layer), unit, r.inverse_one[own])
        r.grad_first[own] = grad
        r.attn_low[at] = grad.astype(LOW)
        tally(r.sums.at[3], grad_in * unit)
        tally(r.sums.at[4], grad_in)
        tally(r.sums.at[5], grad.astype(LOW).astype(F32))

    return stage_of(produce, finish, [r.attn_low], r.back_line)


def qkv_back_stage(r, layer, inner):
    def produce(block):
        total = sum(dot_t(r.grad_proj[member, block], r.qkv_w[member]) for member in range(3))
        r.qkv_line[0][block] = total.astype(LOW)

    def finish(at, own, total):
        grad_in = r.grad_first_in[own] + total
        if not inner:
            r.grad_low[at] = grad_in.astype(LOW)
            r.mixed[at] = r.mixed_own[own]
            return
        unit = r.unit_two[own]
        grad = norm_back(grad_in, vector(r.second_gain, layer), unit, r.inverse_two[own])
        r.grad_second[own] = grad
        r.branch[at] = grad.astype(LOW)
        tally(r.sums.at[0], grad_in * unit)
        tally(r.sums.at[1], grad_in)
        tally(r.sums.at[2], grad.astype(LOW).astype(F32))

    return stage_of(produce, finish, [r.branch] if inner else [r.grad_low, r.mixed], r.qkv_line)


def columns(piece):
    return pl.ds(pl.multiple_of(piece * PIECE, PIECE), PIECE)


def ffn_grads(r, out, first):
    width, hidden = r.up_w.shape

    def up(piece):
        rows = pl.ds(pl.multiple_of(piece * PIECE, PIECE), PIECE)
        out[rows] = dot_tn(r.normed_low[:, columns(piece)], r.pre[...]).astype(LOW)

    def down(piece):
        rows = pl.ds(pl.multiple_of(width + piece * PIECE, PIECE), PIECE)
        out[rows] = dot_tn(r.act[:, columns(piece)], r.branch[...]).astype(LOW)

    return [(first, width // PIECE, up), (first + width // PIECE, hidden // PIECE, down)]


def attn_grads(r, out, first):
    width, part = r.low_in.shape[1], r.context_in.shape[1]

    def piece_of(piece):
        for member in range(3):
            rows = pl.ds(pl.multiple_of(member * width + piece * part, part), part)
            taken = r.low_in[:, pl.ds(pl.multiple_of(piece * part, part), part)]
            out[rows] = dot_tn(taken, r.grad_proj[member]).astype(LOW)
        rows = pl.ds(pl.multiple_of(3 * width + piece * part, part), part)
        taken = r.attn_low_in[:, pl.ds(pl.multiple_of(piece * part, part), part)]
        out[rows] = dot_tn(r.context_in[...], taken).astype(LOW)

    return [(first, width // part, piece_of)]


def at_step(step, work):
    return (step, 1, lambda index: work())


def with_suffix(suffix, named):
    return {name + suffix: value for name, value in named.items()}


def kept_attention(rows, part):
    return dict(
        projected=shape(3, rows, part, kind=LOW),
        log_total=shape(part // HEAD, rows),
        context=shape(rows, part, kind=LOW),
    )


def forward_kernel(size, collective, ins):
    rows, width = ins["low_in_0"].shape
    part, hidden = ins["proj_w_0"].array.shape[1], ins["up_w_0"].array.shape[2]
    half = rows // 2
    chunks = half // CHUNK

    def body(r):
        wait = greet(size)
        clear(r.sums, r.up_sum)
        mark_segments(r)
        below, above = view(r, "_0"), view(r, "_1")
        below.residual = r.low_in_0
        above.low_in, above.residual = r.low_0, r.hidden_0
        r.need("qkv_w_0")
        project(below, 0)
        extras = attend_first(below, half)
        r.need("proj_w_0", "up_w_0", "down_w_0")
        wait()
        line_loop(size, [proj_stage(below, 0, True), ffn_stage(below, 0, False)], extras)
        r.need("qkv_w_1")
        project(above, 1)
        extras = attend_first(above, half)
        r.need("proj_w_1", "up_w_1", "down_w_1")
        stages = [proj_stage(above, 1, False), ffn_stage(above, 1, True), ffn_back_stage(above, 1)]
        first = 4 * LAG * (size - 1) + chunks
        line_loop(size, stages, [*extras, *ffn_grads(above, r.ffn_grad, first)])

    outs = dict(
        **with_suffix("_0", kept_attention(rows, part)),
        **with_suffix("_1", kept_attention(rows, part)),
        unit_one_0=shape(half, width),
        inverse_one_0=shape(half, 1),
        normed_low_0=shape(rows, width, kind=LOW),
        act_0=shape(rows, hidden, kind=LOW),
        slope_0=shape(rows, hidden, kind=LOW),
        unit_two_0=shape(half, width),
        inverse_two_0=shape(half, 1),
        low_0=shape(rows, width, kind=LOW),
        mixed_own=shape(half, width, kind=LOW),
        grad_first=shape(half, width),
        attn_low=shape(rows, width, kind=LOW),
        ffn_grad=shape(width + hidden, width, kind=LOW),
        up_sum=shape(8, hidden),
        sums=shape(6, 8, width),
    )
    scratch = dict(
        hidden_0=pltpu.VMEM((half, width), F32),
        normed=pltpu.VMEM((half, width), F32),
        turned_rows=pltpu.VMEM((part, rows), LOW),
        seg_cols=pltpu.VMEM((rows, QUERIES), F32),
        unit_one_1=pltpu.VMEM((half, width), F32),
        inverse_one_1=pltpu.VMEM((half, 1), F32),
        normed_low_1=pltpu.VMEM((rows, width), LOW),
        act_1=pltpu.VMEM((rows, hidden), LOW),
        slope_1=pltpu.VMEM((rows, hidden), LOW),
        pre=pltpu.VMEM((rows, hidden), LOW),
        branch=pltpu.VMEM((rows, width), LOW),
        grad_second=pltpu.VMEM((half, width), F32),
        proj_line_0=line_scratch(rows, width),
        ffn_line_0=line_scratch(rows, width),
        proj_line_1=line_scratch(rows, width),
        ffn_line_1=line_scratch(rows, width),
        back_line=line_scratch(rows, width),
    )
    return call(collective, body, ins, outs, scratch)


def backward_kernel(size, chips, collective, layers, ins):
    rows, width = ins["attn_low_1"].shape
    part, hidden = ins["proj_w_0"].array.shape[1], ins["up_w"].array.shape[2]
    half = rows // 2
    chunks = half // CHUNK
    span = 2 * LAG * (size - 1)
    ffn_rows, attn_rows = width + hidden, 4 * width
    own_rows = layers * (2 * part + hidden) // width
    count = -(-(own_rows + 6 * layers) // 8) * 8
    teams = 2 * chips

    def row_peer(index):
        row, place = here()
        return (lax.rem(row + index + 1, teams), place)

    def line_peer(index):
        row, place = here()
        return (row, lax.rem(place + index + 1, size))

    def each(number, work):
        def one(index, carry):
            work(index)
            return carry

        lax.fori_loop(0, number, one, 0)

    def body(r):
        row, place = here()
        clear(r.ends, r.sums_0, r.up_sum_0)
        wait = greet(size, line=False, targets=[(teams - 1, row_peer), (size - 1, line_peer)])
        ffn_above = spread_of(chips, r.ffn_whole_1, r.ffn_spread[:5])
        attn_above = spread_of(chips, r.attn_whole_1, r.attn_spread[:5])
        ffn_below = spread_of(chips, r.ffn_whole_0, r.ffn_spread[:2] + r.ffn_spread[5:])
        attn_below = spread_of(chips, r.attn_whole_0, r.attn_spread[:2] + r.attn_spread[5:])
        above, below = view(r, "_1"), view(r, "_0")
        above.grad_first_in, above.attn_low_in = r.grad_first_1, r.attn_low_1
        below.grad_first_in, below.attn_low_in = r.grad_first_0, r.attn_low_0
        middle = types.SimpleNamespace(
            **{**vars(r), "sums": r.sums_0, "up_sum": r.up_sum_0, "grad_first": r.grad_first_0, "attn_low": r.attn_low_0}
        )
        above.sums = r.sums_0
        above.grad_second = middle.grad_second = r.grad_first_0
        below.qkv_line = [*r.qkv_line_1[:2], *r.qkv_sems_0]

        def end_copy(slot, index):
            return pltpu.make_async_remote_copy(
                src_ref=r.small,
                dst_ref=r.ends.at[slot],
                send_sem=r.end_sent.at[slot, index],
                recv_sem=r.end_got.at[slot],
                device_id=line_peer(index),
                device_id_type=MESH,
            )

        def team_copy(index, slot):
            return pltpu.make_async_remote_copy(
                src_ref=r.mine,
                dst_ref=r.others.at[slot],
                send_sem=r.team_sent.at[index],
                recv_sem=r.team_got.at[slot],
                device_id=row_peer(index),
                device_id_type=MESH,
            )

        end_places = ((0, 0), (1, size - 1))

        def small_to_line():
            named = vars(r)
            clear(r.small)
            lines = []
            for layer in range(layers):
                sums = jnp.sum(named["qv_sum_%d" % layer][...], axis=1)
                lines += [sums[0:1], sums[1:2]]
            for layer in range(layers):
                lines += [jnp.sum(named["up_sum_%d" % layer][...], axis=0, keepdims=True)]
            flat = jnp.concatenate(lines, axis=1)
            for number in range(own_rows):
                r.small[number : number + 1] = flat[:, number * width : (number + 1) * width]
            for layer in range(layers):
                sums = jnp.sum(named["sums_%d" % layer][...], axis=1)
                for member in range(6):
                    to = own_rows + member * layers + layer
                    r.small[to : to + 1] = sums[member : member + 1]
            for slot, end in end_places:

                @pl.when(place == end)
                def _():
                    each(size - 1, lambda index: end_copy(slot, index).start())

        def small_to_teams():
            for slot, end in end_places:

                @pl.when(place != end)
                def _():
                    end_copy(slot, 0).wait_recv()

            line_total = r.small[...] + r.ends[0] + r.ends[1]
            number = lax.broadcasted_iota(jnp.int32, (count, width), 0)
            r.mine[...] = jnp.where(number < own_rows, r.small[...], line_total)
            each(teams - 1, lambda index: team_copy(index, row).start())
            r.others[row] = r.mine[...]

        def small_finish():
            each(teams - 1, lambda index: team_copy(index, row_peer(index)[0]).wait_recv())
            r.small_total[...] = lax.fori_loop(
                1, teams, lambda index, total: total + r.others[index], r.others[0]
            )
            each(teams - 1, lambda index: team_copy(index, row).wait_send())
            for slot, end in end_places:

                @pl.when(place == end)
                def _():
                    each(size - 1, lambda index: end_copy(slot, index).wait_send())

        mark_segments(r)
        r.need("ffn_grad_1", "proj_w_1")
        wait()
        ffn_above.to_partner()
        attend_back(above, [lambda: None, ffn_above.to_chips])
        r.need("qkv_w_1", "up_w", "down_w")
        extras = [
            *attn_grads(above, r.attn_whole_1, 1),
            at_step(2, ffn_above.onward),
            at_step(5, ffn_above.give_share),
            at_step(6, attn_above.to_partner),
            at_step(8, attn_above.to_chips),
            at_step(9, ffn_above.pass_on),
            at_step(span - 2, lambda: r.fetch("proj_w_0", "qkv_w_0")),
            at_step(span, attn_above.onward),
            at_step(span + 2, attn_above.give_share),
            at_step(span + 3, ffn_above.to_other_core),
            at_step(span + 5, attn_above.pass_on),
            *ffn_grads(middle, r.ffn_whole_0, span + chunks),
            at_step(span + chunks, ffn_above.settle),
            at_step(span + chunks + 2, attn_above.to_other_core),
            at_step(2 * span + 3, attn_above.settle),
            at_step(2 * span + 4, ffn_below.to_partner),
            at_step(2 * span + 6, ffn_below.to_chips),
        ]
        stages = [qkv_back_stage(above, 0, True), ffn_back_stage(middle, 0)]
        line_loop(size, stages, extras)
        r.need("proj_w_0", "qkv_w_0")
        attend_back(below)
        small_to_line()
        extras = [
            at_step(0, ffn_below.onward),
            *attn_grads(below, r.attn_whole_0, 0),
            at_step(4, attn_below.to_partner),
            at_step(4, ffn_below.give_share),
            at_step(5, small_to_teams),
            at_step(6, attn_below.to_chips),
            at_step(7, ffn_below.pass_on),
            at_step(10, attn_below.onward),
            at_step(12, attn_below.give_share),
            at_step(13, ffn_below.to_other_core),
            at_step(15, attn_below.pass_on),
            at_step(18, attn_below.to_other_core),
        ]
        line_loop(size, [qkv_back_stage(below, 0, False)], extras)
        small_finish()
        for spread in (ffn_below, attn_below):
            spread.settle()

    heads = part // HEAD
    rooms = {"ffn_grad_1": "ffn_whole_1", "qkv_w_0": "qkv_w_1", "proj_w_0": "proj_w_1"}
    outs = dict(
        grad_low=shape(rows, width, kind=LOW),
        mixed=shape(rows, width, kind=LOW),
        ffn_whole_1=shape(ffn_rows, width, kind=LOW),
        attn_whole_1=shape(attn_rows, part, kind=LOW),
        ffn_whole_0=shape(ffn_rows, width, kind=LOW),
        attn_whole_0=shape(attn_rows, part, kind=LOW),
        small_total=shape(count, width),
    )
    scratch = dict(
        seg_cols=pltpu.VMEM((rows, QUERIES), F32),
        turned_rows=pltpu.VMEM((part, rows), LOW),
        grad_context=pltpu.VMEM((rows, part), LOW),
        grad_key=pltpu.VMEM((rows, part), F32),
        grad_value=pltpu.VMEM((rows, part), F32),
        grad_proj=pltpu.VMEM((3, rows, part), LOW),
        head_queries=pltpu.VMEM((heads * QUERIES, part), LOW),
        head_context=pltpu.VMEM((heads * QUERIES, part), LOW),
        score_rows=pltpu.VMEM((rows, heads * QUERIES), LOW),
        prob_rows=pltpu.VMEM((rows, heads * QUERIES), LOW),
        qv_sum_0=pltpu.VMEM((2, 8, part), F32),
        qv_sum_1=pltpu.VMEM((2, 8, part), F32),
        sums_0=pltpu.VMEM((6, 8, width), F32),
        up_sum_0=pltpu.VMEM((8, hidden), F32),
        pre=pltpu.VMEM((rows, hidden), LOW),
        branch=pltpu.VMEM((rows, width), LOW),
        grad_first_0=pltpu.VMEM((half, width), F32),
        attn_low_0=pltpu.VMEM((rows, width), LOW),
        small=pltpu.VMEM((count, width), F32),
        ends=pltpu.VMEM((2, count, width), F32),
        mine=pltpu.VMEM((count, width), F32),
        others=pltpu.VMEM((teams, count, width), F32),
        end_sent=pltpu.SemaphoreType.DMA((2, size - 1)),
        end_got=pltpu.SemaphoreType.DMA((2,)),
        team_sent=pltpu.SemaphoreType.DMA((teams - 1,)),
        team_got=pltpu.SemaphoreType.DMA((teams,)),
        qkv_line_1=line_scratch(rows, width),
        back_line=line_scratch(rows, width),
        qkv_sems_0=line_scratch(rows, width, 2)[2:],
        ffn_spread=Spread.scratch(chips, ffn_rows, width),
        attn_spread=Spread.scratch(chips, attn_rows, part),
    )
    return call(collective, body, ins, outs, scratch, rooms, ("qkv_w_0", "proj_w_0")), own_rows


def assemble(attn_wholes, ffn_wholes, mixed, grad_low, small, own_rows, part):
    layers = len(attn_wholes)
    rows, width = mixed.shape
    hidden = ffn_wholes[0].shape[0] - width
    steps = 8
    cut = width // steps

    def for_layer(number, spec_of):
        def index(layer, step):
            return spec_of(jnp.where(layer == number, step, jnp.where(layer < number, 0, steps - 1)))

        return index

    ins, in_specs = [], []
    for number in range(layers):
        ins += [
            attn_wholes[number].reshape(4, width, part),
            attn_wholes[number].reshape(-1, part, part),
            ffn_wholes[number].reshape(-1, width, width),
        ]
        in_specs += [
            pl.BlockSpec((3, cut, part), for_layer(number, lambda step: (0, step, 0))),
            pl.BlockSpec((width // part, part // steps, part), for_layer(number, lambda step: (3, step, 0))),
            pl.BlockSpec((1 + hidden // width, cut, width), for_layer(number, lambda step: (0, step, 0))),
        ]
    slab = rows // (layers * steps)
    ins += [mixed, grad_low, small]
    row_spec = pl.BlockSpec((slab, width), lambda layer, step: (layer * steps + step, 0))
    in_specs += [row_spec, row_spec, pl.BlockSpec(small.shape, lambda layer, step: (0, 0))]
    def all_of(*dims):
        return pl.BlockSpec(dims, lambda layer, step: (0,) * len(dims))

    out_shape = [
        shape(rows, width),
        shape(rows, width),
        shape(layers, 3, width, part),
        shape(layers, part, width),
        shape(layers, width, hidden),
        shape(layers, hidden, width),
        shape(layers, 2, part),
        shape(layers, hidden),
    ] + [shape(layers, width)] * 6
    out_specs = [
        row_spec,
        row_spec,
        pl.BlockSpec((1, 3, cut, part), lambda layer, step: (layer, 0, step, 0)),
        pl.BlockSpec((1, part // steps, width), lambda layer, step: (layer, step, 0)),
        pl.BlockSpec((1, cut, hidden), lambda layer, step: (layer, step, 0)),
        pl.BlockSpec((1, cut, width), lambda layer, step: (layer, step, 0)),
        all_of(layers, 2, part),
        all_of(layers, hidden),
    ] + [all_of(layers, width)] * 6

    def body(*refs):
        sources = refs[: 3 * layers]
        mixed_in, grad_in, small_in = refs[3 * layers : 3 * layers + 3]
        mixed_out, grad_out, qkv, proj, up, down, qv, up_b, *norms = refs[3 * layers + 3 :]
        mixed_out[...] = mixed_in[...].astype(F32)
        grad_out[...] = grad_in[...].astype(F32)
        for number in range(layers):
            attn_in, proj_in, ffn_in = sources[3 * number : 3 * number + 3]

            @pl.when(pl.program_id(0) == number)
            def _():
                qkv[0] = attn_in[...].astype(F32)
                for block in range(width // part):
                    proj[0, :, block * part : (block + 1) * part] = proj_in[block].astype(F32)
                up[0] = ffn_in[0].astype(F32)
                down[0] = ffn_in[1].astype(F32)

        @pl.when((pl.program_id(0) == 0) & (pl.program_id(1) == 0))
        def _():
            values = small_in[...]
            flat = jnp.concatenate([values[n : n + 1] for n in range(own_rows)], axis=1)
            for layer in range(layers):
                for member in range(2):
                    at = (2 * layer + member) * part
                    qv[layer, member : member + 1] = flat[:, at : at + part]
                at = 2 * layers * part + layer * hidden
                up_b[layer : layer + 1] = flat[:, at : at + hidden]
            for member, norm in enumerate(norms):
                norm[...] = values[own_rows + member * layers : own_rows + (member + 1) * layers]

    return pl.pallas_call(
        body,
        grid=(layers, steps),
        out_shape=out_shape,
        in_specs=in_specs,
        out_specs=out_specs,
        compiler_params=pltpu.CompilerParams(vmem_limit_bytes=48 << 20),
    )(*ins)


def local(
    tokens,
    segment_ids,
    cotangent,
    qkv_weight,
    qv_bias,
    proj_weight,
    proj_bias,
    first_gain,
    first_shift,
    up_weight,
    up_bias,
    down_weight,
    down_bias,
    second_gain,
    second_shift,
):
    seq_count, length, width = tokens.shape
    rows = seq_count * length
    layers = qkv_weight.shape[0]
    size = lax.axis_size("tensor")
    chips = lax.axis_size("dp") // 2
    part = qkv_weight.shape[-1]
    qkv_stack = jnp.transpose(qkv_weight, (0, 2, 1, 3))
    low = tokens.reshape(rows, width)
    weights = dict(qkv_w=qkv_stack, proj_w=proj_weight, up_w=up_weight, down_w=down_weight)
    ins = dict(
        low_in_0=low,
        cotangent=cotangent.reshape(rows, width),
        seg_row=segment_ids,
        qv_bias=qv_bias,
        proj_b=proj_bias,
        first_gain=first_gain,
        first_shift=first_shift,
        up_b=up_bias,
        down_b=down_bias,
        second_gain=second_gain,
        second_shift=second_shift,
    )
    for layer in range(layers):
        for name, array in weights.items():
            ins["%s_%d" % (name, layer)] = Layer(array, layer)
    done = forward_kernel(size, 0, ins)
    last, own_rows = backward_kernel(
        size,
        chips,
        1,
        layers,
        dict(
            seg_row=segment_ids,
            low_in_0=low,
            low_in_1=done.low_0,
            projected_0=done.projected_0,
            projected_1=done.projected_1,
            log_total_0=done.log_total_0,
            log_total_1=done.log_total_1,
            context_in_0=done.context_0,
            context_in_1=done.context_1,
            attn_low_1=done.attn_low,
            grad_first_1=done.grad_first,
            sums_1=done.sums,
            up_sum_1=done.up_sum,
            mixed_own=done.mixed_own,
            unit_two=done.unit_two_0,
            inverse_two=done.inverse_two_0,
            unit_one=done.unit_one_0,
            inverse_one=done.inverse_one_0,
            act=done.act_0,
            slope=done.slope_0,
            normed_low=done.normed_low_0,
            first_gain=first_gain,
            second_gain=second_gain,
            proj_w_1=Layer(proj_weight, 1),
            ffn_grad_1=Layer(done.ffn_grad, None),
            qkv_w_1=Layer(qkv_stack, 1),
            up_w=Layer(up_weight, 0),
            down_w=Layer(down_weight, 0),
            proj_w_0=Layer(proj_weight, 0),
            qkv_w_0=Layer(qkv_stack, 0),
        ),
    )
    ffn_wholes = [last.ffn_whole_0, last.ffn_whole_1]
    attn_wholes = [last.attn_whole_0, last.attn_whole_1]

    mixed, input_grad, qkv, proj, up, down, qv, up_b, *norms = assemble(
        attn_wholes, ffn_wholes, last.mixed, last.grad_low, last.small_total, own_rows, part
    )
    return (
        mixed.reshape(tokens.shape),
        input_grad.reshape(tokens.shape),
        jnp.transpose(qkv, (0, 2, 1, 3)),
        qv,
        proj,
        norms[5],
        norms[3],
        norms[4],
        up,
        up_b,
        down,
        norms[2],
        norms[0],
        norms[1],
    )


def solution(mesh):
    return jax.shard_map(
        local,
        mesh=mesh,
        in_specs=(
            P("dp", None, None),
            P("dp", None),
            P("dp", None, None),
            P(None, None, None, "tensor"),
            P(None, None, "tensor"),
            P(None, "tensor", None),
            P(),
            P(),
            P(),
            P(None, None, "tensor"),
            P(None, "tensor"),
            P(None, "tensor", None),
            P(),
            P(),
            P(),
        ),
        out_specs=(
            P("dp", None, None),
            P("dp", None, None),
            P(None, None, None, "tensor"),
            P(None, None, "tensor"),
            P(None, "tensor", None),
            P(),
            P(),
            P(),
            P(None, None, "tensor"),
            P(None, "tensor"),
            P(None, "tensor", None),
            P(),
            P(),
            P(),
        ),
        check_vma=False,
    )
```

```python
import math
import types

import jax
import jax.numpy as jnp
from jax import lax
from jax.experimental import pallas as pl
from jax.experimental.pallas import tpu as pltpu
from jax.sharding import PartitionSpec as P

HEAD = 64


norm_eps = 1e-12
masked_value = -1000000000.0


MESH = pl.DeviceIdType.MESH
F32 = jnp.float32
LOW = jnp.bfloat16
CHUNK = 32
LAG = 2
PIECE = 512
QUERIES = 128


def dot(a, b):
    return jnp.dot(a, b, preferred_element_type=F32)


def dot_t(a, b):
    return lax.dot_general(a, b, (((1,), (1,)), ((), ())), preferred_element_type=F32)


def dot_tn(a, b):
    return lax.dot_general(a, b, (((0,), (0,)), ((), ())), preferred_element_type=F32)


def here():
    return lax.axis_index("dp"), lax.axis_index("tensor")


def greet(size, line=True, targets=()):
    row, place = here()
    barrier = pltpu.get_barrier_semaphore()
    for count, target in targets:

        def signal(index, carry):
            pl.semaphore_signal(barrier, inc=1, device_id=target(index), device_id_type=MESH)
            return carry

        lax.fori_loop(0, count, signal, 0)
    expected = sum(count for count, _ in targets)
    left, right = place > 0, place < size - 1
    if line:

        @pl.when(left)
        def _():
            pl.semaphore_signal(barrier, inc=1, device_id=(row, place - 1), device_id_type=MESH)

        @pl.when(right)
        def _():
            pl.semaphore_signal(barrier, inc=1, device_id=(row, place + 1), device_id_type=MESH)

    def wait():
        if not line:
            pl.semaphore_wait(barrier, expected)
            return

        @pl.when(left & right)
        def _():
            pl.semaphore_wait(barrier, expected + 2)

        @pl.when(jnp.logical_not(left & right))
        def _():
            pl.semaphore_wait(barrier, expected + 1)

    return wait


def partner():
    row, place = here()
    return (row + 1 - 2 * lax.rem(row, 2), place)


def line_loop(size, stages, extras=()):
    row, place = here()
    half = stages[0].part.shape[0] // 2
    chunks = half // CHUNK
    end = size - 1
    span = 2 * LAG * end

    def rows_of(side, chunk):
        return pl.ds(pl.multiple_of(side * half + chunk * CHUNK, CHUNK), CHUNK)

    def sum_copy(stage, side, chunk, target):
        rows = rows_of(side, chunk)
        return pltpu.make_async_remote_copy(
            src_ref=stage.part.at[rows],
            dst_ref=stage.recv.at[rows],
            send_sem=stage.sems[0].at[side, chunk],
            recv_sem=stage.sems[1].at[side, chunk],
            device_id=(row, target),
            device_id_type=MESH,
        )

    def row_copy(stage, which, side, chunk, target):
        rows = rows_of(side, chunk)
        return pltpu.make_async_remote_copy(
            src_ref=stage.outs[which].at[rows],
            dst_ref=stage.outs[which].at[rows],
            send_sem=stage.sems[2].at[which, side, chunk],
            recv_sem=stage.sems[3].at[which, side, chunk],
            device_id=(row, target),
            device_id_type=MESH,
        )

    def side_facts(side):
        if side == 0:
            return place, place + 1, place - 1
        return end - place, place - 1, place + 1

    def bring_back(stage, since):
        for side in range(2):
            at, onward, back = side_facts(side)
            chunk = since - LAG * end - LAG * (end - at)

            @pl.when((at < end) & (chunk >= 0) & (chunk < chunks))
            def _():
                for which in range(len(stage.outs)):
                    row_copy(stage, which, side, chunk, back).wait_recv()

                    @pl.when(at > 0)
                    def _():
                        row_copy(stage, which, side, chunk, back).start()

    def sum_up(stage, since):
        for side in range(2):
            at, onward, back = side_facts(side)
            chunk = since - LAG * at

            @pl.when((chunk >= 0) & (chunk < chunks))
            def _():
                @pl.when(at > 0)
                def _():
                    sum_copy(stage, side, chunk, onward).wait_recv()

                @pl.when(at < end)
                def _():
                    @pl.when(at > 0)
                    def _():
                        rows = rows_of(side, chunk)
                        total = stage.part[rows].astype(F32) + stage.recv[rows].astype(F32)
                        stage.part[rows] = total.astype(LOW)

                    sum_copy(stage, side, chunk, onward).start()

                @pl.when(at == end)
                def _():
                    rows = rows_of(side, chunk)
                    own = pl.ds(pl.multiple_of(chunk * CHUNK, CHUNK), CHUNK)
                    stage.finish(rows, own, stage.part[rows].astype(F32) + stage.recv[rows].astype(F32))
                    for which in range(len(stage.outs)):
                        row_copy(stage, which, side, chunk, back).start()

    def step(now, carry):
        for number, stage in enumerate(stages):
            bring_back(stage, now - number * span)
        for number, stage in enumerate(stages):
            since = now - number * span

            @pl.when((since >= 0) & (since < chunks))
            def _():
                for side in range(2):
                    stage.produce(rows_of(side, since))

            sum_up(stage, since)
        for first, count, work in extras:

            @pl.when((now >= first) & (now < first + count))
            def _():
                work(now - first)

        return carry

    lax.fori_loop(0, chunks + span * len(stages), step, 0)

    def drain(chunk, carry):
        for stage in stages:
            for side in range(2):
                at, onward, back = side_facts(side)

                @pl.when(at < end)
                def _():
                    sum_copy(stage, side, chunk, onward).wait_send()

                @pl.when(at > 0)
                def _():
                    for which in range(len(stage.outs)):
                        row_copy(stage, which, side, chunk, back).wait_send()

        return carry

    lax.fori_loop(0, chunks, drain, 0)


def by_rows(count, work, block=32):
    def one(index, carry):
        work(pl.ds(pl.multiple_of(index * block, block), block), index * block)
        return carry

    block = min(block, count)
    lax.fori_loop(0, count // block, one, 0)


class Spread:
    def __init__(self, chips, grads, scratch):
        self.chips, self.grads = chips, grads
        self.half = grads.shape[0] // 2
        self.near, self.far, self.near_sems, self.far_sems, self.free = scratch
        row, place = here()
        self.core, self.chip, self.place = lax.rem(row, 2), row // 2, place

    @staticmethod
    def scratch(chips, rows, width):
        half = rows // 2
        far = half * 3 // 4 if chips == 4 else half // chips * (chips - 1)
        copies = 8 if chips == 4 else 2 * (chips - 1)
        sems = [
            pltpu.SemaphoreType.DMA((4,)),
            pltpu.SemaphoreType.DMA((2, copies)),
            pltpu.SemaphoreType.REGULAR,
        ]
        return [pltpu.VMEM((half, width), LOW), pltpu.VMEM((far, width), LOW), *sems, *sems]

    def rows(self, first, count):
        return pl.ds(pl.multiple_of(first, 16), count)

    def core_copy(self, source, target, number):
        return pltpu.make_async_remote_copy(
            src_ref=source,
            dst_ref=target,
            send_sem=self.near_sems.at[2 * number],
            recv_sem=self.near_sems.at[2 * number + 1],
            device_id=partner(),
            device_id_type=MESH,
        )

    def near_copy(self):
        other = self.rows((1 - self.core) * self.half, self.half)
        return self.core_copy(self.grads.at[other], self.near, 0)

    def last_copy(self):
        own = self.grads.at[self.rows(self.core * self.half, self.half)]
        return self.core_copy(own, own, 1)

    def chip_copy(self, source, target, number, chip):
        return pltpu.make_async_remote_copy(
            src_ref=source,
            dst_ref=target,
            send_sem=self.far_sems.at[0, number],
            recv_sem=self.far_sems.at[1, number],
            device_id=(chip * 2 + self.core, self.place),
            device_id_type=MESH,
        )

    def to_partner(self):
        self.near_copy().start()

    def add_partner(self):
        self.near_copy().wait_send()
        pl.semaphore_signal(self.free, inc=1, device_id=partner(), device_id_type=MESH)
        self.near_copy().wait_recv()
        base = self.core * self.half

        def add(rows, first):
            own = self.grads[self.rows(base + first, rows.size)]
            self.near[rows] = self.near[rows] + own

        by_rows(self.half, add)

    def to_other_core(self):
        self.take_back()
        self.settle_chips()
        pl.semaphore_wait(self.free, 1)
        self.last_copy().start()

    def settle(self):
        self.last_copy().wait_recv()
        self.last_copy().wait_send()


class DirectSpread(Spread):
    def each(self, work):
        def one(index, carry):
            work(index)
            return carry

        lax.fori_loop(0, self.chips - 1, one, 0)

    def peer(self, index):
        return lax.rem(self.chip + index + 1, self.chips)

    def far_copy(self, index):
        count = self.half // self.chips
        chip = self.peer(index)
        source = self.near.at[self.rows(chip * count, count)]
        return self.chip_copy(source, self.far.at[self.rows(index * count, count)], index, chip)

    def back_copy(self, index):
        count = self.half // self.chips
        share = self.grads.at[self.rows(self.core * self.half + self.chip * count, count)]
        return self.chip_copy(share, share, self.chips - 1 + index, self.peer(index))

    def to_chips(self):
        self.add_partner()
        self.each(lambda index: self.far_copy(index).start())

    def onward(self):
        pass

    def give_share(self):
        self.each(lambda index: self.far_copy(index).wait_recv())
        count = self.half // self.chips
        base = self.chip * count

        def add(rows, first):
            def one(index, total):
                return total + self.far[self.rows(index * count + first, rows.size)].astype(F32)

            own = self.near[self.rows(base + first, rows.size)].astype(F32)
            total = lax.fori_loop(0, self.chips - 1, one, own)
            self.grads[self.rows(self.core * self.half + base + first, rows.size)] = total.astype(LOW)

        by_rows(count, add)
        self.each(lambda index: self.back_copy(index).start())

    def pass_on(self):
        pass

    def take_back(self):
        self.each(lambda index: self.back_copy(index).wait_recv())

    def settle_chips(self):
        self.each(lambda index: self.far_copy(index).wait_send())
        self.each(lambda index: self.back_copy(index).wait_send())


class SquareSpread(Spread):
    def __init__(self, chips, grads, scratch):
        super().__init__(chips, grads, scratch)
        quarter = self.half // 4
        eighth = self.half // 8
        first, second = lax.rem(self.chip, 2), self.chip // 2
        along = self.chip + 1 - 2 * first
        across = self.chip + 2 - 4 * second
        self.quarter, self.eighth = quarter, eighth
        self.chips_of = ((along, across), (across, along))
        self.bits = ((first, second), (second, first))
        self.part = [side * 2 * quarter for side in range(2)]
        self.kept = [self.part[side] + self.bits[side][0] * quarter for side in range(2)]
        self.own = [self.kept[side] + self.bits[side][1] * eighth for side in range(2)]

    def first_copy(self, side):
        sent = self.part[side] + (1 - self.bits[side][0]) * self.quarter
        room = self.far.at[pl.ds(side * self.quarter, self.quarter)]
        source = self.near.at[self.rows(sent, self.quarter)]
        return self.chip_copy(source, room, side, self.chips_of[side][0])

    def second_copy(self, side):
        sent = self.kept[side] + (1 - self.bits[side][1]) * self.eighth
        room = self.far.at[pl.ds(2 * self.quarter + side * self.eighth, self.eighth)]
        source = self.near.at[self.rows(sent, self.eighth)]
        return self.chip_copy(source, room, 2 + side, self.chips_of[side][1])

    def share_copy(self, side):
        share = self.grads.at[self.rows(self.core * self.half + self.own[side], self.eighth)]
        return self.chip_copy(share, share, 4 + side, self.chips_of[side][1])

    def pass_copy(self, side):
        share = self.grads.at[self.rows(self.core * self.half + self.kept[side], self.quarter)]
        return self.chip_copy(share, share, 6 + side, self.chips_of[side][0])

    def to_chips(self):
        self.add_partner()
        for side in range(2):
            self.first_copy(side).start()

    def onward(self):
        for side in range(2):
            self.first_copy(side).wait_recv()
            base = self.kept[side]

            def add(rows, first, side=side, base=base):
                at = self.rows(base + first, rows.size)
                came = self.far[self.rows(side * self.quarter + first, rows.size)]
                self.near[at] = self.near[at] + came

            by_rows(self.quarter, add)
            self.second_copy(side).start()

    def give_share(self):
        for side in range(2):
            self.second_copy(side).wait_recv()
            base = self.own[side]

            def add(rows, first, side=side, base=base):
                came = self.far[self.rows(2 * self.quarter + side * self.eighth + first, rows.size)]
                total = self.near[self.rows(base + first, rows.size)].astype(F32) + came.astype(F32)
                to = self.rows(self.core * self.half + base + first, rows.size)
                self.grads[to] = total.astype(LOW)

            by_rows(self.eighth, add)
            self.share_copy(side).start()

    def pass_on(self):
        for side in range(2):
            self.share_copy(side).wait_recv()
            self.pass_copy(side).start()

    def take_back(self):
        for side in range(2):
            self.pass_copy(side).wait_recv()

    def settle_chips(self):
        for side in range(2):
            self.first_copy(side).wait_send()
            self.second_copy(side).wait_send()
            self.share_copy(side).wait_send()
            self.pass_copy(side).wait_send()


def spread_of(chips, grads, scratch):
    return (SquareSpread if chips == 4 else DirectSpread)(chips, grads, scratch)


def normalize(residual):
    centred = residual - jnp.mean(residual, axis=-1, keepdims=True)
    inverse = lax.rsqrt(jnp.mean(centred * centred, axis=-1, keepdims=True) + norm_eps)
    return centred * inverse, inverse


def norm_back(grad, gain, unit, inverse):
    scaled = grad * gain
    return (
        scaled
        - jnp.mean(scaled, axis=-1, keepdims=True)
        - unit * jnp.mean(scaled * unit, axis=-1, keepdims=True)
    ) * inverse


def tally(total, values):
    total[...] += jnp.sum(values.reshape(-1, 8, values.shape[-1]), axis=0)


class Layer:
    def __init__(self, array, layer):
        self.array, self.layer = array, layer

    def room(self):
        return self.array.shape if self.layer is None else self.array.shape[1:]


def whole(array):
    return Layer(array, None)


def view(refs, suffix):
    named = dict(vars(refs))
    for name, ref in vars(refs).items():
        if name.endswith(suffix):
            named[name[: -len(suffix)]] = ref
    return types.SimpleNamespace(**named)


def call(collective, body, ins, outs, scratch, into=types.MappingProxyType({}), later=(), sent=()):
    vmem = pl.BlockSpec(memory_space=pltpu.VMEM)
    names = [*ins, *outs]
    fetched = {name: value for name, value in ins.items() if isinstance(value, Layer)}
    inside = {name: value for name, value in fetched.items() if name not in into}
    extra = {name: spec if isinstance(spec, list) else [spec] for name, spec in scratch.items()}

    def run(*refs):
        named = dict(zip(names, refs))
        rest = list(refs[len(names) :])
        copies, leaving = {}, {}
        arrivals, departures = rest.pop(0), rest.pop(0)
        for number, name in enumerate(sent):
            room = rest.pop(0)
            leaving[name] = pltpu.make_async_copy(room, named[name], departures.at[number])
            named[name] = room
        for number, (name, value) in enumerate(fetched.items()):
            room = named[into[name]] if name in into else rest.pop(0)
            source = named[name] if value.layer is None else named[name].at[value.layer]
            copies[name] = pltpu.make_async_copy(source, room, arrivals.at[number])
            if name not in later:
                copies[name].start()
            named[name] = room
        for name, specs in extra.items():
            taken = [rest.pop(0) for _ in specs]
            named[name] = taken if isinstance(scratch[name], list) else taken[0]

        def need(*wanted):
            for name in wanted:
                copies[name].wait()

        def fetch(*wanted):
            for name in wanted:
                copies[name].start()

        def send(*wanted):
            for name in wanted:
                leaving[name].start()

        body(types.SimpleNamespace(**named, need=need, fetch=fetch, send=send))
        for copy in leaving.values():
            copy.wait()

    results = pl.pallas_call(
        run,
        out_shape=list(outs.values()),
        in_specs=[pl.BlockSpec(memory_space=pl.ANY) if name in fetched else vmem for name in ins],
        out_specs=[pl.BlockSpec(memory_space=pl.ANY) if name in sent else vmem for name in outs],
        scratch_shapes=[
            pltpu.SemaphoreType.DMA((len(fetched),)),
            pltpu.SemaphoreType.DMA((max(1, len(sent)),)),
            *(pltpu.VMEM(outs[name].shape, outs[name].dtype) for name in sent),
            *(pltpu.VMEM(value.room(), value.array.dtype) for value in inside.values()),
            *(spec for specs in extra.values() for spec in specs),
        ],
        compiler_params=pltpu.CompilerParams(
            collective_id=collective, has_side_effects=True, vmem_limit_bytes=60 << 20
        ),
    )(*(value.array if isinstance(value, Layer) else value for value in ins.values()))
    return types.SimpleNamespace(**dict(zip(outs, results)))


def shape(*dims, kind=F32):
    return jax.ShapeDtypeStruct(dims, kind)


def line_scratch(rows, width, outs=1):
    chunks = rows // 2 // CHUNK
    return [
        pltpu.VMEM((rows, width), LOW),
        pltpu.VMEM((rows, width), LOW),
        pltpu.SemaphoreType.DMA((2, chunks)),
        pltpu.SemaphoreType.DMA((2, chunks)),
        pltpu.SemaphoreType.DMA((outs, 2, chunks)),
        pltpu.SemaphoreType.DMA((outs, 2, chunks)),
    ]


def stage_of(produce, finish, outs, scratch):
    part, recv, *sems = scratch
    return types.SimpleNamespace(
        produce=produce, finish=finish, outs=outs, part=part, recv=recv, sems=sems
    )


def clear(*refs):
    for ref in refs:
        ref[...] = jnp.zeros_like(ref)


def vector(ref, layer):
    return ref[...].astype(F32)[layer : layer + 1]


def head_lanes(values, head):
    lane = lax.broadcasted_iota(jnp.int32, values.shape, 1)
    return jnp.where(lane // HEAD == head, values, jnp.zeros_like(values))


def turned(values):
    return jnp.transpose(values.astype(F32)).astype(LOW)


def mark_segments(r):
    length = r.seg_row.shape[1]
    wide = jnp.broadcast_to(r.seg_row[...].astype(F32), (QUERIES, length))
    r.seg_cols[...] = jnp.transpose(wide)


def masked_block(r, keys, queries, at):
    same = r.seg_cols[...] == r.seg_row[:, at].astype(F32)
    return jnp.where(same, dot_t(keys, queries) * HEAD ** (-0.5), masked_value)


def project(r, layer):
    bias = r.qv_bias[layer].astype(F32)
    for member in range(3):
        rows = dot(r.low_in[...], r.qkv_w[member])
        if member != 1:
            rows += bias[member // 2 : member // 2 + 1]
        r.projected[member] = rows.astype(LOW)
    r.turned_rows[...] = turned(r.projected[2])


def attend(r, block):
    at = pl.ds(pl.multiple_of(block * QUERIES, QUERIES), QUERIES)
    queries = r.projected[0, at]
    heads = queries.shape[1] // HEAD
    parts = []
    for head in range(heads):
        scores = masked_block(r, r.projected[1], head_lanes(queries, head), at)
        row_max = jnp.max(scores, axis=0, keepdims=True)
        exponent = jnp.exp(scores - row_max)
        row_total = jnp.sum(exponent, axis=0, keepdims=True)
        r.log_total[head : head + 1, at] = row_max + jnp.log(row_total)
        probs = (exponent * (1.0 / row_total)).astype(LOW)
        parts.append(dot(r.turned_rows[head * HEAD : (head + 1) * HEAD], probs))
    r.context[at] = jnp.transpose(jnp.concatenate(parts, axis=0)).astype(LOW)


def attend_first(r, half):
    per_side = half // QUERIES
    for side in range(2):
        attend(r, side * per_side)
    extras = []
    for block in range(1, per_side):
        for side in range(2):
            step = max(0, block * QUERIES // CHUNK - 2 + side)
            extras.append(at_step(step, lambda block=side * per_side + block: attend(r, block)))
    return extras


def attend_back(r, between=()):
    rows = r.attn_low_in.shape[0]
    heads = r.qkv_w.shape[2] // HEAD
    scale = HEAD ** (-0.5)
    r.grad_context[...] = dot_t(r.attn_low_in[...], r.proj_w[...]).astype(LOW)
    r.turned_rows[...] = turned(r.projected[1])
    clear(r.grad_key, r.grad_value)
    for number in range(rows // QUERIES):
        at = slice(number * QUERIES, (number + 1) * QUERIES)
        queries, context_rows = r.projected[0, at], r.grad_context[at]
        parts = []
        for head in range(heads):
            to = slice(head * QUERIES, (head + 1) * QUERIES)
            r.head_queries[to] = head_lanes(queries, head)
            r.head_context[to] = head_lanes(context_rows, head)
            scores = masked_block(r, r.projected[1], r.head_queries[to], at)
            probability = jnp.exp(scores - r.log_total[head : head + 1, at])
            grad_probs = dot_t(r.projected[2], r.head_context[to])
            inner = jnp.sum(probability * grad_probs, axis=0, keepdims=True)
            grad_scores = (probability * (grad_probs - inner)).astype(LOW)
            r.score_rows[:, to] = grad_scores
            r.prob_rows[:, to] = probability.astype(LOW)
            parts.append(dot(r.turned_rows[head * HEAD : (head + 1) * HEAD], grad_scores))
        r.grad_key[...] += dot(r.score_rows[...], r.head_queries[...])
        r.grad_value[...] += dot(r.prob_rows[...], r.head_context[...])
        r.grad_proj[0, at] = (jnp.transpose(jnp.concatenate(parts, axis=0)) * scale).astype(LOW)
        if number < len(between):
            between[number]()
    r.grad_proj[1] = (r.grad_key[...] * scale).astype(LOW)
    r.grad_proj[2] = r.grad_value[...].astype(LOW)
    for slot, member in ((0, 0), (1, 2)):
        r.qv_sum[slot] = jnp.sum(r.grad_proj[member].astype(F32).reshape(-1, 8, r.qv_sum.shape[2]), axis=0)


def proj_stage(r, layer, whole):
    def produce(block):
        r.proj_line[0][block] = dot(r.context[block], r.proj_w[...]).astype(LOW)

    def finish(at, own, total):
        came = r.residual[at if whole else own].astype(F32)
        unit, inverse = normalize(came + total + vector(r.proj_b, layer))
        r.unit_one[own] = unit
        r.inverse_one[own] = inverse
        result = unit * vector(r.first_gain, layer) + vector(r.first_shift, layer)
        r.normed[own] = result
        r.normed_low[at] = result.astype(LOW)

    return stage_of(produce, finish, [r.normed_low], r.proj_line)


def ffn_stage(r, layer, last):
    def produce(block):
        pre = dot(r.normed_low[block], r.up_w[...]) + vector(r.up_b, layer)
        cdf = 0.5 * lax.erf(pre * math.sqrt(0.5)) + 0.5
        act = (pre * cdf).astype(LOW)
        slope = cdf + pre * jnp.exp(-0.5 * pre * pre) * (1.0 / math.sqrt(2 * math.pi))
        r.slope[block] = slope.astype(LOW)
        r.act[block] = act
        r.ffn_line[0][block] = dot(act, r.down_w[...]).astype(LOW)

    def finish(at, own, total):
        unit, inverse = normalize(r.normed[own] + total + vector(r.down_b, layer))
        gain = vector(r.second_gain, layer)
        result = unit * gain + vector(r.second_shift, layer)
        if last:
            r.mixed_own[own] = result.astype(LOW)
            grad_in = r.cotangent[at].astype(F32)
            grad = norm_back(grad_in, gain, unit, inverse)
            r.grad_second[own] = grad
            r.branch[at] = grad.astype(LOW)
            tally(r.sums.at[0], grad_in * unit)
            tally(r.sums.at[1], grad_in)
            tally(r.sums.at[2], grad.astype(LOW).astype(F32))
        else:
            r.unit_two[own] = unit
            r.inverse_two[own] = inverse
            r.hidden[own] = result
            r.low[at] = result.astype(LOW)

    return stage_of(produce, finish, [r.branch if last else r.low], r.ffn_line)


def ffn_back_stage(r, layer):
    def produce(block):
        pre = (dot_t(r.branch[block], r.down_w[...]) * r.slope[block].astype(F32)).astype(LOW)
        r.pre[block] = pre
        tally(r.up_sum, pre.astype(F32))
        r.back_line[0][block] = dot_t(pre, r.up_w[...]).astype(LOW)

    def finish(at, own, total):
        grad_in = r.grad_second[own] + total
        unit = r.unit_one[own]
        grad = norm_back(grad_in, vector(r.first_gain, layer), unit, r.inverse_one[own])
        r.grad_first[own] = grad
        r.attn_low[at] = grad.astype(LOW)
        tally(r.sums.at[3], grad_in * unit)
        tally(r.sums.at[4], grad_in)
        tally(r.sums.at[5], grad.astype(LOW).astype(F32))

    return stage_of(produce, finish, [r.attn_low], r.back_line)


def qkv_back_stage(r, layer, inner):
    def produce(block):
        total = sum(dot_t(r.grad_proj[member, block], r.qkv_w[member]) for member in range(3))
        r.qkv_line[0][block] = total.astype(LOW)

    def finish(at, own, total):
        grad_in = r.grad_first_in[own] + total
        if not inner:
            r.grad_low[at] = grad_in.astype(LOW)
            r.mixed[at] = r.mixed_own[own]
            return
        unit = r.unit_two[own]
        grad = norm_back(grad_in, vector(r.second_gain, layer), unit, r.inverse_two[own])
        r.grad_second[own] = grad
        r.branch[at] = grad.astype(LOW)
        tally(r.sums.at[0], grad_in * unit)
        tally(r.sums.at[1], grad_in)
        tally(r.sums.at[2], grad.astype(LOW).astype(F32))

    return stage_of(produce, finish, [r.branch] if inner else [r.grad_low, r.mixed], r.qkv_line)


def columns(piece):
    return pl.ds(pl.multiple_of(piece * PIECE, PIECE), PIECE)


def ffn_grads(r, out, first):
    width, hidden = r.up_w.shape

    def up(piece):
        rows = pl.ds(pl.multiple_of(piece * PIECE, PIECE), PIECE)
        out[rows] = dot_tn(r.normed_low[:, columns(piece)], r.pre[...]).astype(LOW)

    def down(piece):
        rows = pl.ds(pl.multiple_of(width + piece * PIECE, PIECE), PIECE)
        out[rows] = dot_tn(r.act[:, columns(piece)], r.branch[...]).astype(LOW)

    return [(first, width // PIECE, up), (first + width // PIECE, hidden // PIECE, down)]


def attn_grads(r, out, first):
    width, part = r.low_in.shape[1], r.context_in.shape[1]

    def piece_of(piece):
        for member in range(3):
            rows = pl.ds(pl.multiple_of(member * width + piece * part, part), part)
            taken = r.low_in[:, pl.ds(pl.multiple_of(piece * part, part), part)]
            out[rows] = dot_tn(taken, r.grad_proj[member]).astype(LOW)
        rows = pl.ds(pl.multiple_of(3 * width + piece * part, part), part)
        taken = r.attn_low_in[:, pl.ds(pl.multiple_of(piece * part, part), part)]
        out[rows] = dot_tn(r.context_in[...], taken).astype(LOW)

    return [(first, width // part, piece_of)]


def at_step(step, work):
    return (step, 1, lambda index: work())


def with_suffix(suffix, named):
    return {name + suffix: value for name, value in named.items()}


def kept_attention(rows, part):
    return dict(
        projected=shape(3, rows, part, kind=LOW),
        log_total=shape(part // HEAD, rows),
        context=shape(rows, part, kind=LOW),
    )


def forward_kernel(size, collective, ins):
    rows, width = ins["low_in_0"].shape
    part, hidden = ins["proj_w_0"].array.shape[1], ins["up_w_0"].array.shape[2]
    half = rows // 2
    chunks = half // CHUNK

    def body(r):
        wait = greet(size)
        clear(r.sums, r.up_sum)
        mark_segments(r)
        below, above = view(r, "_0"), view(r, "_1")
        below.residual = r.low_in_0
        above.low_in, above.residual = r.low_0, r.hidden_0
        r.need("qkv_w_0")
        project(below, 0)
        extras = attend_first(below, half)
        r.need("proj_w_0", "up_w_0", "down_w_0")
        wait()
        line_loop(size, [proj_stage(below, 0, True), ffn_stage(below, 0, False)], extras)
        r.send("projected_0", "context_0", "unit_one_0", "normed_low_0", "act_0", "slope_0", "unit_two_0", "low_0")
        r.need("qkv_w_1")
        project(above, 1)
        extras = attend_first(above, half)
        r.need("proj_w_1", "up_w_1", "down_w_1")
        stages = [proj_stage(above, 1, False), ffn_stage(above, 1, True), ffn_back_stage(above, 1)]
        first = 4 * LAG * (size - 1) + chunks
        line_loop(
            size,
            stages,
            [
                *extras,
                at_step(2 * chunks, lambda: r.send("projected_1", "context_1")),
                *ffn_grads(above, r.ffn_grad, first),
                at_step(first + 2 * width // PIECE, lambda: r.send("ffn_grad", "mixed_own")),
            ],
        )
        r.send("grad_first", "attn_low")

    outs = dict(
        **with_suffix("_0", kept_attention(rows, part)),
        **with_suffix("_1", kept_attention(rows, part)),
        unit_one_0=shape(half, width),
        inverse_one_0=shape(half, 1),
        normed_low_0=shape(rows, width, kind=LOW),
        act_0=shape(rows, hidden, kind=LOW),
        slope_0=shape(rows, hidden, kind=LOW),
        unit_two_0=shape(half, width),
        inverse_two_0=shape(half, 1),
        low_0=shape(rows, width, kind=LOW),
        mixed_own=shape(half, width, kind=LOW),
        grad_first=shape(half, width),
        attn_low=shape(rows, width, kind=LOW),
        ffn_grad=shape(width + hidden, width, kind=LOW),
        up_sum=shape(8, hidden),
        sums=shape(6, 8, width),
    )
    scratch = dict(
        hidden_0=pltpu.VMEM((half, width), F32),
        normed=pltpu.VMEM((half, width), F32),
        turned_rows=pltpu.VMEM((part, rows), LOW),
        seg_cols=pltpu.VMEM((rows, QUERIES), F32),
        unit_one_1=pltpu.VMEM((half, width), F32),
        inverse_one_1=pltpu.VMEM((half, 1), F32),
        normed_low_1=pltpu.VMEM((rows, width), LOW),
        act_1=pltpu.VMEM((rows, hidden), LOW),
        slope_1=pltpu.VMEM((rows, hidden), LOW),
        pre=pltpu.VMEM((rows, hidden), LOW),
        branch=pltpu.VMEM((rows, width), LOW),
        grad_second=pltpu.VMEM((half, width), F32),
        proj_line_0=line_scratch(rows, width),
        ffn_line_0=line_scratch(rows, width),
        proj_line_1=line_scratch(rows, width),
        ffn_line_1=line_scratch(rows, width),
        back_line=line_scratch(rows, width),
    )
    sent = [name for name, out in outs.items() if out.dtype == LOW or name in ("unit_one_0", "unit_two_0", "grad_first")]
    return call(collective, body, ins, outs, scratch, sent=sent)


def backward_kernel(size, chips, collective, layers, ins):
    rows, width = ins["attn_low_1"].array.shape
    part, hidden = ins["proj_w_0"].array.shape[1], ins["up_w"].array.shape[2]
    half = rows // 2
    chunks = half // CHUNK
    span = 2 * LAG * (size - 1)
    ffn_rows, attn_rows = width + hidden, 4 * width
    own_rows = layers * (2 * part + hidden) // width
    count = -(-(own_rows + 6 * layers) // 8) * 8
    teams = 2 * chips

    def row_peer(index):
        row, place = here()
        return (lax.rem(row + index + 1, teams), place)

    def line_peer(index):
        row, place = here()
        return (row, lax.rem(place + index + 1, size))

    def each(number, work):
        def one(index, carry):
            work(index)
            return carry

        lax.fori_loop(0, number, one, 0)

    def body(r):
        row, place = here()
        clear(r.ends, r.sums_0, r.up_sum_0)
        wait = greet(size, line=False, targets=[(teams - 1, row_peer), (size - 1, line_peer)])
        ffn_above = spread_of(chips, r.ffn_whole_1, r.ffn_spread[:5])
        attn_above = spread_of(chips, r.attn_whole_1, r.attn_spread[:5])
        ffn_below = spread_of(chips, r.ffn_whole_0, r.ffn_spread[:2] + r.ffn_spread[5:])
        attn_below = spread_of(chips, r.attn_whole_0, r.attn_spread[:2] + r.attn_spread[5:])
        above, below = view(r, "_1"), view(r, "_0")
        above.grad_first_in, above.attn_low_in = r.grad_first_1, r.attn_low_1
        below.grad_first_in, below.attn_low_in = r.grad_first_0, r.attn_low_0
        middle = types.SimpleNamespace(
            **{**vars(r), "sums": r.sums_0, "up_sum": r.up_sum_0, "grad_first": r.grad_first_0, "attn_low": r.attn_low_0}
        )
        above.sums = r.sums_0
        above.grad_second = middle.grad_second = r.grad_first_0
        below.qkv_line = [*r.qkv_line_1[:2], *r.qkv_sems_0]

        def end_copy(slot, index):
            return pltpu.make_async_remote_copy(
                src_ref=r.small,
                dst_ref=r.ends.at[slot],
                send_sem=r.end_sent.at[slot, index],
                recv_sem=r.end_got.at[slot],
                device_id=line_peer(index),
                device_id_type=MESH,
            )

        def team_copy(index, slot):
            return pltpu.make_async_remote_copy(
                src_ref=r.mine,
                dst_ref=r.others.at[slot],
                send_sem=r.team_sent.at[index],
                recv_sem=r.team_got.at[slot],
                device_id=row_peer(index),
                device_id_type=MESH,
            )

        end_places = ((0, 0), (1, size - 1))

        def small_to_line():
            named = vars(r)
            clear(r.small)
            lines = []
            for layer in range(layers):
                sums = jnp.sum(named["qv_sum_%d" % layer][...], axis=1)
                lines += [sums[0:1], sums[1:2]]
            for layer in range(layers):
                lines += [jnp.sum(named["up_sum_%d" % layer][...], axis=0, keepdims=True)]
            flat = jnp.concatenate(lines, axis=1)
            for number in range(own_rows):
                r.small[number : number + 1] = flat[:, number * width : (number + 1) * width]
            for layer in range(layers):
                sums = jnp.sum(named["sums_%d" % layer][...], axis=1)
                for member in range(6):
                    to = own_rows + member * layers + layer
                    r.small[to : to + 1] = sums[member : member + 1]
            for slot, end in end_places:

                @pl.when(place == end)
                def _():
                    each(size - 1, lambda index: end_copy(slot, index).start())

        def small_to_teams():
            for slot, end in end_places:

                @pl.when(place != end)
                def _():
                    end_copy(slot, 0).wait_recv()

            line_total = r.small[...] + r.ends[0] + r.ends[1]
            number = lax.broadcasted_iota(jnp.int32, (count, width), 0)
            r.mine[...] = jnp.where(number < own_rows, r.small[...], line_total)
            each(teams - 1, lambda index: team_copy(index, row).start())
            r.others[row] = r.mine[...]

        def small_finish():
            each(teams - 1, lambda index: team_copy(index, row_peer(index)[0]).wait_recv())
            r.small_total[...] = lax.fori_loop(
                1, teams, lambda index, total: total + r.others[index], r.others[0]
            )
            each(teams - 1, lambda index: team_copy(index, row).wait_send())
            for slot, end in end_places:

                @pl.when(place == end)
                def _():
                    each(size - 1, lambda index: end_copy(slot, index).wait_send())

        mark_segments(r)
        r.need("proj_w_1", "attn_low_1", "projected_1", "ffn_grad_1")
        wait()
        ffn_above.to_partner()
        attend_back(above, [lambda: None, ffn_above.to_chips])
        r.need("qkv_w_1", "grad_first_1", "unit_two", "context_in_1", "low_in_1")
        r.need("up_w", "down_w", "slope", "unit_one", "act", "normed_low")
        extras = [
            *attn_grads(above, r.attn_whole_1, 1),
            at_step(4, ffn_above.onward),
            at_step(6, attn_above.to_partner),
            at_step(8, ffn_above.give_share),
            at_step(9, attn_above.to_chips),
            at_step(11, ffn_above.pass_on),
            at_step(span - 2, lambda: r.fetch("proj_w_0", "qkv_w_0")),
            at_step(span + 2, attn_above.onward),
            at_step(span + 5, attn_above.give_share),
            at_step(span + 6, ffn_above.to_other_core),
            at_step(span + 8, attn_above.pass_on),
            *ffn_grads(middle, r.ffn_whole_0, span + chunks),
            at_step(span + chunks + 2, lambda: (ffn_above.settle(), r.send("ffn_whole_1"))),
            at_step(2 * span, ffn_below.to_partner),
            at_step(2 * span + 1, attn_above.to_other_core),
            at_step(2 * span + 2, ffn_below.to_chips),
            at_step(2 * span + 4, lambda: (attn_above.settle(), r.send("attn_whole_1"))),
        ]
        stages = [qkv_back_stage(above, 0, True), ffn_back_stage(middle, 0)]
        line_loop(size, stages, extras)
        r.need("proj_w_0", "qkv_w_0", "projected_0")
        attend_back(below)
        small_to_line()
        r.need("context_in_0", "low_in_0", "mixed_own")
        extras = [
            at_step(0, ffn_below.onward),
            *attn_grads(below, r.attn_whole_0, 0),
            at_step(4, attn_below.to_partner),
            at_step(4, ffn_below.give_share),
            at_step(6, small_to_teams),
            at_step(6, attn_below.to_chips),
            at_step(8, ffn_below.pass_on),
            at_step(11, attn_below.onward),
            at_step(13, attn_below.give_share),
            at_step(15, ffn_below.to_other_core),
            at_step(16, attn_below.pass_on),
        ]
        line_loop(size, [qkv_back_stage(below, 0, False)], extras)
        r.send("grad_low", "mixed")
        small_finish()
        ffn_below.settle()
        r.send("ffn_whole_0")
        attn_below.to_other_core()
        attn_below.settle()
        r.send("attn_whole_0")

    heads = part // HEAD
    rooms = {"ffn_grad_1": "ffn_whole_1", "qkv_w_0": "qkv_w_1", "proj_w_0": "proj_w_1"}
    outs = dict(
        grad_low=shape(rows, width, kind=LOW),
        mixed=shape(rows, width, kind=LOW),
        ffn_whole_1=shape(ffn_rows, width, kind=LOW),
        attn_whole_1=shape(attn_rows, part, kind=LOW),
        ffn_whole_0=shape(ffn_rows, width, kind=LOW),
        attn_whole_0=shape(attn_rows, part, kind=LOW),
        small_total=shape(count, width),
    )
    scratch = dict(
        seg_cols=pltpu.VMEM((rows, QUERIES), F32),
        turned_rows=pltpu.VMEM((part, rows), LOW),
        grad_context=pltpu.VMEM((rows, part), LOW),
        grad_key=pltpu.VMEM((rows, part), F32),
        grad_value=pltpu.VMEM((rows, part), F32),
        grad_proj=pltpu.VMEM((3, rows, part), LOW),
        head_queries=pltpu.VMEM((heads * QUERIES, part), LOW),
        head_context=pltpu.VMEM((heads * QUERIES, part), LOW),
        score_rows=pltpu.VMEM((rows, heads * QUERIES), LOW),
        prob_rows=pltpu.VMEM((rows, heads * QUERIES), LOW),
        qv_sum_0=pltpu.VMEM((2, 8, part), F32),
        qv_sum_1=pltpu.VMEM((2, 8, part), F32),
        sums_0=pltpu.VMEM((6, 8, width), F32),
        up_sum_0=pltpu.VMEM((8, hidden), F32),
        pre=pltpu.VMEM((rows, hidden), LOW),
        branch=pltpu.VMEM((rows, width), LOW),
        grad_first_0=pltpu.VMEM((half, width), F32),
        attn_low_0=pltpu.VMEM((rows, width), LOW),
        small=pltpu.VMEM((count, width), F32),
        ends=pltpu.VMEM((2, count, width), F32),
        mine=pltpu.VMEM((count, width), F32),
        others=pltpu.VMEM((teams, count, width), F32),
        end_sent=pltpu.SemaphoreType.DMA((2, size - 1)),
        end_got=pltpu.SemaphoreType.DMA((2,)),
        team_sent=pltpu.SemaphoreType.DMA((teams - 1,)),
        team_got=pltpu.SemaphoreType.DMA((teams,)),
        qkv_line_1=line_scratch(rows, width),
        back_line=line_scratch(rows, width),
        qkv_sems_0=line_scratch(rows, width, 2)[2:],
        ffn_spread=Spread.scratch(chips, ffn_rows, width),
        attn_spread=Spread.scratch(chips, attn_rows, part),
    )
    return call(collective, body, ins, outs, scratch, rooms, ("qkv_w_0", "proj_w_0"), [*outs][:-1]), own_rows


def assemble(attn_wholes, ffn_wholes, mixed, grad_low, small, own_rows, part):
    layers = len(attn_wholes)
    rows, width = mixed.shape
    hidden = ffn_wholes[0].shape[0] - width
    steps = 4
    cut = width // steps

    def for_layer(number, spec_of):
        def index(layer, step):
            return spec_of(jnp.where(layer == number, step, jnp.where(layer < number, 0, steps - 1)))

        return index

    ins, in_specs = [], []
    for number in range(layers):
        ins += [
            attn_wholes[number].reshape(4, width, part),
            attn_wholes[number].reshape(-1, part, part),
            ffn_wholes[number].reshape(-1, width, width),
        ]
        in_specs += [
            pl.BlockSpec((3, cut, part), for_layer(number, lambda step: (0, step, 0))),
            pl.BlockSpec((width // part, part // steps, part), for_layer(number, lambda step: (3, step, 0))),
            pl.BlockSpec((1 + hidden // width, cut, width), for_layer(number, lambda step: (0, step, 0))),
        ]
    slab = rows // (layers * steps)
    ins += [mixed, grad_low, small]
    row_spec = pl.BlockSpec((slab, width), lambda layer, step: (layer * steps + step, 0))
    in_specs += [row_spec, row_spec, pl.BlockSpec(small.shape, lambda layer, step: (0, 0))]
    def all_of(*dims):
        return pl.BlockSpec(dims, lambda layer, step: (0,) * len(dims))

    out_shape = [
        shape(rows, width),
        shape(rows, width),
        shape(layers, 3, width, part),
        shape(layers, part, width),
        shape(layers, width, hidden),
        shape(layers, hidden, width),
        shape(layers, 2, part),
        shape(layers, hidden),
    ] + [shape(layers, width)] * 6
    out_specs = [
        row_spec,
        row_spec,
        pl.BlockSpec((1, 3, cut, part), lambda layer, step: (layer, 0, step, 0)),
        pl.BlockSpec((1, part // steps, width), lambda layer, step: (layer, step, 0)),
        pl.BlockSpec((1, cut, hidden), lambda layer, step: (layer, step, 0)),
        pl.BlockSpec((1, cut, width), lambda layer, step: (layer, step, 0)),
        all_of(layers, 2, part),
        all_of(layers, hidden),
    ] + [all_of(layers, width)] * 6

    def body(*refs):
        sources = refs[: 3 * layers]
        mixed_in, grad_in, small_in = refs[3 * layers : 3 * layers + 3]
        mixed_out, grad_out, qkv, proj, up, down, qv, up_b, *norms = refs[3 * layers + 3 :]
        mixed_out[...] = mixed_in[...].astype(F32)
        grad_out[...] = grad_in[...].astype(F32)
        for number in range(layers):
            attn_in, proj_in, ffn_in = sources[3 * number : 3 * number + 3]

            @pl.when(pl.program_id(0) == number)
            def _():
                qkv[0] = attn_in[...].astype(F32)
                for block in range(width // part):
                    proj[0, :, block * part : (block + 1) * part] = proj_in[block].astype(F32)
                up[0] = ffn_in[0].astype(F32)
                down[0] = ffn_in[1].astype(F32)

        @pl.when((pl.program_id(0) == 0) & (pl.program_id(1) == 0))
        def _():
            values = small_in[...]
            flat = jnp.concatenate([values[n : n + 1] for n in range(own_rows)], axis=1)
            for layer in range(layers):
                for member in range(2):
                    at = (2 * layer + member) * part
                    qv[layer, member : member + 1] = flat[:, at : at + part]
                at = 2 * layers * part + layer * hidden
                up_b[layer : layer + 1] = flat[:, at : at + hidden]
            for member, norm in enumerate(norms):
                norm[...] = values[own_rows + member * layers : own_rows + (member + 1) * layers]

    return pl.pallas_call(
        body,
        grid=(layers, steps),
        out_shape=out_shape,
        in_specs=in_specs,
        out_specs=out_specs,
        compiler_params=pltpu.CompilerParams(vmem_limit_bytes=48 << 20),
    )(*ins)


def local(
    tokens,
    segment_ids,
    cotangent,
    qkv_weight,
    qv_bias,
    proj_weight,
    proj_bias,
    first_gain,
    first_shift,
    up_weight,
    up_bias,
    down_weight,
    down_bias,
    second_gain,
    second_shift,
):
    seq_count, length, width = tokens.shape
    rows = seq_count * length
    layers = qkv_weight.shape[0]
    size = lax.axis_size("tensor")
    chips = lax.axis_size("dp") // 2
    part = qkv_weight.shape[-1]
    qkv_stack = jnp.transpose(qkv_weight, (0, 2, 1, 3))
    low = tokens.reshape(rows, width)
    weights = dict(qkv_w=qkv_stack, proj_w=proj_weight, up_w=up_weight, down_w=down_weight)
    ins = dict(
        low_in_0=low,
        cotangent=cotangent.reshape(rows, width),
        seg_row=segment_ids,
        qv_bias=qv_bias,
        proj_b=proj_bias,
        first_gain=first_gain,
        first_shift=first_shift,
        up_b=up_bias,
        down_b=down_bias,
        second_gain=second_gain,
        second_shift=second_shift,
    )
    for layer in range(layers):
        for name, array in weights.items():
            ins["%s_%d" % (name, layer)] = Layer(array, layer)
    done = forward_kernel(size, 0, ins)
    last, own_rows = backward_kernel(
        size,
        chips,
        1,
        layers,
        dict(
            seg_row=segment_ids,
            log_total_0=done.log_total_0,
            log_total_1=done.log_total_1,
            sums_1=done.sums,
            up_sum_1=done.up_sum,
            inverse_two=done.inverse_two_0,
            inverse_one=done.inverse_one_0,
            first_gain=first_gain,
            second_gain=second_gain,
            proj_w_1=Layer(proj_weight, 1),
            attn_low_1=whole(done.attn_low),
            projected_1=whole(done.projected_1),
            ffn_grad_1=whole(done.ffn_grad),
            qkv_w_1=Layer(qkv_stack, 1),
            grad_first_1=whole(done.grad_first),
            unit_two=whole(done.unit_two_0),
            context_in_1=whole(done.context_1),
            low_in_1=whole(done.low_0),
            up_w=Layer(up_weight, 0),
            down_w=Layer(down_weight, 0),
            slope=whole(done.slope_0),
            unit_one=whole(done.unit_one_0),
            act=whole(done.act_0),
            normed_low=whole(done.normed_low_0),
            proj_w_0=Layer(proj_weight, 0),
            qkv_w_0=Layer(qkv_stack, 0),
            projected_0=whole(done.projected_0),
            context_in_0=whole(done.context_0),
            low_in_0=whole(low),
            mixed_own=whole(done.mixed_own),
        ),
    )
    ffn_wholes = [last.ffn_whole_0, last.ffn_whole_1]
    attn_wholes = [last.attn_whole_0, last.attn_whole_1]

    mixed, input_grad, qkv, proj, up, down, qv, up_b, *norms = assemble(
        attn_wholes, ffn_wholes, last.mixed, last.grad_low, last.small_total, own_rows, part
    )
    return (
        mixed.reshape(tokens.shape),
        input_grad.reshape(tokens.shape),
        jnp.transpose(qkv, (0, 2, 1, 3)),
        qv,
        proj,
        norms[5],
        norms[3],
        norms[4],
        up,
        up_b,
        down,
        norms[2],
        norms[0],
        norms[1],
    )


def solution(mesh):
    return jax.shard_map(
        local,
        mesh=mesh,
        in_specs=(
            P("dp", None, None),
            P("dp", None),
            P("dp", None, None),
            P(None, None, None, "tensor"),
            P(None, None, "tensor"),
            P(None, "tensor", None),
            P(),
            P(),
            P(),
            P(None, None, "tensor"),
            P(None, "tensor"),
            P(None, "tensor", None),
            P(),
            P(),
            P(),
        ),
        out_specs=(
            P("dp", None, None),
            P("dp", None, None),
            P(None, None, None, "tensor"),
            P(None, None, "tensor"),
            P(None, "tensor", None),
            P(),
            P(),
            P(),
            P(None, None, "tensor"),
            P(None, "tensor"),
            P(None, "tensor", None),
            P(),
            P(),
            P(),
        ),
        check_vma=False,
    )
```

```python
import math
import types

import jax
import jax.numpy as jnp
from jax import lax
from jax.experimental import pallas as pl
from jax.experimental.pallas import tpu as pltpu
from jax.sharding import PartitionSpec as P

HEAD = 64


norm_eps = 1e-12
masked_value = -1000000000.0


MESH = pl.DeviceIdType.MESH
F32 = jnp.float32
LOW = jnp.bfloat16
CHUNK = 32
LAG = 2
PIECE = 512
QUERIES = 128


def dot(a, b):
    return jnp.dot(a, b, preferred_element_type=F32)


def dot_t(a, b):
    return lax.dot_general(a, b, (((1,), (1,)), ((), ())), preferred_element_type=F32)


def dot_tn(a, b):
    return lax.dot_general(a, b, (((0,), (0,)), ((), ())), preferred_element_type=F32)


def here():
    return lax.axis_index("dp"), lax.axis_index("tensor")


def greet(size, line=True, targets=()):
    row, place = here()
    barrier = pltpu.get_barrier_semaphore()
    for count, target in targets:

        def signal(index, carry):
            pl.semaphore_signal(barrier, inc=1, device_id=target(index), device_id_type=MESH)
            return carry

        lax.fori_loop(0, count, signal, 0)
    expected = sum(count for count, _ in targets)
    left, right = place > 0, place < size - 1
    if line:

        @pl.when(left)
        def _():
            pl.semaphore_signal(barrier, inc=1, device_id=(row, place - 1), device_id_type=MESH)

        @pl.when(right)
        def _():
            pl.semaphore_signal(barrier, inc=1, device_id=(row, place + 1), device_id_type=MESH)

    def wait():
        if not line:
            pl.semaphore_wait(barrier, expected)
            return

        @pl.when(left & right)
        def _():
            pl.semaphore_wait(barrier, expected + 2)

        @pl.when(jnp.logical_not(left & right))
        def _():
            pl.semaphore_wait(barrier, expected + 1)

    return wait


def partner():
    row, place = here()
    return (row + 1 - 2 * lax.rem(row, 2), place)


def line_loop(size, stages, extras=(), lag=LAG):
    row, place = here()
    half = stages[0].part.shape[0] // 2
    chunks = half // CHUNK
    end = size - 1
    span = 2 * lag * end

    def rows_of(side, chunk):
        return pl.ds(pl.multiple_of(side * half + chunk * CHUNK, CHUNK), CHUNK)

    def sum_copy(stage, side, chunk, target):
        rows = rows_of(side, chunk)
        return pltpu.make_async_remote_copy(
            src_ref=stage.part.at[rows],
            dst_ref=stage.recv.at[rows],
            send_sem=stage.sems[0].at[side, chunk],
            recv_sem=stage.sems[1].at[side, chunk],
            device_id=(row, target),
            device_id_type=MESH,
        )

    def row_copy(stage, which, side, chunk, target):
        rows = rows_of(side, chunk)
        return pltpu.make_async_remote_copy(
            src_ref=stage.outs[which].at[rows],
            dst_ref=stage.outs[which].at[rows],
            send_sem=stage.sems[2].at[which, side, chunk],
            recv_sem=stage.sems[3].at[which, side, chunk],
            device_id=(row, target),
            device_id_type=MESH,
        )

    def side_facts(side):
        if side == 0:
            return place, place + 1, place - 1
        return end - place, place - 1, place + 1

    def bring_back(stage, since):
        for side in range(2):
            at, onward, back = side_facts(side)
            chunk = since - lag * end - lag * (end - at)

            @pl.when((at < end) & (chunk >= 0) & (chunk < chunks))
            def _():
                for which in range(len(stage.outs)):
                    row_copy(stage, which, side, chunk, back).wait_recv()

                    @pl.when(at > 0)
                    def _():
                        row_copy(stage, which, side, chunk, back).start()

    def sum_up(stage, since):
        for side in range(2):
            at, onward, back = side_facts(side)
            chunk = since - lag * at

            @pl.when((chunk >= 0) & (chunk < chunks))
            def _():
                @pl.when(at > 0)
                def _():
                    sum_copy(stage, side, chunk, onward).wait_recv()

                @pl.when(at < end)
                def _():
                    @pl.when(at > 0)
                    def _():
                        rows = rows_of(side, chunk)
                        total = stage.part[rows].astype(F32) + stage.recv[rows].astype(F32)
                        stage.part[rows] = total.astype(LOW)

                    sum_copy(stage, side, chunk, onward).start()

                @pl.when(at == end)
                def _():
                    rows = rows_of(side, chunk)
                    own = pl.ds(pl.multiple_of(chunk * CHUNK, CHUNK), CHUNK)
                    stage.finish(rows, own, stage.part[rows].astype(F32) + stage.recv[rows].astype(F32))
                    for which in range(len(stage.outs)):
                        row_copy(stage, which, side, chunk, back).start()

    def step(now, carry):
        for number, stage in enumerate(stages):
            bring_back(stage, now - number * span)
        for number, stage in enumerate(stages):
            since = now - number * span

            @pl.when((since >= 0) & (since < chunks))
            def _():
                stage.produce([rows_of(side, since) for side in range(2)])

            sum_up(stage, since)
        for first, count, work in extras:

            @pl.when((now >= first) & (now < first + count))
            def _():
                work(now - first)

        return carry

    lax.fori_loop(0, chunks + span * len(stages), step, 0)

    def drain(chunk, carry):
        for stage in stages:
            for side in range(2):
                at, onward, back = side_facts(side)

                @pl.when(at < end)
                def _():
                    sum_copy(stage, side, chunk, onward).wait_send()

                @pl.when(at > 0)
                def _():
                    for which in range(len(stage.outs)):
                        row_copy(stage, which, side, chunk, back).wait_send()

        return carry

    lax.fori_loop(0, chunks, drain, 0)


def by_rows(count, work, block=32):
    def one(index, carry):
        work(pl.ds(pl.multiple_of(index * block, block), block), index * block)
        return carry

    block = min(block, count)
    lax.fori_loop(0, count // block, one, 0)


class Spread:
    def __init__(self, chips, grads, scratch):
        self.chips, self.grads = chips, grads
        self.half = grads.shape[0] // 2
        self.near, self.far, self.near_sems, self.far_sems, self.free = scratch
        row, place = here()
        self.core, self.chip, self.place = lax.rem(row, 2), row // 2, place

    @staticmethod
    def scratch(chips, rows, width):
        half = rows // 2
        far = half * 3 // 4 if chips == 4 else half // chips * (chips - 1)
        copies = 8 if chips == 4 else 2 * (chips - 1)
        sems = [
            pltpu.SemaphoreType.DMA((4,)),
            pltpu.SemaphoreType.DMA((2, copies)),
            pltpu.SemaphoreType.REGULAR,
        ]
        return [pltpu.VMEM((half, width), LOW), pltpu.VMEM((far, width), LOW), *sems, *sems]

    def rows(self, first, count):
        return pl.ds(pl.multiple_of(first, 16), count)

    def core_copy(self, source, target, number):
        return pltpu.make_async_remote_copy(
            src_ref=source,
            dst_ref=target,
            send_sem=self.near_sems.at[2 * number],
            recv_sem=self.near_sems.at[2 * number + 1],
            device_id=partner(),
            device_id_type=MESH,
        )

    def near_copy(self):
        other = self.rows((1 - self.core) * self.half, self.half)
        return self.core_copy(self.grads.at[other], self.near, 0)

    def last_copy(self):
        own = self.grads.at[self.rows(self.core * self.half, self.half)]
        return self.core_copy(own, own, 1)

    def chip_copy(self, source, target, number, chip):
        return pltpu.make_async_remote_copy(
            src_ref=source,
            dst_ref=target,
            send_sem=self.far_sems.at[0, number],
            recv_sem=self.far_sems.at[1, number],
            device_id=(chip * 2 + self.core, self.place),
            device_id_type=MESH,
        )

    def to_partner(self):
        self.near_copy().start()

    def add_partner(self):
        self.near_copy().wait_send()
        pl.semaphore_signal(self.free, inc=1, device_id=partner(), device_id_type=MESH)
        self.near_copy().wait_recv()
        base = self.core * self.half

        def add(rows, first):
            own = self.grads[self.rows(base + first, rows.size)]
            self.near[rows] = self.near[rows] + own

        by_rows(self.half, add)

    def to_other_core(self):
        self.take_back()
        self.settle_chips()
        pl.semaphore_wait(self.free, 1)
        self.last_copy().start()

    def settle(self):
        self.last_copy().wait_recv()
        self.last_copy().wait_send()


class DirectSpread(Spread):
    def each(self, work):
        def one(index, carry):
            work(index)
            return carry

        lax.fori_loop(0, self.chips - 1, one, 0)

    def peer(self, index):
        return lax.rem(self.chip + index + 1, self.chips)

    def far_copy(self, index):
        count = self.half // self.chips
        chip = self.peer(index)
        source = self.near.at[self.rows(chip * count, count)]
        return self.chip_copy(source, self.far.at[self.rows(index * count, count)], index, chip)

    def back_copy(self, index):
        count = self.half // self.chips
        share = self.grads.at[self.rows(self.core * self.half + self.chip * count, count)]
        return self.chip_copy(share, share, self.chips - 1 + index, self.peer(index))

    def to_chips(self):
        self.add_partner()
        self.each(lambda index: self.far_copy(index).start())

    def onward(self):
        pass

    def give_share(self):
        self.each(lambda index: self.far_copy(index).wait_recv())
        count = self.half // self.chips
        base = self.chip * count

        def add(rows, first):
            def one(index, total):
                return total + self.far[self.rows(index * count + first, rows.size)].astype(F32)

            own = self.near[self.rows(base + first, rows.size)].astype(F32)
            total = lax.fori_loop(0, self.chips - 1, one, own)
            self.grads[self.rows(self.core * self.half + base + first, rows.size)] = total.astype(LOW)

        by_rows(count, add)
        self.each(lambda index: self.back_copy(index).start())

    def pass_on(self):
        pass

    def take_back(self):
        self.each(lambda index: self.back_copy(index).wait_recv())

    def settle_chips(self):
        self.each(lambda index: self.far_copy(index).wait_send())
        self.each(lambda index: self.back_copy(index).wait_send())


class SquareSpread(Spread):
    def __init__(self, chips, grads, scratch):
        super().__init__(chips, grads, scratch)
        quarter = self.half // 4
        eighth = self.half // 8
        first, second = lax.rem(self.chip, 2), self.chip // 2
        along = self.chip + 1 - 2 * first
        across = self.chip + 2 - 4 * second
        self.quarter, self.eighth = quarter, eighth
        self.chips_of = ((along, across), (across, along))
        self.bits = ((first, second), (second, first))
        self.part = [side * 2 * quarter for side in range(2)]
        self.kept = [self.part[side] + self.bits[side][0] * quarter for side in range(2)]
        self.own = [self.kept[side] + self.bits[side][1] * eighth for side in range(2)]

    def first_copy(self, side):
        sent = self.part[side] + (1 - self.bits[side][0]) * self.quarter
        room = self.far.at[pl.ds(side * self.quarter, self.quarter)]
        source = self.near.at[self.rows(sent, self.quarter)]
        return self.chip_copy(source, room, side, self.chips_of[side][0])

    def second_copy(self, side):
        sent = self.kept[side] + (1 - self.bits[side][1]) * self.eighth
        room = self.far.at[pl.ds(2 * self.quarter + side * self.eighth, self.eighth)]
        source = self.near.at[self.rows(sent, self.eighth)]
        return self.chip_copy(source, room, 2 + side, self.chips_of[side][1])

    def share_copy(self, side):
        share = self.grads.at[self.rows(self.core * self.half + self.own[side], self.eighth)]
        return self.chip_copy(share, share, 4 + side, self.chips_of[side][1])

    def pass_copy(self, side):
        share = self.grads.at[self.rows(self.core * self.half + self.kept[side], self.quarter)]
        return self.chip_copy(share, share, 6 + side, self.chips_of[side][0])

    def to_chips(self):
        self.add_partner()
        for side in range(2):
            self.first_copy(side).start()

    def onward(self):
        for side in range(2):
            self.first_copy(side).wait_recv()
            base = self.kept[side]

            def add(rows, first, side=side, base=base):
                at = self.rows(base + first, rows.size)
                came = self.far[self.rows(side * self.quarter + first, rows.size)]
                self.near[at] = self.near[at] + came

            by_rows(self.quarter, add)
            self.second_copy(side).start()

    def give_share(self):
        for side in range(2):
            self.second_copy(side).wait_recv()
            base = self.own[side]

            def add(rows, first, side=side, base=base):
                came = self.far[self.rows(2 * self.quarter + side * self.eighth + first, rows.size)]
                total = self.near[self.rows(base + first, rows.size)].astype(F32) + came.astype(F32)
                to = self.rows(self.core * self.half + base + first, rows.size)
                self.grads[to] = total.astype(LOW)

            by_rows(self.eighth, add)
            self.share_copy(side).start()

    def pass_on(self):
        for side in range(2):
            self.share_copy(side).wait_recv()
            self.pass_copy(side).start()

    def take_back(self):
        for side in range(2):
            self.pass_copy(side).wait_recv()

    def settle_chips(self):
        for side in range(2):
            self.first_copy(side).wait_send()
            self.second_copy(side).wait_send()
            self.share_copy(side).wait_send()
            self.pass_copy(side).wait_send()


def spread_of(chips, grads, scratch):
    return (SquareSpread if chips == 4 else DirectSpread)(chips, grads, scratch)


def normalize(residual):
    centred = residual - jnp.mean(residual, axis=-1, keepdims=True)
    inverse = lax.rsqrt(jnp.mean(centred * centred, axis=-1, keepdims=True) + norm_eps)
    return centred * inverse, inverse


def norm_back(grad, gain, unit, inverse):
    scaled = grad * gain
    return (
        scaled
        - jnp.mean(scaled, axis=-1, keepdims=True)
        - unit * jnp.mean(scaled * unit, axis=-1, keepdims=True)
    ) * inverse


def tally(total, values):
    total[...] += jnp.sum(values.reshape(-1, 8, values.shape[-1]), axis=0)


class Layer:
    def __init__(self, array, layer):
        self.array, self.layer = array, layer

    def room(self):
        return self.array.shape if self.layer is None else self.array.shape[1:]


def whole(array):
    return Layer(array, None)


def view(refs, suffix):
    named = dict(vars(refs))
    for name, ref in vars(refs).items():
        if name.endswith(suffix):
            named[name[: -len(suffix)]] = ref
    return types.SimpleNamespace(**named)


def call(collective, body, ins, outs, scratch, into=types.MappingProxyType({}), later=(), sent=()):
    vmem = pl.BlockSpec(memory_space=pltpu.VMEM)
    names = [*ins, *outs]
    fetched = {name: value for name, value in ins.items() if isinstance(value, Layer)}
    inside = {name: value for name, value in fetched.items() if name not in into}
    extra = {name: spec if isinstance(spec, list) else [spec] for name, spec in scratch.items()}

    def run(*refs):
        named = dict(zip(names, refs))
        rest = list(refs[len(names) :])
        copies, leaving = {}, {}
        arrivals, departures = rest.pop(0), rest.pop(0)
        for number, name in enumerate(sent):
            room = rest.pop(0)
            leaving[name] = pltpu.make_async_copy(room, named[name], departures.at[number])
            named[name] = room
        for number, (name, value) in enumerate(fetched.items()):
            room = named[into[name]] if name in into else rest.pop(0)
            source = named[name] if value.layer is None else named[name].at[value.layer]
            copies[name] = pltpu.make_async_copy(source, room, arrivals.at[number])
            if name not in later:
                copies[name].start()
            named[name] = room
        for name, specs in extra.items():
            taken = [rest.pop(0) for _ in specs]
            named[name] = taken if isinstance(scratch[name], list) else taken[0]

        def need(*wanted):
            for name in wanted:
                copies[name].wait()

        def fetch(*wanted):
            for name in wanted:
                copies[name].start()

        def send(*wanted):
            for name in wanted:
                leaving[name].start()

        body(types.SimpleNamespace(**named, need=need, fetch=fetch, send=send))
        for copy in leaving.values():
            copy.wait()

    results = pl.pallas_call(
        run,
        out_shape=list(outs.values()),
        in_specs=[pl.BlockSpec(memory_space=pl.ANY) if name in fetched else vmem for name in ins],
        out_specs=[pl.BlockSpec(memory_space=pl.ANY) if name in sent else vmem for name in outs],
        scratch_shapes=[
            pltpu.SemaphoreType.DMA((len(fetched),)),
            pltpu.SemaphoreType.DMA((max(1, len(sent)),)),
            *(pltpu.VMEM(outs[name].shape, outs[name].dtype) for name in sent),
            *(pltpu.VMEM(value.room(), value.array.dtype) for value in inside.values()),
            *(spec for specs in extra.values() for spec in specs),
        ],
        compiler_params=pltpu.CompilerParams(
            collective_id=collective, has_side_effects=True, vmem_limit_bytes=60 << 20
        ),
    )(*(value.array if isinstance(value, Layer) else value for value in ins.values()))
    return types.SimpleNamespace(**dict(zip(outs, results)))


def shape(*dims, kind=F32):
    return jax.ShapeDtypeStruct(dims, kind)


def line_scratch(rows, width, outs=1):
    chunks = rows // 2 // CHUNK
    return [
        pltpu.VMEM((rows, width), LOW),
        pltpu.VMEM((rows, width), LOW),
        pltpu.SemaphoreType.DMA((2, chunks)),
        pltpu.SemaphoreType.DMA((2, chunks)),
        pltpu.SemaphoreType.DMA((outs, 2, chunks)),
        pltpu.SemaphoreType.DMA((outs, 2, chunks)),
    ]


def stage_of(produce, finish, outs, scratch):
    part, recv, *sems = scratch
    return types.SimpleNamespace(
        produce=produce, finish=finish, outs=outs, part=part, recv=recv, sems=sems
    )


def clear(*refs):
    for ref in refs:
        ref[...] = jnp.zeros_like(ref)


def vector(ref, layer):
    return ref[...].astype(F32)[layer : layer + 1]


def head_lanes(values, head):
    lane = lax.broadcasted_iota(jnp.int32, values.shape, 1)
    return jnp.where(lane // HEAD == head, values, jnp.zeros_like(values))


def turned(values):
    return jnp.transpose(values.astype(F32)).astype(LOW)


def mark_segments(r):
    length = r.seg_row.shape[1]
    wide = jnp.broadcast_to(r.seg_row[...].astype(F32), (QUERIES, length))
    r.seg_cols[...] = jnp.transpose(wide)


def masked_block(r, keys, queries, at):
    same = r.seg_cols[...] == r.seg_row[:, at].astype(F32)
    return jnp.where(same, dot_t(keys, queries) * HEAD ** (-0.5), masked_value)


def project(r, layer):
    bias = r.qv_bias[layer].astype(F32)
    for member in range(3):
        rows = dot(r.low_in[...], r.qkv_w[member])
        if member != 1:
            rows += bias[member // 2 : member // 2 + 1]
        r.projected[member] = rows.astype(LOW)
    r.turned_rows[...] = turned(r.projected[2])


def attend(r, block):
    at = pl.ds(pl.multiple_of(block * QUERIES, QUERIES), QUERIES)
    queries = r.projected[0, at]
    heads = queries.shape[1] // HEAD
    parts = []
    for head in range(heads):
        scores = masked_block(r, r.projected[1], head_lanes(queries, head), at)
        row_max = jnp.max(scores, axis=0, keepdims=True)
        exponent = jnp.exp(scores - row_max)
        row_total = jnp.sum(exponent, axis=0, keepdims=True)
        r.log_total[head : head + 1, at] = row_max + jnp.log(row_total)
        probs = (exponent * (1.0 / row_total)).astype(LOW)
        parts.append(dot(r.turned_rows[head * HEAD : (head + 1) * HEAD], probs))
    r.context[at] = jnp.transpose(jnp.concatenate(parts, axis=0)).astype(LOW)


def attend_first(r, half):
    per_side = half // QUERIES
    for side in range(2):
        attend(r, side * per_side)
    extras = []
    for block in range(1, per_side):
        for side in range(2):
            step = max(0, block * QUERIES // CHUNK - 2 + side)
            extras.append(at_step(step, lambda block=side * per_side + block: attend(r, block)))
    return extras


def attend_back(r, between=()):
    rows = r.attn_low_in.shape[0]
    heads = r.qkv_w.shape[2] // HEAD
    scale = HEAD ** (-0.5)
    r.grad_context[...] = dot_t(r.attn_low_in[...], r.proj_w[...]).astype(LOW)
    r.turned_rows[...] = turned(r.projected[1])
    clear(r.grad_key, r.grad_value)
    for number in range(rows // QUERIES):
        at = slice(number * QUERIES, (number + 1) * QUERIES)
        queries, context_rows = r.projected[0, at], r.grad_context[at]
        parts = []
        for head in range(heads):
            to = slice(head * QUERIES, (head + 1) * QUERIES)
            r.head_queries[to] = head_lanes(queries, head)
            r.head_context[to] = head_lanes(context_rows, head)
            scores = masked_block(r, r.projected[1], r.head_queries[to], at)
            probability = jnp.exp(scores - r.log_total[head : head + 1, at])
            grad_probs = dot_t(r.projected[2], r.head_context[to])
            inner = jnp.sum(probability * grad_probs, axis=0, keepdims=True)
            grad_scores = (probability * (grad_probs - inner)).astype(LOW)
            r.score_rows[:, to] = grad_scores
            r.prob_rows[:, to] = probability.astype(LOW)
            parts.append(dot(r.turned_rows[head * HEAD : (head + 1) * HEAD], grad_scores))
        r.grad_key[...] += dot(r.score_rows[...], r.head_queries[...])
        r.grad_value[...] += dot(r.prob_rows[...], r.head_context[...])
        r.grad_proj[0, at] = (jnp.transpose(jnp.concatenate(parts, axis=0)) * scale).astype(LOW)
        if number < len(between):
            between[number]()
    r.grad_proj[1] = (r.grad_key[...] * scale).astype(LOW)
    r.grad_proj[2] = r.grad_value[...].astype(LOW)
    for slot, member in ((0, 0), (1, 2)):
        r.qv_sum[slot] = jnp.sum(r.grad_proj[member].astype(F32).reshape(-1, 8, r.qv_sum.shape[2]), axis=0)


def take(ref, blocks):
    return jnp.concatenate([ref[block] for block in blocks], axis=0)


def put(ref, blocks, values):
    count = values.shape[0] // len(blocks)
    for number, block in enumerate(blocks):
        ref[block] = values[number * count : (number + 1) * count]


def proj_stage(r, layer, whole):
    def produce(blocks):
        put(r.proj_line[0], blocks, dot(take(r.context, blocks), r.proj_w[...]).astype(LOW))

    def finish(at, own, total):
        came = r.residual[at if whole else own].astype(F32)
        unit, inverse = normalize(came + total + vector(r.proj_b, layer))
        r.unit_one[own] = unit
        r.inverse_one[own] = inverse
        result = unit * vector(r.first_gain, layer) + vector(r.first_shift, layer)
        r.normed[own] = result
        r.normed_low[at] = result.astype(LOW)

    return stage_of(produce, finish, [r.normed_low], r.proj_line)


def ffn_stage(r, layer, last):
    def produce(blocks):
        pre = dot(take(r.normed_low, blocks), r.up_w[...]) + vector(r.up_b, layer)
        cdf = 0.5 * lax.erf(pre * math.sqrt(0.5)) + 0.5
        act = (pre * cdf).astype(LOW)
        slope = cdf + pre * jnp.exp(-0.5 * pre * pre) * (1.0 / math.sqrt(2 * math.pi))
        put(r.slope, blocks, slope.astype(LOW))
        put(r.act, blocks, act)
        put(r.ffn_line[0], blocks, dot(act, r.down_w[...]).astype(LOW))

    def finish(at, own, total):
        unit, inverse = normalize(r.normed[own] + total + vector(r.down_b, layer))
        gain = vector(r.second_gain, layer)
        result = unit * gain + vector(r.second_shift, layer)
        if last:
            r.mixed_own[own] = result.astype(LOW)
            grad_in = r.cotangent[at].astype(F32)
            grad = norm_back(grad_in, gain, unit, inverse)
            r.grad_second[own] = grad
            r.branch[at] = grad.astype(LOW)
            tally(r.sums.at[0], grad_in * unit)
            tally(r.sums.at[1], grad_in)
            tally(r.sums.at[2], grad.astype(LOW).astype(F32))
        else:
            r.unit_two[own] = unit
            r.inverse_two[own] = inverse
            r.hidden[own] = result
            r.low[at] = result.astype(LOW)

    return stage_of(produce, finish, [r.branch if last else r.low], r.ffn_line)


def ffn_back_stage(r, layer):
    def produce(blocks):
        grad = dot_t(take(r.branch, blocks), r.down_w[...])
        pre = (grad * take(r.slope, blocks).astype(F32)).astype(LOW)
        put(r.pre, blocks, pre)
        tally(r.up_sum, pre.astype(F32))
        put(r.back_line[0], blocks, dot_t(pre, r.up_w[...]).astype(LOW))

    def finish(at, own, total):
        grad_in = r.grad_second[own] + total
        unit = r.unit_one[own]
        grad = norm_back(grad_in, vector(r.first_gain, layer), unit, r.inverse_one[own])
        r.grad_first[own] = grad
        r.attn_low[at] = grad.astype(LOW)
        tally(r.sums.at[3], grad_in * unit)
        tally(r.sums.at[4], grad_in)
        tally(r.sums.at[5], grad.astype(LOW).astype(F32))

    return stage_of(produce, finish, [r.attn_low], r.back_line)


def qkv_back_stage(r, layer, inner):
    def produce(blocks):
        total = sum(dot_t(take(r.grad_proj.at[member], blocks), r.qkv_w[member]) for member in range(3))
        put(r.qkv_line[0], blocks, total.astype(LOW))

    def finish(at, own, total):
        grad_in = r.grad_first_in[own] + total
        if not inner:
            r.grad_low[at] = grad_in.astype(LOW)
            return
        unit = r.unit_two[own]
        grad = norm_back(grad_in, vector(r.second_gain, layer), unit, r.inverse_two[own])
        r.grad_second[own] = grad
        r.branch[at] = grad.astype(LOW)
        tally(r.sums.at[0], grad_in * unit)
        tally(r.sums.at[1], grad_in)
        tally(r.sums.at[2], grad.astype(LOW).astype(F32))

    return stage_of(produce, finish, [r.branch] if inner else [r.grad_low], r.qkv_line)


def columns(piece):
    return pl.ds(pl.multiple_of(piece * PIECE, PIECE), PIECE)


def ffn_grads(r, out, first):
    width, hidden = r.up_w.shape

    def up(piece):
        rows = pl.ds(pl.multiple_of(piece * PIECE, PIECE), PIECE)
        out[rows] = dot_tn(r.normed_low[:, columns(piece)], r.pre[...]).astype(LOW)

    def down(piece):
        rows = pl.ds(pl.multiple_of(width + piece * PIECE, PIECE), PIECE)
        out[rows] = dot_tn(r.act[:, columns(piece)], r.branch[...]).astype(LOW)

    return [(first, width // PIECE, up), (first + width // PIECE, hidden // PIECE, down)]


def attn_grads(r, out, first):
    width, part = r.low_in.shape[1], r.context_in.shape[1]

    def piece_of(piece):
        for member in range(3):
            rows = pl.ds(pl.multiple_of(member * width + piece * part, part), part)
            taken = r.low_in[:, pl.ds(pl.multiple_of(piece * part, part), part)]
            out[rows] = dot_tn(taken, r.grad_proj[member]).astype(LOW)
        rows = pl.ds(pl.multiple_of(3 * width + piece * part, part), part)
        taken = r.attn_low_in[:, pl.ds(pl.multiple_of(piece * part, part), part)]
        out[rows] = dot_tn(r.context_in[...], taken).astype(LOW)

    def all_pieces():
        lax.fori_loop(0, width // part, lambda piece, carry: (piece_of(piece), carry)[1], 0)

    return [at_step(first, all_pieces)]


def at_step(step, work):
    return (step, 1, lambda index: work())


def with_suffix(suffix, named):
    return {name + suffix: value for name, value in named.items()}


def kept_attention(rows, part):
    return dict(
        projected=shape(3, rows, part, kind=LOW),
        log_total=shape(part // HEAD, rows),
        context=shape(rows, part, kind=LOW),
    )


def forward_kernel(size, collective, ins):
    rows, width = ins["low_in_0"].shape
    part, hidden = ins["proj_w_0"].array.shape[1], ins["up_w_0"].array.shape[2]
    half = rows // 2
    chunks = half // CHUNK

    def body(r):
        wait = greet(size)
        clear(r.sums, r.up_sum)
        mark_segments(r)
        below, above = view(r, "_0"), view(r, "_1")
        below.residual = r.low_in_0
        above.low_in, above.residual = r.low_0, r.hidden_0
        r.need("qkv_w_0")
        project(below, 0)
        extras = attend_first(below, half)
        r.need("proj_w_0", "up_w_0", "down_w_0")
        wait()
        line_loop(size, [proj_stage(below, 0, True), ffn_stage(below, 0, False)], extras, 3)
        r.send("projected_0", "context_0", "unit_one_0", "normed_low_0", "act_0", "slope_0", "unit_two_0", "low_0")
        r.need("qkv_w_1")
        project(above, 1)
        extras = attend_first(above, half)
        r.need("proj_w_1", "up_w_1", "down_w_1")
        stages = [proj_stage(above, 1, False), ffn_stage(above, 1, True), ffn_back_stage(above, 1)]
        first = 4 * LAG * (size - 1) + chunks
        line_loop(
            size,
            stages,
            [
                *extras,
                at_step(2 * chunks, lambda: r.send("projected_1", "context_1")),
                *ffn_grads(above, r.ffn_grad, first),
                at_step(first + 2 * width // PIECE, lambda: r.send("ffn_grad", "mixed_own")),
            ],
        )
        r.send("grad_first", "attn_low")

    outs = dict(
        **with_suffix("_0", kept_attention(rows, part)),
        **with_suffix("_1", kept_attention(rows, part)),
        unit_one_0=shape(half, width),
        inverse_one_0=shape(half, 1),
        normed_low_0=shape(rows, width, kind=LOW),
        act_0=shape(rows, hidden, kind=LOW),
        slope_0=shape(rows, hidden, kind=LOW),
        unit_two_0=shape(half, width),
        inverse_two_0=shape(half, 1),
        low_0=shape(rows, width, kind=LOW),
        mixed_own=shape(half, width, kind=LOW),
        grad_first=shape(half, width),
        attn_low=shape(rows, width, kind=LOW),
        ffn_grad=shape(width + hidden, width, kind=LOW),
        up_sum=shape(8, hidden),
        sums=shape(6, 8, width),
    )
    scratch = dict(
        hidden_0=pltpu.VMEM((half, width), F32),
        normed=pltpu.VMEM((half, width), F32),
        turned_rows=pltpu.VMEM((part, rows), LOW),
        seg_cols=pltpu.VMEM((rows, QUERIES), F32),
        unit_one_1=pltpu.VMEM((half, width), F32),
        inverse_one_1=pltpu.VMEM((half, 1), F32),
        normed_low_1=pltpu.VMEM((rows, width), LOW),
        act_1=pltpu.VMEM((rows, hidden), LOW),
        slope_1=pltpu.VMEM((rows, hidden), LOW),
        pre=pltpu.VMEM((rows, hidden), LOW),
        branch=pltpu.VMEM((rows, width), LOW),
        grad_second=pltpu.VMEM((half, width), F32),
        proj_line_0=line_scratch(rows, width),
        ffn_line_0=line_scratch(rows, width),
        proj_line_1=line_scratch(rows, width),
        ffn_line_1=line_scratch(rows, width),
        back_line=line_scratch(rows, width),
    )
    sent = [name for name, out in outs.items() if out.dtype == LOW or name in ("unit_one_0", "unit_two_0", "grad_first")]
    return call(collective, body, ins, outs, scratch, sent=sent)


def backward_kernel(size, chips, collective, layers, ins):
    rows, width = ins["attn_low_1"].array.shape
    part, hidden = ins["proj_w_0"].array.shape[1], ins["up_w"].array.shape[2]
    half = rows // 2
    chunks = half // CHUNK
    span = 2 * LAG * (size - 1)
    ffn_rows, attn_rows = width + hidden, 4 * width
    own_rows = layers * (2 * part + hidden) // width
    count = -(-(own_rows + 6 * layers) // 8) * 8
    teams = 2 * chips

    def row_peer(index):
        row, place = here()
        return (lax.rem(row + index + 1, teams), place)

    def line_peer(index):
        row, place = here()
        return (row, lax.rem(place + index + 1, size))

    def each(number, work):
        def one(index, carry):
            work(index)
            return carry

        lax.fori_loop(0, number, one, 0)

    def body(r):
        row, place = here()
        clear(r.ends, r.sums_0, r.up_sum_0)
        wait = greet(size, line=False, targets=[(teams - 1, row_peer), (size - 1, line_peer)])
        ffn_above = spread_of(chips, r.ffn_whole_1, r.ffn_spread[:5])
        attn_above = spread_of(chips, r.attn_whole_1, r.attn_spread[:5])
        ffn_below = spread_of(chips, r.ffn_whole_0, r.ffn_spread[:2] + r.ffn_spread[5:])
        attn_below = spread_of(chips, r.attn_whole_0, r.attn_spread[:2] + r.attn_spread[5:])
        above, below = view(r, "_1"), view(r, "_0")
        above.grad_first_in, above.attn_low_in = r.grad_first_1, r.attn_low_1
        below.grad_first_in, below.attn_low_in = r.grad_first_0, r.attn_low_0
        middle = types.SimpleNamespace(
            **{**vars(r), "sums": r.sums_0, "up_sum": r.up_sum_0, "grad_first": r.grad_first_0, "attn_low": r.attn_low_0}
        )
        above.sums = r.sums_0
        above.grad_second = middle.grad_second = r.grad_first_0
        below.qkv_line = [*r.qkv_line_1[:2], *r.qkv_sems_0]

        def end_copy(slot, index):
            return pltpu.make_async_remote_copy(
                src_ref=r.small,
                dst_ref=r.ends.at[slot],
                send_sem=r.end_sent.at[slot, index],
                recv_sem=r.end_got.at[slot],
                device_id=line_peer(index),
                device_id_type=MESH,
            )

        def team_copy(index, slot):
            return pltpu.make_async_remote_copy(
                src_ref=r.mine,
                dst_ref=r.others.at[slot],
                send_sem=r.team_sent.at[index],
                recv_sem=r.team_got.at[slot],
                device_id=row_peer(index),
                device_id_type=MESH,
            )

        end_places = ((0, 0), (1, size - 1))
        end = size - 1

        def side_rows(side):
            at, back = (place, place - 1) if side == 0 else (end - place, place + 1)
            return at, back, r.mixed.at[pl.ds(side * half, half)]

        def mixed_copy(side):
            at, back, rows_at = side_rows(side)
            return pltpu.make_async_remote_copy(
                src_ref=rows_at,
                dst_ref=rows_at,
                send_sem=r.mixed_sent.at[side],
                recv_sem=r.mixed_got.at[side],
                device_id=(row, back),
                device_id_type=MESH,
            )

        def mixed_hop(number):
            for side in range(2):
                at, _, rows_at = side_rows(side)

                @pl.when(at == end - number)
                def _():
                    if number:
                        mixed_copy(side).wait_recv()
                    else:
                        rows_at[...] = r.mixed_own[...]
                    mixed_copy(side).start()

        def mixed_settle():
            for side in range(2):
                at, _, _ = side_rows(side)

                @pl.when(at == 0)
                def _():
                    mixed_copy(side).wait_recv()

                @pl.when(at > 0)
                def _():
                    mixed_copy(side).wait_send()

        def small_to_line():
            named = vars(r)
            clear(r.small)
            lines = []
            for layer in range(layers):
                sums = jnp.sum(named["qv_sum_%d" % layer][...], axis=1)
                lines += [sums[0:1], sums[1:2]]
            for layer in range(layers):
                lines += [jnp.sum(named["up_sum_%d" % layer][...], axis=0, keepdims=True)]
            flat = jnp.concatenate(lines, axis=1)
            for number in range(own_rows):
                r.small[number : number + 1] = flat[:, number * width : (number + 1) * width]
            for layer in range(layers):
                sums = jnp.sum(named["sums_%d" % layer][...], axis=1)
                for member in range(6):
                    to = own_rows + member * layers + layer
                    r.small[to : to + 1] = sums[member : member + 1]
            for slot, end in end_places:

                @pl.when(place == end)
                def _():
                    each(size - 1, lambda index: end_copy(slot, index).start())

        def small_to_teams():
            for slot, end in end_places:

                @pl.when(place != end)
                def _():
                    end_copy(slot, 0).wait_recv()

            line_total = r.small[...] + r.ends[0] + r.ends[1]
            number = lax.broadcasted_iota(jnp.int32, (count, width), 0)
            r.mine[...] = jnp.where(number < own_rows, r.small[...], line_total)
            each(teams - 1, lambda index: team_copy(index, row).start())
            r.others[row] = r.mine[...]

        def small_finish():
            each(teams - 1, lambda index: team_copy(index, row_peer(index)[0]).wait_recv())
            r.small_total[...] = lax.fori_loop(
                1, teams, lambda index, total: total + r.others[index], r.others[0]
            )
            each(teams - 1, lambda index: team_copy(index, row).wait_send())
            for slot, end in end_places:

                @pl.when(place == end)
                def _():
                    each(size - 1, lambda index: end_copy(slot, index).wait_send())

        mark_segments(r)
        r.need("proj_w_1", "attn_low_1", "projected_1", "mixed_own", "ffn_grad_1")
        wait()
        ffn_above.to_partner()
        mixed_hop(0)
        attend_back(above, [lambda: None, ffn_above.to_chips])
        r.need("qkv_w_1", "grad_first_1", "unit_two", "context_in_1", "low_in_1")
        r.need("up_w", "down_w", "slope", "unit_one", "act", "normed_low")
        extras = [
            *attn_grads(above, r.attn_whole_1, 2),
            at_step(4, ffn_above.onward),
            at_step(6, attn_above.to_partner),
            at_step(8, ffn_above.give_share),
            at_step(9, attn_above.to_chips),
            at_step(11, ffn_above.pass_on),
            at_step(span - 2, lambda: r.fetch("proj_w_0", "qkv_w_0")),
            at_step(span + 2, attn_above.onward),
            at_step(span + 5, attn_above.give_share),
            at_step(span + 6, ffn_above.to_other_core),
            at_step(span + 8, attn_above.pass_on),
            *ffn_grads(middle, r.ffn_whole_0, span + chunks),
            at_step(span + chunks + 2, lambda: (ffn_above.settle(), r.send("ffn_whole_1"))),
            at_step(2 * span, ffn_below.to_partner),
            at_step(2 * span + 1, attn_above.to_other_core),
            at_step(2 * span + 2, ffn_below.to_chips),
            at_step(2 * span + 5, lambda: (attn_above.settle(), r.send("attn_whole_1"))),
        ]
        stages = [qkv_back_stage(above, 0, True), ffn_back_stage(middle, 0)]
        line_loop(size, stages, extras)
        r.need("proj_w_0", "qkv_w_0", "projected_0")
        mixed_hop(1)
        attend_back(below, [lambda: None, ffn_below.onward])
        ffn_below.give_share()
        r.need("context_in_0", "low_in_0")
        extras = [
            *attn_grads(below, r.attn_whole_0, 0),
            at_step(1, attn_below.to_partner),
            at_step(2, small_to_line),
            *(at_step(3 + 6 * (hop - 2), lambda hop=hop: mixed_hop(hop)) for hop in range(2, end)),
            at_step(3, ffn_below.pass_on),
            at_step(3, attn_below.to_chips),
            at_step(6, small_to_teams),
            at_step(8, attn_below.onward),
            at_step(10, ffn_below.to_other_core),
            at_step(11, attn_below.give_share),
            at_step(13, attn_below.pass_on),
            at_step(14, small_finish),
            at_step(15, lambda: (ffn_below.settle(), r.send("ffn_whole_0"))),
            at_step(17, attn_below.to_other_core),
        ]
        line_loop(size, [qkv_back_stage(below, 0, False)], extras)
        mixed_settle()
        r.send("grad_low", "mixed")
        attn_below.settle()
        r.send("attn_whole_0")

    heads = part // HEAD
    rooms = {"ffn_grad_1": "ffn_whole_1", "qkv_w_0": "qkv_w_1", "proj_w_0": "proj_w_1"}
    outs = dict(
        grad_low=shape(rows, width, kind=LOW),
        mixed=shape(rows, width, kind=LOW),
        ffn_whole_1=shape(ffn_rows, width, kind=LOW),
        attn_whole_1=shape(attn_rows, part, kind=LOW),
        ffn_whole_0=shape(ffn_rows, width, kind=LOW),
        attn_whole_0=shape(attn_rows, part, kind=LOW),
        small_total=shape(count, width),
    )
    scratch = dict(
        seg_cols=pltpu.VMEM((rows, QUERIES), F32),
        turned_rows=pltpu.VMEM((part, rows), LOW),
        grad_context=pltpu.VMEM((rows, part), LOW),
        grad_key=pltpu.VMEM((rows, part), F32),
        grad_value=pltpu.VMEM((rows, part), F32),
        grad_proj=pltpu.VMEM((3, rows, part), LOW),
        head_queries=pltpu.VMEM((heads * QUERIES, part), LOW),
        head_context=pltpu.VMEM((heads * QUERIES, part), LOW),
        score_rows=pltpu.VMEM((rows, heads * QUERIES), LOW),
        prob_rows=pltpu.VMEM((rows, heads * QUERIES), LOW),
        qv_sum_0=pltpu.VMEM((2, 8, part), F32),
        qv_sum_1=pltpu.VMEM((2, 8, part), F32),
        sums_0=pltpu.VMEM((6, 8, width), F32),
        up_sum_0=pltpu.VMEM((8, hidden), F32),
        pre=pltpu.VMEM((rows, hidden), LOW),
        branch=pltpu.VMEM((rows, width), LOW),
        grad_first_0=pltpu.VMEM((half, width), F32),
        attn_low_0=pltpu.VMEM((rows, width), LOW),
        small=pltpu.VMEM((count, width), F32),
        ends=pltpu.VMEM((2, count, width), F32),
        mine=pltpu.VMEM((count, width), F32),
        others=pltpu.VMEM((teams, count, width), F32),
        end_sent=pltpu.SemaphoreType.DMA((2, size - 1)),
        end_got=pltpu.SemaphoreType.DMA((2,)),
        team_sent=pltpu.SemaphoreType.DMA((teams - 1,)),
        team_got=pltpu.SemaphoreType.DMA((teams,)),
        mixed_sent=pltpu.SemaphoreType.DMA((2,)),
        mixed_got=pltpu.SemaphoreType.DMA((2,)),
        qkv_line_1=line_scratch(rows, width),
        back_line=line_scratch(rows, width),
        qkv_sems_0=line_scratch(rows, width)[2:],
        ffn_spread=Spread.scratch(chips, ffn_rows, width),
        attn_spread=Spread.scratch(chips, attn_rows, part),
    )
    return call(collective, body, ins, outs, scratch, rooms, ("qkv_w_0", "proj_w_0"), [*outs][:-1]), own_rows


def assemble(attn_wholes, ffn_wholes, mixed, grad_low, small, own_rows, part):
    layers = len(attn_wholes)
    rows, width = mixed.shape
    hidden = ffn_wholes[0].shape[0] - width
    steps = 4
    cut = width // steps

    def for_layer(number, spec_of):
        def index(layer, step):
            return spec_of(jnp.where(layer == number, step, jnp.where(layer < number, 0, steps - 1)))

        return index

    ins, in_specs = [], []
    for number in range(layers):
        ins += [
            attn_wholes[number].reshape(4, width, part),
            attn_wholes[number].reshape(-1, part, part),
            ffn_wholes[number].reshape(-1, width, width),
        ]
        in_specs += [
            pl.BlockSpec((3, cut, part), for_layer(number, lambda step: (0, step, 0))),
            pl.BlockSpec((width // part, part // steps, part), for_layer(number, lambda step: (3, step, 0))),
            pl.BlockSpec((1 + hidden // width, cut, width), for_layer(number, lambda step: (0, step, 0))),
        ]
    slab = rows // (layers * steps)
    ins += [mixed, grad_low, small]
    row_spec = pl.BlockSpec((slab, width), lambda layer, step: (layer * steps + step, 0))
    in_specs += [row_spec, row_spec, pl.BlockSpec(small.shape, lambda layer, step: (0, 0))]
    def all_of(*dims):
        return pl.BlockSpec(dims, lambda layer, step: (0,) * len(dims))

    out_shape = [
        shape(rows, width),
        shape(rows, width),
        shape(layers, 3, width, part),
        shape(layers, part, width),
        shape(layers, width, hidden),
        shape(layers, hidden, width),
        shape(layers, 2, part),
        shape(layers, hidden),
    ] + [shape(layers, width)] * 6
    out_specs = [
        row_spec,
        row_spec,
        pl.BlockSpec((1, 3, cut, part), lambda layer, step: (layer, 0, step, 0)),
        pl.BlockSpec((1, part // steps, width), lambda layer, step: (layer, step, 0)),
        pl.BlockSpec((1, cut, hidden), lambda layer, step: (layer, step, 0)),
        pl.BlockSpec((1, cut, width), lambda layer, step: (layer, step, 0)),
        all_of(layers, 2, part),
        all_of(layers, hidden),
    ] + [all_of(layers, width)] * 6

    def body(*refs):
        sources = refs[: 3 * layers]
        mixed_in, grad_in, small_in = refs[3 * layers : 3 * layers + 3]
        mixed_out, grad_out, qkv, proj, up, down, qv, up_b, *norms = refs[3 * layers + 3 :]
        mixed_out[...] = mixed_in[...].astype(F32)
        grad_out[...] = grad_in[...].astype(F32)
        for number in range(layers):
            attn_in, proj_in, ffn_in = sources[3 * number : 3 * number + 3]

            @pl.when(pl.program_id(0) == number)
            def _():
                qkv[0] = attn_in[...].astype(F32)
                for block in range(width // part):
                    proj[0, :, block * part : (block + 1) * part] = proj_in[block].astype(F32)
                up[0] = ffn_in[0].astype(F32)
                down[0] = ffn_in[1].astype(F32)

        @pl.when((pl.program_id(0) == 0) & (pl.program_id(1) == 0))
        def _():
            values = small_in[...]
            flat = jnp.concatenate([values[n : n + 1] for n in range(own_rows)], axis=1)
            for layer in range(layers):
                for member in range(2):
                    at = (2 * layer + member) * part
                    qv[layer, member : member + 1] = flat[:, at : at + part]
                at = 2 * layers * part + layer * hidden
                up_b[layer : layer + 1] = flat[:, at : at + hidden]
            for member, norm in enumerate(norms):
                norm[...] = values[own_rows + member * layers : own_rows + (member + 1) * layers]

    return pl.pallas_call(
        body,
        grid=(layers, steps),
        out_shape=out_shape,
        in_specs=in_specs,
        out_specs=out_specs,
        compiler_params=pltpu.CompilerParams(vmem_limit_bytes=60 << 20),
    )(*ins)


def local(
    tokens,
    segment_ids,
    cotangent,
    qkv_weight,
    qv_bias,
    proj_weight,
    proj_bias,
    first_gain,
    first_shift,
    up_weight,
    up_bias,
    down_weight,
    down_bias,
    second_gain,
    second_shift,
):
    seq_count, length, width = tokens.shape
    rows = seq_count * length
    layers = qkv_weight.shape[0]
    size = lax.axis_size("tensor")
    chips = lax.axis_size("dp") // 2
    part = qkv_weight.shape[-1]
    qkv_stack = jnp.transpose(qkv_weight, (0, 2, 1, 3))
    low = tokens.reshape(rows, width)
    weights = dict(qkv_w=qkv_stack, proj_w=proj_weight, up_w=up_weight, down_w=down_weight)
    ins = dict(
        low_in_0=low,
        cotangent=cotangent.reshape(rows, width),
        seg_row=segment_ids,
        qv_bias=qv_bias,
        proj_b=proj_bias,
        first_gain=first_gain,
        first_shift=first_shift,
        up_b=up_bias,
        down_b=down_bias,
        second_gain=second_gain,
        second_shift=second_shift,
    )
    for layer in range(layers):
        for name, array in weights.items():
            ins["%s_%d" % (name, layer)] = Layer(array, layer)
    done = forward_kernel(size, 0, ins)
    last, own_rows = backward_kernel(
        size,
        chips,
        1,
        layers,
        dict(
            seg_row=segment_ids,
            log_total_0=done.log_total_0,
            log_total_1=done.log_total_1,
            sums_1=done.sums,
            up_sum_1=done.up_sum,
            inverse_two=done.inverse_two_0,
            inverse_one=done.inverse_one_0,
            first_gain=first_gain,
            second_gain=second_gain,
            proj_w_1=Layer(proj_weight, 1),
            attn_low_1=whole(done.attn_low),
            projected_1=whole(done.projected_1),
            mixed_own=whole(done.mixed_own),
            ffn_grad_1=whole(done.ffn_grad),
            qkv_w_1=Layer(qkv_stack, 1),
            grad_first_1=whole(done.grad_first),
            unit_two=whole(done.unit_two_0),
            context_in_1=whole(done.context_1),
            low_in_1=whole(done.low_0),
            up_w=Layer(up_weight, 0),
            down_w=Layer(down_weight, 0),
            slope=whole(done.slope_0),
            unit_one=whole(done.unit_one_0),
            act=whole(done.act_0),
            normed_low=whole(done.normed_low_0),
            proj_w_0=Layer(proj_weight, 0),
            qkv_w_0=Layer(qkv_stack, 0),
            projected_0=whole(done.projected_0),
            context_in_0=whole(done.context_0),
            low_in_0=whole(low),
        ),
    )
    ffn_wholes = [last.ffn_whole_0, last.ffn_whole_1]
    attn_wholes = [last.attn_whole_0, last.attn_whole_1]

    mixed, input_grad, qkv, proj, up, down, qv, up_b, *norms = assemble(
        attn_wholes, ffn_wholes, last.mixed, last.grad_low, last.small_total, own_rows, part
    )
    return (
        mixed.reshape(tokens.shape),
        input_grad.reshape(tokens.shape),
        jnp.transpose(qkv, (0, 2, 1, 3)),
        qv,
        proj,
        norms[5],
        norms[3],
        norms[4],
        up,
        up_b,
        down,
        norms[2],
        norms[0],
        norms[1],
    )


def solution(mesh):
    return jax.shard_map(
        local,
        mesh=mesh,
        in_specs=(
            P("dp", None, None),
            P("dp", None),
            P("dp", None, None),
            P(None, None, None, "tensor"),
            P(None, None, "tensor"),
            P(None, "tensor", None),
            P(),
            P(),
            P(),
            P(None, None, "tensor"),
            P(None, "tensor"),
            P(None, "tensor", None),
            P(),
            P(),
            P(),
        ),
        out_specs=(
            P("dp", None, None),
            P("dp", None, None),
            P(None, None, None, "tensor"),
            P(None, None, "tensor"),
            P(None, "tensor", None),
            P(),
            P(),
            P(),
            P(None, None, "tensor"),
            P(None, "tensor"),
            P(None, "tensor", None),
            P(),
            P(),
            P(),
        ),
        check_vma=False,
    )
```

```python
import math
import types

import jax
import jax.numpy as jnp
from jax import lax
from jax.experimental import pallas as pl
from jax.experimental.pallas import tpu as pltpu
from jax.sharding import PartitionSpec as P

HEAD = 64


norm_eps = 1e-12
masked_value = -1000000000.0


MESH = pl.DeviceIdType.MESH
F32 = jnp.float32
LOW = jnp.bfloat16
CHUNK = 32
LAG = 2
PIECE = 512
QUERIES = 128


def dot(a, b):
    return jnp.dot(a, b, preferred_element_type=F32)


def dot_t(a, b):
    return lax.dot_general(a, b, (((1,), (1,)), ((), ())), preferred_element_type=F32)


def dot_tn(a, b):
    return lax.dot_general(a, b, (((0,), (0,)), ((), ())), preferred_element_type=F32)


def here():
    return lax.axis_index("dp"), lax.axis_index("tensor")


def greet(size, line=True, targets=()):
    row, place = here()
    barrier = pltpu.get_barrier_semaphore()
    for count, target in targets:

        def signal(index, carry):
            pl.semaphore_signal(barrier, inc=1, device_id=target(index), device_id_type=MESH)
            return carry

        lax.fori_loop(0, count, signal, 0)
    expected = sum(count for count, _ in targets)
    left, right = place > 0, place < size - 1
    if line:

        @pl.when(left)
        def _():
            pl.semaphore_signal(barrier, inc=1, device_id=(row, place - 1), device_id_type=MESH)

        @pl.when(right)
        def _():
            pl.semaphore_signal(barrier, inc=1, device_id=(row, place + 1), device_id_type=MESH)

    def wait():
        if not line:
            pl.semaphore_wait(barrier, expected)
            return

        @pl.when(left & right)
        def _():
            pl.semaphore_wait(barrier, expected + 2)

        @pl.when(jnp.logical_not(left & right))
        def _():
            pl.semaphore_wait(barrier, expected + 1)

    return wait


def partner():
    row, place = here()
    return (row + 1 - 2 * lax.rem(row, 2), place)


def plane_peer(chips, index):
    row, place = here()
    return (lax.rem(row // 2 + index + 1, chips) * 2 + lax.rem(row, 2), place)


def line_loop(size, stages, extras=(), lag=LAG):
    row, place = here()
    half = stages[0].part.shape[0] // 2
    chunks = half // CHUNK
    end = size - 1
    span = 2 * lag * end

    def rows_of(side, chunk):
        return pl.ds(pl.multiple_of(side * half + chunk * CHUNK, CHUNK), CHUNK)

    def sum_copy(stage, side, chunk, target):
        rows = rows_of(side, chunk)
        return pltpu.make_async_remote_copy(
            src_ref=stage.part.at[rows],
            dst_ref=stage.recv.at[rows],
            send_sem=stage.sems[0].at[side, chunk],
            recv_sem=stage.sems[1].at[side, chunk],
            device_id=(row, target),
            device_id_type=MESH,
        )

    def row_copy(stage, which, side, chunk, target):
        rows = rows_of(side, chunk)
        return pltpu.make_async_remote_copy(
            src_ref=stage.outs[which].at[rows],
            dst_ref=stage.outs[which].at[rows],
            send_sem=stage.sems[2].at[which, side, chunk],
            recv_sem=stage.sems[3].at[which, side, chunk],
            device_id=(row, target),
            device_id_type=MESH,
        )

    def side_facts(side):
        if side == 0:
            return place, place + 1, place - 1
        return end - place, place - 1, place + 1

    def bring_back(stage, since):
        for side in range(2):
            at, onward, back = side_facts(side)
            chunk = since - lag * end - lag * (end - at)

            @pl.when((at < end) & (chunk >= 0) & (chunk < chunks))
            def _():
                for which in range(len(stage.outs)):
                    row_copy(stage, which, side, chunk, back).wait_recv()

                    @pl.when(at > 0)
                    def _():
                        row_copy(stage, which, side, chunk, back).start()

    def sum_up(stage, since):
        for side in range(2):
            at, onward, back = side_facts(side)
            chunk = since - lag * at

            @pl.when((chunk >= 0) & (chunk < chunks))
            def _():
                @pl.when(at > 0)
                def _():
                    sum_copy(stage, side, chunk, onward).wait_recv()

                @pl.when(at < end)
                def _():
                    @pl.when(at > 0)
                    def _():
                        rows = rows_of(side, chunk)
                        stage.part[rows] = stage.part[rows] + stage.recv[rows]

                    sum_copy(stage, side, chunk, onward).start()

                @pl.when(at == end)
                def _():
                    rows = rows_of(side, chunk)
                    own = pl.ds(pl.multiple_of(chunk * CHUNK, CHUNK), CHUNK)
                    stage.finish(rows, own, stage.part[rows].astype(F32) + stage.recv[rows].astype(F32))
                    for which in range(len(stage.outs)):
                        row_copy(stage, which, side, chunk, back).start()

    def step(now, carry):
        for number, stage in enumerate(stages):
            bring_back(stage, now - number * span)
        for number, stage in enumerate(stages):
            since = now - number * span

            @pl.when((since >= 0) & (since < chunks))
            def _():
                stage.produce([rows_of(side, since) for side in range(2)])

            sum_up(stage, since)
        for first, count, work in extras:

            @pl.when((now >= first) & (now < first + count))
            def _():
                work(now - first)

        return carry

    lax.fori_loop(0, chunks + span * len(stages), step, 0)

    def drain(chunk, carry):
        for stage in stages:
            for side in range(2):
                at, onward, back = side_facts(side)

                @pl.when(at < end)
                def _():
                    sum_copy(stage, side, chunk, onward).wait_send()

                @pl.when(at > 0)
                def _():
                    for which in range(len(stage.outs)):
                        row_copy(stage, which, side, chunk, back).wait_send()

        return carry

    lax.fori_loop(0, chunks, drain, 0)


def by_rows(count, work, block=32):
    def one(index, carry):
        work(pl.ds(pl.multiple_of(index * block, block), block), index * block)
        return carry

    block = min(block, count)
    lax.fori_loop(0, count // block, one, 0)


class Spread:
    def __init__(self, chips, grads, scratch):
        self.chips, self.grads = chips, grads
        self.half = grads.shape[0] // 2
        self.near, self.far, self.near_sems, self.far_sems, self.free = scratch
        row, place = here()
        self.core, self.chip, self.place = lax.rem(row, 2), row // 2, place

    @staticmethod
    def scratch(chips, rows, width):
        half = rows // 2
        far = half * 3 // 4 if chips == 4 else half // chips * (chips - 1)
        copies = 8 if chips == 4 else 2 * (chips - 1)
        sems = [
            pltpu.SemaphoreType.DMA((4,)),
            pltpu.SemaphoreType.DMA((2, copies)),
            pltpu.SemaphoreType.REGULAR,
        ]
        return [pltpu.VMEM((half, width), LOW), pltpu.VMEM((far, width), LOW), *sems, *sems]

    def rows(self, first, count):
        return pl.ds(pl.multiple_of(first, 16), count)

    def core_copy(self, source, target, number):
        return pltpu.make_async_remote_copy(
            src_ref=source,
            dst_ref=target,
            send_sem=self.near_sems.at[2 * number],
            recv_sem=self.near_sems.at[2 * number + 1],
            device_id=partner(),
            device_id_type=MESH,
        )

    def near_copy(self):
        other = self.rows((1 - self.core) * self.half, self.half)
        return self.core_copy(self.grads.at[other], self.near, 0)

    def last_copy(self):
        own = self.grads.at[self.rows(self.core * self.half, self.half)]
        return self.core_copy(own, own, 1)

    def chip_copy(self, source, target, number, chip):
        return pltpu.make_async_remote_copy(
            src_ref=source,
            dst_ref=target,
            send_sem=self.far_sems.at[0, number],
            recv_sem=self.far_sems.at[1, number],
            device_id=(chip * 2 + self.core, self.place),
            device_id_type=MESH,
        )

    def to_partner(self):
        self.near_copy().start()

    def add_partner(self):
        self.near_copy().wait_send()
        pl.semaphore_signal(self.free, inc=1, device_id=partner(), device_id_type=MESH)
        self.near_copy().wait_recv()
        base = self.core * self.half

        def add(rows, first):
            own = self.grads[self.rows(base + first, rows.size)]
            self.near[rows] = self.near[rows] + own

        by_rows(self.half, add)

    def settle_sum(self):
        self.settle_there()
        pl.semaphore_wait(self.free, 1)

    def give_share(self):
        self.sum_share(self.grads, self.own_rows())
        self.start_back()

    def keep_share(self, share):
        count = share.shape[0] // len(self.own_rows())
        for number, base in enumerate(self.own_rows()):

            def keep(rows, first, number=number, base=base):
                came = share[self.rows(number * count + first, rows.size)]
                self.grads[self.rows(base + first, rows.size)] = came

            by_rows(count, keep)
        self.summed = False
        self.start_back()

    summed = True

    def to_other_core(self):
        self.take_back()
        if self.summed:
            self.settle_sum()
        self.settle_back()
        self.last_copy().start()

    def settle(self):
        self.last_copy().wait_recv()
        self.last_copy().wait_send()


class DirectSpread(Spread):
    def each(self, work):
        def one(index, carry):
            work(index)
            return carry

        lax.fori_loop(0, self.chips - 1, one, 0)

    def peer(self, index):
        return lax.rem(self.chip + index + 1, self.chips)

    def far_copy(self, index):
        count = self.half // self.chips
        chip = self.peer(index)
        source = self.near.at[self.rows(chip * count, count)]
        return self.chip_copy(source, self.far.at[self.rows(index * count, count)], index, chip)

    def back_copy(self, index):
        count = self.half // self.chips
        share = self.grads.at[self.rows(self.core * self.half + self.chip * count, count)]
        return self.chip_copy(share, share, self.chips - 1 + index, self.peer(index))

    def to_chips(self):
        self.add_partner()
        self.each(lambda index: self.far_copy(index).start())

    def onward(self):
        pass

    def own_rows(self):
        return [self.core * self.half + self.chip * (self.half // self.chips)]

    def sum_share(self, target, starts):
        self.each(lambda index: self.far_copy(index).wait_recv())
        count = self.half // self.chips
        base = self.chip * count

        def add(rows, first):
            def one(index, total):
                return total + self.far[self.rows(index * count + first, rows.size)].astype(F32)

            own = self.near[self.rows(base + first, rows.size)].astype(F32)
            total = lax.fori_loop(0, self.chips - 1, one, own)
            target[self.rows(starts[0] + first, rows.size)] = total.astype(LOW)

        by_rows(count, add)

    def start_back(self):
        self.each(lambda index: self.back_copy(index).start())

    def pass_on(self):
        pass

    def take_back(self):
        self.each(lambda index: self.back_copy(index).wait_recv())

    def settle_there(self):
        self.each(lambda index: self.far_copy(index).wait_send())

    def settle_back(self):
        self.each(lambda index: self.back_copy(index).wait_send())


class SquareSpread(Spread):
    def __init__(self, chips, grads, scratch):
        super().__init__(chips, grads, scratch)
        quarter = self.half // 4
        eighth = self.half // 8
        first, second = lax.rem(self.chip, 2), self.chip // 2
        along = self.chip + 1 - 2 * first
        across = self.chip + 2 - 4 * second
        self.quarter, self.eighth = quarter, eighth
        self.chips_of = ((along, across), (across, along))
        self.bits = ((first, second), (second, first))
        self.part = [side * 2 * quarter for side in range(2)]
        self.kept = [self.part[side] + self.bits[side][0] * quarter for side in range(2)]
        self.own = [self.kept[side] + self.bits[side][1] * eighth for side in range(2)]

    def first_copy(self, side):
        sent = self.part[side] + (1 - self.bits[side][0]) * self.quarter
        room = self.far.at[pl.ds(side * self.quarter, self.quarter)]
        source = self.near.at[self.rows(sent, self.quarter)]
        return self.chip_copy(source, room, side, self.chips_of[side][0])

    def second_copy(self, side):
        sent = self.kept[side] + (1 - self.bits[side][1]) * self.eighth
        room = self.far.at[pl.ds(2 * self.quarter + side * self.eighth, self.eighth)]
        source = self.near.at[self.rows(sent, self.eighth)]
        return self.chip_copy(source, room, 2 + side, self.chips_of[side][1])

    def share_copy(self, side):
        share = self.grads.at[self.rows(self.core * self.half + self.own[side], self.eighth)]
        return self.chip_copy(share, share, 4 + side, self.chips_of[side][1])

    def pass_copy(self, side):
        share = self.grads.at[self.rows(self.core * self.half + self.kept[side], self.quarter)]
        return self.chip_copy(share, share, 6 + side, self.chips_of[side][0])

    def to_chips(self):
        self.add_partner()
        for side in range(2):
            self.first_copy(side).start()

    def onward(self):
        for side in range(2):
            self.first_copy(side).wait_recv()
            base = self.kept[side]

            def add(rows, first, side=side, base=base):
                at = self.rows(base + first, rows.size)
                came = self.far[self.rows(side * self.quarter + first, rows.size)]
                self.near[at] = self.near[at] + came

            by_rows(self.quarter, add)
            self.second_copy(side).start()

    def own_rows(self):
        return [self.core * self.half + self.own[side] for side in range(2)]

    def sum_share(self, target, starts):
        for side in range(2):
            self.second_copy(side).wait_recv()
            base, start = self.own[side], starts[side]

            def add(rows, first, side=side, base=base, start=start):
                came = self.far[self.rows(2 * self.quarter + side * self.eighth + first, rows.size)]
                own = self.near[self.rows(base + first, rows.size)]
                target[self.rows(start + first, rows.size)] = own + came

            by_rows(self.eighth, add)

    def start_back(self):
        for side in range(2):
            self.share_copy(side).start()

    def pass_on(self):
        for side in range(2):
            self.share_copy(side).wait_recv()
            self.pass_copy(side).start()

    def take_back(self):
        for side in range(2):
            self.pass_copy(side).wait_recv()

    def settle_there(self):
        for side in range(2):
            self.first_copy(side).wait_send()
            self.second_copy(side).wait_send()

    def settle_back(self):
        for side in range(2):
            self.share_copy(side).wait_send()
            self.pass_copy(side).wait_send()


def spread_of(chips, grads, scratch):
    return (SquareSpread if chips == 4 else DirectSpread)(chips, grads, scratch)


def normalize(residual):
    centred = residual - jnp.mean(residual, axis=-1, keepdims=True)
    inverse = lax.rsqrt(jnp.mean(centred * centred, axis=-1, keepdims=True) + norm_eps)
    return centred * inverse, inverse


def norm_back(grad, gain, unit, inverse):
    scaled = grad * gain
    return (
        scaled
        - jnp.mean(scaled, axis=-1, keepdims=True)
        - unit * jnp.mean(scaled * unit, axis=-1, keepdims=True)
    ) * inverse


def tally(total, values):
    total[...] += jnp.sum(values.reshape(-1, 8, values.shape[-1]), axis=0)


class Layer:
    def __init__(self, array, layer):
        self.array, self.layer = array, layer

    def room(self):
        return self.array.shape if self.layer is None else self.array.shape[1:]


def whole(array):
    return Layer(array, None)


def view(refs, suffix):
    named = dict(vars(refs))
    for name, ref in vars(refs).items():
        if name.endswith(suffix):
            named[name[: -len(suffix)]] = ref
    return types.SimpleNamespace(**named)


def call(collective, body, ins, outs, scratch, into=types.MappingProxyType({}), later=(), sent=()):
    vmem = pl.BlockSpec(memory_space=pltpu.VMEM)
    names = [*ins, *outs]
    fetched = {name: value for name, value in ins.items() if isinstance(value, Layer)}
    inside = {name: value for name, value in fetched.items() if name not in into}
    extra = {name: spec if isinstance(spec, list) else [spec] for name, spec in scratch.items()}

    def run(*refs):
        named = dict(zip(names, refs))
        rest = list(refs[len(names) :])
        copies, leaving = {}, {}
        arrivals, departures = rest.pop(0), rest.pop(0)
        for number, name in enumerate(sent):
            room = rest.pop(0)
            leaving[name] = pltpu.make_async_copy(room, named[name], departures.at[number])
            named[name] = room
        for number, (name, value) in enumerate(fetched.items()):
            room = named[into[name]] if name in into else rest.pop(0)
            source = named[name] if value.layer is None else named[name].at[value.layer]
            copies[name] = pltpu.make_async_copy(source, room, arrivals.at[number])
            if name not in later:
                copies[name].start()
            named[name] = room
        for name, specs in extra.items():
            taken = [rest.pop(0) for _ in specs]
            named[name] = taken if isinstance(scratch[name], list) else taken[0]

        def need(*wanted):
            for name in wanted:
                copies[name].wait()

        def fetch(*wanted):
            for name in wanted:
                copies[name].start()

        def send(*wanted):
            for name in wanted:
                leaving[name].start()

        body(types.SimpleNamespace(**named, need=need, fetch=fetch, send=send))
        for copy in leaving.values():
            copy.wait()

    results = pl.pallas_call(
        run,
        out_shape=list(outs.values()),
        in_specs=[pl.BlockSpec(memory_space=pl.ANY) if name in fetched else vmem for name in ins],
        out_specs=[pl.BlockSpec(memory_space=pl.ANY) if name in sent else vmem for name in outs],
        scratch_shapes=[
            pltpu.SemaphoreType.DMA((len(fetched),)),
            pltpu.SemaphoreType.DMA((max(1, len(sent)),)),
            *(pltpu.VMEM(outs[name].shape, outs[name].dtype) for name in sent),
            *(pltpu.VMEM(value.room(), value.array.dtype) for value in inside.values()),
            *(spec for specs in extra.values() for spec in specs),
        ],
        compiler_params=pltpu.CompilerParams(
            collective_id=collective, has_side_effects=True, vmem_limit_bytes=60 << 20
        ),
    )(*(value.array if isinstance(value, Layer) else value for value in ins.values()))
    return types.SimpleNamespace(**dict(zip(outs, results)))


def shape(*dims, kind=F32):
    return jax.ShapeDtypeStruct(dims, kind)


def line_scratch(rows, width, outs=1):
    chunks = rows // 2 // CHUNK
    return [
        pltpu.VMEM((rows, width), LOW),
        pltpu.VMEM((rows, width), LOW),
        pltpu.SemaphoreType.DMA((2, chunks)),
        pltpu.SemaphoreType.DMA((2, chunks)),
        pltpu.SemaphoreType.DMA((outs, 2, chunks)),
        pltpu.SemaphoreType.DMA((outs, 2, chunks)),
    ]


def stage_of(produce, finish, outs, scratch):
    part, recv, *sems = scratch
    return types.SimpleNamespace(
        produce=produce, finish=finish, outs=outs, part=part, recv=recv, sems=sems
    )


def clear(*refs):
    for ref in refs:
        ref[...] = jnp.zeros_like(ref)


def vector(ref, layer):
    return ref[...].astype(F32)[layer : layer + 1]


def head_lanes(values, head):
    lane = lax.broadcasted_iota(jnp.int32, values.shape, 1)
    return jnp.where(lane // HEAD == head, values, jnp.zeros_like(values))


def turned(values):
    return jnp.transpose(values.astype(F32)).astype(LOW)


def mark_segments(r):
    length = r.seg_row.shape[1]
    wide = jnp.broadcast_to(r.seg_row[...].astype(F32), (QUERIES, length))
    r.seg_cols[...] = jnp.transpose(wide)


def masked_block(r, keys, queries, at):
    same = r.seg_cols[...] == r.seg_row[:, at].astype(F32)
    return jnp.where(same, dot_t(keys, queries) * HEAD ** (-0.5), masked_value)


def project(r, layer):
    bias = r.qv_bias[layer].astype(F32)
    for member in range(3):
        rows = dot(r.low_in[...], r.qkv_w[member])
        if member != 1:
            rows += bias[member // 2 : member // 2 + 1]
        r.projected[member] = rows.astype(LOW)
    r.turned_rows[...] = turned(r.projected[2])


def attend(r, block):
    at = pl.ds(pl.multiple_of(block * QUERIES, QUERIES), QUERIES)
    queries = r.projected[0, at]
    heads = queries.shape[1] // HEAD
    parts = []
    for head in range(heads):
        scores = masked_block(r, r.projected[1], head_lanes(queries, head), at)
        row_max = jnp.max(scores, axis=0, keepdims=True)
        exponent = jnp.exp(scores - row_max)
        row_total = jnp.sum(exponent, axis=0, keepdims=True)
        r.log_total[head : head + 1, at] = row_max + jnp.log(row_total)
        probs = (exponent * (1.0 / row_total)).astype(LOW)
        parts.append(dot(r.turned_rows[head * HEAD : (head + 1) * HEAD], probs))
    r.context[at] = jnp.transpose(jnp.concatenate(parts, axis=0)).astype(LOW)


def attend_first(r, half):
    per_side = half // QUERIES
    for side in range(2):
        attend(r, side * per_side)
    extras = []
    for block in range(1, per_side):
        for side in range(2):
            step = max(0, block * QUERIES // CHUNK - 2 + side)
            extras.append(at_step(step, lambda block=side * per_side + block: attend(r, block)))
    return extras


def attend_back(r, between=()):
    rows = r.attn_low_in.shape[0]
    heads = r.qkv_w.shape[2] // HEAD
    scale = HEAD ** (-0.5)
    r.grad_context[...] = dot_t(r.attn_low_in[...], r.proj_w[...]).astype(LOW)
    r.turned_rows[...] = turned(r.projected[1])
    clear(r.grad_key, r.grad_value)
    for number in range(rows // QUERIES):
        at = slice(number * QUERIES, (number + 1) * QUERIES)
        queries, context_rows = r.projected[0, at], r.grad_context[at]
        parts = []
        for head in range(heads):
            to = slice(head * QUERIES, (head + 1) * QUERIES)
            r.head_queries[to] = head_lanes(queries, head)
            r.head_context[to] = head_lanes(context_rows, head)
            scores = masked_block(r, r.projected[1], r.head_queries[to], at)
            probability = jnp.exp(scores - r.log_total[head : head + 1, at])
            grad_probs = dot_t(r.projected[2], r.head_context[to])
            inner = jnp.sum(probability * grad_probs, axis=0, keepdims=True)
            grad_scores = (probability * (grad_probs - inner)).astype(LOW)
            r.score_rows[:, to] = grad_scores
            r.prob_rows[:, to] = probability.astype(LOW)
            parts.append(dot(r.turned_rows[head * HEAD : (head + 1) * HEAD], grad_scores))
        r.grad_key[...] += dot(r.score_rows[...], r.head_queries[...])
        r.grad_value[...] += dot(r.prob_rows[...], r.head_context[...])
        r.grad_proj[0, at] = (jnp.transpose(jnp.concatenate(parts, axis=0)) * scale).astype(LOW)
        if number < len(between):
            between[number]()
    r.grad_proj[1] = (r.grad_key[...] * scale).astype(LOW)
    r.grad_proj[2] = r.grad_value[...].astype(LOW)
    for slot, member in ((0, 0), (1, 2)):
        r.qv_sum[slot] = jnp.sum(r.grad_proj[member].astype(F32).reshape(-1, 8, r.qv_sum.shape[2]), axis=0)


def take(ref, blocks):
    return jnp.concatenate([ref[block] for block in blocks], axis=0)


def put(ref, blocks, values):
    count = values.shape[0] // len(blocks)
    for number, block in enumerate(blocks):
        ref[block] = values[number * count : (number + 1) * count]


def proj_stage(r, layer, whole):
    def produce(blocks):
        put(r.proj_line[0], blocks, dot(take(r.context, blocks), r.proj_w[...]).astype(LOW))

    def finish(at, own, total):
        came = r.residual[at if whole else own].astype(F32)
        unit, inverse = normalize(came + total + vector(r.proj_b, layer))
        r.unit_one[own] = unit
        r.inverse_one[own] = inverse
        result = unit * vector(r.first_gain, layer) + vector(r.first_shift, layer)
        r.normed[own] = result
        r.normed_low[at] = result.astype(LOW)

    return stage_of(produce, finish, [r.normed_low], r.proj_line)


def ffn_stage(r, layer, last):
    def produce(blocks):
        pre = dot(take(r.normed_low, blocks), r.up_w[...]) + vector(r.up_b, layer)
        cdf = 0.5 * lax.erf(pre * math.sqrt(0.5)) + 0.5
        act = (pre * cdf).astype(LOW)
        slope = cdf + pre * jnp.exp(-0.5 * pre * pre) * (1.0 / math.sqrt(2 * math.pi))
        put(r.slope, blocks, slope.astype(LOW))
        put(r.act, blocks, act)
        put(r.ffn_line[0], blocks, dot(act, r.down_w[...]).astype(LOW))

    def finish(at, own, total):
        unit, inverse = normalize(r.normed[own] + total + vector(r.down_b, layer))
        gain = vector(r.second_gain, layer)
        result = unit * gain + vector(r.second_shift, layer)
        if last:
            r.mixed_own[own] = result.astype(LOW)
            grad_in = r.cotangent[at].astype(F32)
            grad = norm_back(grad_in, gain, unit, inverse)
            r.grad_second[own] = grad
            r.branch[at] = grad.astype(LOW)
            tally(r.sums.at[0], grad_in * unit)
            tally(r.sums.at[1], grad_in)
            tally(r.sums.at[2], grad.astype(LOW).astype(F32))
        else:
            r.unit_two[own] = unit
            r.inverse_two[own] = inverse
            r.hidden[own] = result
            r.low[at] = result.astype(LOW)

    return stage_of(produce, finish, [r.branch if last else r.low], r.ffn_line)


def ffn_back_stage(r, layer):
    def produce(blocks):
        grad = dot_t(take(r.branch, blocks), r.down_w[...])
        pre = (grad * take(r.slope, blocks).astype(F32)).astype(LOW)
        put(r.pre, blocks, pre)
        tally(r.up_sum, pre.astype(F32))
        put(r.back_line[0], blocks, dot_t(pre, r.up_w[...]).astype(LOW))

    def finish(at, own, total):
        grad_in = r.grad_second[own] + total
        unit = r.unit_one[own]
        grad = norm_back(grad_in, vector(r.first_gain, layer), unit, r.inverse_one[own])
        r.grad_first[own] = grad
        r.attn_low[at] = grad.astype(LOW)
        tally(r.sums.at[3], grad_in * unit)
        tally(r.sums.at[4], grad_in)
        tally(r.sums.at[5], grad.astype(LOW).astype(F32))

    return stage_of(produce, finish, [r.attn_low], r.back_line)


def qkv_back_stage(r, layer, inner):
    def produce(blocks):
        total = sum(dot_t(take(r.grad_proj.at[member], blocks), r.qkv_w[member]) for member in range(3))
        put(r.qkv_line[0], blocks, total.astype(LOW))

    def finish(at, own, total):
        grad_in = r.grad_first_in[own] + total
        if not inner:
            r.grad_low[at] = grad_in.astype(LOW)
            return
        unit = r.unit_two[own]
        grad = norm_back(grad_in, vector(r.second_gain, layer), unit, r.inverse_two[own])
        r.grad_second[own] = grad
        r.branch[at] = grad.astype(LOW)
        tally(r.sums.at[0], grad_in * unit)
        tally(r.sums.at[1], grad_in)
        tally(r.sums.at[2], grad.astype(LOW).astype(F32))

    return stage_of(produce, finish, [r.branch] if inner else [r.grad_low], r.qkv_line)


def columns(piece):
    return pl.ds(pl.multiple_of(piece * PIECE, PIECE), PIECE)


def ffn_grads(r, out, first):
    width, hidden = r.up_w.shape

    def up(piece):
        rows = pl.ds(pl.multiple_of(piece * PIECE, PIECE), PIECE)
        out[rows] = dot_tn(r.normed_low[:, columns(piece)], r.pre[...]).astype(LOW)

    def down(piece):
        rows = pl.ds(pl.multiple_of(width + piece * PIECE, PIECE), PIECE)
        out[rows] = dot_tn(r.act[:, columns(piece)], r.branch[...]).astype(LOW)

    def all_of(pieces, work):
        lax.fori_loop(0, pieces, lambda piece, carry: (work(piece), carry)[1], 0)

    return [
        at_step(first, lambda: all_of(width // PIECE, up)),
        at_step(first + 1, lambda: all_of(hidden // PIECE, down)),
    ]


def attn_grads(r, out, first):
    width, part = r.low_in.shape[1], r.context_in.shape[1]

    def piece_of(piece):
        for member in range(3):
            rows = pl.ds(pl.multiple_of(member * width + piece * part, part), part)
            taken = r.low_in[:, pl.ds(pl.multiple_of(piece * part, part), part)]
            out[rows] = dot_tn(taken, r.grad_proj[member]).astype(LOW)
        rows = pl.ds(pl.multiple_of(3 * width + piece * part, part), part)
        taken = r.attn_low_in[:, pl.ds(pl.multiple_of(piece * part, part), part)]
        out[rows] = dot_tn(r.context_in[...], taken).astype(LOW)

    def all_pieces():
        lax.fori_loop(0, width // part, lambda piece, carry: (piece_of(piece), carry)[1], 0)

    return [at_step(first, all_pieces)]


def at_step(step, work):
    return (step, 1, lambda index: work())


def with_suffix(suffix, named):
    return {name + suffix: value for name, value in named.items()}


def kept_attention(rows, part):
    return dict(
        projected=shape(3, rows, part, kind=LOW),
        log_total=shape(part // HEAD, rows),
        context=shape(rows, part, kind=LOW),
    )


def forward_kernel(size, chips, collective, ins):
    rows, width = ins["low_in_0"].shape
    part, hidden = ins["proj_w_0"].array.shape[1], ins["up_w_0"].array.shape[2]
    half = rows // 2
    chunks = half // CHUNK

    def body(r):
        wait = greet(size, targets=[(1, lambda index: partner()), (chips - 1, lambda index: plane_peer(chips, index))])
        ffn_sum = spread_of(chips, r.ffn_grad, r.ffn_spread[:5])
        clear(r.sums, r.up_sum)
        mark_segments(r)
        below, above = view(r, "_0"), view(r, "_1")
        below.residual = r.low_in_0
        above.low_in, above.residual = r.low_0, r.hidden_0
        r.need("qkv_w_0")
        project(below, 0)
        extras = attend_first(below, half)
        r.need("proj_w_0", "up_w_0", "down_w_0")
        wait()
        line_loop(size, [proj_stage(below, 0, True), ffn_stage(below, 0, False)], extras, 3)
        r.send("projected_0", "context_0", "unit_one_0", "normed_low_0", "act_0", "slope_0", "unit_two_0", "low_0")
        r.need("qkv_w_1")
        project(above, 1)
        extras = attend_first(above, half)
        r.need("proj_w_1", "up_w_1", "down_w_1")
        stages = [proj_stage(above, 1, False), ffn_stage(above, 1, True), ffn_back_stage(above, 1)]
        first = 4 * 3 * (size - 1) + chunks
        line_loop(
            size,
            stages,
            [
                *extras,
                at_step(2 * chunks, lambda: r.send("projected_1", "context_1")),
                *ffn_grads(above, r.ffn_grad, first),
                at_step(first + 2, lambda: (ffn_sum.to_partner(), r.send("mixed_own"))),
                at_step(first + 5, ffn_sum.to_chips),
                at_step(first + 15, ffn_sum.onward),
            ],
            3,
        )
        r.send("grad_first", "attn_low")
        share = r.ffn_share.shape[0]
        ffn_sum.sum_share(r.ffn_share, [0, share // 2])
        ffn_sum.settle_sum()

    outs = dict(
        **with_suffix("_0", kept_attention(rows, part)),
        **with_suffix("_1", kept_attention(rows, part)),
        unit_one_0=shape(half, width),
        inverse_one_0=shape(half, 1),
        normed_low_0=shape(rows, width, kind=LOW),
        act_0=shape(rows, hidden, kind=LOW),
        slope_0=shape(rows, hidden, kind=LOW),
        unit_two_0=shape(half, width),
        inverse_two_0=shape(half, 1),
        low_0=shape(rows, width, kind=LOW),
        mixed_own=shape(half, width, kind=LOW),
        grad_first=shape(half, width),
        attn_low=shape(rows, width, kind=LOW),
        ffn_share=shape((width + hidden) // 2 // chips, width, kind=LOW),
        up_sum=shape(8, hidden),
        sums=shape(6, 8, width),
    )
    scratch = dict(
        hidden_0=pltpu.VMEM((half, width), F32),
        normed=pltpu.VMEM((half, width), F32),
        turned_rows=pltpu.VMEM((part, rows), LOW),
        seg_cols=pltpu.VMEM((rows, QUERIES), F32),
        unit_one_1=pltpu.VMEM((half, width), F32),
        inverse_one_1=pltpu.VMEM((half, 1), F32),
        normed_low_1=pltpu.VMEM((rows, width), LOW),
        act_1=pltpu.VMEM((rows, hidden), LOW),
        slope_1=pltpu.VMEM((rows, hidden), LOW),
        pre=pltpu.VMEM((rows, hidden), LOW),
        branch=pltpu.VMEM((rows, width), LOW),
        grad_second=pltpu.VMEM((half, width), F32),
        proj_line_0=line_scratch(rows, width),
        ffn_line_0=line_scratch(rows, width),
        proj_line_1=line_scratch(rows, width),
        ffn_line_1=line_scratch(rows, width),
        back_line=line_scratch(rows, width),
        ffn_grad=pltpu.VMEM((width + hidden, width), LOW),
        ffn_spread=Spread.scratch(chips, width + hidden, width),
    )
    sent = [name for name, out in outs.items() if out.dtype == LOW and name != "ffn_share" or name in ("unit_one_0", "unit_two_0", "grad_first")]
    return call(collective, body, ins, outs, scratch, sent=sent)


def backward_kernel(size, chips, collective, layers, ins):
    rows, width = ins["attn_low_1"].array.shape
    part, hidden = ins["proj_w_0"].array.shape[1], ins["up_w"].array.shape[2]
    half = rows // 2
    chunks = half // CHUNK
    span = 2 * LAG * (size - 1)
    ffn_rows, attn_rows = width + hidden, 4 * width
    own_rows = layers * (2 * part + hidden) // width
    count = -(-(own_rows + 6 * layers) // 8) * 8
    teams = 2 * chips

    def row_peer(index):
        row, place = here()
        return (lax.rem(row + index + 1, teams), place)

    def line_peer(index):
        row, place = here()
        return (row, lax.rem(place + index + 1, size))

    def each(number, work):
        def one(index, carry):
            work(index)
            return carry

        lax.fori_loop(0, number, one, 0)

    def body(r):
        row, place = here()
        clear(r.ends, r.sums_0, r.up_sum_0)
        wait = greet(size, line=False, targets=[(teams - 1, row_peer), (size - 1, line_peer)])
        ffn_above = spread_of(chips, r.ffn_whole_1, r.ffn_spread[:5])
        attn_above = spread_of(chips, r.attn_whole_1, r.attn_spread[:5])
        ffn_below = spread_of(chips, r.ffn_whole_0, r.ffn_spread[:2] + r.ffn_spread[5:])
        attn_below = spread_of(chips, r.attn_whole_0, r.attn_spread[:2] + r.attn_spread[5:])
        above, below = view(r, "_1"), view(r, "_0")
        above.grad_first_in, above.attn_low_in = r.grad_first_1, r.attn_low_1
        below.grad_first_in, below.attn_low_in = r.grad_first_0, r.attn_low_0
        middle = types.SimpleNamespace(
            **{**vars(r), "sums": r.sums_0, "up_sum": r.up_sum_0, "grad_first": r.grad_first_0, "attn_low": r.attn_low_0}
        )
        above.sums = r.sums_0
        above.grad_second = middle.grad_second = r.grad_first_0
        below.qkv_line = [*r.qkv_line_1[:2], *r.qkv_sems_0]

        def end_copy(slot, index):
            return pltpu.make_async_remote_copy(
                src_ref=r.small,
                dst_ref=r.ends.at[slot],
                send_sem=r.end_sent.at[slot, index],
                recv_sem=r.end_got.at[slot],
                device_id=line_peer(index),
                device_id_type=MESH,
            )

        def team_copy(index, slot):
            return pltpu.make_async_remote_copy(
                src_ref=r.mine,
                dst_ref=r.others.at[slot],
                send_sem=r.team_sent.at[index],
                recv_sem=r.team_got.at[slot],
                device_id=row_peer(index),
                device_id_type=MESH,
            )

        end_places = ((0, 0), (1, size - 1))
        end = size - 1

        def side_rows(side):
            at, back = (place, place - 1) if side == 0 else (end - place, place + 1)
            return at, back, r.mixed.at[pl.ds(side * half, half)]

        def mixed_copy(side):
            at, back, rows_at = side_rows(side)
            return pltpu.make_async_remote_copy(
                src_ref=rows_at,
                dst_ref=rows_at,
                send_sem=r.mixed_sent.at[side],
                recv_sem=r.mixed_got.at[side],
                device_id=(row, back),
                device_id_type=MESH,
            )

        def mixed_hop(number):
            for side in range(2):
                at, _, rows_at = side_rows(side)

                @pl.when(at == end - number)
                def _():
                    if number:
                        mixed_copy(side).wait_recv()
                    else:
                        rows_at[...] = r.mixed_own[...]
                    mixed_copy(side).start()

        def mixed_settle():
            for side in range(2):
                at, _, _ = side_rows(side)

                @pl.when(at == 0)
                def _():
                    mixed_copy(side).wait_recv()

                @pl.when(at > 0)
                def _():
                    mixed_copy(side).wait_send()

        def small_to_line():
            named = vars(r)
            clear(r.small)
            lines = []
            for layer in range(layers):
                sums = jnp.sum(named["qv_sum_%d" % layer][...], axis=1)
                lines += [sums[0:1], sums[1:2]]
            for layer in range(layers):
                lines += [jnp.sum(named["up_sum_%d" % layer][...], axis=0, keepdims=True)]
            flat = jnp.concatenate(lines, axis=1)
            for number in range(own_rows):
                r.small[number : number + 1] = flat[:, number * width : (number + 1) * width]
            for layer in range(layers):
                sums = jnp.sum(named["sums_%d" % layer][...], axis=1)
                for member in range(6):
                    to = own_rows + member * layers + layer
                    r.small[to : to + 1] = sums[member : member + 1]
            for slot, end in end_places:

                @pl.when(place == end)
                def _():
                    each(size - 1, lambda index: end_copy(slot, index).start())

        def small_to_teams():
            for slot, end in end_places:

                @pl.when(place != end)
                def _():
                    end_copy(slot, 0).wait_recv()

            line_total = r.small[...] + r.ends[0] + r.ends[1]
            number = lax.broadcasted_iota(jnp.int32, (count, width), 0)
            r.mine[...] = jnp.where(number < own_rows, r.small[...], line_total)
            each(teams - 1, lambda index: team_copy(index, row).start())
            r.others[row] = r.mine[...]

        def small_finish():
            each(teams - 1, lambda index: team_copy(index, row_peer(index)[0]).wait_recv())
            r.small_total[...] = lax.fori_loop(
                1, teams, lambda index, total: total + r.others[index], r.others[0]
            )
            each(teams - 1, lambda index: team_copy(index, row).wait_send())
            for slot, end in end_places:

                @pl.when(place == end)
                def _():
                    each(size - 1, lambda index: end_copy(slot, index).wait_send())

        mark_segments(r)
        r.need("proj_w_1", "attn_low_1", "projected_1", "mixed_own")
        wait()
        ffn_above.keep_share(r.ffn_share_1)
        mixed_hop(0)
        attend_back(above)
        r.need("qkv_w_1", "grad_first_1", "unit_two", "context_in_1", "low_in_1")
        r.need("up_w", "down_w", "slope", "unit_one", "act", "normed_low")
        extras = [
            *attn_grads(above, r.attn_whole_1, 2),
            at_step(span, lambda: r.fetch("proj_w_0", "qkv_w_0")),
            *ffn_grads(middle, r.ffn_whole_0, 6 * (size - 1) + chunks),
            at_step(3, ffn_above.pass_on),
            at_step(5, attn_above.to_partner),
            at_step(8, attn_above.to_chips),
            at_step(12, ffn_above.to_other_core),
            at_step(15, attn_above.onward),
            at_step(16, lambda: (ffn_above.settle(), r.send("ffn_whole_1"))),
            at_step(6 * (size - 1) + 1, attn_above.give_share),
            at_step(6 * (size - 1) + 5, attn_above.pass_on),
            at_step(6 * (size - 1) + 10, attn_above.to_other_core),
            at_step(6 * (size - 1) + 11, ffn_below.to_partner),
            at_step(6 * (size - 1) + 13, lambda: (attn_above.settle(), r.send("attn_whole_1"))),
            at_step(6 * (size - 1) + 14, ffn_below.to_chips),
            at_step(12 * (size - 1) + 6, ffn_below.onward),
        ]
        stages = [qkv_back_stage(above, 0, True), ffn_back_stage(middle, 0)]
        line_loop(size, stages, extras, 3)
        r.need("proj_w_0", "qkv_w_0", "projected_0")
        mixed_hop(1)
        attend_back(below)
        ffn_below.give_share()
        r.need("context_in_0", "low_in_0")
        extras = [
            *attn_grads(below, r.attn_whole_0, 0),
            at_step(2, small_to_line),
            *(at_step(4 + 6 * (hop - 2), lambda hop=hop: mixed_hop(hop)) for hop in range(2, end)),
            at_step(7, small_to_teams),
            at_step(15, small_finish),
            at_step(1, attn_below.to_partner),
            at_step(3, ffn_below.pass_on),
            at_step(3, attn_below.to_chips),
            at_step(9, ffn_below.to_other_core),
            at_step(9, attn_below.onward),
            at_step(11, lambda: (ffn_below.settle(), r.send("ffn_whole_0"))),
            at_step(12, attn_below.give_share),
            at_step(14, attn_below.pass_on),
            at_step(18, attn_below.to_other_core),
        ]
        line_loop(size, [qkv_back_stage(below, 0, False)], extras)
        mixed_settle()
        r.send("grad_low", "mixed")
        attn_below.settle()
        r.send("attn_whole_0")

    heads = part // HEAD
    rooms = {"qkv_w_0": "qkv_w_1", "proj_w_0": "proj_w_1"}
    outs = dict(
        grad_low=shape(rows, width, kind=LOW),
        mixed=shape(rows, width, kind=LOW),
        ffn_whole_1=shape(ffn_rows, width, kind=LOW),
        attn_whole_1=shape(attn_rows, part, kind=LOW),
        ffn_whole_0=shape(ffn_rows, width, kind=LOW),
        attn_whole_0=shape(attn_rows, part, kind=LOW),
        small_total=shape(count, width),
    )
    scratch = dict(
        seg_cols=pltpu.VMEM((rows, QUERIES), F32),
        turned_rows=pltpu.VMEM((part, rows), LOW),
        grad_context=pltpu.VMEM((rows, part), LOW),
        grad_key=pltpu.VMEM((rows, part), F32),
        grad_value=pltpu.VMEM((rows, part), F32),
        grad_proj=pltpu.VMEM((3, rows, part), LOW),
        head_queries=pltpu.VMEM((heads * QUERIES, part), LOW),
        head_context=pltpu.VMEM((heads * QUERIES, part), LOW),
        score_rows=pltpu.VMEM((rows, heads * QUERIES), LOW),
        prob_rows=pltpu.VMEM((rows, heads * QUERIES), LOW),
        qv_sum_0=pltpu.VMEM((2, 8, part), F32),
        qv_sum_1=pltpu.VMEM((2, 8, part), F32),
        sums_0=pltpu.VMEM((6, 8, width), F32),
        up_sum_0=pltpu.VMEM((8, hidden), F32),
        pre=pltpu.VMEM((rows, hidden), LOW),
        branch=pltpu.VMEM((rows, width), LOW),
        grad_first_0=pltpu.VMEM((half, width), F32),
        attn_low_0=pltpu.VMEM((rows, width), LOW),
        small=pltpu.VMEM((count, width), F32),
        ends=pltpu.VMEM((2, count, width), F32),
        mine=pltpu.VMEM((count, width), F32),
        others=pltpu.VMEM((teams, count, width), F32),
        end_sent=pltpu.SemaphoreType.DMA((2, size - 1)),
        end_got=pltpu.SemaphoreType.DMA((2,)),
        team_sent=pltpu.SemaphoreType.DMA((teams - 1,)),
        team_got=pltpu.SemaphoreType.DMA((teams,)),
        mixed_sent=pltpu.SemaphoreType.DMA((2,)),
        mixed_got=pltpu.SemaphoreType.DMA((2,)),
        qkv_line_1=line_scratch(rows, width),
        back_line=line_scratch(rows, width),
        qkv_sems_0=line_scratch(rows, width)[2:],
        ffn_spread=Spread.scratch(chips, ffn_rows, width),
        attn_spread=Spread.scratch(chips, attn_rows, part),
    )
    return call(collective, body, ins, outs, scratch, rooms, ("qkv_w_0", "proj_w_0"), [*outs][:-1]), own_rows


def assemble(attn_wholes, ffn_wholes, mixed, grad_low, small, own_rows, part):
    layers = len(attn_wholes)
    rows, width = mixed.shape
    hidden = ffn_wholes[0].shape[0] - width
    steps = 4
    cut = width // steps

    def for_layer(number, spec_of):
        def index(layer, step):
            return spec_of(jnp.where(layer == number, step, jnp.where(layer < number, 0, steps - 1)))

        return index

    ins, in_specs = [], []
    for number in range(layers):
        ins += [
            attn_wholes[number].reshape(4, width, part),
            attn_wholes[number].reshape(-1, part, part),
            ffn_wholes[number].reshape(-1, width, width),
        ]
        in_specs += [
            pl.BlockSpec((3, cut, part), for_layer(number, lambda step: (0, step, 0))),
            pl.BlockSpec((width // part, part // steps, part), for_layer(number, lambda step: (3, step, 0))),
            pl.BlockSpec((1 + hidden // width, cut, width), for_layer(number, lambda step: (0, step, 0))),
        ]
    slab = rows // (layers * steps)
    ins += [mixed, grad_low, small]
    row_spec = pl.BlockSpec((slab, width), lambda layer, step: (layer * steps + step, 0))
    in_specs += [row_spec, row_spec, pl.BlockSpec(small.shape, lambda layer, step: (0, 0))]
    def all_of(*dims):
        return pl.BlockSpec(dims, lambda layer, step: (0,) * len(dims))

    out_shape = [
        shape(rows, width),
        shape(rows, width),
        shape(layers, 3, width, part),
        shape(layers, part, width),
        shape(layers, width, hidden),
        shape(layers, hidden, width),
        shape(layers, 2, part),
        shape(layers, hidden),
    ] + [shape(layers, width)] * 6
    out_specs = [
        row_spec,
        row_spec,
        pl.BlockSpec((1, 3, cut, part), lambda layer, step: (layer, 0, step, 0)),
        pl.BlockSpec((1, part // steps, width), lambda layer, step: (layer, step, 0)),
        pl.BlockSpec((1, cut, hidden), lambda layer, step: (layer, step, 0)),
        pl.BlockSpec((1, cut, width), lambda layer, step: (layer, step, 0)),
        all_of(layers, 2, part),
        all_of(layers, hidden),
    ] + [all_of(layers, width)] * 6

    def body(*refs):
        sources = refs[: 3 * layers]
        mixed_in, grad_in, small_in = refs[3 * layers : 3 * layers + 3]
        mixed_out, grad_out, qkv, proj, up, down, qv, up_b, *norms = refs[3 * layers + 3 :]
        mixed_out[...] = mixed_in[...].astype(F32)
        grad_out[...] = grad_in[...].astype(F32)
        for number in range(layers):
            attn_in, proj_in, ffn_in = sources[3 * number : 3 * number + 3]

            @pl.when(pl.program_id(0) == number)
            def _():
                qkv[0] = attn_in[...].astype(F32)
                for block in range(width // part):
                    proj[0, :, block * part : (block + 1) * part] = proj_in[block].astype(F32)
                up[0] = ffn_in[0].astype(F32)
                down[0] = ffn_in[1].astype(F32)

        @pl.when((pl.program_id(0) == 0) & (pl.program_id(1) == 0))
        def _():
            values = small_in[...]
            flat = jnp.concatenate([values[n : n + 1] for n in range(own_rows)], axis=1)
            for layer in range(layers):
                for member in range(2):
                    at = (2 * layer + member) * part
                    qv[layer, member : member + 1] = flat[:, at : at + part]
                at = 2 * layers * part + layer * hidden
                up_b[layer : layer + 1] = flat[:, at : at + hidden]
            for member, norm in enumerate(norms):
                norm[...] = values[own_rows + member * layers : own_rows + (member + 1) * layers]

    return pl.pallas_call(
        body,
        grid=(layers, steps),
        out_shape=out_shape,
        in_specs=in_specs,
        out_specs=out_specs,
        compiler_params=pltpu.CompilerParams(vmem_limit_bytes=60 << 20),
    )(*ins)


def local(
    tokens,
    segment_ids,
    cotangent,
    qkv_weight,
    qv_bias,
    proj_weight,
    proj_bias,
    first_gain,
    first_shift,
    up_weight,
    up_bias,
    down_weight,
    down_bias,
    second_gain,
    second_shift,
):
    seq_count, length, width = tokens.shape
    rows = seq_count * length
    layers = qkv_weight.shape[0]
    size = lax.axis_size("tensor")
    chips = lax.axis_size("dp") // 2
    part = qkv_weight.shape[-1]
    qkv_stack = jnp.transpose(qkv_weight, (0, 2, 1, 3))
    low = tokens.reshape(rows, width)
    weights = dict(qkv_w=qkv_stack, proj_w=proj_weight, up_w=up_weight, down_w=down_weight)
    ins = dict(
        low_in_0=low,
        cotangent=cotangent.reshape(rows, width),
        seg_row=segment_ids,
        qv_bias=qv_bias,
        proj_b=proj_bias,
        first_gain=first_gain,
        first_shift=first_shift,
        up_b=up_bias,
        down_b=down_bias,
        second_gain=second_gain,
        second_shift=second_shift,
    )
    for layer in range(layers):
        for name, array in weights.items():
            ins["%s_%d" % (name, layer)] = Layer(array, layer)
    done = forward_kernel(size, chips, 0, ins)
    last, own_rows = backward_kernel(
        size,
        chips,
        1,
        layers,
        dict(
            seg_row=segment_ids,
            log_total_0=done.log_total_0,
            log_total_1=done.log_total_1,
            sums_1=done.sums,
            ffn_share_1=done.ffn_share,
            up_sum_1=done.up_sum,
            inverse_two=done.inverse_two_0,
            inverse_one=done.inverse_one_0,
            first_gain=first_gain,
            second_gain=second_gain,
            proj_w_1=Layer(proj_weight, 1),
            attn_low_1=whole(done.attn_low),
            projected_1=whole(done.projected_1),
            mixed_own=whole(done.mixed_own),
            qkv_w_1=Layer(qkv_stack, 1),
            grad_first_1=whole(done.grad_first),
            unit_two=whole(done.unit_two_0),
            context_in_1=whole(done.context_1),
            low_in_1=whole(done.low_0),
            up_w=Layer(up_weight, 0),
            down_w=Layer(down_weight, 0),
            slope=whole(done.slope_0),
            unit_one=whole(done.unit_one_0),
            act=whole(done.act_0),
            normed_low=whole(done.normed_low_0),
            proj_w_0=Layer(proj_weight, 0),
            qkv_w_0=Layer(qkv_stack, 0),
            projected_0=whole(done.projected_0),
            context_in_0=whole(done.context_0),
            low_in_0=whole(low),
        ),
    )
    ffn_wholes = [last.ffn_whole_0, last.ffn_whole_1]
    attn_wholes = [last.attn_whole_0, last.attn_whole_1]

    mixed, input_grad, qkv, proj, up, down, qv, up_b, *norms = assemble(
        attn_wholes, ffn_wholes, last.mixed, last.grad_low, last.small_total, own_rows, part
    )
    return (
        mixed.reshape(tokens.shape),
        input_grad.reshape(tokens.shape),
        jnp.transpose(qkv, (0, 2, 1, 3)),
        qv,
        proj,
        norms[5],
        norms[3],
        norms[4],
        up,
        up_b,
        down,
        norms[2],
        norms[0],
        norms[1],
    )


def solution(mesh):
    return jax.shard_map(
        local,
        mesh=mesh,
        in_specs=(
            P("dp", None, None),
            P("dp", None),
            P("dp", None, None),
            P(None, None, None, "tensor"),
            P(None, None, "tensor"),
            P(None, "tensor", None),
            P(),
            P(),
            P(),
            P(None, None, "tensor"),
            P(None, "tensor"),
            P(None, "tensor", None),
            P(),
            P(),
            P(),
        ),
        out_specs=(
            P("dp", None, None),
            P("dp", None, None),
            P(None, None, None, "tensor"),
            P(None, None, "tensor"),
            P(None, "tensor", None),
            P(),
            P(),
            P(),
            P(None, None, "tensor"),
            P(None, "tensor"),
            P(None, "tensor", None),
            P(),
            P(),
            P(),
        ),
        check_vma=False,
    )
```

```python
import math
import types

import jax
import jax.numpy as jnp
from jax import lax
from jax.experimental import pallas as pl
from jax.experimental.pallas import tpu as pltpu
from jax.sharding import PartitionSpec as P

HEAD = 64


norm_eps = 1e-12
masked_value = -1000000000.0


MESH = pl.DeviceIdType.MESH
F32 = jnp.float32
LOW = jnp.bfloat16
CHUNK = 32
LAG = 2
PIECE = 512
QUERIES = 128


def dot(a, b):
    return jnp.dot(a, b, preferred_element_type=F32)


def dot_t(a, b):
    return lax.dot_general(a, b, (((1,), (1,)), ((), ())), preferred_element_type=F32)


def dot_tn(a, b):
    return lax.dot_general(a, b, (((0,), (0,)), ((), ())), preferred_element_type=F32)


def here():
    return lax.axis_index("dp"), lax.axis_index("tensor")


def greet(size, line=True, targets=()):
    row, place = here()
    barrier = pltpu.get_barrier_semaphore()
    for count, target in targets:

        def signal(index, carry):
            pl.semaphore_signal(barrier, inc=1, device_id=target(index), device_id_type=MESH)
            return carry

        lax.fori_loop(0, count, signal, 0)
    expected = sum(count for count, _ in targets)
    left, right = place > 0, place < size - 1
    if line:

        @pl.when(left)
        def _():
            pl.semaphore_signal(barrier, inc=1, device_id=(row, place - 1), device_id_type=MESH)

        @pl.when(right)
        def _():
            pl.semaphore_signal(barrier, inc=1, device_id=(row, place + 1), device_id_type=MESH)

    def wait():
        if not line:
            pl.semaphore_wait(barrier, expected)
            return

        @pl.when(left & right)
        def _():
            pl.semaphore_wait(barrier, expected + 2)

        @pl.when(jnp.logical_not(left & right))
        def _():
            pl.semaphore_wait(barrier, expected + 1)

    return wait


def partner():
    row, place = here()
    return (row + 1 - 2 * lax.rem(row, 2), place)


def plane_peer(chips, index):
    row, place = here()
    return (lax.rem(row // 2 + index + 1, chips) * 2 + lax.rem(row, 2), place)


def line_loop(size, stages, extras=(), lag=LAG):
    row, place = here()
    half = stages[0].part.shape[0] // 2
    chunks = half // CHUNK
    end = size - 1
    span = 2 * lag * end

    def rows_of(side, chunk):
        return pl.ds(pl.multiple_of(side * half + chunk * CHUNK, CHUNK), CHUNK)

    def sum_copy(stage, side, chunk, target):
        rows = rows_of(side, chunk)
        return pltpu.make_async_remote_copy(
            src_ref=stage.part.at[rows],
            dst_ref=stage.recv.at[rows],
            send_sem=stage.sems[0].at[side, chunk],
            recv_sem=stage.sems[1].at[side, chunk],
            device_id=(row, target),
            device_id_type=MESH,
        )

    def row_copy(stage, which, side, chunk, target):
        rows = rows_of(side, chunk)
        return pltpu.make_async_remote_copy(
            src_ref=stage.outs[which].at[rows],
            dst_ref=stage.outs[which].at[rows],
            send_sem=stage.sems[2].at[which, side, chunk],
            recv_sem=stage.sems[3].at[which, side, chunk],
            device_id=(row, target),
            device_id_type=MESH,
        )

    def side_facts(side):
        if side == 0:
            return place, place + 1, place - 1
        return end - place, place - 1, place + 1

    def bring_back(stage, since):
        for side in range(2):
            at, onward, back = side_facts(side)
            chunk = since - lag * end - lag * (end - at)

            @pl.when((at < end) & (chunk >= 0) & (chunk < chunks))
            def _():
                for which in range(len(stage.outs)):
                    row_copy(stage, which, side, chunk, back).wait_recv()

                    @pl.when(at > 0)
                    def _():
                        row_copy(stage, which, side, chunk, back).start()

    def sum_up(stage, since):
        for side in range(2):
            at, onward, back = side_facts(side)
            chunk = since - lag * at

            @pl.when((chunk >= 0) & (chunk < chunks))
            def _():
                @pl.when(at > 0)
                def _():
                    sum_copy(stage, side, chunk, onward).wait_recv()

                @pl.when(at < end)
                def _():
                    @pl.when(at > 0)
                    def _():
                        rows = rows_of(side, chunk)
                        stage.part[rows] = stage.part[rows] + stage.recv[rows]

                    sum_copy(stage, side, chunk, onward).start()

                @pl.when(at == end)
                def _():
                    rows = rows_of(side, chunk)
                    own = pl.ds(pl.multiple_of(chunk * CHUNK, CHUNK), CHUNK)
                    rest = stage.finish(rows, own, stage.part[rows].astype(F32) + stage.recv[rows].astype(F32))
                    for which in range(len(stage.outs)):
                        row_copy(stage, which, side, chunk, back).start()
                    rest()

    def step(now, carry):
        for number, stage in enumerate(stages):
            bring_back(stage, now - number * span)
        for number, stage in enumerate(stages):
            since = now - number * span

            @pl.when((since >= 0) & (since < chunks))
            def _():
                stage.produce([rows_of(side, since) for side in range(2)])

            sum_up(stage, since)
        for first, count, work in extras:

            @pl.when((now >= first) & (now < first + count))
            def _():
                work(now - first)

        return carry

    lax.fori_loop(0, chunks + span * len(stages), step, 0)

    def drain(chunk, carry):
        for stage in stages:
            for side in range(2):
                at, onward, back = side_facts(side)

                @pl.when(at < end)
                def _():
                    sum_copy(stage, side, chunk, onward).wait_send()

                @pl.when(at > 0)
                def _():
                    for which in range(len(stage.outs)):
                        row_copy(stage, which, side, chunk, back).wait_send()

        return carry

    lax.fori_loop(0, chunks, drain, 0)


def chunk_rows(half, chunk):
    return [pl.ds(pl.multiple_of(side * half + chunk * CHUNK, CHUNK), CHUNK) for side in range(2)]


def by_rows(count, work, block=32):
    def one(index, carry):
        work(pl.ds(pl.multiple_of(index * block, block), block), index * block)
        return carry

    block = min(block, count)
    lax.fori_loop(0, count // block, one, 0)


class Spread:
    def __init__(self, chips, grads, scratch):
        self.chips, self.grads = chips, grads
        self.half = grads.shape[0] // 2
        self.near, self.far, self.near_sems, self.far_sems, self.free = scratch
        row, place = here()
        self.core, self.chip, self.place = lax.rem(row, 2), row // 2, place

    @staticmethod
    def scratch(chips, rows, width):
        half = rows // 2
        far = half * 3 // 4 if chips == 4 else half // chips * (chips - 1)
        copies = 8 if chips == 4 else 2 * (chips - 1)
        sems = [
            pltpu.SemaphoreType.DMA((4,)),
            pltpu.SemaphoreType.DMA((2, copies)),
            pltpu.SemaphoreType.REGULAR,
        ]
        return [pltpu.VMEM((half, width), LOW), pltpu.VMEM((far, width), LOW), *sems, *sems]

    def rows(self, first, count):
        return pl.ds(pl.multiple_of(first, 16), count)

    def core_copy(self, source, target, number):
        return pltpu.make_async_remote_copy(
            src_ref=source,
            dst_ref=target,
            send_sem=self.near_sems.at[2 * number],
            recv_sem=self.near_sems.at[2 * number + 1],
            device_id=partner(),
            device_id_type=MESH,
        )

    def near_copy(self):
        other = self.rows((1 - self.core) * self.half, self.half)
        return self.core_copy(self.grads.at[other], self.near, 0)

    def last_copy(self):
        own = self.grads.at[self.rows(self.core * self.half, self.half)]
        return self.core_copy(own, own, 1)

    def chip_copy(self, source, target, number, chip):
        return pltpu.make_async_remote_copy(
            src_ref=source,
            dst_ref=target,
            send_sem=self.far_sems.at[0, number],
            recv_sem=self.far_sems.at[1, number],
            device_id=(chip * 2 + self.core, self.place),
            device_id_type=MESH,
        )

    def to_partner(self):
        self.near_copy().start()

    def add_partner(self):
        self.near_copy().wait_send()
        pl.semaphore_signal(self.free, inc=1, device_id=partner(), device_id_type=MESH)
        self.near_copy().wait_recv()
        base = self.core * self.half

        def add(rows, first):
            own = self.grads[self.rows(base + first, rows.size)]
            self.near[rows] = self.near[rows] + own

        by_rows(self.half, add)

    def settle_sum(self):
        self.settle_there()
        pl.semaphore_wait(self.free, 1)

    def give_share(self):
        self.sum_share(self.grads, self.own_rows())
        self.start_back()

    def keep_share(self, share):
        count = share.shape[0] // len(self.own_rows())
        for number, base in enumerate(self.own_rows()):

            def keep(rows, first, number=number, base=base):
                came = share[self.rows(number * count + first, rows.size)]
                self.grads[self.rows(base + first, rows.size)] = came

            by_rows(count, keep)
        self.summed = False
        self.start_back()

    summed = True

    def to_other_core(self):
        self.take_back()
        if self.summed:
            self.settle_sum()
        self.settle_back()
        self.last_copy().start()

    def settle(self):
        self.last_copy().wait_recv()
        self.last_copy().wait_send()


class DirectSpread(Spread):
    def each(self, work):
        def one(index, carry):
            work(index)
            return carry

        lax.fori_loop(0, self.chips - 1, one, 0)

    def peer(self, index):
        return lax.rem(self.chip + index + 1, self.chips)

    def far_copy(self, index):
        count = self.half // self.chips
        chip = self.peer(index)
        source = self.near.at[self.rows(chip * count, count)]
        return self.chip_copy(source, self.far.at[self.rows(index * count, count)], index, chip)

    def back_copy(self, index):
        count = self.half // self.chips
        share = self.grads.at[self.rows(self.core * self.half + self.chip * count, count)]
        return self.chip_copy(share, share, self.chips - 1 + index, self.peer(index))

    def to_chips(self):
        self.add_partner()
        self.each(lambda index: self.far_copy(index).start())

    def onward(self):
        pass

    def own_rows(self):
        return [self.core * self.half + self.chip * (self.half // self.chips)]

    def sum_share(self, target, starts):
        self.each(lambda index: self.far_copy(index).wait_recv())
        count = self.half // self.chips
        base = self.chip * count

        def add(rows, first):
            def one(index, total):
                return total + self.far[self.rows(index * count + first, rows.size)].astype(F32)

            own = self.near[self.rows(base + first, rows.size)].astype(F32)
            total = lax.fori_loop(0, self.chips - 1, one, own)
            target[self.rows(starts[0] + first, rows.size)] = total.astype(LOW)

        by_rows(count, add)

    def start_back(self):
        self.each(lambda index: self.back_copy(index).start())

    def pass_on(self):
        pass

    def take_back(self):
        self.each(lambda index: self.back_copy(index).wait_recv())

    def settle_there(self):
        self.each(lambda index: self.far_copy(index).wait_send())

    def settle_back(self):
        self.each(lambda index: self.back_copy(index).wait_send())


class SquareSpread(Spread):
    def __init__(self, chips, grads, scratch):
        super().__init__(chips, grads, scratch)
        quarter = self.half // 4
        eighth = self.half // 8
        first, second = lax.rem(self.chip, 2), self.chip // 2
        along = self.chip + 1 - 2 * first
        across = self.chip + 2 - 4 * second
        self.quarter, self.eighth = quarter, eighth
        self.chips_of = ((along, across), (across, along))
        self.bits = ((first, second), (second, first))
        self.part = [side * 2 * quarter for side in range(2)]
        self.kept = [self.part[side] + self.bits[side][0] * quarter for side in range(2)]
        self.own = [self.kept[side] + self.bits[side][1] * eighth for side in range(2)]

    def first_copy(self, side):
        sent = self.part[side] + (1 - self.bits[side][0]) * self.quarter
        room = self.far.at[pl.ds(side * self.quarter, self.quarter)]
        source = self.near.at[self.rows(sent, self.quarter)]
        return self.chip_copy(source, room, side, self.chips_of[side][0])

    def second_copy(self, side):
        sent = self.kept[side] + (1 - self.bits[side][1]) * self.eighth
        room = self.far.at[pl.ds(2 * self.quarter + side * self.eighth, self.eighth)]
        source = self.near.at[self.rows(sent, self.eighth)]
        return self.chip_copy(source, room, 2 + side, self.chips_of[side][1])

    def share_copy(self, side):
        share = self.grads.at[self.rows(self.core * self.half + self.own[side], self.eighth)]
        return self.chip_copy(share, share, 4 + side, self.chips_of[side][1])

    def pass_copy(self, side):
        share = self.grads.at[self.rows(self.core * self.half + self.kept[side], self.quarter)]
        return self.chip_copy(share, share, 6 + side, self.chips_of[side][0])

    def to_chips(self):
        self.add_partner()
        for side in range(2):
            self.first_copy(side).start()

    def onward(self):
        for side in range(2):
            self.first_copy(side).wait_recv()
            base = self.kept[side]

            def add(rows, first, side=side, base=base):
                at = self.rows(base + first, rows.size)
                came = self.far[self.rows(side * self.quarter + first, rows.size)]
                self.near[at] = self.near[at] + came

            by_rows(self.quarter, add)
            self.second_copy(side).start()

    def own_rows(self):
        return [self.core * self.half + self.own[side] for side in range(2)]

    def sum_share(self, target, starts):
        for side in range(2):
            self.second_copy(side).wait_recv()
            base, start = self.own[side], starts[side]

            def add(rows, first, side=side, base=base, start=start):
                came = self.far[self.rows(2 * self.quarter + side * self.eighth + first, rows.size)]
                own = self.near[self.rows(base + first, rows.size)]
                target[self.rows(start + first, rows.size)] = own + came

            by_rows(self.eighth, add)

    def start_back(self):
        for side in range(2):
            self.share_copy(side).start()

    def pass_on(self):
        for side in range(2):
            self.share_copy(side).wait_recv()
            self.pass_copy(side).start()

    def take_back(self):
        for side in range(2):
            self.pass_copy(side).wait_recv()

    def settle_there(self):
        for side in range(2):
            self.first_copy(side).wait_send()
            self.second_copy(side).wait_send()

    def settle_back(self):
        for side in range(2):
            self.share_copy(side).wait_send()
            self.pass_copy(side).wait_send()


def spread_of(chips, grads, scratch):
    return (SquareSpread if chips == 4 else DirectSpread)(chips, grads, scratch)


def normalize(residual):
    centred = residual - jnp.mean(residual, axis=-1, keepdims=True)
    inverse = lax.rsqrt(jnp.mean(centred * centred, axis=-1, keepdims=True) + norm_eps)
    return centred * inverse, inverse


def norm_back(grad, gain, unit, inverse):
    scaled = grad * gain
    return (
        scaled
        - jnp.mean(scaled, axis=-1, keepdims=True)
        - unit * jnp.mean(scaled * unit, axis=-1, keepdims=True)
    ) * inverse


def tally(total, values):
    total[...] += jnp.sum(values.reshape(-1, 8, values.shape[-1]), axis=0)


class Layer:
    def __init__(self, array, layer):
        self.array, self.layer = array, layer

    def room(self):
        return self.array.shape if self.layer is None else self.array.shape[1:]


def whole(array):
    return Layer(array, None)


def view(refs, suffix):
    named = dict(vars(refs))
    for name, ref in vars(refs).items():
        if name.endswith(suffix):
            named[name[: -len(suffix)]] = ref
    return types.SimpleNamespace(**named)


def call(collective, body, ins, outs, scratch, into=types.MappingProxyType({}), later=(), sent=()):
    vmem = pl.BlockSpec(memory_space=pltpu.VMEM)
    names = [*ins, *outs]
    fetched = {name: value for name, value in ins.items() if isinstance(value, Layer)}
    inside = {name: value for name, value in fetched.items() if name not in into}
    extra = {name: spec if isinstance(spec, list) else [spec] for name, spec in scratch.items()}

    def run(*refs):
        named = dict(zip(names, refs))
        rest = list(refs[len(names) :])
        copies, leaving = {}, {}
        arrivals, departures = rest.pop(0), rest.pop(0)
        for number, name in enumerate(sent):
            room = rest.pop(0)
            leaving[name] = pltpu.make_async_copy(room, named[name], departures.at[number])
            named[name] = room
        for number, (name, value) in enumerate(fetched.items()):
            room = named[into[name]] if name in into else rest.pop(0)
            source = named[name] if value.layer is None else named[name].at[value.layer]
            copies[name] = pltpu.make_async_copy(source, room, arrivals.at[number])
            if name not in later:
                copies[name].start()
            named[name] = room
        for name, specs in extra.items():
            taken = [rest.pop(0) for _ in specs]
            named[name] = taken if isinstance(scratch[name], list) else taken[0]

        def need(*wanted):
            for name in wanted:
                copies[name].wait()

        def fetch(*wanted):
            for name in wanted:
                copies[name].start()

        def send(*wanted):
            for name in wanted:
                leaving[name].start()

        body(types.SimpleNamespace(**named, need=need, fetch=fetch, send=send))
        for copy in leaving.values():
            copy.wait()

    results = pl.pallas_call(
        run,
        out_shape=list(outs.values()),
        in_specs=[pl.BlockSpec(memory_space=pl.ANY) if name in fetched else vmem for name in ins],
        out_specs=[pl.BlockSpec(memory_space=pl.ANY) if name in sent else vmem for name in outs],
        scratch_shapes=[
            pltpu.SemaphoreType.DMA((len(fetched),)),
            pltpu.SemaphoreType.DMA((max(1, len(sent)),)),
            *(pltpu.VMEM(outs[name].shape, outs[name].dtype) for name in sent),
            *(pltpu.VMEM(value.room(), value.array.dtype) for value in inside.values()),
            *(spec for specs in extra.values() for spec in specs),
        ],
        compiler_params=pltpu.CompilerParams(
            collective_id=collective, has_side_effects=True, vmem_limit_bytes=60 << 20
        ),
    )(*(value.array if isinstance(value, Layer) else value for value in ins.values()))
    return types.SimpleNamespace(**dict(zip(outs, results)))


def shape(*dims, kind=F32):
    return jax.ShapeDtypeStruct(dims, kind)


def line_scratch(rows, width, outs=1):
    chunks = rows // 2 // CHUNK
    return [
        pltpu.VMEM((rows, width), LOW),
        pltpu.VMEM((rows, width), LOW),
        pltpu.SemaphoreType.DMA((2, chunks)),
        pltpu.SemaphoreType.DMA((2, chunks)),
        pltpu.SemaphoreType.DMA((outs, 2, chunks)),
        pltpu.SemaphoreType.DMA((outs, 2, chunks)),
    ]


def stage_of(produce, finish, outs, scratch):
    part, recv, *sems = scratch
    return types.SimpleNamespace(
        produce=produce, finish=finish, outs=outs, part=part, recv=recv, sems=sems
    )


def clear(*refs):
    for ref in refs:
        ref[...] = jnp.zeros_like(ref)


def vector(ref, layer):
    return ref[...].astype(F32)[layer : layer + 1]


def head_lanes(values, head):
    lane = lax.broadcasted_iota(jnp.int32, values.shape, 1)
    return jnp.where(lane // HEAD == head, values, jnp.zeros_like(values))


def turned(values):
    return jnp.transpose(values.astype(F32)).astype(LOW)


def mark_segments(r):
    length = r.seg_row.shape[1]
    wide = jnp.broadcast_to(r.seg_row[...].astype(F32), (QUERIES, length))
    r.seg_cols[...] = jnp.transpose(wide)


def masked_block(r, keys, queries, at):
    same = r.seg_cols[...] == r.seg_row[:, at].astype(F32)
    return jnp.where(same, dot_t(keys, queries) * HEAD ** (-0.5), masked_value)


def project(r, layer, blocks):
    bias = r.qv_bias[layer].astype(F32)
    taken = take(r.low_in, blocks)
    for member in range(3):
        rows = dot(taken, r.qkv_w[member])
        if member != 1:
            rows += bias[member // 2 : member // 2 + 1]
        put(r.projected.at[member], blocks, rows.astype(LOW))


def attend(r, block):
    at = pl.ds(pl.multiple_of(block * QUERIES, QUERIES), QUERIES)
    queries = r.projected[0, at]
    heads = queries.shape[1] // HEAD
    parts = []
    for head in range(heads):
        scores = masked_block(r, r.projected[1], head_lanes(queries, head), at)
        row_max = jnp.max(scores, axis=0, keepdims=True)
        exponent = jnp.exp(scores - row_max)
        row_total = jnp.sum(exponent, axis=0, keepdims=True)
        r.log_total[head : head + 1, at] = row_max + jnp.log(row_total)
        probs = (exponent * (1.0 / row_total)).astype(LOW)
        parts.append(dot(r.turned_rows[head * HEAD : (head + 1) * HEAD], probs))
    r.context[at] = jnp.transpose(jnp.concatenate(parts, axis=0)).astype(LOW)


def attend_first(r, half):
    per_side = half // QUERIES
    r.turned_rows[...] = turned(r.projected[2])
    for side in range(2):
        attend(r, side * per_side)
    extras = []
    for block in range(1, per_side):
        for side in range(2):
            step = max(0, block * QUERIES // CHUNK - 2 + side)
            extras.append(at_step(step, lambda block=side * per_side + block: attend(r, block)))
    return extras


def context_back(r, blocks):
    put(r.grad_context, blocks, dot_t(take(r.attn_low_in, blocks), r.proj_w[...]).astype(LOW))


def attend_back(r, between=()):
    rows = r.attn_low_in.shape[0]
    heads = r.qkv_w.shape[2] // HEAD
    scale = HEAD ** (-0.5)
    r.turned_rows[...] = turned(r.projected[1])
    clear(r.grad_key, r.grad_value)
    for number in range(rows // QUERIES):
        at = slice(number * QUERIES, (number + 1) * QUERIES)
        queries, context_rows = r.projected[0, at], r.grad_context[at]
        parts = []
        for head in range(heads):
            to = slice(head * QUERIES, (head + 1) * QUERIES)
            r.head_queries[to] = head_lanes(queries, head)
            r.head_context[to] = head_lanes(context_rows, head)
            scores = masked_block(r, r.projected[1], r.head_queries[to], at)
            probability = jnp.exp(scores - r.log_total[head : head + 1, at])
            grad_probs = dot_t(r.projected[2], r.head_context[to])
            inner = jnp.sum(probability * grad_probs, axis=0, keepdims=True)
            grad_scores = (probability * (grad_probs - inner)).astype(LOW)
            r.score_rows[:, to] = grad_scores
            r.prob_rows[:, to] = probability.astype(LOW)
            parts.append(dot(r.turned_rows[head * HEAD : (head + 1) * HEAD], grad_scores))
        r.grad_key[...] += dot(r.score_rows[...], r.head_queries[...])
        r.grad_value[...] += dot(r.prob_rows[...], r.head_context[...])
        r.grad_proj[0, at] = (jnp.transpose(jnp.concatenate(parts, axis=0)) * scale).astype(LOW)
        if number < len(between):
            between[number]()
    r.grad_proj[1] = (r.grad_key[...] * scale).astype(LOW)
    r.grad_proj[2] = r.grad_value[...].astype(LOW)
    for slot, member in ((0, 0), (1, 2)):
        r.qv_sum[slot] = jnp.sum(r.grad_proj[member].astype(F32).reshape(-1, 8, r.qv_sum.shape[2]), axis=0)


def take(ref, blocks):
    return jnp.concatenate([ref[block] for block in blocks], axis=0)


def put(ref, blocks, values):
    count = values.shape[0] // len(blocks)
    for number, block in enumerate(blocks):
        ref[block] = values[number * count : (number + 1) * count]


def proj_stage(r, layer, whole):
    def produce(blocks):
        put(r.proj_line[0], blocks, dot(take(r.context, blocks), r.proj_w[...]).astype(LOW))

    def finish(at, own, total):
        came = r.residual[at if whole else own].astype(F32)
        unit, inverse = normalize(came + total + vector(r.proj_b, layer))
        result = unit * vector(r.first_gain, layer) + vector(r.first_shift, layer)
        r.normed_low[at] = result.astype(LOW)

        def rest():
            r.unit_one[own] = unit
            r.inverse_one[own] = inverse
            r.normed[own] = result

        return rest

    return stage_of(produce, finish, [r.normed_low], r.proj_line)


def ffn_stage(r, layer, last):
    def produce(blocks):
        pre = dot(take(r.normed_low, blocks), r.up_w[...]) + vector(r.up_b, layer)
        cdf = 0.5 * lax.erf(pre * math.sqrt(0.5)) + 0.5
        act = (pre * cdf).astype(LOW)
        slope = cdf + pre * jnp.exp(-0.5 * pre * pre) * (1.0 / math.sqrt(2 * math.pi))
        put(r.slope, blocks, slope.astype(LOW))
        put(r.act, blocks, act)
        put(r.ffn_line[0], blocks, dot(act, r.down_w[...]).astype(LOW))

    def finish(at, own, total):
        unit, inverse = normalize(r.normed[own] + total + vector(r.down_b, layer))
        gain = vector(r.second_gain, layer)
        result = unit * gain + vector(r.second_shift, layer)
        if last:
            grad_in = r.cotangent[at].astype(F32)
            grad = norm_back(grad_in, gain, unit, inverse)
            r.branch[at] = grad.astype(LOW)
        else:
            r.low[at] = result.astype(LOW)

        def rest():
            if last:
                r.mixed_own[own] = result.astype(LOW)
                r.grad_second[own] = grad
                tally(r.sums.at[0], grad_in * unit)
                tally(r.sums.at[1], grad_in)
                tally(r.sums.at[2], grad.astype(LOW).astype(F32))
            else:
                r.unit_two[own] = unit
                r.inverse_two[own] = inverse
                r.hidden[own] = result

        return rest

    return stage_of(produce, finish, [r.branch if last else r.low], r.ffn_line)


def ffn_back_stage(r, layer):
    def produce(blocks):
        grad = dot_t(take(r.branch, blocks), r.down_w[...])
        pre = (grad * take(r.slope, blocks).astype(F32)).astype(LOW)
        put(r.pre, blocks, pre)
        tally(r.up_sum, pre.astype(F32))
        put(r.back_line[0], blocks, dot_t(pre, r.up_w[...]).astype(LOW))

    def finish(at, own, total):
        grad_in = r.grad_second[own] + total
        unit = r.unit_one[own]
        grad = norm_back(grad_in, vector(r.first_gain, layer), unit, r.inverse_one[own])
        r.attn_low[at] = grad.astype(LOW)

        def rest():
            r.grad_first[own] = grad
            tally(r.sums.at[3], grad_in * unit)
            tally(r.sums.at[4], grad_in)
            tally(r.sums.at[5], grad.astype(LOW).astype(F32))

        return rest

    return stage_of(produce, finish, [r.attn_low], r.back_line)


def qkv_back_stage(r, layer, inner):
    def produce(blocks):
        total = sum(dot_t(take(r.grad_proj.at[member], blocks), r.qkv_w[member]) for member in range(3))
        put(r.qkv_line[0], blocks, total.astype(LOW))

    def finish(at, own, total):
        grad_in = r.grad_first_in[own] + total
        if not inner:
            r.grad_low[at] = grad_in.astype(LOW)
            return lambda: None
        unit = r.unit_two[own]
        grad = norm_back(grad_in, vector(r.second_gain, layer), unit, r.inverse_two[own])
        r.branch[at] = grad.astype(LOW)

        def rest():
            r.grad_second[own] = grad
            tally(r.sums.at[0], grad_in * unit)
            tally(r.sums.at[1], grad_in)
            tally(r.sums.at[2], grad.astype(LOW).astype(F32))

        return rest

    return stage_of(produce, finish, [r.branch] if inner else [r.grad_low], r.qkv_line)


def columns(piece):
    return pl.ds(pl.multiple_of(piece * PIECE, PIECE), PIECE)


def ffn_grads(r, out, first):
    width, hidden = r.up_w.shape

    def up(piece):
        rows = pl.ds(pl.multiple_of(piece * PIECE, PIECE), PIECE)
        out[rows] = dot_tn(r.normed_low[:, columns(piece)], r.pre[...]).astype(LOW)

    def down(piece):
        rows = pl.ds(pl.multiple_of(width + piece * PIECE, PIECE), PIECE)
        out[rows] = dot_tn(r.act[:, columns(piece)], r.branch[...]).astype(LOW)

    def all_of(pieces, work):
        lax.fori_loop(0, pieces, lambda piece, carry: (work(piece), carry)[1], 0)

    return [
        at_step(first, lambda: all_of(width // PIECE, up)),
        at_step(first + 1, lambda: all_of(hidden // PIECE, down)),
    ]


def attn_grads(r, out, first):
    width, part = r.low_in.shape[1], r.context_in.shape[1]

    def piece_of(piece):
        for member in range(3):
            rows = pl.ds(pl.multiple_of(member * width + piece * part, part), part)
            taken = r.low_in[:, pl.ds(pl.multiple_of(piece * part, part), part)]
            out[rows] = dot_tn(taken, r.grad_proj[member]).astype(LOW)
        rows = pl.ds(pl.multiple_of(3 * width + piece * part, part), part)
        taken = r.attn_low_in[:, pl.ds(pl.multiple_of(piece * part, part), part)]
        out[rows] = dot_tn(r.context_in[...], taken).astype(LOW)

    def all_pieces():
        lax.fori_loop(0, width // part, lambda piece, carry: (piece_of(piece), carry)[1], 0)

    return [at_step(first, all_pieces)]


def at_step(step, work):
    return (step, 1, lambda index: work())


def with_suffix(suffix, named):
    return {name + suffix: value for name, value in named.items()}


def kept_attention(rows, part):
    return dict(
        projected=shape(3, rows, part, kind=LOW),
        log_total=shape(part // HEAD, rows),
        context=shape(rows, part, kind=LOW),
    )


def forward_kernel(size, chips, collective, ins):
    rows, width = ins["low_in_0"].shape
    part, hidden = ins["proj_w_0"].array.shape[1], ins["up_w_0"].array.shape[2]
    half = rows // 2
    chunks = half // CHUNK

    def body(r):
        wait = greet(size, targets=[(1, lambda index: partner()), (chips - 1, lambda index: plane_peer(chips, index))])
        ffn_sum = spread_of(chips, r.ffn_grad, r.ffn_spread[:5])
        clear(r.sums, r.up_sum)
        mark_segments(r)
        below, above = view(r, "_0"), view(r, "_1")
        below.residual = r.low_in_0
        above.low_in, above.residual = r.low_0, r.hidden_0
        r.need("qkv_w_0")
        project(below, 0, [slice(0, rows)])
        extras = attend_first(below, half)
        r.need("proj_w_0", "up_w_0", "down_w_0", "qkv_w_1")
        wait()

        def project_chunk(chunk):
            project(above, 1, chunk_rows(half, chunk))

        extras.append((4 * 3 * (size - 1), chunks, project_chunk))
        line_loop(size, [proj_stage(below, 0, True), ffn_stage(below, 0, False)], extras, 3)
        r.send("projected_0", "context_0", "unit_one_0", "normed_low_0", "act_0", "slope_0", "unit_two_0", "low_0")
        extras = attend_first(above, half)
        r.need("proj_w_1", "up_w_1", "down_w_1")
        stages = [proj_stage(above, 1, False), ffn_stage(above, 1, True), ffn_back_stage(above, 1)]
        first = 4 * 3 * (size - 1) + chunks
        line_loop(
            size,
            stages,
            [
                *extras,
                at_step(2 * chunks, lambda: r.send("projected_1", "context_1")),
                *ffn_grads(above, r.ffn_grad, first),
                at_step(first + 2, lambda: (ffn_sum.to_partner(), r.send("mixed_own"))),
                at_step(first + 5, ffn_sum.to_chips),
                at_step(first + 15, ffn_sum.onward),
            ],
            3,
        )
        r.send("grad_first", "attn_low")
        share = r.ffn_share.shape[0]
        ffn_sum.sum_share(r.ffn_share, [0, share // 2])
        ffn_sum.settle_sum()

    outs = dict(
        **with_suffix("_0", kept_attention(rows, part)),
        **with_suffix("_1", kept_attention(rows, part)),
        unit_one_0=shape(half, width),
        inverse_one_0=shape(half, 1),
        normed_low_0=shape(rows, width, kind=LOW),
        act_0=shape(rows, hidden, kind=LOW),
        slope_0=shape(rows, hidden, kind=LOW),
        unit_two_0=shape(half, width),
        inverse_two_0=shape(half, 1),
        low_0=shape(rows, width, kind=LOW),
        mixed_own=shape(half, width, kind=LOW),
        grad_first=shape(half, width),
        attn_low=shape(rows, width, kind=LOW),
        ffn_share=shape((width + hidden) // 2 // chips, width, kind=LOW),
        up_sum=shape(8, hidden),
        sums=shape(6, 8, width),
    )
    scratch = dict(
        hidden_0=pltpu.VMEM((half, width), F32),
        normed=pltpu.VMEM((half, width), F32),
        turned_rows=pltpu.VMEM((part, rows), LOW),
        seg_cols=pltpu.VMEM((rows, QUERIES), F32),
        unit_one_1=pltpu.VMEM((half, width), F32),
        inverse_one_1=pltpu.VMEM((half, 1), F32),
        normed_low_1=pltpu.VMEM((rows, width), LOW),
        act_1=pltpu.VMEM((rows, hidden), LOW),
        slope_1=pltpu.VMEM((rows, hidden), LOW),
        pre=pltpu.VMEM((rows, hidden), LOW),
        branch=pltpu.VMEM((rows, width), LOW),
        grad_second=pltpu.VMEM((half, width), F32),
        proj_line_0=line_scratch(rows, width),
        ffn_line_0=line_scratch(rows, width),
        proj_line_1=line_scratch(rows, width),
        ffn_line_1=line_scratch(rows, width),
        back_line=line_scratch(rows, width),
        ffn_grad=pltpu.VMEM((width + hidden, width), LOW),
        ffn_spread=Spread.scratch(chips, width + hidden, width),
    )
    sent = [name for name, out in outs.items() if out.dtype == LOW and name != "ffn_share" or name in ("unit_one_0", "unit_two_0", "grad_first")]
    return call(collective, body, ins, outs, scratch, sent=sent)


def backward_kernel(size, chips, collective, layers, ins):
    rows, width = ins["attn_low_1"].array.shape
    part, hidden = ins["proj_w_0"].array.shape[1], ins["up_w"].array.shape[2]
    half = rows // 2
    chunks = half // CHUNK
    span = 2 * LAG * (size - 1)
    ffn_rows, attn_rows = width + hidden, 4 * width
    own_rows = layers * (2 * part + hidden) // width
    count = -(-(own_rows + 6 * layers) // 8) * 8
    teams = 2 * chips

    def row_peer(index):
        row, place = here()
        return (lax.rem(row + index + 1, teams), place)

    def line_peer(index):
        row, place = here()
        return (row, lax.rem(place + index + 1, size))

    def each(number, work):
        def one(index, carry):
            work(index)
            return carry

        lax.fori_loop(0, number, one, 0)

    def body(r):
        row, place = here()
        clear(r.ends, r.sums_0, r.up_sum_0)
        wait = greet(size, line=False, targets=[(teams - 1, row_peer), (size - 1, line_peer)])
        ffn_above = spread_of(chips, r.ffn_whole_1, r.ffn_spread[:5])
        attn_above = spread_of(chips, r.attn_whole_1, r.attn_spread[:5])
        ffn_below = spread_of(chips, r.ffn_whole_0, r.ffn_spread[:2] + r.ffn_spread[5:])
        attn_below = spread_of(chips, r.attn_whole_0, r.attn_spread[:2] + r.attn_spread[5:])
        above, below = view(r, "_1"), view(r, "_0")
        above.grad_first_in, above.attn_low_in = r.grad_first_1, r.attn_low_1
        below.grad_first_in, below.attn_low_in = r.grad_first_0, r.attn_low_0
        middle = types.SimpleNamespace(
            **{**vars(r), "sums": r.sums_0, "up_sum": r.up_sum_0, "grad_first": r.grad_first_0, "attn_low": r.attn_low_0}
        )
        above.sums = r.sums_0
        above.grad_second = middle.grad_second = r.grad_first_0
        below.qkv_line = [*r.qkv_line_1[:2], *r.qkv_sems_0]

        def end_copy(slot, index):
            return pltpu.make_async_remote_copy(
                src_ref=r.small,
                dst_ref=r.ends.at[slot],
                send_sem=r.end_sent.at[slot, index],
                recv_sem=r.end_got.at[slot],
                device_id=line_peer(index),
                device_id_type=MESH,
            )

        def team_copy(index, slot):
            return pltpu.make_async_remote_copy(
                src_ref=r.mine,
                dst_ref=r.others.at[slot],
                send_sem=r.team_sent.at[index],
                recv_sem=r.team_got.at[slot],
                device_id=row_peer(index),
                device_id_type=MESH,
            )

        end_places = ((0, 0), (1, size - 1))
        end = size - 1

        def side_rows(side):
            at, back = (place, place - 1) if side == 0 else (end - place, place + 1)
            return at, back, r.mixed.at[pl.ds(side * half, half)]

        def mixed_copy(side):
            at, back, rows_at = side_rows(side)
            return pltpu.make_async_remote_copy(
                src_ref=rows_at,
                dst_ref=rows_at,
                send_sem=r.mixed_sent.at[side],
                recv_sem=r.mixed_got.at[side],
                device_id=(row, back),
                device_id_type=MESH,
            )

        def mixed_hop(number):
            for side in range(2):
                at, _, rows_at = side_rows(side)

                @pl.when(at == end - number)
                def _():
                    if number:
                        mixed_copy(side).wait_recv()
                    else:
                        rows_at[...] = r.mixed_own[...]
                    mixed_copy(side).start()

        def mixed_settle():
            for side in range(2):
                at, _, _ = side_rows(side)

                @pl.when(at == 0)
                def _():
                    mixed_copy(side).wait_recv()

                @pl.when(at > 0)
                def _():
                    mixed_copy(side).wait_send()

        def small_to_line():
            named = vars(r)
            clear(r.small)
            lines = []
            for layer in range(layers):
                sums = jnp.sum(named["qv_sum_%d" % layer][...], axis=1)
                lines += [sums[0:1], sums[1:2]]
            for layer in range(layers):
                lines += [jnp.sum(named["up_sum_%d" % layer][...], axis=0, keepdims=True)]
            flat = jnp.concatenate(lines, axis=1)
            for number in range(own_rows):
                r.small[number : number + 1] = flat[:, number * width : (number + 1) * width]
            for layer in range(layers):
                sums = jnp.sum(named["sums_%d" % layer][...], axis=1)
                for member in range(6):
                    to = own_rows + member * layers + layer
                    r.small[to : to + 1] = sums[member : member + 1]
            for slot, end in end_places:

                @pl.when(place == end)
                def _():
                    each(size - 1, lambda index: end_copy(slot, index).start())

        def small_to_teams():
            for slot, end in end_places:

                @pl.when(place != end)
                def _():
                    end_copy(slot, 0).wait_recv()

            line_total = r.small[...] + r.ends[0] + r.ends[1]
            number = lax.broadcasted_iota(jnp.int32, (count, width), 0)
            r.mine[...] = jnp.where(number < own_rows, r.small[...], line_total)
            each(teams - 1, lambda index: team_copy(index, row).start())
            r.others[row] = r.mine[...]

        def small_finish():
            each(teams - 1, lambda index: team_copy(index, row_peer(index)[0]).wait_recv())
            r.small_total[...] = lax.fori_loop(
                1, teams, lambda index, total: total + r.others[index], r.others[0]
            )
            each(teams - 1, lambda index: team_copy(index, row).wait_send())
            for slot, end in end_places:

                @pl.when(place == end)
                def _():
                    each(size - 1, lambda index: end_copy(slot, index).wait_send())

        mark_segments(r)
        r.need("proj_w_1", "attn_low_1", "projected_1", "mixed_own")
        wait()
        ffn_above.keep_share(r.ffn_share_1)
        mixed_hop(0)
        context_back(above, [slice(0, rows)])
        attend_back(above)
        r.need("qkv_w_1", "grad_first_1", "unit_two", "context_in_1", "low_in_1")
        r.need("up_w", "down_w", "slope", "unit_one", "act", "normed_low")
        extras = [
            *attn_grads(above, r.attn_whole_1, 2),
            at_step(span, lambda: r.fetch("proj_w_0", "qkv_w_0")),
            *ffn_grads(middle, r.ffn_whole_0, 6 * (size - 1) + chunks),
            at_step(3, ffn_above.pass_on),
            at_step(5, attn_above.to_partner),
            at_step(8, attn_above.to_chips),
            at_step(12, ffn_above.to_other_core),
            at_step(15, attn_above.onward),
            at_step(16, lambda: (ffn_above.settle(), r.send("ffn_whole_1"))),
            at_step(6 * (size - 1) + 1, attn_above.give_share),
            at_step(6 * (size - 1) + 5, attn_above.pass_on),
            at_step(6 * (size - 1) + 10, attn_above.to_other_core),
            at_step(6 * (size - 1) + 11, ffn_below.to_partner),
            at_step(6 * (size - 1) + 13, lambda: (attn_above.settle(), r.send("attn_whole_1"))),
            at_step(6 * (size - 1) + 14, ffn_below.to_chips),
            at_step(12 * (size - 1) + 6, ffn_below.onward),
        ]
        extras += [
            at_step(12 * (size - 1), lambda: r.need("proj_w_0")),
            (12 * (size - 1), chunks, lambda chunk: context_back(below, chunk_rows(half, chunk))),
        ]
        stages = [qkv_back_stage(above, 0, True), ffn_back_stage(middle, 0)]
        line_loop(size, stages, extras, 3)
        r.need("qkv_w_0", "projected_0")
        mixed_hop(1)
        attend_back(below)
        ffn_below.give_share()
        r.need("context_in_0", "low_in_0")
        extras = [
            *attn_grads(below, r.attn_whole_0, 0),
            at_step(1, attn_below.to_partner),
            at_step(2, small_to_line),
            at_step(4, ffn_below.pass_on),
            at_step(4, attn_below.to_chips),
            *(at_step(5 + 6 * (hop - 2), lambda hop=hop: mixed_hop(hop)) for hop in range(2, end)),
            at_step(9, small_to_teams),
            at_step(11, attn_below.onward),
            at_step(12, ffn_below.to_other_core),
            at_step(14, lambda: (ffn_below.settle(), r.send("ffn_whole_0"))),
            at_step(15, attn_below.give_share),
            at_step(18, attn_below.pass_on),
            at_step(19, small_finish),
            at_step(23, attn_below.to_other_core),
        ]
        line_loop(size, [qkv_back_stage(below, 0, False)], extras, 3)
        mixed_settle()
        r.send("grad_low", "mixed")
        attn_below.settle()
        r.send("attn_whole_0")

    heads = part // HEAD
    rooms = {"qkv_w_0": "qkv_w_1", "proj_w_0": "proj_w_1"}
    outs = dict(
        grad_low=shape(rows, width, kind=LOW),
        mixed=shape(rows, width, kind=LOW),
        ffn_whole_1=shape(ffn_rows, width, kind=LOW),
        attn_whole_1=shape(attn_rows, part, kind=LOW),
        ffn_whole_0=shape(ffn_rows, width, kind=LOW),
        attn_whole_0=shape(attn_rows, part, kind=LOW),
        small_total=shape(count, width),
    )
    scratch = dict(
        seg_cols=pltpu.VMEM((rows, QUERIES), F32),
        turned_rows=pltpu.VMEM((part, rows), LOW),
        grad_context=pltpu.VMEM((rows, part), LOW),
        grad_key=pltpu.VMEM((rows, part), F32),
        grad_value=pltpu.VMEM((rows, part), F32),
        grad_proj=pltpu.VMEM((3, rows, part), LOW),
        head_queries=pltpu.VMEM((heads * QUERIES, part), LOW),
        head_context=pltpu.VMEM((heads * QUERIES, part), LOW),
        score_rows=pltpu.VMEM((rows, heads * QUERIES), LOW),
        prob_rows=pltpu.VMEM((rows, heads * QUERIES), LOW),
        qv_sum_0=pltpu.VMEM((2, 8, part), F32),
        qv_sum_1=pltpu.VMEM((2, 8, part), F32),
        sums_0=pltpu.VMEM((6, 8, width), F32),
        up_sum_0=pltpu.VMEM((8, hidden), F32),
        pre=pltpu.VMEM((rows, hidden), LOW),
        branch=pltpu.VMEM((rows, width), LOW),
        grad_first_0=pltpu.VMEM((half, width), F32),
        attn_low_0=pltpu.VMEM((rows, width), LOW),
        small=pltpu.VMEM((count, width), F32),
        ends=pltpu.VMEM((2, count, width), F32),
        mine=pltpu.VMEM((count, width), F32),
        others=pltpu.VMEM((teams, count, width), F32),
        end_sent=pltpu.SemaphoreType.DMA((2, size - 1)),
        end_got=pltpu.SemaphoreType.DMA((2,)),
        team_sent=pltpu.SemaphoreType.DMA((teams - 1,)),
        team_got=pltpu.SemaphoreType.DMA((teams,)),
        mixed_sent=pltpu.SemaphoreType.DMA((2,)),
        mixed_got=pltpu.SemaphoreType.DMA((2,)),
        qkv_line_1=line_scratch(rows, width),
        back_line=line_scratch(rows, width),
        qkv_sems_0=line_scratch(rows, width)[2:],
        ffn_spread=Spread.scratch(chips, ffn_rows, width),
        attn_spread=Spread.scratch(chips, attn_rows, part),
    )
    return call(collective, body, ins, outs, scratch, rooms, ("qkv_w_0", "proj_w_0"), [*outs][:-1]), own_rows


def assemble(attn_wholes, ffn_wholes, mixed, grad_low, small, own_rows, part):
    layers = len(attn_wholes)
    rows, width = mixed.shape
    hidden = ffn_wholes[0].shape[0] - width
    steps = 2
    cut = width // steps

    def for_layer(number, spec_of):
        def index(layer, step):
            return spec_of(jnp.where(layer == number, step, jnp.where(layer < number, 0, steps - 1)))

        return index

    ins, in_specs = [], []
    for number in range(layers):
        ins += [
            attn_wholes[number].reshape(4, width, part),
            attn_wholes[number].reshape(-1, part, part),
            ffn_wholes[number].reshape(-1, width, width),
        ]
        in_specs += [
            pl.BlockSpec((3, cut, part), for_layer(number, lambda step: (0, step, 0))),
            pl.BlockSpec((width // part, part // steps, part), for_layer(number, lambda step: (3, step, 0))),
            pl.BlockSpec((1 + hidden // width, cut, width), for_layer(number, lambda step: (0, step, 0))),
        ]
    slab = rows // (layers * steps)
    ins += [mixed, grad_low, small]
    row_spec = pl.BlockSpec((slab, width), lambda layer, step: (layer * steps + step, 0))
    in_specs += [row_spec, row_spec, pl.BlockSpec(small.shape, lambda layer, step: (0, 0))]
    def all_of(*dims):
        return pl.BlockSpec(dims, lambda layer, step: (0,) * len(dims))

    out_shape = [
        shape(rows, width),
        shape(rows, width),
        shape(layers, 3, width, part),
        shape(layers, part, width),
        shape(layers, width, hidden),
        shape(layers, hidden, width),
        shape(layers, 2, part),
        shape(layers, hidden),
    ] + [shape(layers, width)] * 6
    out_specs = [
        row_spec,
        row_spec,
        pl.BlockSpec((1, 3, cut, part), lambda layer, step: (layer, 0, step, 0)),
        pl.BlockSpec((1, part // steps, width), lambda layer, step: (layer, step, 0)),
        pl.BlockSpec((1, cut, hidden), lambda layer, step: (layer, step, 0)),
        pl.BlockSpec((1, cut, width), lambda layer, step: (layer, step, 0)),
        all_of(layers, 2, part),
        all_of(layers, hidden),
    ] + [all_of(layers, width)] * 6

    def body(*refs):
        sources = refs[: 3 * layers]
        mixed_in, grad_in, small_in = refs[3 * layers : 3 * layers + 3]
        mixed_out, grad_out, qkv, proj, up, down, qv, up_b, *norms = refs[3 * layers + 3 :]
        mixed_out[...] = mixed_in[...].astype(F32)
        grad_out[...] = grad_in[...].astype(F32)
        for number in range(layers):
            attn_in, proj_in, ffn_in = sources[3 * number : 3 * number + 3]

            @pl.when(pl.program_id(0) == number)
            def _():
                qkv[0] = attn_in[...].astype(F32)
                for block in range(width // part):
                    proj[0, :, block * part : (block + 1) * part] = proj_in[block].astype(F32)
                up[0] = ffn_in[0].astype(F32)
                down[0] = ffn_in[1].astype(F32)

        @pl.when((pl.program_id(0) == 0) & (pl.program_id(1) == 0))
        def _():
            values = small_in[...]
            flat = jnp.concatenate([values[n : n + 1] for n in range(own_rows)], axis=1)
            for layer in range(layers):
                for member in range(2):
                    at = (2 * layer + member) * part
                    qv[layer, member : member + 1] = flat[:, at : at + part]
                at = 2 * layers * part + layer * hidden
                up_b[layer : layer + 1] = flat[:, at : at + hidden]
            for member, norm in enumerate(norms):
                norm[...] = values[own_rows + member * layers : own_rows + (member + 1) * layers]

    return pl.pallas_call(
        body,
        grid=(layers, steps),
        out_shape=out_shape,
        in_specs=in_specs,
        out_specs=out_specs,
        compiler_params=pltpu.CompilerParams(vmem_limit_bytes=60 << 20),
    )(*ins)


def local(
    tokens,
    segment_ids,
    cotangent,
    qkv_weight,
    qv_bias,
    proj_weight,
    proj_bias,
    first_gain,
    first_shift,
    up_weight,
    up_bias,
    down_weight,
    down_bias,
    second_gain,
    second_shift,
):
    seq_count, length, width = tokens.shape
    rows = seq_count * length
    layers = qkv_weight.shape[0]
    size = lax.axis_size("tensor")
    chips = lax.axis_size("dp") // 2
    part = qkv_weight.shape[-1]
    qkv_stack = jnp.transpose(qkv_weight, (0, 2, 1, 3))
    low = tokens.reshape(rows, width)
    weights = dict(qkv_w=qkv_stack, proj_w=proj_weight, up_w=up_weight, down_w=down_weight)
    ins = dict(
        low_in_0=low,
        cotangent=cotangent.reshape(rows, width),
        seg_row=segment_ids,
        qv_bias=qv_bias,
        proj_b=proj_bias,
        first_gain=first_gain,
        first_shift=first_shift,
        up_b=up_bias,
        down_b=down_bias,
        second_gain=second_gain,
        second_shift=second_shift,
    )
    for layer in range(layers):
        for name, array in weights.items():
            ins["%s_%d" % (name, layer)] = Layer(array, layer)
    done = forward_kernel(size, chips, 0, ins)
    last, own_rows = backward_kernel(
        size,
        chips,
        1,
        layers,
        dict(
            seg_row=segment_ids,
            log_total_0=done.log_total_0,
            log_total_1=done.log_total_1,
            sums_1=done.sums,
            ffn_share_1=done.ffn_share,
            up_sum_1=done.up_sum,
            inverse_two=done.inverse_two_0,
            inverse_one=done.inverse_one_0,
            first_gain=first_gain,
            second_gain=second_gain,
            proj_w_1=Layer(proj_weight, 1),
            attn_low_1=whole(done.attn_low),
            projected_1=whole(done.projected_1),
            mixed_own=whole(done.mixed_own),
            qkv_w_1=Layer(qkv_stack, 1),
            grad_first_1=whole(done.grad_first),
            unit_two=whole(done.unit_two_0),
            context_in_1=whole(done.context_1),
            low_in_1=whole(done.low_0),
            up_w=Layer(up_weight, 0),
            down_w=Layer(down_weight, 0),
            slope=whole(done.slope_0),
            unit_one=whole(done.unit_one_0),
            act=whole(done.act_0),
            normed_low=whole(done.normed_low_0),
            proj_w_0=Layer(proj_weight, 0),
            qkv_w_0=Layer(qkv_stack, 0),
            projected_0=whole(done.projected_0),
            context_in_0=whole(done.context_0),
            low_in_0=whole(low),
        ),
    )
    ffn_wholes = [last.ffn_whole_0, last.ffn_whole_1]
    attn_wholes = [last.attn_whole_0, last.attn_whole_1]

    mixed, input_grad, qkv, proj, up, down, qv, up_b, *norms = assemble(
        attn_wholes, ffn_wholes, last.mixed, last.grad_low, last.small_total, own_rows, part
    )
    return (
        mixed.reshape(tokens.shape),
        input_grad.reshape(tokens.shape),
        jnp.transpose(qkv, (0, 2, 1, 3)),
        qv,
        proj,
        norms[5],
        norms[3],
        norms[4],
        up,
        up_b,
        down,
        norms[2],
        norms[0],
        norms[1],
    )


def solution(mesh):
    return jax.shard_map(
        local,
        mesh=mesh,
        in_specs=(
            P("dp", None, None),
            P("dp", None),
            P("dp", None, None),
            P(None, None, None, "tensor"),
            P(None, None, "tensor"),
            P(None, "tensor", None),
            P(),
            P(),
            P(),
            P(None, None, "tensor"),
            P(None, "tensor"),
            P(None, "tensor", None),
            P(),
            P(),
            P(),
        ),
        out_specs=(
            P("dp", None, None),
            P("dp", None, None),
            P(None, None, None, "tensor"),
            P(None, None, "tensor"),
            P(None, "tensor", None),
            P(),
            P(),
            P(),
            P(None, None, "tensor"),
            P(None, "tensor"),
            P(None, "tensor", None),
            P(),
            P(),
            P(),
        ),
        check_vma=False,
    )
```

```python
import math
import types

import jax
import jax.numpy as jnp
from jax import lax
from jax.experimental import pallas as pl
from jax.experimental.pallas import tpu as pltpu
from jax.sharding import PartitionSpec as P

HEAD = 64


norm_eps = 1e-12
masked_value = -1000000000.0


MESH = pl.DeviceIdType.MESH
F32 = jnp.float32
LOW = jnp.bfloat16
CHUNK = 32
LAG = 2
PIECE = 512
QUERIES = 128


def dot(a, b):
    return jnp.dot(a, b, preferred_element_type=F32)


def dot_t(a, b):
    return lax.dot_general(a, b, (((1,), (1,)), ((), ())), preferred_element_type=F32)


def dot_tn(a, b):
    return lax.dot_general(a, b, (((0,), (0,)), ((), ())), preferred_element_type=F32)


def here():
    return lax.axis_index("dp"), lax.axis_index("tensor")


def greet(size, line=True, targets=()):
    row, place = here()
    barrier = pltpu.get_barrier_semaphore()
    for count, target in targets:

        def signal(index, carry):
            pl.semaphore_signal(barrier, inc=1, device_id=target(index), device_id_type=MESH)
            return carry

        lax.fori_loop(0, count, signal, 0)
    expected = sum(count for count, _ in targets)
    left, right = place > 0, place < size - 1
    if line:

        @pl.when(left)
        def _():
            pl.semaphore_signal(barrier, inc=1, device_id=(row, place - 1), device_id_type=MESH)

        @pl.when(right)
        def _():
            pl.semaphore_signal(barrier, inc=1, device_id=(row, place + 1), device_id_type=MESH)

    def wait():
        if not line:
            pl.semaphore_wait(barrier, expected)
            return

        @pl.when(left & right)
        def _():
            pl.semaphore_wait(barrier, expected + 2)

        @pl.when(jnp.logical_not(left & right))
        def _():
            pl.semaphore_wait(barrier, expected + 1)

    return wait


def partner():
    row, place = here()
    return (row + 1 - 2 * lax.rem(row, 2), place)


def plane_peer(chips, index):
    row, place = here()
    return (lax.rem(row // 2 + index + 1, chips) * 2 + lax.rem(row, 2), place)


def line_loop(size, stages, extras=(), lag=LAG):
    row, place = here()
    half = stages[0].part.shape[0] // 2
    chunks = half // CHUNK
    end = size - 1
    span = 2 * lag * end

    def rows_of(side, chunk):
        return pl.ds(pl.multiple_of(side * half + chunk * CHUNK, CHUNK), CHUNK)

    def sum_copy(stage, side, chunk, target):
        rows = rows_of(side, chunk)
        return pltpu.make_async_remote_copy(
            src_ref=stage.part.at[rows],
            dst_ref=stage.recv.at[rows],
            send_sem=stage.sems[0].at[side, chunk],
            recv_sem=stage.sems[1].at[side, chunk],
            device_id=(row, target),
            device_id_type=MESH,
        )

    def row_copy(stage, which, side, chunk, target):
        rows = rows_of(side, chunk)
        return pltpu.make_async_remote_copy(
            src_ref=stage.outs[which].at[rows],
            dst_ref=stage.outs[which].at[rows],
            send_sem=stage.sems[2].at[which, side, chunk],
            recv_sem=stage.sems[3].at[which, side, chunk],
            device_id=(row, target),
            device_id_type=MESH,
        )

    def side_facts(side):
        if side == 0:
            return place, place + 1, place - 1
        return end - place, place - 1, place + 1

    def bring_back(stage, since):
        for side in range(2):
            at, onward, back = side_facts(side)
            chunk = since - lag * end - lag * (end - at)

            @pl.when((at < end) & (chunk >= 0) & (chunk < chunks))
            def _():
                for which in range(len(stage.outs)):
                    row_copy(stage, which, side, chunk, back).wait_recv()

                    @pl.when(at > 0)
                    def _():
                        row_copy(stage, which, side, chunk, back).start()

    def begin_sum(stage, since):
        for side in range(2):
            at, onward, back = side_facts(side)

            @pl.when(at == 0)
            def _():
                sum_copy(stage, side, since, onward).start()

    def sum_up(stage, since):
        for side in range(2):
            at, onward, back = side_facts(side)
            chunk = since - lag * at

            @pl.when((at > 0) & (chunk >= 0) & (chunk < chunks))
            def _():
                sum_copy(stage, side, chunk, onward).wait_recv()

                @pl.when(at < end)
                def _():
                    rows = rows_of(side, chunk)
                    stage.part[rows] = stage.part[rows] + stage.recv[rows]
                    sum_copy(stage, side, chunk, onward).start()

                @pl.when(at == end)
                def _():
                    rows = rows_of(side, chunk)
                    own = pl.ds(pl.multiple_of(chunk * CHUNK, CHUNK), CHUNK)
                    rest = stage.finish(rows, own, stage.part[rows].astype(F32) + stage.recv[rows].astype(F32))
                    for which in range(len(stage.outs)):
                        row_copy(stage, which, side, chunk, back).start()
                    rest()

    def step(now, carry):
        for number, stage in enumerate(stages):
            bring_back(stage, now - number * span)
        for number, stage in enumerate(stages):
            sum_up(stage, now - number * span)
        for number, stage in enumerate(stages):
            since = now - number * span

            @pl.when((since >= 0) & (since < chunks))
            def _():
                stage.produce([rows_of(side, since) for side in range(2)])
                begin_sum(stage, since)

        for first, count, work in extras:

            @pl.when((now >= first) & (now < first + count))
            def _():
                work(now - first)

        return carry

    lax.fori_loop(0, chunks + span * len(stages), step, 0)

    def drain(chunk, carry):
        for stage in stages:
            for side in range(2):
                at, onward, back = side_facts(side)

                @pl.when(at < end)
                def _():
                    sum_copy(stage, side, chunk, onward).wait_send()

                @pl.when(at > 0)
                def _():
                    for which in range(len(stage.outs)):
                        row_copy(stage, which, side, chunk, back).wait_send()

        return carry

    lax.fori_loop(0, chunks, drain, 0)


def chunk_rows(half, chunk):
    return [pl.ds(pl.multiple_of(side * half + chunk * CHUNK, CHUNK), CHUNK) for side in range(2)]


def by_rows(count, work, block=32):
    def one(index, carry):
        work(pl.ds(pl.multiple_of(index * block, block), block), index * block)
        return carry

    block = min(block, count)
    lax.fori_loop(0, count // block, one, 0)


class Spread:
    def __init__(self, chips, grads, scratch):
        self.chips, self.grads = chips, grads
        self.half = grads.shape[0] // 2
        self.near, self.far, self.near_sems, self.far_sems, self.free = scratch
        row, place = here()
        self.core, self.chip, self.place = lax.rem(row, 2), row // 2, place

    @staticmethod
    def scratch(chips, rows, width):
        half = rows // 2
        far = half * 3 // 4 if chips == 4 else half // chips * (chips - 1)
        copies = 8 if chips == 4 else 2 * (chips - 1)
        sems = [
            pltpu.SemaphoreType.DMA((4,)),
            pltpu.SemaphoreType.DMA((2, copies)),
            pltpu.SemaphoreType.REGULAR,
        ]
        return [pltpu.VMEM((half, width), LOW), pltpu.VMEM((far, width), LOW), *sems, *sems]

    def rows(self, first, count):
        return pl.ds(pl.multiple_of(first, 16), count)

    def core_copy(self, source, target, number):
        return pltpu.make_async_remote_copy(
            src_ref=source,
            dst_ref=target,
            send_sem=self.near_sems.at[2 * number],
            recv_sem=self.near_sems.at[2 * number + 1],
            device_id=partner(),
            device_id_type=MESH,
        )

    def near_copy(self):
        other = self.rows((1 - self.core) * self.half, self.half)
        return self.core_copy(self.grads.at[other], self.near, 0)

    def last_copy(self):
        own = self.grads.at[self.rows(self.core * self.half, self.half)]
        return self.core_copy(own, own, 1)

    def chip_copy(self, source, target, number, chip):
        return pltpu.make_async_remote_copy(
            src_ref=source,
            dst_ref=target,
            send_sem=self.far_sems.at[0, number],
            recv_sem=self.far_sems.at[1, number],
            device_id=(chip * 2 + self.core, self.place),
            device_id_type=MESH,
        )

    def to_partner(self):
        self.near_copy().start()

    def add_partner(self):
        self.near_copy().wait_send()
        pl.semaphore_signal(self.free, inc=1, device_id=partner(), device_id_type=MESH)
        self.near_copy().wait_recv()
        base = self.core * self.half

        def add(rows, first):
            own = self.grads[self.rows(base + first, rows.size)]
            self.near[rows] = self.near[rows] + own

        by_rows(self.half, add)

    def settle_sum(self):
        self.settle_there()
        pl.semaphore_wait(self.free, 1)

    def give_share(self):
        self.sum_share(self.grads, self.own_rows())
        self.start_back()

    def keep_share(self, share):
        count = share.shape[0] // len(self.own_rows())
        for number, base in enumerate(self.own_rows()):

            def keep(rows, first, number=number, base=base):
                came = share[self.rows(number * count + first, rows.size)]
                self.grads[self.rows(base + first, rows.size)] = came

            by_rows(count, keep)
        self.summed = False
        self.start_back()

    summed = True

    def to_other_core(self):
        self.take_back()
        if self.summed:
            self.settle_sum()
        self.settle_back()
        self.last_copy().start()

    def settle(self):
        self.last_copy().wait_recv()
        self.last_copy().wait_send()


class DirectSpread(Spread):
    def each(self, work):
        def one(index, carry):
            work(index)
            return carry

        lax.fori_loop(0, self.chips - 1, one, 0)

    def peer(self, index):
        return lax.rem(self.chip + index + 1, self.chips)

    def far_copy(self, index):
        count = self.half // self.chips
        chip = self.peer(index)
        source = self.near.at[self.rows(chip * count, count)]
        return self.chip_copy(source, self.far.at[self.rows(index * count, count)], index, chip)

    def back_copy(self, index):
        count = self.half // self.chips
        share = self.grads.at[self.rows(self.core * self.half + self.chip * count, count)]
        return self.chip_copy(share, share, self.chips - 1 + index, self.peer(index))

    def to_chips(self):
        self.add_partner()
        self.each(lambda index: self.far_copy(index).start())

    def onward(self):
        pass

    def own_rows(self):
        return [self.core * self.half + self.chip * (self.half // self.chips)]

    def sum_share(self, target, starts):
        self.each(lambda index: self.far_copy(index).wait_recv())
        count = self.half // self.chips
        base = self.chip * count

        def add(rows, first):
            def one(index, total):
                return total + self.far[self.rows(index * count + first, rows.size)].astype(F32)

            own = self.near[self.rows(base + first, rows.size)].astype(F32)
            total = lax.fori_loop(0, self.chips - 1, one, own)
            target[self.rows(starts[0] + first, rows.size)] = total.astype(LOW)

        by_rows(count, add)

    def start_back(self):
        self.each(lambda index: self.back_copy(index).start())

    def pass_on(self):
        pass

    def take_back(self):
        self.each(lambda index: self.back_copy(index).wait_recv())

    def settle_there(self):
        self.each(lambda index: self.far_copy(index).wait_send())

    def settle_back(self):
        self.each(lambda index: self.back_copy(index).wait_send())


class SquareSpread(Spread):
    def __init__(self, chips, grads, scratch):
        super().__init__(chips, grads, scratch)
        quarter = self.half // 4
        eighth = self.half // 8
        first, second = lax.rem(self.chip, 2), self.chip // 2
        along = self.chip + 1 - 2 * first
        across = self.chip + 2 - 4 * second
        self.quarter, self.eighth = quarter, eighth
        self.chips_of = ((along, across), (across, along))
        self.bits = ((first, second), (second, first))
        self.part = [side * 2 * quarter for side in range(2)]
        self.kept = [self.part[side] + self.bits[side][0] * quarter for side in range(2)]
        self.own = [self.kept[side] + self.bits[side][1] * eighth for side in range(2)]

    def first_copy(self, side):
        sent = self.part[side] + (1 - self.bits[side][0]) * self.quarter
        room = self.far.at[pl.ds(side * self.quarter, self.quarter)]
        source = self.near.at[self.rows(sent, self.quarter)]
        return self.chip_copy(source, room, side, self.chips_of[side][0])

    def second_copy(self, side):
        sent = self.kept[side] + (1 - self.bits[side][1]) * self.eighth
        room = self.far.at[pl.ds(2 * self.quarter + side * self.eighth, self.eighth)]
        source = self.near.at[self.rows(sent, self.eighth)]
        return self.chip_copy(source, room, 2 + side, self.chips_of[side][1])

    def share_copy(self, side):
        share = self.grads.at[self.rows(self.core * self.half + self.own[side], self.eighth)]
        return self.chip_copy(share, share, 4 + side, self.chips_of[side][1])

    def pass_copy(self, side):
        share = self.grads.at[self.rows(self.core * self.half + self.kept[side], self.quarter)]
        return self.chip_copy(share, share, 6 + side, self.chips_of[side][0])

    def to_chips(self):
        self.add_partner()
        for side in range(2):
            self.first_copy(side).start()

    def onward(self):
        for side in range(2):
            self.first_copy(side).wait_recv()
            base = self.kept[side]

            def add(rows, first, side=side, base=base):
                at = self.rows(base + first, rows.size)
                came = self.far[self.rows(side * self.quarter + first, rows.size)]
                self.near[at] = self.near[at] + came

            by_rows(self.quarter, add)
            self.second_copy(side).start()

    def own_rows(self):
        return [self.core * self.half + self.own[side] for side in range(2)]

    def sum_share(self, target, starts):
        for side in range(2):
            self.second_copy(side).wait_recv()
            base, start = self.own[side], starts[side]

            def add(rows, first, side=side, base=base, start=start):
                came = self.far[self.rows(2 * self.quarter + side * self.eighth + first, rows.size)]
                own = self.near[self.rows(base + first, rows.size)]
                target[self.rows(start + first, rows.size)] = own + came

            by_rows(self.eighth, add)

    def start_back(self):
        for side in range(2):
            self.share_copy(side).start()

    def pass_on(self):
        for side in range(2):
            self.share_copy(side).wait_recv()
            self.pass_copy(side).start()

    def take_back(self):
        for side in range(2):
            self.pass_copy(side).wait_recv()

    def settle_there(self):
        for side in range(2):
            self.first_copy(side).wait_send()
            self.second_copy(side).wait_send()

    def settle_back(self):
        for side in range(2):
            self.share_copy(side).wait_send()
            self.pass_copy(side).wait_send()


def spread_of(chips, grads, scratch):
    return (SquareSpread if chips == 4 else DirectSpread)(chips, grads, scratch)


def normalize(residual):
    centred = residual - jnp.mean(residual, axis=-1, keepdims=True)
    inverse = lax.rsqrt(jnp.mean(centred * centred, axis=-1, keepdims=True) + norm_eps)
    return centred * inverse, inverse


def norm_back(grad, gain, unit, inverse):
    scaled = grad * gain
    return (
        scaled
        - jnp.mean(scaled, axis=-1, keepdims=True)
        - unit * jnp.mean(scaled * unit, axis=-1, keepdims=True)
    ) * inverse


def tally(total, values):
    total[...] += jnp.sum(values.reshape(-1, 8, values.shape[-1]), axis=0)


class Layer:
    def __init__(self, array, layer):
        self.array, self.layer = array, layer

    def room(self):
        return self.array.shape if self.layer is None else self.array.shape[1:]


def whole(array):
    return Layer(array, None)


def view(refs, suffix):
    named = dict(vars(refs))
    for name, ref in vars(refs).items():
        if name.endswith(suffix):
            named[name[: -len(suffix)]] = ref
    return types.SimpleNamespace(**named)


def call(collective, body, ins, outs, scratch, into=types.MappingProxyType({}), later=(), sent=()):
    vmem = pl.BlockSpec(memory_space=pltpu.VMEM)
    names = [*ins, *outs]
    fetched = {name: value for name, value in ins.items() if isinstance(value, Layer)}
    inside = {name: value for name, value in fetched.items() if name not in into}
    extra = {name: spec if isinstance(spec, list) else [spec] for name, spec in scratch.items()}

    def run(*refs):
        named = dict(zip(names, refs))
        rest = list(refs[len(names) :])
        copies, leaving = {}, {}
        arrivals, departures = rest.pop(0), rest.pop(0)
        for number, name in enumerate(sent):
            room = rest.pop(0)
            leaving[name] = pltpu.make_async_copy(room, named[name], departures.at[number])
            named[name] = room
        for number, (name, value) in enumerate(fetched.items()):
            room = named[into[name]] if name in into else rest.pop(0)
            source = named[name] if value.layer is None else named[name].at[value.layer]
            copies[name] = pltpu.make_async_copy(source, room, arrivals.at[number])
            if name not in later:
                copies[name].start()
            named[name] = room
        for name, specs in extra.items():
            taken = [rest.pop(0) for _ in specs]
            named[name] = taken if isinstance(scratch[name], list) else taken[0]

        def need(*wanted):
            for name in wanted:
                copies[name].wait()

        def fetch(*wanted):
            for name in wanted:
                copies[name].start()

        def send(*wanted):
            for name in wanted:
                leaving[name].start()

        body(types.SimpleNamespace(**named, need=need, fetch=fetch, send=send))
        for copy in leaving.values():
            copy.wait()

    results = pl.pallas_call(
        run,
        out_shape=list(outs.values()),
        in_specs=[pl.BlockSpec(memory_space=pl.ANY) if name in fetched else vmem for name in ins],
        out_specs=[pl.BlockSpec(memory_space=pl.ANY) if name in sent else vmem for name in outs],
        scratch_shapes=[
            pltpu.SemaphoreType.DMA((len(fetched),)),
            pltpu.SemaphoreType.DMA((max(1, len(sent)),)),
            *(pltpu.VMEM(outs[name].shape, outs[name].dtype) for name in sent),
            *(pltpu.VMEM(value.room(), value.array.dtype) for value in inside.values()),
            *(spec for specs in extra.values() for spec in specs),
        ],
        compiler_params=pltpu.CompilerParams(
            collective_id=collective, has_side_effects=True, vmem_limit_bytes=60 << 20
        ),
    )(*(value.array if isinstance(value, Layer) else value for value in ins.values()))
    return types.SimpleNamespace(**dict(zip(outs, results)))


def shape(*dims, kind=F32):
    return jax.ShapeDtypeStruct(dims, kind)


def line_scratch(rows, width, outs=1):
    chunks = rows // 2 // CHUNK
    return [
        pltpu.VMEM((rows, width), LOW),
        pltpu.VMEM((rows, width), LOW),
        pltpu.SemaphoreType.DMA((2, chunks)),
        pltpu.SemaphoreType.DMA((2, chunks)),
        pltpu.SemaphoreType.DMA((outs, 2, chunks)),
        pltpu.SemaphoreType.DMA((outs, 2, chunks)),
    ]


def stage_of(produce, finish, outs, scratch):
    part, recv, *sems = scratch
    return types.SimpleNamespace(
        produce=produce, finish=finish, outs=outs, part=part, recv=recv, sems=sems
    )


def clear(*refs):
    for ref in refs:
        ref[...] = jnp.zeros_like(ref)


def vector(ref, layer):
    return ref[...].astype(F32)[layer : layer + 1]


def head_lanes(values, head):
    lane = lax.broadcasted_iota(jnp.int32, values.shape, 1)
    return jnp.where(lane // HEAD == head, values, jnp.zeros_like(values))


def turned(values):
    return jnp.transpose(values.astype(F32)).astype(LOW)


def mark_segments(r):
    length = r.seg_row.shape[1]
    wide = jnp.broadcast_to(r.seg_row[...].astype(F32), (QUERIES, length))
    r.seg_cols[...] = jnp.transpose(wide)


def masked_block(r, keys, queries, at):
    same = r.seg_cols[...] == r.seg_row[:, at].astype(F32)
    return jnp.where(same, dot_t(keys, queries) * HEAD ** (-0.5), masked_value)


def project(r, layer, blocks):
    bias = r.qv_bias[layer].astype(F32)
    taken = take(r.low_in, blocks)
    for member in range(3):
        rows = dot(taken, r.qkv_w[member])
        if member != 1:
            rows += bias[member // 2 : member // 2 + 1]
        put(r.projected.at[member], blocks, rows.astype(LOW))


def attend(r, block):
    at = pl.ds(pl.multiple_of(block * QUERIES, QUERIES), QUERIES)
    queries = r.projected[0, at]
    heads = queries.shape[1] // HEAD
    parts = []
    for head in range(heads):
        scores = masked_block(r, r.projected[1], head_lanes(queries, head), at)
        row_max = jnp.max(scores, axis=0, keepdims=True)
        exponent = jnp.exp(scores - row_max)
        row_total = jnp.sum(exponent, axis=0, keepdims=True)
        r.log_total[head : head + 1, at] = row_max + jnp.log(row_total)
        probs = (exponent * (1.0 / row_total)).astype(LOW)
        parts.append(dot(r.turned_rows[head * HEAD : (head + 1) * HEAD], probs))
    r.context[at] = jnp.transpose(jnp.concatenate(parts, axis=0)).astype(LOW)


def attend_first(r, half):
    per_side = half // QUERIES
    r.turned_rows[...] = turned(r.projected[2])
    for side in range(2):
        attend(r, side * per_side)
    extras = []
    for block in range(1, per_side):
        for side in range(2):
            step = max(0, block * QUERIES // CHUNK - 2 + side)
            extras.append(at_step(step, lambda block=side * per_side + block: attend(r, block)))
    return extras


def context_back(r, blocks):
    put(r.grad_context, blocks, dot_t(take(r.attn_low_in, blocks), r.proj_w[...]).astype(LOW))


def attend_back(r, between=()):
    rows = r.attn_low_in.shape[0]
    heads = r.qkv_w.shape[2] // HEAD
    scale = HEAD ** (-0.5)
    r.turned_rows[...] = turned(r.projected[1])
    clear(r.grad_key, r.grad_value)
    for number in range(rows // QUERIES):
        at = slice(number * QUERIES, (number + 1) * QUERIES)
        queries, context_rows = r.projected[0, at], r.grad_context[at]
        parts = []
        for head in range(heads):
            to = slice(head * QUERIES, (head + 1) * QUERIES)
            r.head_queries[to] = head_lanes(queries, head)
            r.head_context[to] = head_lanes(context_rows, head)
            scores = masked_block(r, r.projected[1], r.head_queries[to], at)
            probability = jnp.exp(scores - r.log_total[head : head + 1, at])
            grad_probs = dot_t(r.projected[2], r.head_context[to])
            inner = jnp.sum(probability * grad_probs, axis=0, keepdims=True)
            grad_scores = (probability * (grad_probs - inner)).astype(LOW)
            r.score_rows[:, to] = grad_scores
            r.prob_rows[:, to] = probability.astype(LOW)
            parts.append(dot(r.turned_rows[head * HEAD : (head + 1) * HEAD], grad_scores))
        r.grad_key[...] += dot(r.score_rows[...], r.head_queries[...])
        r.grad_value[...] += dot(r.prob_rows[...], r.head_context[...])
        r.grad_proj[0, at] = (jnp.transpose(jnp.concatenate(parts, axis=0)) * scale).astype(LOW)
        if number < len(between):
            between[number]()
    r.grad_proj[1] = (r.grad_key[...] * scale).astype(LOW)
    r.grad_proj[2] = r.grad_value[...].astype(LOW)
    for slot, member in ((0, 0), (1, 2)):
        r.qv_sum[slot] = jnp.sum(r.grad_proj[member].astype(F32).reshape(-1, 8, r.qv_sum.shape[2]), axis=0)


def take(ref, blocks):
    return jnp.concatenate([ref[block] for block in blocks], axis=0)


def put(ref, blocks, values):
    count = values.shape[0] // len(blocks)
    for number, block in enumerate(blocks):
        ref[block] = values[number * count : (number + 1) * count]


def proj_stage(r, layer, whole):
    def produce(blocks):
        put(r.proj_line[0], blocks, dot(take(r.context, blocks), r.proj_w[...]).astype(LOW))

    def finish(at, own, total):
        came = r.residual[at if whole else own].astype(F32)
        unit, inverse = normalize(came + total + vector(r.proj_b, layer))
        result = unit * vector(r.first_gain, layer) + vector(r.first_shift, layer)
        r.normed_low[at] = result.astype(LOW)

        def rest():
            r.unit_one[own] = unit
            r.inverse_one[own] = inverse
            r.normed[own] = result

        return rest

    return stage_of(produce, finish, [r.normed_low], r.proj_line)


def ffn_stage(r, layer, last):
    def produce(blocks):
        pre = dot(take(r.normed_low, blocks), r.up_w[...]) + vector(r.up_b, layer)
        cdf = 0.5 * lax.erf(pre * math.sqrt(0.5)) + 0.5
        act = (pre * cdf).astype(LOW)
        slope = cdf + pre * jnp.exp(-0.5 * pre * pre) * (1.0 / math.sqrt(2 * math.pi))
        put(r.slope, blocks, slope.astype(LOW))
        put(r.act, blocks, act)
        put(r.ffn_line[0], blocks, dot(act, r.down_w[...]).astype(LOW))

    def finish(at, own, total):
        unit, inverse = normalize(r.normed[own] + total + vector(r.down_b, layer))
        gain = vector(r.second_gain, layer)
        result = unit * gain + vector(r.second_shift, layer)
        if last:
            grad_in = r.cotangent[at].astype(F32)
            grad = norm_back(grad_in, gain, unit, inverse)
            r.branch[at] = grad.astype(LOW)
        else:
            r.low[at] = result.astype(LOW)

        def rest():
            if last:
                r.mixed_own[own] = result.astype(LOW)
                r.grad_second[own] = grad
                tally(r.sums.at[0], grad_in * unit)
                tally(r.sums.at[1], grad_in)
                tally(r.sums.at[2], grad.astype(LOW).astype(F32))
            else:
                r.unit_two[own] = unit
                r.inverse_two[own] = inverse
                r.hidden[own] = result

        return rest

    return stage_of(produce, finish, [r.branch if last else r.low], r.ffn_line)


def ffn_back_stage(r, layer):
    def produce(blocks):
        grad = dot_t(take(r.branch, blocks), r.down_w[...])
        pre = (grad * take(r.slope, blocks).astype(F32)).astype(LOW)
        put(r.pre, blocks, pre)
        tally(r.up_sum, pre.astype(F32))
        put(r.back_line[0], blocks, dot_t(pre, r.up_w[...]).astype(LOW))

    def finish(at, own, total):
        grad_in = r.grad_second[own] + total
        unit = r.unit_one[own]
        grad = norm_back(grad_in, vector(r.first_gain, layer), unit, r.inverse_one[own])
        r.attn_low[at] = grad.astype(LOW)

        def rest():
            r.grad_first[own] = grad
            tally(r.sums.at[3], grad_in * unit)
            tally(r.sums.at[4], grad_in)
            tally(r.sums.at[5], grad.astype(LOW).astype(F32))

        return rest

    return stage_of(produce, finish, [r.attn_low], r.back_line)


def qkv_back_stage(r, layer, inner):
    def produce(blocks):
        total = sum(dot_t(take(r.grad_proj.at[member], blocks), r.qkv_w[member]) for member in range(3))
        put(r.qkv_line[0], blocks, total.astype(LOW))

    def finish(at, own, total):
        grad_in = r.grad_first_in[own] + total
        if not inner:
            r.grad_low[at] = grad_in.astype(LOW)
            return lambda: None
        unit = r.unit_two[own]
        grad = norm_back(grad_in, vector(r.second_gain, layer), unit, r.inverse_two[own])
        r.branch[at] = grad.astype(LOW)

        def rest():
            r.grad_second[own] = grad
            tally(r.sums.at[0], grad_in * unit)
            tally(r.sums.at[1], grad_in)
            tally(r.sums.at[2], grad.astype(LOW).astype(F32))

        return rest

    return stage_of(produce, finish, [r.branch] if inner else [r.grad_low], r.qkv_line)


def columns(piece):
    return pl.ds(pl.multiple_of(piece * PIECE, PIECE), PIECE)


def ffn_grads(r, out, first):
    width, hidden = r.up_w.shape

    def up(piece):
        rows = pl.ds(pl.multiple_of(piece * PIECE, PIECE), PIECE)
        out[rows] = dot_tn(r.normed_low[:, columns(piece)], r.pre[...]).astype(LOW)

    def down(piece):
        rows = pl.ds(pl.multiple_of(width + piece * PIECE, PIECE), PIECE)
        out[rows] = dot_tn(r.act[:, columns(piece)], r.branch[...]).astype(LOW)

    def all_of(pieces, work):
        lax.fori_loop(0, pieces, lambda piece, carry: (work(piece), carry)[1], 0)

    return [
        at_step(first, lambda: all_of(width // PIECE, up)),
        at_step(first + 1, lambda: all_of(hidden // PIECE, down)),
    ]


def attn_grads(r, out, first):
    width, part = r.low_in.shape[1], r.context_in.shape[1]

    def piece_of(piece):
        for member in range(3):
            rows = pl.ds(pl.multiple_of(member * width + piece * part, part), part)
            taken = r.low_in[:, pl.ds(pl.multiple_of(piece * part, part), part)]
            out[rows] = dot_tn(taken, r.grad_proj[member]).astype(LOW)
        rows = pl.ds(pl.multiple_of(3 * width + piece * part, part), part)
        taken = r.attn_low_in[:, pl.ds(pl.multiple_of(piece * part, part), part)]
        out[rows] = dot_tn(r.context_in[...], taken).astype(LOW)

    def all_pieces():
        lax.fori_loop(0, width // part, lambda piece, carry: (piece_of(piece), carry)[1], 0)

    return [at_step(first, all_pieces)]


def at_step(step, work):
    return (step, 1, lambda index: work())


def with_suffix(suffix, named):
    return {name + suffix: value for name, value in named.items()}


def kept_attention(rows, part):
    return dict(
        projected=shape(3, rows, part, kind=LOW),
        log_total=shape(part // HEAD, rows),
        context=shape(rows, part, kind=LOW),
    )


def forward_kernel(size, chips, collective, ins):
    rows, width = ins["low_in_0"].shape
    part, hidden = ins["proj_w_0"].array.shape[1], ins["up_w_0"].array.shape[2]
    half = rows // 2
    chunks = half // CHUNK

    def body(r):
        wait = greet(size, targets=[(1, lambda index: partner()), (chips - 1, lambda index: plane_peer(chips, index))])
        ffn_sum = spread_of(chips, r.ffn_grad, r.ffn_spread[:5])
        clear(r.sums, r.up_sum)
        mark_segments(r)
        below, above = view(r, "_0"), view(r, "_1")
        below.residual = r.low_in_0
        above.low_in, above.residual = r.low_0, r.hidden_0
        r.need("qkv_w_0")
        project(below, 0, [slice(0, rows)])
        extras = attend_first(below, half)
        r.need("proj_w_0", "up_w_0", "down_w_0", "qkv_w_1")
        wait()

        def project_chunk(chunk):
            project(above, 1, chunk_rows(half, chunk))

        extras.append((4 * 3 * (size - 1), chunks, project_chunk))
        line_loop(size, [proj_stage(below, 0, True), ffn_stage(below, 0, False)], extras, 3)
        r.send("projected_0", "context_0", "unit_one_0", "normed_low_0", "act_0", "slope_0", "unit_two_0", "low_0")
        extras = attend_first(above, half)
        r.need("proj_w_1", "up_w_1", "down_w_1")
        stages = [proj_stage(above, 1, False), ffn_stage(above, 1, True), ffn_back_stage(above, 1)]
        first = 4 * 3 * (size - 1) + chunks
        line_loop(
            size,
            stages,
            [
                *extras,
                at_step(2 * chunks, lambda: r.send("projected_1", "context_1")),
                *ffn_grads(above, r.ffn_grad, first),
                at_step(first + 2, lambda: (ffn_sum.to_partner(), r.send("mixed_own"))),
                at_step(first + 5, ffn_sum.to_chips),
                at_step(first + 15, ffn_sum.onward),
            ],
            3,
        )
        r.send("grad_first", "attn_low")
        share = r.ffn_share.shape[0]
        ffn_sum.sum_share(r.ffn_share, [0, share // 2])
        ffn_sum.settle_sum()

    outs = dict(
        **with_suffix("_0", kept_attention(rows, part)),
        **with_suffix("_1", kept_attention(rows, part)),
        unit_one_0=shape(half, width),
        inverse_one_0=shape(half, 1),
        normed_low_0=shape(rows, width, kind=LOW),
        act_0=shape(rows, hidden, kind=LOW),
        slope_0=shape(rows, hidden, kind=LOW),
        unit_two_0=shape(half, width),
        inverse_two_0=shape(half, 1),
        low_0=shape(rows, width, kind=LOW),
        mixed_own=shape(half, width, kind=LOW),
        grad_first=shape(half, width),
        attn_low=shape(rows, width, kind=LOW),
        ffn_share=shape((width + hidden) // 2 // chips, width, kind=LOW),
        up_sum=shape(8, hidden),
        sums=shape(6, 8, width),
    )
    scratch = dict(
        hidden_0=pltpu.VMEM((half, width), F32),
        normed=pltpu.VMEM((half, width), F32),
        turned_rows=pltpu.VMEM((part, rows), LOW),
        seg_cols=pltpu.VMEM((rows, QUERIES), F32),
        unit_one_1=pltpu.VMEM((half, width), F32),
        inverse_one_1=pltpu.VMEM((half, 1), F32),
        normed_low_1=pltpu.VMEM((rows, width), LOW),
        act_1=pltpu.VMEM((rows, hidden), LOW),
        slope_1=pltpu.VMEM((rows, hidden), LOW),
        pre=pltpu.VMEM((rows, hidden), LOW),
        branch=pltpu.VMEM((rows, width), LOW),
        grad_second=pltpu.VMEM((half, width), F32),
        proj_line_0=line_scratch(rows, width),
        ffn_line_0=line_scratch(rows, width),
        proj_line_1=line_scratch(rows, width),
        ffn_line_1=line_scratch(rows, width),
        back_line=line_scratch(rows, width),
        ffn_grad=pltpu.VMEM((width + hidden, width), LOW),
        ffn_spread=Spread.scratch(chips, width + hidden, width),
    )
    sent = [name for name, out in outs.items() if out.dtype == LOW and name != "ffn_share" or name in ("unit_one_0", "unit_two_0", "grad_first")]
    return call(collective, body, ins, outs, scratch, sent=sent)


def backward_kernel(size, chips, collective, layers, ins):
    rows, width = ins["attn_low_1"].array.shape
    part, hidden = ins["proj_w_0"].array.shape[1], ins["up_w"].array.shape[2]
    half = rows // 2
    chunks = half // CHUNK
    span = 2 * LAG * (size - 1)
    ffn_rows, attn_rows = width + hidden, 4 * width
    own_rows = layers * (2 * part + hidden) // width
    count = -(-(own_rows + 6 * layers) // 8) * 8
    teams = 2 * chips

    def row_peer(index):
        row, place = here()
        return (lax.rem(row + index + 1, teams), place)

    def line_peer(index):
        row, place = here()
        return (row, lax.rem(place + index + 1, size))

    def each(number, work):
        def one(index, carry):
            work(index)
            return carry

        lax.fori_loop(0, number, one, 0)

    def body(r):
        row, place = here()
        clear(r.ends, r.sums_0, r.up_sum_0)
        wait = greet(size, line=False, targets=[(teams - 1, row_peer), (size - 1, line_peer)])
        ffn_above = spread_of(chips, r.ffn_whole_1, r.ffn_spread[:5])
        attn_above = spread_of(chips, r.attn_whole_1, r.attn_spread[:5])
        ffn_below = spread_of(chips, r.ffn_whole_0, r.ffn_spread[:2] + r.ffn_spread[5:])
        attn_below = spread_of(chips, r.attn_whole_0, r.attn_spread[:2] + r.attn_spread[5:])
        above, below = view(r, "_1"), view(r, "_0")
        above.grad_first_in, above.attn_low_in = r.grad_first_1, r.attn_low_1
        below.grad_first_in, below.attn_low_in = r.grad_first_0, r.attn_low_0
        middle = types.SimpleNamespace(
            **{**vars(r), "sums": r.sums_0, "up_sum": r.up_sum_0, "grad_first": r.grad_first_0, "attn_low": r.attn_low_0}
        )
        above.sums = r.sums_0
        above.grad_second = middle.grad_second = r.grad_first_0
        below.qkv_line = [*r.qkv_line_1[:2], *r.qkv_sems_0]

        def end_copy(slot, index):
            return pltpu.make_async_remote_copy(
                src_ref=r.small,
                dst_ref=r.ends.at[slot],
                send_sem=r.end_sent.at[slot, index],
                recv_sem=r.end_got.at[slot],
                device_id=line_peer(index),
                device_id_type=MESH,
            )

        def team_copy(index, slot):
            return pltpu.make_async_remote_copy(
                src_ref=r.mine,
                dst_ref=r.others.at[slot],
                send_sem=r.team_sent.at[index],
                recv_sem=r.team_got.at[slot],
                device_id=row_peer(index),
                device_id_type=MESH,
            )

        end_places = ((0, 0), (1, size - 1))
        end = size - 1

        def side_rows(side):
            at, back = (place, place - 1) if side == 0 else (end - place, place + 1)
            return at, back, r.mixed.at[pl.ds(side * half, half)]

        def mixed_copy(side):
            at, back, rows_at = side_rows(side)
            return pltpu.make_async_remote_copy(
                src_ref=rows_at,
                dst_ref=rows_at,
                send_sem=r.mixed_sent.at[side],
                recv_sem=r.mixed_got.at[side],
                device_id=(row, back),
                device_id_type=MESH,
            )

        def mixed_hop(number):
            for side in range(2):
                at, _, rows_at = side_rows(side)

                @pl.when(at == end - number)
                def _():
                    if number:
                        mixed_copy(side).wait_recv()
                    else:
                        rows_at[...] = r.mixed_own[...]
                    mixed_copy(side).start()

        def mixed_settle():
            for side in range(2):
                at, _, _ = side_rows(side)

                @pl.when(at == 0)
                def _():
                    mixed_copy(side).wait_recv()

                @pl.when(at > 0)
                def _():
                    mixed_copy(side).wait_send()

        def small_to_line():
            named = vars(r)
            clear(r.small)
            lines = []
            for layer in range(layers):
                sums = jnp.sum(named["qv_sum_%d" % layer][...], axis=1)
                lines += [sums[0:1], sums[1:2]]
            for layer in range(layers):
                lines += [jnp.sum(named["up_sum_%d" % layer][...], axis=0, keepdims=True)]
            flat = jnp.concatenate(lines, axis=1)
            for number in range(own_rows):
                r.small[number : number + 1] = flat[:, number * width : (number + 1) * width]
            for layer in range(layers):
                sums = jnp.sum(named["sums_%d" % layer][...], axis=1)
                for member in range(6):
                    to = own_rows + member * layers + layer
                    r.small[to : to + 1] = sums[member : member + 1]
            for slot, end in end_places:

                @pl.when(place == end)
                def _():
                    each(size - 1, lambda index: end_copy(slot, index).start())

        def small_to_teams():
            for slot, end in end_places:

                @pl.when(place != end)
                def _():
                    end_copy(slot, 0).wait_recv()

            line_total = r.small[...] + r.ends[0] + r.ends[1]
            number = lax.broadcasted_iota(jnp.int32, (count, width), 0)
            r.mine[...] = jnp.where(number < own_rows, r.small[...], line_total)
            each(teams - 1, lambda index: team_copy(index, row).start())
            r.others[row] = r.mine[...]

        def small_finish():
            each(teams - 1, lambda index: team_copy(index, row_peer(index)[0]).wait_recv())
            r.small_total[...] = lax.fori_loop(
                1, teams, lambda index, total: total + r.others[index], r.others[0]
            )
            each(teams - 1, lambda index: team_copy(index, row).wait_send())
            for slot, end in end_places:

                @pl.when(place == end)
                def _():
                    each(size - 1, lambda index: end_copy(slot, index).wait_send())

        mark_segments(r)
        r.need("proj_w_1", "attn_low_1", "projected_1", "mixed_own")
        wait()
        ffn_above.keep_share(r.ffn_share_1)
        mixed_hop(0)
        context_back(above, [slice(0, rows)])
        attend_back(above)
        r.need("qkv_w_1", "grad_first_1", "unit_two", "context_in_1", "low_in_1")
        r.need("up_w", "down_w", "slope", "unit_one", "act", "normed_low")
        extras = [
            *attn_grads(above, r.attn_whole_1, 2),
            at_step(span, lambda: r.fetch("proj_w_0", "qkv_w_0")),
            *ffn_grads(middle, r.ffn_whole_0, 6 * (size - 1) + chunks),
            at_step(3, ffn_above.pass_on),
            at_step(5, attn_above.to_partner),
            at_step(8, attn_above.to_chips),
            at_step(12, ffn_above.to_other_core),
            at_step(15, attn_above.onward),
            at_step(16, lambda: (ffn_above.settle(), r.send("ffn_whole_1"))),
            at_step(6 * (size - 1) + 1, attn_above.give_share),
            at_step(6 * (size - 1) + 5, attn_above.pass_on),
            at_step(6 * (size - 1) + 10, attn_above.to_other_core),
            at_step(6 * (size - 1) + 11, ffn_below.to_partner),
            at_step(6 * (size - 1) + 13, lambda: (attn_above.settle(), r.send("attn_whole_1"))),
            at_step(6 * (size - 1) + 14, ffn_below.to_chips),
            at_step(12 * (size - 1) + 6, ffn_below.onward),
        ]
        extras += [
            at_step(12 * (size - 1), lambda: r.need("proj_w_0")),
            (12 * (size - 1), chunks, lambda chunk: context_back(below, chunk_rows(half, chunk))),
        ]
        stages = [qkv_back_stage(above, 0, True), ffn_back_stage(middle, 0)]
        line_loop(size, stages, extras, 3)
        r.need("qkv_w_0", "projected_0")
        mixed_hop(1)
        attend_back(below)
        ffn_below.give_share()
        r.need("context_in_0", "low_in_0")
        extras = [
            *attn_grads(below, r.attn_whole_0, 0),
            at_step(1, attn_below.to_partner),
            at_step(2, small_to_line),
            at_step(4, ffn_below.pass_on),
            at_step(4, attn_below.to_chips),
            *(at_step(5 + 6 * (hop - 2), lambda hop=hop: mixed_hop(hop)) for hop in range(2, end)),
            at_step(9, small_to_teams),
            at_step(11, attn_below.onward),
            at_step(12, ffn_below.to_other_core),
            at_step(14, lambda: (ffn_below.settle(), r.send("ffn_whole_0"))),
            at_step(15, attn_below.give_share),
            at_step(18, attn_below.pass_on),
            at_step(19, small_finish),
            at_step(23, attn_below.to_other_core),
        ]
        line_loop(size, [qkv_back_stage(below, 0, False)], extras, 3)
        mixed_settle()
        r.send("grad_low", "mixed")
        attn_below.settle()
        r.send("attn_whole_0")

    heads = part // HEAD
    rooms = {"qkv_w_0": "qkv_w_1", "proj_w_0": "proj_w_1"}
    outs = dict(
        grad_low=shape(rows, width, kind=LOW),
        mixed=shape(rows, width, kind=LOW),
        ffn_whole_1=shape(ffn_rows, width, kind=LOW),
        attn_whole_1=shape(attn_rows, part, kind=LOW),
        ffn_whole_0=shape(ffn_rows, width, kind=LOW),
        attn_whole_0=shape(attn_rows, part, kind=LOW),
        small_total=shape(count, width),
    )
    scratch = dict(
        seg_cols=pltpu.VMEM((rows, QUERIES), F32),
        turned_rows=pltpu.VMEM((part, rows), LOW),
        grad_context=pltpu.VMEM((rows, part), LOW),
        grad_key=pltpu.VMEM((rows, part), F32),
        grad_value=pltpu.VMEM((rows, part), F32),
        grad_proj=pltpu.VMEM((3, rows, part), LOW),
        head_queries=pltpu.VMEM((heads * QUERIES, part), LOW),
        head_context=pltpu.VMEM((heads * QUERIES, part), LOW),
        score_rows=pltpu.VMEM((rows, heads * QUERIES), LOW),
        prob_rows=pltpu.VMEM((rows, heads * QUERIES), LOW),
        qv_sum_0=pltpu.VMEM((2, 8, part), F32),
        qv_sum_1=pltpu.VMEM((2, 8, part), F32),
        sums_0=pltpu.VMEM((6, 8, width), F32),
        up_sum_0=pltpu.VMEM((8, hidden), F32),
        pre=pltpu.VMEM((rows, hidden), LOW),
        branch=pltpu.VMEM((rows, width), LOW),
        grad_first_0=pltpu.VMEM((half, width), F32),
        attn_low_0=pltpu.VMEM((rows, width), LOW),
        small=pltpu.VMEM((count, width), F32),
        ends=pltpu.VMEM((2, count, width), F32),
        mine=pltpu.VMEM((count, width), F32),
        others=pltpu.VMEM((teams, count, width), F32),
        end_sent=pltpu.SemaphoreType.DMA((2, size - 1)),
        end_got=pltpu.SemaphoreType.DMA((2,)),
        team_sent=pltpu.SemaphoreType.DMA((teams - 1,)),
        team_got=pltpu.SemaphoreType.DMA((teams,)),
        mixed_sent=pltpu.SemaphoreType.DMA((2,)),
        mixed_got=pltpu.SemaphoreType.DMA((2,)),
        qkv_line_1=line_scratch(rows, width),
        back_line=line_scratch(rows, width),
        qkv_sems_0=line_scratch(rows, width)[2:],
        ffn_spread=Spread.scratch(chips, ffn_rows, width),
        attn_spread=Spread.scratch(chips, attn_rows, part),
    )
    return call(collective, body, ins, outs, scratch, rooms, ("qkv_w_0", "proj_w_0"), [*outs][:-1]), own_rows


def assemble(attn_wholes, ffn_wholes, mixed, grad_low, small, own_rows, part):
    layers = len(attn_wholes)
    rows, width = mixed.shape
    hidden = ffn_wholes[0].shape[0] - width
    steps = 2
    cut = width // steps

    def for_layer(number, spec_of):
        def index(layer, step):
            return spec_of(jnp.where(layer == number, step, jnp.where(layer < number, 0, steps - 1)))

        return index

    ins, in_specs = [], []
    for number in range(layers):
        ins += [
            attn_wholes[number].reshape(4, width, part),
            attn_wholes[number].reshape(-1, part, part),
            ffn_wholes[number].reshape(-1, width, width),
        ]
        in_specs += [
            pl.BlockSpec((3, cut, part), for_layer(number, lambda step: (0, step, 0))),
            pl.BlockSpec((width // part, part // steps, part), for_layer(number, lambda step: (3, step, 0))),
            pl.BlockSpec((1 + hidden // width, cut, width), for_layer(number, lambda step: (0, step, 0))),
        ]
    slab = rows // (layers * steps)
    ins += [mixed, grad_low, small]
    row_spec = pl.BlockSpec((slab, width), lambda layer, step: (layer * steps + step, 0))
    in_specs += [row_spec, row_spec, pl.BlockSpec(small.shape, lambda layer, step: (0, 0))]
    def all_of(*dims):
        return pl.BlockSpec(dims, lambda layer, step: (0,) * len(dims))

    out_shape = [
        shape(rows, width),
        shape(rows, width),
        shape(layers, 3, width, part),
        shape(layers, part, width),
        shape(layers, width, hidden),
        shape(layers, hidden, width),
        shape(layers, 2, part),
        shape(layers, hidden),
    ] + [shape(layers, width)] * 6
    out_specs = [
        row_spec,
        row_spec,
        pl.BlockSpec((1, 3, cut, part), lambda layer, step: (layer, 0, step, 0)),
        pl.BlockSpec((1, part // steps, width), lambda layer, step: (layer, step, 0)),
        pl.BlockSpec((1, cut, hidden), lambda layer, step: (layer, step, 0)),
        pl.BlockSpec((1, cut, width), lambda layer, step: (layer, step, 0)),
        all_of(layers, 2, part),
        all_of(layers, hidden),
    ] + [all_of(layers, width)] * 6

    def body(*refs):
        sources = refs[: 3 * layers]
        mixed_in, grad_in, small_in = refs[3 * layers : 3 * layers + 3]
        mixed_out, grad_out, qkv, proj, up, down, qv, up_b, *norms = refs[3 * layers + 3 :]
        mixed_out[...] = mixed_in[...].astype(F32)
        grad_out[...] = grad_in[...].astype(F32)
        for number in range(layers):
            attn_in, proj_in, ffn_in = sources[3 * number : 3 * number + 3]

            @pl.when(pl.program_id(0) == number)
            def _():
                qkv[0] = attn_in[...].astype(F32)
                for block in range(width // part):
                    proj[0, :, block * part : (block + 1) * part] = proj_in[block].astype(F32)
                up[0] = ffn_in[0].astype(F32)
                down[0] = ffn_in[1].astype(F32)

        @pl.when((pl.program_id(0) == 0) & (pl.program_id(1) == 0))
        def _():
            values = small_in[...]
            flat = jnp.concatenate([values[n : n + 1] for n in range(own_rows)], axis=1)
            for layer in range(layers):
                for member in range(2):
                    at = (2 * layer + member) * part
                    qv[layer, member : member + 1] = flat[:, at : at + part]
                at = 2 * layers * part + layer * hidden
                up_b[layer : layer + 1] = flat[:, at : at + hidden]
            for member, norm in enumerate(norms):
                norm[...] = values[own_rows + member * layers : own_rows + (member + 1) * layers]

    return pl.pallas_call(
        body,
        grid=(layers, steps),
        out_shape=out_shape,
        in_specs=in_specs,
        out_specs=out_specs,
        compiler_params=pltpu.CompilerParams(vmem_limit_bytes=60 << 20),
    )(*ins)


def local(
    tokens,
    segment_ids,
    cotangent,
    qkv_weight,
    qv_bias,
    proj_weight,
    proj_bias,
    first_gain,
    first_shift,
    up_weight,
    up_bias,
    down_weight,
    down_bias,
    second_gain,
    second_shift,
):
    seq_count, length, width = tokens.shape
    rows = seq_count * length
    layers = qkv_weight.shape[0]
    size = lax.axis_size("tensor")
    chips = lax.axis_size("dp") // 2
    part = qkv_weight.shape[-1]
    qkv_stack = jnp.transpose(qkv_weight, (0, 2, 1, 3))
    low = tokens.reshape(rows, width)
    weights = dict(qkv_w=qkv_stack, proj_w=proj_weight, up_w=up_weight, down_w=down_weight)
    ins = dict(
        low_in_0=low,
        cotangent=cotangent.reshape(rows, width),
        seg_row=segment_ids,
        qv_bias=qv_bias,
        proj_b=proj_bias,
        first_gain=first_gain,
        first_shift=first_shift,
        up_b=up_bias,
        down_b=down_bias,
        second_gain=second_gain,
        second_shift=second_shift,
    )
    for layer in range(layers):
        for name, array in weights.items():
            ins["%s_%d" % (name, layer)] = Layer(array, layer)
    done = forward_kernel(size, chips, 0, ins)
    last, own_rows = backward_kernel(
        size,
        chips,
        1,
        layers,
        dict(
            seg_row=segment_ids,
            log_total_0=done.log_total_0,
            log_total_1=done.log_total_1,
            sums_1=done.sums,
            ffn_share_1=done.ffn_share,
            up_sum_1=done.up_sum,
            inverse_two=done.inverse_two_0,
            inverse_one=done.inverse_one_0,
            first_gain=first_gain,
            second_gain=second_gain,
            proj_w_1=Layer(proj_weight, 1),
            attn_low_1=whole(done.attn_low),
            projected_1=whole(done.projected_1),
            mixed_own=whole(done.mixed_own),
            qkv_w_1=Layer(qkv_stack, 1),
            grad_first_1=whole(done.grad_first),
            unit_two=whole(done.unit_two_0),
            context_in_1=whole(done.context_1),
            low_in_1=whole(done.low_0),
            up_w=Layer(up_weight, 0),
            down_w=Layer(down_weight, 0),
            slope=whole(done.slope_0),
            unit_one=whole(done.unit_one_0),
            act=whole(done.act_0),
            normed_low=whole(done.normed_low_0),
            proj_w_0=Layer(proj_weight, 0),
            qkv_w_0=Layer(qkv_stack, 0),
            projected_0=whole(done.projected_0),
            context_in_0=whole(done.context_0),
            low_in_0=whole(low),
        ),
    )
    ffn_wholes = [last.ffn_whole_0, last.ffn_whole_1]
    attn_wholes = [last.attn_whole_0, last.attn_whole_1]

    mixed, input_grad, qkv, proj, up, down, qv, up_b, *norms = assemble(
        attn_wholes, ffn_wholes, last.mixed, last.grad_low, last.small_total, own_rows, part
    )
    return (
        mixed.reshape(tokens.shape),
        input_grad.reshape(tokens.shape),
        jnp.transpose(qkv, (0, 2, 1, 3)),
        qv,
        proj,
        norms[5],
        norms[3],
        norms[4],
        up,
        up_b,
        down,
        norms[2],
        norms[0],
        norms[1],
    )


def solution(mesh):
    return jax.shard_map(
        local,
        mesh=mesh,
        in_specs=(
            P("dp", None, None),
            P("dp", None),
            P("dp", None, None),
            P(None, None, None, "tensor"),
            P(None, None, "tensor"),
            P(None, "tensor", None),
            P(),
            P(),
            P(),
            P(None, None, "tensor"),
            P(None, "tensor"),
            P(None, "tensor", None),
            P(),
            P(),
            P(),
        ),
        out_specs=(
            P("dp", None, None),
            P("dp", None, None),
            P(None, None, None, "tensor"),
            P(None, None, "tensor"),
            P(None, "tensor", None),
            P(),
            P(),
            P(),
            P(None, None, "tensor"),
            P(None, "tensor"),
            P(None, "tensor", None),
            P(),
            P(),
            P(),
        ),
        check_vma=False,
    )
```

```python
import math
import types

import jax
import jax.numpy as jnp
from jax import lax
from jax.experimental import pallas as pl
from jax.experimental.pallas import tpu as pltpu
from jax.sharding import PartitionSpec as P

HEAD = 64


norm_eps = 1e-12
masked_value = -1000000000.0


MESH = pl.DeviceIdType.MESH
F32 = jnp.float32
LOW = jnp.bfloat16
CHUNK = 32
LAG = 2
PIECE = 512
QUERIES = 128


def dot(a, b):
    return jnp.dot(a, b, preferred_element_type=F32)


def dot_t(a, b):
    return lax.dot_general(a, b, (((1,), (1,)), ((), ())), preferred_element_type=F32)


def dot_tn(a, b):
    return lax.dot_general(a, b, (((0,), (0,)), ((), ())), preferred_element_type=F32)


def here():
    return lax.axis_index("dp"), lax.axis_index("tensor")


def greet(size, line=True, targets=()):
    row, place = here()
    barrier = pltpu.get_barrier_semaphore()
    for count, target in targets:

        def signal(index, carry):
            pl.semaphore_signal(barrier, inc=1, device_id=target(index), device_id_type=MESH)
            return carry

        lax.fori_loop(0, count, signal, 0)
    expected = sum(count for count, _ in targets)
    left, right = place > 0, place < size - 1
    if line:

        @pl.when(left)
        def _():
            pl.semaphore_signal(barrier, inc=1, device_id=(row, place - 1), device_id_type=MESH)

        @pl.when(right)
        def _():
            pl.semaphore_signal(barrier, inc=1, device_id=(row, place + 1), device_id_type=MESH)

    def wait():
        if not line:
            pl.semaphore_wait(barrier, expected)
            return

        @pl.when(left & right)
        def _():
            pl.semaphore_wait(barrier, expected + 2)

        @pl.when(jnp.logical_not(left & right))
        def _():
            pl.semaphore_wait(barrier, expected + 1)

    return wait


def partner():
    row, place = here()
    return (row + 1 - 2 * lax.rem(row, 2), place)


def plane_peer(chips, index):
    row, place = here()
    return (lax.rem(row // 2 + index + 1, chips) * 2 + lax.rem(row, 2), place)


def line_loop(size, stages, extras=(), lag=LAG):
    row, place = here()
    half = stages[0].part.shape[0] // 2
    chunks = half // CHUNK
    end = size - 1
    span = 2 * lag * end

    def rows_of(side, chunk):
        return pl.ds(pl.multiple_of(side * half + chunk * CHUNK, CHUNK), CHUNK)

    def sum_copy(stage, side, chunk, target):
        rows = rows_of(side, chunk)
        return pltpu.make_async_remote_copy(
            src_ref=stage.part.at[rows],
            dst_ref=stage.recv.at[rows],
            send_sem=stage.sems[0].at[side, chunk],
            recv_sem=stage.sems[1].at[side, chunk],
            device_id=(row, target),
            device_id_type=MESH,
        )

    def row_copy(stage, which, side, chunk, target):
        rows = rows_of(side, chunk)
        return pltpu.make_async_remote_copy(
            src_ref=stage.outs[which].at[rows],
            dst_ref=stage.outs[which].at[rows],
            send_sem=stage.sems[2].at[which, side, chunk],
            recv_sem=stage.sems[3].at[which, side, chunk],
            device_id=(row, target),
            device_id_type=MESH,
        )

    def side_facts(side):
        if side == 0:
            return place, place + 1, place - 1
        return end - place, place - 1, place + 1

    def bring_back(stage, since):
        for side in range(2):
            at, onward, back = side_facts(side)
            chunk = since - lag * end - lag * (end - at)

            @pl.when((at < end) & (chunk >= 0) & (chunk < chunks))
            def _():
                for which in range(len(stage.outs)):
                    row_copy(stage, which, side, chunk, back).wait_recv()

                    @pl.when(at > 0)
                    def _():
                        row_copy(stage, which, side, chunk, back).start()

    def begin_sum(stage, since):
        for side in range(2):
            at, onward, back = side_facts(side)

            @pl.when(at == 0)
            def _():
                sum_copy(stage, side, since, onward).start()

    def sum_up(stage, since):
        for side in range(2):
            at, onward, back = side_facts(side)
            chunk = since - lag * at

            @pl.when((at > 0) & (chunk >= 0) & (chunk < chunks))
            def _():
                sum_copy(stage, side, chunk, onward).wait_recv()

                @pl.when(at < end)
                def _():
                    rows = rows_of(side, chunk)
                    stage.part[rows] = stage.part[rows] + stage.recv[rows]
                    sum_copy(stage, side, chunk, onward).start()

                @pl.when(at == end)
                def _():
                    rows = rows_of(side, chunk)
                    own = pl.ds(pl.multiple_of(chunk * CHUNK, CHUNK), CHUNK)
                    rest = stage.finish(rows, own, stage.part[rows].astype(F32) + stage.recv[rows].astype(F32))
                    for which in range(len(stage.outs)):
                        row_copy(stage, which, side, chunk, back).start()
                    rest()

    def step(now, carry):
        for number, stage in enumerate(stages):
            bring_back(stage, now - number * span)
        for number, stage in enumerate(stages):
            sum_up(stage, now - number * span)
        for number, stage in enumerate(stages):
            since = now - number * span

            @pl.when((since >= 0) & (since < chunks))
            def _():
                stage.produce([rows_of(side, since) for side in range(2)])
                begin_sum(stage, since)

        for first, count, work in extras:

            @pl.when((now >= first) & (now < first + count))
            def _():
                work(now - first)

        return carry

    lax.fori_loop(0, chunks + span * len(stages), step, 0)

    def drain(chunk, carry):
        for stage in stages:
            for side in range(2):
                at, onward, back = side_facts(side)

                @pl.when(at < end)
                def _():
                    sum_copy(stage, side, chunk, onward).wait_send()

                @pl.when(at > 0)
                def _():
                    for which in range(len(stage.outs)):
                        row_copy(stage, which, side, chunk, back).wait_send()

        return carry

    lax.fori_loop(0, chunks, drain, 0)


def chunk_rows(half, chunk):
    return [pl.ds(pl.multiple_of(side * half + chunk * CHUNK, CHUNK), CHUNK) for side in range(2)]


def by_rows(count, work, block=32):
    def one(index, carry):
        work(pl.ds(pl.multiple_of(index * block, block), block), index * block)
        return carry

    block = min(block, count)
    lax.fori_loop(0, count // block, one, 0)


class Spread:
    def __init__(self, chips, grads, scratch):
        self.chips, self.grads = chips, grads
        self.half = grads.shape[0] // 2
        self.near, self.far, self.near_sems, self.far_sems, self.free = scratch
        row, place = here()
        self.core, self.chip, self.place = lax.rem(row, 2), row // 2, place

    @staticmethod
    def scratch(chips, rows, width):
        half = rows // 2
        far = half * 3 // 4 if chips == 4 else half // chips * (chips - 1)
        copies = 8 if chips == 4 else 2 * (chips - 1)
        sems = [
            pltpu.SemaphoreType.DMA((4,)),
            pltpu.SemaphoreType.DMA((2, copies)),
            pltpu.SemaphoreType.REGULAR,
        ]
        return [pltpu.VMEM((half, width), LOW), pltpu.VMEM((far, width), LOW), *sems, *sems]

    def rows(self, first, count):
        return pl.ds(pl.multiple_of(first, 16), count)

    def core_copy(self, source, target, number):
        return pltpu.make_async_remote_copy(
            src_ref=source,
            dst_ref=target,
            send_sem=self.near_sems.at[2 * number],
            recv_sem=self.near_sems.at[2 * number + 1],
            device_id=partner(),
            device_id_type=MESH,
        )

    def near_copy(self):
        other = self.rows((1 - self.core) * self.half, self.half)
        return self.core_copy(self.grads.at[other], self.near, 0)

    def last_copy(self):
        own = self.grads.at[self.rows(self.core * self.half, self.half)]
        return self.core_copy(own, own, 1)

    def chip_copy(self, source, target, number, chip):
        return pltpu.make_async_remote_copy(
            src_ref=source,
            dst_ref=target,
            send_sem=self.far_sems.at[0, number],
            recv_sem=self.far_sems.at[1, number],
            device_id=(chip * 2 + self.core, self.place),
            device_id_type=MESH,
        )

    def to_partner(self):
        self.near_copy().start()

    def add_partner(self):
        self.near_copy().wait_send()
        pl.semaphore_signal(self.free, inc=1, device_id=partner(), device_id_type=MESH)
        self.near_copy().wait_recv()
        base = self.core * self.half

        def add(rows, first):
            own = self.grads[self.rows(base + first, rows.size)]
            self.near[rows] = self.near[rows] + own

        by_rows(self.half, add)

    def settle_sum(self):
        self.settle_there()
        pl.semaphore_wait(self.free, 1)

    def give_share(self):
        self.sum_share(self.grads, self.own_rows())
        self.start_back()

    def keep_share(self, share):
        count = share.shape[0] // len(self.own_rows())
        for number, base in enumerate(self.own_rows()):

            def keep(rows, first, number=number, base=base):
                came = share[self.rows(number * count + first, rows.size)]
                self.grads[self.rows(base + first, rows.size)] = came

            by_rows(count, keep)
        self.summed = False
        self.start_back()

    summed = True

    def to_other_core(self):
        self.take_back()
        if self.summed:
            self.settle_sum()
        self.settle_back()
        self.last_copy().start()

    def settle(self):
        self.last_copy().wait_recv()
        self.last_copy().wait_send()


class DirectSpread(Spread):
    def each(self, work):
        def one(index, carry):
            work(index)
            return carry

        lax.fori_loop(0, self.chips - 1, one, 0)

    def peer(self, index):
        return lax.rem(self.chip + index + 1, self.chips)

    def far_copy(self, index):
        count = self.half // self.chips
        chip = self.peer(index)
        source = self.near.at[self.rows(chip * count, count)]
        return self.chip_copy(source, self.far.at[self.rows(index * count, count)], index, chip)

    def back_copy(self, index):
        count = self.half // self.chips
        share = self.grads.at[self.rows(self.core * self.half + self.chip * count, count)]
        return self.chip_copy(share, share, self.chips - 1 + index, self.peer(index))

    def to_chips(self):
        self.add_partner()
        self.each(lambda index: self.far_copy(index).start())

    def onward(self):
        pass

    def own_rows(self):
        return [self.core * self.half + self.chip * (self.half // self.chips)]

    def sum_share(self, target, starts):
        self.each(lambda index: self.far_copy(index).wait_recv())
        count = self.half // self.chips
        base = self.chip * count

        def add(rows, first):
            def one(index, total):
                return total + self.far[self.rows(index * count + first, rows.size)].astype(F32)

            own = self.near[self.rows(base + first, rows.size)].astype(F32)
            total = lax.fori_loop(0, self.chips - 1, one, own)
            target[self.rows(starts[0] + first, rows.size)] = total.astype(LOW)

        by_rows(count, add)

    def start_back(self):
        self.each(lambda index: self.back_copy(index).start())

    def pass_on(self):
        pass

    def take_back(self):
        self.each(lambda index: self.back_copy(index).wait_recv())

    def settle_there(self):
        self.each(lambda index: self.far_copy(index).wait_send())

    def settle_back(self):
        self.each(lambda index: self.back_copy(index).wait_send())


class SquareSpread(Spread):
    def __init__(self, chips, grads, scratch):
        super().__init__(chips, grads, scratch)
        quarter = self.half // 4
        eighth = self.half // 8
        first, second = lax.rem(self.chip, 2), self.chip // 2
        along = self.chip + 1 - 2 * first
        across = self.chip + 2 - 4 * second
        self.quarter, self.eighth = quarter, eighth
        self.chips_of = ((along, across), (across, along))
        self.bits = ((first, second), (second, first))
        self.part = [side * 2 * quarter for side in range(2)]
        self.kept = [self.part[side] + self.bits[side][0] * quarter for side in range(2)]
        self.own = [self.kept[side] + self.bits[side][1] * eighth for side in range(2)]

    def first_copy(self, side):
        sent = self.part[side] + (1 - self.bits[side][0]) * self.quarter
        room = self.far.at[pl.ds(side * self.quarter, self.quarter)]
        source = self.near.at[self.rows(sent, self.quarter)]
        return self.chip_copy(source, room, side, self.chips_of[side][0])

    def second_copy(self, side):
        sent = self.kept[side] + (1 - self.bits[side][1]) * self.eighth
        room = self.far.at[pl.ds(2 * self.quarter + side * self.eighth, self.eighth)]
        source = self.near.at[self.rows(sent, self.eighth)]
        return self.chip_copy(source, room, 2 + side, self.chips_of[side][1])

    def share_copy(self, side):
        share = self.grads.at[self.rows(self.core * self.half + self.own[side], self.eighth)]
        return self.chip_copy(share, share, 4 + side, self.chips_of[side][1])

    def pass_copy(self, side):
        share = self.grads.at[self.rows(self.core * self.half + self.kept[side], self.quarter)]
        return self.chip_copy(share, share, 6 + side, self.chips_of[side][0])

    def to_chips(self):
        self.add_partner()
        for side in range(2):
            self.first_copy(side).start()

    def onward(self):
        for side in range(2):
            self.first_copy(side).wait_recv()
            base = self.kept[side]

            def add(rows, first, side=side, base=base):
                at = self.rows(base + first, rows.size)
                came = self.far[self.rows(side * self.quarter + first, rows.size)]
                self.near[at] = self.near[at] + came

            by_rows(self.quarter, add)
            self.second_copy(side).start()

    def own_rows(self):
        return [self.core * self.half + self.own[side] for side in range(2)]

    def sum_share(self, target, starts):
        for side in range(2):
            self.second_copy(side).wait_recv()
            base, start = self.own[side], starts[side]

            def add(rows, first, side=side, base=base, start=start):
                came = self.far[self.rows(2 * self.quarter + side * self.eighth + first, rows.size)]
                own = self.near[self.rows(base + first, rows.size)]
                target[self.rows(start + first, rows.size)] = own + came

            by_rows(self.eighth, add)

    def start_back(self):
        for side in range(2):
            self.share_copy(side).start()

    def pass_on(self):
        for side in range(2):
            self.share_copy(side).wait_recv()
            self.pass_copy(side).start()

    def take_back(self):
        for side in range(2):
            self.pass_copy(side).wait_recv()

    def settle_there(self):
        for side in range(2):
            self.first_copy(side).wait_send()
            self.second_copy(side).wait_send()

    def settle_back(self):
        for side in range(2):
            self.share_copy(side).wait_send()
            self.pass_copy(side).wait_send()


def spread_of(chips, grads, scratch):
    return (SquareSpread if chips == 4 else DirectSpread)(chips, grads, scratch)


def normalize(residual):
    centred = residual - jnp.mean(residual, axis=-1, keepdims=True)
    inverse = lax.rsqrt(jnp.mean(centred * centred, axis=-1, keepdims=True) + norm_eps)
    return centred * inverse, inverse


def norm_back(grad, gain, unit, inverse):
    scaled = grad * gain
    return (
        scaled
        - jnp.mean(scaled, axis=-1, keepdims=True)
        - unit * jnp.mean(scaled * unit, axis=-1, keepdims=True)
    ) * inverse


def tally(total, values):
    total[...] += jnp.sum(values.reshape(-1, 8, values.shape[-1]), axis=0)


class Layer:
    def __init__(self, array, layer):
        self.array, self.layer = array, layer

    def room(self):
        return self.array.shape if self.layer is None else self.array.shape[1:]


def whole(array):
    return Layer(array, None)


def view(refs, suffix):
    named = dict(vars(refs))
    for name, ref in vars(refs).items():
        if name.endswith(suffix):
            named[name[: -len(suffix)]] = ref
    return types.SimpleNamespace(**named)


def call(collective, body, ins, outs, scratch, into=types.MappingProxyType({}), later=(), sent=()):
    vmem = pl.BlockSpec(memory_space=pltpu.VMEM)
    names = [*ins, *outs]
    fetched = {name: value for name, value in ins.items() if isinstance(value, Layer)}
    inside = {name: value for name, value in fetched.items() if name not in into}
    extra = {name: spec if isinstance(spec, list) else [spec] for name, spec in scratch.items()}

    def run(*refs):
        named = dict(zip(names, refs))
        rest = list(refs[len(names) :])
        copies, leaving = {}, {}
        arrivals, departures = rest.pop(0), rest.pop(0)
        for number, name in enumerate(sent):
            room = rest.pop(0)
            leaving[name] = pltpu.make_async_copy(room, named[name], departures.at[number])
            named[name] = room
        for number, (name, value) in enumerate(fetched.items()):
            room = named[into[name]] if name in into else rest.pop(0)
            source = named[name] if value.layer is None else named[name].at[value.layer]
            copies[name] = pltpu.make_async_copy(source, room, arrivals.at[number])
            if name not in later:
                copies[name].start()
            named[name] = room
        for name, specs in extra.items():
            taken = [rest.pop(0) for _ in specs]
            named[name] = taken if isinstance(scratch[name], list) else taken[0]

        def need(*wanted):
            for name in wanted:
                copies[name].wait()

        def fetch(*wanted):
            for name in wanted:
                copies[name].start()

        def send(*wanted):
            for name in wanted:
                leaving[name].start()

        body(types.SimpleNamespace(**named, need=need, fetch=fetch, send=send))
        for copy in leaving.values():
            copy.wait()

    results = pl.pallas_call(
        run,
        out_shape=list(outs.values()),
        in_specs=[pl.BlockSpec(memory_space=pl.ANY) if name in fetched else vmem for name in ins],
        out_specs=[pl.BlockSpec(memory_space=pl.ANY) if name in sent else vmem for name in outs],
        scratch_shapes=[
            pltpu.SemaphoreType.DMA((len(fetched),)),
            pltpu.SemaphoreType.DMA((max(1, len(sent)),)),
            *(pltpu.VMEM(outs[name].shape, outs[name].dtype) for name in sent),
            *(pltpu.VMEM(value.room(), value.array.dtype) for value in inside.values()),
            *(spec for specs in extra.values() for spec in specs),
        ],
        compiler_params=pltpu.CompilerParams(
            collective_id=collective, has_side_effects=True, vmem_limit_bytes=60 << 20
        ),
    )(*(value.array if isinstance(value, Layer) else value for value in ins.values()))
    return types.SimpleNamespace(**dict(zip(outs, results)))


def shape(*dims, kind=F32):
    return jax.ShapeDtypeStruct(dims, kind)


def line_scratch(rows, width, outs=1):
    chunks = rows // 2 // CHUNK
    return [
        pltpu.VMEM((rows, width), LOW),
        pltpu.VMEM((rows, width), LOW),
        pltpu.SemaphoreType.DMA((2, chunks)),
        pltpu.SemaphoreType.DMA((2, chunks)),
        pltpu.SemaphoreType.DMA((outs, 2, chunks)),
        pltpu.SemaphoreType.DMA((outs, 2, chunks)),
    ]


def stage_of(produce, finish, outs, scratch):
    part, recv, *sems = scratch
    return types.SimpleNamespace(
        produce=produce, finish=finish, outs=outs, part=part, recv=recv, sems=sems
    )


def clear(*refs):
    for ref in refs:
        ref[...] = jnp.zeros_like(ref)


def vector(ref, layer):
    return ref[...].astype(F32)[layer : layer + 1]


def head_lanes(values, head):
    lane = lax.broadcasted_iota(jnp.int32, values.shape, 1)
    return jnp.where(lane // HEAD == head, values, jnp.zeros_like(values))


def turned(values):
    return jnp.transpose(values.astype(F32)).astype(LOW)


def mark_segments(r):
    length = r.seg_row.shape[1]
    wide = jnp.broadcast_to(r.seg_row[...].astype(F32), (QUERIES, length))
    r.seg_cols[...] = jnp.transpose(wide)


def masked_block(r, keys, queries, at):
    same = r.seg_cols[...] == r.seg_row[:, at].astype(F32)
    return jnp.where(same, dot_t(keys, queries) * HEAD ** (-0.5), masked_value)


def project(r, layer, blocks):
    bias = r.qv_bias[layer].astype(F32)
    taken = take(r.low_in, blocks)
    for member in range(3):
        rows = dot(taken, r.qkv_w[member])
        if member != 1:
            rows += bias[member // 2 : member // 2 + 1]
        put(r.projected.at[member], blocks, rows.astype(LOW))


def attend(r, block):
    at = pl.ds(pl.multiple_of(block * QUERIES, QUERIES), QUERIES)
    queries = r.projected[0, at]
    heads = queries.shape[1] // HEAD
    parts = []
    for head in range(heads):
        scores = masked_block(r, r.projected[1], head_lanes(queries, head), at)
        row_max = jnp.max(scores, axis=0, keepdims=True)
        exponent = jnp.exp(scores - row_max)
        row_total = jnp.sum(exponent, axis=0, keepdims=True)
        r.log_total[head : head + 1, at] = row_max + jnp.log(row_total)
        probs = (exponent * (1.0 / row_total)).astype(LOW)
        parts.append(dot(r.turned_rows[head * HEAD : (head + 1) * HEAD], probs))
    r.context[at] = jnp.transpose(jnp.concatenate(parts, axis=0)).astype(LOW)


def attend_first(r, half):
    per_side = half // QUERIES
    r.turned_rows[...] = turned(r.projected[2])
    for side in range(2):
        attend(r, side * per_side)
    extras = []
    for block in range(1, per_side):
        for side in range(2):
            step = max(0, block * QUERIES // CHUNK - 2 + side)
            extras.append(at_step(step, lambda block=side * per_side + block: attend(r, block)))
    return extras


def context_back(r, blocks):
    put(r.grad_context, blocks, dot_t(take(r.attn_low_in, blocks), r.proj_w[...]).astype(LOW))


def attend_back(r, between=()):
    rows = r.attn_low_in.shape[0]
    heads = r.qkv_w.shape[2] // HEAD
    scale = HEAD ** (-0.5)
    r.turned_rows[...] = turned(r.projected[1])
    clear(r.grad_key, r.grad_value)
    for number in range(rows // QUERIES):
        at = slice(number * QUERIES, (number + 1) * QUERIES)
        queries, context_rows = r.projected[0, at], r.grad_context[at]
        parts = []
        for head in range(heads):
            to = slice(head * QUERIES, (head + 1) * QUERIES)
            r.head_queries[to] = head_lanes(queries, head)
            r.head_context[to] = head_lanes(context_rows, head)
            scores = masked_block(r, r.projected[1], r.head_queries[to], at)
            probability = jnp.exp(scores - r.log_total[head : head + 1, at])
            grad_probs = dot_t(r.projected[2], r.head_context[to])
            inner = jnp.sum(probability * grad_probs, axis=0, keepdims=True)
            grad_scores = (probability * (grad_probs - inner)).astype(LOW)
            r.score_rows[:, to] = grad_scores
            r.prob_rows[:, to] = probability.astype(LOW)
            parts.append(dot(r.turned_rows[head * HEAD : (head + 1) * HEAD], grad_scores))
        r.grad_key[...] += dot(r.score_rows[...], r.head_queries[...])
        r.grad_value[...] += dot(r.prob_rows[...], r.head_context[...])
        r.grad_proj[0, at] = (jnp.transpose(jnp.concatenate(parts, axis=0)) * scale).astype(LOW)
        if number < len(between):
            between[number]()
    r.grad_proj[1] = (r.grad_key[...] * scale).astype(LOW)
    r.grad_proj[2] = r.grad_value[...].astype(LOW)
    for slot, member in ((0, 0), (1, 2)):
        r.qv_sum[slot] = jnp.sum(r.grad_proj[member].astype(F32).reshape(-1, 8, r.qv_sum.shape[2]), axis=0)


def take(ref, blocks):
    return jnp.concatenate([ref[block] for block in blocks], axis=0)


def put(ref, blocks, values):
    count = values.shape[0] // len(blocks)
    for number, block in enumerate(blocks):
        ref[block] = values[number * count : (number + 1) * count]


def proj_stage(r, layer, whole):
    def produce(blocks):
        put(r.proj_line[0], blocks, dot(take(r.context, blocks), r.proj_w[...]).astype(LOW))

    def finish(at, own, total):
        came = r.residual[at if whole else own].astype(F32)
        unit, inverse = normalize(came + total + vector(r.proj_b, layer))
        result = unit * vector(r.first_gain, layer) + vector(r.first_shift, layer)
        r.normed_low[at] = result.astype(LOW)

        def rest():
            r.unit_one[own] = unit
            r.inverse_one[own] = inverse
            r.normed[own] = result

        return rest

    return stage_of(produce, finish, [r.normed_low], r.proj_line)


def ffn_stage(r, layer, last):
    def produce(blocks):
        pre = dot(take(r.normed_low, blocks), r.up_w[...]) + vector(r.up_b, layer)
        cdf = 0.5 * lax.erf(pre * math.sqrt(0.5)) + 0.5
        act = (pre * cdf).astype(LOW)
        slope = cdf + pre * jnp.exp(-0.5 * pre * pre) * (1.0 / math.sqrt(2 * math.pi))
        put(r.slope, blocks, slope.astype(LOW))
        put(r.act, blocks, act)
        put(r.ffn_line[0], blocks, dot(act, r.down_w[...]).astype(LOW))

    def finish(at, own, total):
        unit, inverse = normalize(r.normed[own] + total + vector(r.down_b, layer))
        gain = vector(r.second_gain, layer)
        result = unit * gain + vector(r.second_shift, layer)
        if last:
            grad_in = r.cotangent[at].astype(F32)
            grad = norm_back(grad_in, gain, unit, inverse)
            r.branch[at] = grad.astype(LOW)
        else:
            r.low[at] = result.astype(LOW)

        def rest():
            if last:
                r.mixed_own[own] = result.astype(LOW)
                r.grad_second[own] = grad
                tally(r.sums.at[0], grad_in * unit)
                tally(r.sums.at[1], grad_in)
                tally(r.sums.at[2], grad.astype(LOW).astype(F32))
            else:
                r.unit_two[own] = unit
                r.inverse_two[own] = inverse
                r.hidden[own] = result

        return rest

    return stage_of(produce, finish, [r.branch if last else r.low], r.ffn_line)


def ffn_back_stage(r, layer):
    def produce(blocks):
        grad = dot_t(take(r.branch, blocks), r.down_w[...])
        pre = (grad * take(r.slope, blocks).astype(F32)).astype(LOW)
        put(r.pre, blocks, pre)
        tally(r.up_sum, pre.astype(F32))
        put(r.back_line[0], blocks, dot_t(pre, r.up_w[...]).astype(LOW))

    def finish(at, own, total):
        grad_in = r.grad_second[own] + total
        unit = r.unit_one[own]
        grad = norm_back(grad_in, vector(r.first_gain, layer), unit, r.inverse_one[own])
        r.attn_low[at] = grad.astype(LOW)

        def rest():
            r.grad_first[own] = grad
            tally(r.sums.at[3], grad_in * unit)
            tally(r.sums.at[4], grad_in)
            tally(r.sums.at[5], grad.astype(LOW).astype(F32))

        return rest

    return stage_of(produce, finish, [r.attn_low], r.back_line)


def qkv_back_stage(r, layer, inner):
    def produce(blocks):
        total = sum(dot_t(take(r.grad_proj.at[member], blocks), r.qkv_w[member]) for member in range(3))
        put(r.qkv_line[0], blocks, total.astype(LOW))

    def finish(at, own, total):
        grad_in = r.grad_first_in[own] + total
        if not inner:
            r.grad_low[at] = grad_in.astype(LOW)
            return lambda: None
        unit = r.unit_two[own]
        grad = norm_back(grad_in, vector(r.second_gain, layer), unit, r.inverse_two[own])
        r.branch[at] = grad.astype(LOW)

        def rest():
            r.grad_second[own] = grad
            tally(r.sums.at[0], grad_in * unit)
            tally(r.sums.at[1], grad_in)
            tally(r.sums.at[2], grad.astype(LOW).astype(F32))

        return rest

    return stage_of(produce, finish, [r.branch] if inner else [r.grad_low], r.qkv_line)


def columns(piece):
    return pl.ds(pl.multiple_of(piece * PIECE, PIECE), PIECE)


def ffn_grads(r, out, first):
    width, hidden = r.up_w.shape

    def up(piece):
        rows = pl.ds(pl.multiple_of(piece * PIECE, PIECE), PIECE)
        out[rows] = dot_tn(r.normed_low[:, columns(piece)], r.pre[...]).astype(LOW)

    def down(piece):
        rows = pl.ds(pl.multiple_of(width + piece * PIECE, PIECE), PIECE)
        out[rows] = dot_tn(r.act[:, columns(piece)], r.branch[...]).astype(LOW)

    def all_of(pieces, work):
        lax.fori_loop(0, pieces, lambda piece, carry: (work(piece), carry)[1], 0)

    return [
        at_step(first, lambda: all_of(width // PIECE, up)),
        at_step(first + 1, lambda: all_of(hidden // PIECE, down)),
    ]


def attn_grads(r, out, first):
    width, part = r.low_in.shape[1], r.context_in.shape[1]

    def piece_of(piece):
        for member in range(3):
            rows = pl.ds(pl.multiple_of(member * width + piece * part, part), part)
            taken = r.low_in[:, pl.ds(pl.multiple_of(piece * part, part), part)]
            out[rows] = dot_tn(taken, r.grad_proj[member]).astype(LOW)
        rows = pl.ds(pl.multiple_of(3 * width + piece * part, part), part)
        taken = r.attn_low_in[:, pl.ds(pl.multiple_of(piece * part, part), part)]
        out[rows] = dot_tn(r.context_in[...], taken).astype(LOW)

    def all_pieces():
        lax.fori_loop(0, width // part, lambda piece, carry: (piece_of(piece), carry)[1], 0)

    return [at_step(first, all_pieces)]


def at_step(step, work):
    return (step, 1, lambda index: work())


def with_suffix(suffix, named):
    return {name + suffix: value for name, value in named.items()}


def kept_attention(rows, part):
    return dict(
        projected=shape(3, rows, part, kind=LOW),
        log_total=shape(part // HEAD, rows),
        context=shape(rows, part, kind=LOW),
    )


def forward_kernel(size, chips, collective, ins):
    rows, width = ins["low_in_0"].shape
    part, hidden = ins["proj_w_0"].array.shape[1], ins["up_w_0"].array.shape[2]
    half = rows // 2
    chunks = half // CHUNK

    def body(r):
        wait = greet(size, targets=[(1, lambda index: partner()), (chips - 1, lambda index: plane_peer(chips, index))])
        ffn_sum = spread_of(chips, r.ffn_grad, r.ffn_spread[:5])
        clear(r.sums, r.up_sum)
        mark_segments(r)
        below, above = view(r, "_0"), view(r, "_1")
        below.residual = r.low_in_0
        above.low_in, above.residual = r.low_0, r.hidden_0
        r.need("qkv_w_0")
        project(below, 0, [slice(0, rows)])
        extras = attend_first(below, half)
        r.need("proj_w_0", "up_w_0", "down_w_0", "qkv_w_1")
        wait()

        def project_chunk(chunk):
            project(above, 1, chunk_rows(half, chunk))

        extras.append((4 * 3 * (size - 1), chunks, project_chunk))
        line_loop(size, [proj_stage(below, 0, True), ffn_stage(below, 0, False)], extras, 3)
        r.send("projected_0", "context_0", "unit_one_0", "normed_low_0", "act_0", "slope_0", "unit_two_0", "low_0")
        extras = attend_first(above, half)
        r.need("proj_w_1", "up_w_1", "down_w_1")
        stages = [proj_stage(above, 1, False), ffn_stage(above, 1, True), ffn_back_stage(above, 1)]
        first = 4 * 3 * (size - 1) + chunks
        line_loop(
            size,
            stages,
            [
                *extras,
                at_step(2 * chunks, lambda: r.send("projected_1", "context_1")),
                *ffn_grads(above, r.ffn_grad, first),
                at_step(first + 2, lambda: (ffn_sum.to_partner(), r.send("mixed_own"))),
                at_step(first + 5, ffn_sum.to_chips),
                at_step(first + 15, ffn_sum.onward),
            ],
            3,
        )
        r.send("grad_first", "attn_low")
        share = r.ffn_share.shape[0]
        ffn_sum.sum_share(r.ffn_share, [0, share // 2])
        ffn_sum.settle_sum()

    outs = dict(
        **with_suffix("_0", kept_attention(rows, part)),
        **with_suffix("_1", kept_attention(rows, part)),
        unit_one_0=shape(half, width),
        inverse_one_0=shape(half, 1),
        normed_low_0=shape(rows, width, kind=LOW),
        act_0=shape(rows, hidden, kind=LOW),
        slope_0=shape(rows, hidden, kind=LOW),
        unit_two_0=shape(half, width),
        inverse_two_0=shape(half, 1),
        low_0=shape(rows, width, kind=LOW),
        mixed_own=shape(half, width, kind=LOW),
        grad_first=shape(half, width),
        attn_low=shape(rows, width, kind=LOW),
        ffn_share=shape((width + hidden) // 2 // chips, width, kind=LOW),
        up_sum=shape(8, hidden),
        sums=shape(6, 8, width),
    )
    scratch = dict(
        hidden_0=pltpu.VMEM((half, width), F32),
        normed=pltpu.VMEM((half, width), F32),
        turned_rows=pltpu.VMEM((part, rows), LOW),
        seg_cols=pltpu.VMEM((rows, QUERIES), F32),
        unit_one_1=pltpu.VMEM((half, width), F32),
        inverse_one_1=pltpu.VMEM((half, 1), F32),
        normed_low_1=pltpu.VMEM((rows, width), LOW),
        act_1=pltpu.VMEM((rows, hidden), LOW),
        slope_1=pltpu.VMEM((rows, hidden), LOW),
        pre=pltpu.VMEM((rows, hidden), LOW),
        branch=pltpu.VMEM((rows, width), LOW),
        grad_second=pltpu.VMEM((half, width), F32),
        proj_line_0=line_scratch(rows, width),
        ffn_line_0=line_scratch(rows, width),
        proj_line_1=line_scratch(rows, width),
        ffn_line_1=line_scratch(rows, width),
        back_line=line_scratch(rows, width),
        ffn_grad=pltpu.VMEM((width + hidden, width), LOW),
        ffn_spread=Spread.scratch(chips, width + hidden, width),
    )
    sent = [name for name, out in outs.items() if out.dtype == LOW and name != "ffn_share" or name in ("unit_one_0", "unit_two_0", "grad_first")]
    return call(collective, body, ins, outs, scratch, sent=sent)


def backward_kernel(size, chips, collective, layers, ins):
    rows, width = ins["attn_low_1"].array.shape
    part, hidden = ins["proj_w_0"].array.shape[1], ins["up_w"].array.shape[2]
    half = rows // 2
    chunks = half // CHUNK
    span = 2 * LAG * (size - 1)
    ffn_rows, attn_rows = width + hidden, 4 * width
    own_rows = layers * (2 * part + hidden) // width
    count = -(-(own_rows + 6 * layers) // 8) * 8
    teams = 2 * chips

    def row_peer(index):
        row, place = here()
        return (lax.rem(row + index + 1, teams), place)

    def line_peer(index):
        row, place = here()
        return (row, lax.rem(place + index + 1, size))

    def each(number, work):
        def one(index, carry):
            work(index)
            return carry

        lax.fori_loop(0, number, one, 0)

    def body(r):
        row, place = here()
        clear(r.ends, r.sums_0, r.up_sum_0)
        wait = greet(size, line=False, targets=[(teams - 1, row_peer), (size - 1, line_peer)])
        ffn_above = spread_of(chips, r.ffn_whole_1, r.ffn_spread[:5])
        attn_above = spread_of(chips, r.attn_whole_1, r.attn_spread[:5])
        ffn_below = spread_of(chips, r.ffn_whole_0, r.ffn_spread[:2] + r.ffn_spread[5:])
        attn_below = spread_of(chips, r.attn_whole_0, r.attn_spread[:2] + r.attn_spread[5:])
        above, below = view(r, "_1"), view(r, "_0")
        above.grad_first_in, above.attn_low_in = r.grad_first_1, r.attn_low_1
        below.grad_first_in, below.attn_low_in = r.grad_first_0, r.attn_low_0
        middle = types.SimpleNamespace(
            **{**vars(r), "sums": r.sums_0, "up_sum": r.up_sum_0, "grad_first": r.grad_first_0, "attn_low": r.attn_low_0}
        )
        above.sums = r.sums_0
        above.grad_second = middle.grad_second = r.grad_first_0
        below.qkv_line = [*r.qkv_line_1[:2], *r.qkv_sems_0]

        def end_copy(slot, index):
            return pltpu.make_async_remote_copy(
                src_ref=r.small,
                dst_ref=r.ends.at[slot],
                send_sem=r.end_sent.at[slot, index],
                recv_sem=r.end_got.at[slot],
                device_id=line_peer(index),
                device_id_type=MESH,
            )

        def team_copy(index, slot):
            return pltpu.make_async_remote_copy(
                src_ref=r.mine,
                dst_ref=r.others.at[slot],
                send_sem=r.team_sent.at[index],
                recv_sem=r.team_got.at[slot],
                device_id=row_peer(index),
                device_id_type=MESH,
            )

        end_places = ((0, 0), (1, size - 1))
        end = size - 1

        def side_rows(side):
            at, back = (place, place - 1) if side == 0 else (end - place, place + 1)
            return at, back, r.mixed.at[pl.ds(side * half, half)]

        def mixed_copy(side):
            at, back, rows_at = side_rows(side)
            return pltpu.make_async_remote_copy(
                src_ref=rows_at,
                dst_ref=rows_at,
                send_sem=r.mixed_sent.at[side],
                recv_sem=r.mixed_got.at[side],
                device_id=(row, back),
                device_id_type=MESH,
            )

        def mixed_hop(number):
            for side in range(2):
                at, _, rows_at = side_rows(side)

                @pl.when(at == end - number)
                def _():
                    if number:
                        mixed_copy(side).wait_recv()
                    else:
                        rows_at[...] = r.mixed_own[...]
                    mixed_copy(side).start()

        def mixed_settle():
            for side in range(2):
                at, _, _ = side_rows(side)

                @pl.when(at == 0)
                def _():
                    mixed_copy(side).wait_recv()

                @pl.when(at > 0)
                def _():
                    mixed_copy(side).wait_send()

        def small_to_line():
            named = vars(r)
            clear(r.small)
            lines = []
            for layer in range(layers):
                sums = jnp.sum(named["qv_sum_%d" % layer][...], axis=1)
                lines += [sums[0:1], sums[1:2]]
            for layer in range(layers):
                lines += [jnp.sum(named["up_sum_%d" % layer][...], axis=0, keepdims=True)]
            flat = jnp.concatenate(lines, axis=1)
            for number in range(own_rows):
                r.small[number : number + 1] = flat[:, number * width : (number + 1) * width]
            for layer in range(layers):
                sums = jnp.sum(named["sums_%d" % layer][...], axis=1)
                for member in range(6):
                    to = own_rows + member * layers + layer
                    r.small[to : to + 1] = sums[member : member + 1]
            for slot, end in end_places:

                @pl.when(place == end)
                def _():
                    each(size - 1, lambda index: end_copy(slot, index).start())

        def small_to_teams():
            for slot, end in end_places:

                @pl.when(place != end)
                def _():
                    end_copy(slot, 0).wait_recv()

            line_total = r.small[...] + r.ends[0] + r.ends[1]
            number = lax.broadcasted_iota(jnp.int32, (count, width), 0)
            r.mine[...] = jnp.where(number < own_rows, r.small[...], line_total)
            each(teams - 1, lambda index: team_copy(index, row).start())
            r.others[row] = r.mine[...]

        def small_finish():
            each(teams - 1, lambda index: team_copy(index, row_peer(index)[0]).wait_recv())
            r.small_total[...] = lax.fori_loop(
                1, teams, lambda index, total: total + r.others[index], r.others[0]
            )
            each(teams - 1, lambda index: team_copy(index, row).wait_send())
            for slot, end in end_places:

                @pl.when(place == end)
                def _():
                    each(size - 1, lambda index: end_copy(slot, index).wait_send())

        mark_segments(r)
        r.need("proj_w_1", "attn_low_1", "projected_1", "mixed_own")
        wait()
        ffn_above.keep_share(r.ffn_share_1)
        mixed_hop(0)
        context_back(above, [slice(0, rows)])
        attend_back(above)
        r.need("qkv_w_1", "grad_first_1", "unit_two", "context_in_1", "low_in_1")
        r.need("up_w", "down_w", "slope", "unit_one", "act", "normed_low")
        extras = [
            *attn_grads(above, r.attn_whole_1, 2),
            at_step(span, lambda: r.fetch("proj_w_0", "qkv_w_0")),
            *ffn_grads(middle, r.ffn_whole_0, 6 * (size - 1) + chunks),
            at_step(3, ffn_above.pass_on),
            at_step(5, attn_above.to_partner),
            at_step(8, attn_above.to_chips),
            at_step(12, ffn_above.to_other_core),
            at_step(15, attn_above.onward),
            at_step(16, lambda: (ffn_above.settle(), r.send("ffn_whole_1"))),
            at_step(6 * (size - 1) + 1, attn_above.give_share),
            at_step(6 * (size - 1) + 5, attn_above.pass_on),
            at_step(6 * (size - 1) + 10, attn_above.to_other_core),
            at_step(6 * (size - 1) + 11, ffn_below.to_partner),
            at_step(6 * (size - 1) + 13, lambda: (attn_above.settle(), r.send("attn_whole_1"))),
            at_step(6 * (size - 1) + 14, ffn_below.to_chips),
            at_step(12 * (size - 1) + 6, ffn_below.onward),
        ]
        extras += [
            at_step(12 * (size - 1), lambda: r.need("proj_w_0")),
            (12 * (size - 1), chunks, lambda chunk: context_back(below, chunk_rows(half, chunk))),
        ]
        stages = [qkv_back_stage(above, 0, True), ffn_back_stage(middle, 0)]
        line_loop(size, stages, extras, 3)
        r.need("qkv_w_0", "projected_0")
        mixed_hop(1)
        attend_back(below)
        ffn_below.give_share()
        r.need("context_in_0", "low_in_0")
        extras = [
            *attn_grads(below, r.attn_whole_0, 0),
            at_step(1, attn_below.to_partner),
            at_step(2, small_to_line),
            at_step(4, ffn_below.pass_on),
            at_step(4, attn_below.to_chips),
            *(at_step(5 + 6 * (hop - 2), lambda hop=hop: mixed_hop(hop)) for hop in range(2, end)),
            at_step(9, small_to_teams),
            at_step(10, attn_below.onward),
            at_step(12, ffn_below.to_other_core),
            at_step(14, lambda: (ffn_below.settle(), r.send("ffn_whole_0"))),
            at_step(13, attn_below.give_share),
            at_step(16, attn_below.pass_on),
            at_step(19, small_finish),
            at_step(21, attn_below.to_other_core),
        ]
        line_loop(size, [qkv_back_stage(below, 0, False)], extras, 3)
        mixed_settle()
        r.send("grad_low", "mixed")
        attn_below.settle()
        r.send("attn_whole_0")

    heads = part // HEAD
    rooms = {"qkv_w_0": "qkv_w_1", "proj_w_0": "proj_w_1"}
    outs = dict(
        grad_low=shape(rows, width, kind=LOW),
        mixed=shape(rows, width, kind=LOW),
        ffn_whole_1=shape(ffn_rows, width, kind=LOW),
        attn_whole_1=shape(attn_rows, part, kind=LOW),
        ffn_whole_0=shape(ffn_rows, width, kind=LOW),
        attn_whole_0=shape(attn_rows, part, kind=LOW),
        small_total=shape(count, width),
    )
    scratch = dict(
        seg_cols=pltpu.VMEM((rows, QUERIES), F32),
        turned_rows=pltpu.VMEM((part, rows), LOW),
        grad_context=pltpu.VMEM((rows, part), LOW),
        grad_key=pltpu.VMEM((rows, part), F32),
        grad_value=pltpu.VMEM((rows, part), F32),
        grad_proj=pltpu.VMEM((3, rows, part), LOW),
        head_queries=pltpu.VMEM((heads * QUERIES, part), LOW),
        head_context=pltpu.VMEM((heads * QUERIES, part), LOW),
        score_rows=pltpu.VMEM((rows, heads * QUERIES), LOW),
        prob_rows=pltpu.VMEM((rows, heads * QUERIES), LOW),
        qv_sum_0=pltpu.VMEM((2, 8, part), F32),
        qv_sum_1=pltpu.VMEM((2, 8, part), F32),
        sums_0=pltpu.VMEM((6, 8, width), F32),
        up_sum_0=pltpu.VMEM((8, hidden), F32),
        pre=pltpu.VMEM((rows, hidden), LOW),
        branch=pltpu.VMEM((rows, width), LOW),
        grad_first_0=pltpu.VMEM((half, width), F32),
        attn_low_0=pltpu.VMEM((rows, width), LOW),
        small=pltpu.VMEM((count, width), F32),
        ends=pltpu.VMEM((2, count, width), F32),
        mine=pltpu.VMEM((count, width), F32),
        others=pltpu.VMEM((teams, count, width), F32),
        end_sent=pltpu.SemaphoreType.DMA((2, size - 1)),
        end_got=pltpu.SemaphoreType.DMA((2,)),
        team_sent=pltpu.SemaphoreType.DMA((teams - 1,)),
        team_got=pltpu.SemaphoreType.DMA((teams,)),
        mixed_sent=pltpu.SemaphoreType.DMA((2,)),
        mixed_got=pltpu.SemaphoreType.DMA((2,)),
        qkv_line_1=line_scratch(rows, width),
        back_line=line_scratch(rows, width),
        qkv_sems_0=line_scratch(rows, width)[2:],
        ffn_spread=Spread.scratch(chips, ffn_rows, width),
        attn_spread=Spread.scratch(chips, attn_rows, part),
    )
    return call(collective, body, ins, outs, scratch, rooms, ("qkv_w_0", "proj_w_0"), [*outs][:-1]), own_rows


def assemble(attn_wholes, ffn_wholes, mixed, grad_low, small, own_rows, part):
    layers = len(attn_wholes)
    rows, width = mixed.shape
    hidden = ffn_wholes[0].shape[0] - width
    steps = 2
    cut = width // steps

    def for_layer(number, spec_of):
        def index(layer, step):
            return spec_of(jnp.where(layer == number, step, jnp.where(layer < number, 0, steps - 1)))

        return index

    ins, in_specs = [], []
    for number in range(layers):
        ins += [
            attn_wholes[number].reshape(4, width, part),
            attn_wholes[number].reshape(-1, part, part),
            ffn_wholes[number].reshape(-1, width, width),
        ]
        in_specs += [
            pl.BlockSpec((3, cut, part), for_layer(number, lambda step: (0, step, 0))),
            pl.BlockSpec((width // part, part // steps, part), for_layer(number, lambda step: (3, step, 0))),
            pl.BlockSpec((1 + hidden // width, cut, width), for_layer(number, lambda step: (0, step, 0))),
        ]
    slab = rows // (layers * steps)
    ins += [mixed, grad_low, small]
    row_spec = pl.BlockSpec((slab, width), lambda layer, step: (layer * steps + step, 0))
    in_specs += [row_spec, row_spec, pl.BlockSpec(small.shape, lambda layer, step: (0, 0))]
    def all_of(*dims):
        return pl.BlockSpec(dims, lambda layer, step: (0,) * len(dims))

    out_shape = [
        shape(rows, width),
        shape(rows, width),
        shape(layers, 3, width, part),
        shape(layers, part, width),
        shape(layers, width, hidden),
        shape(layers, hidden, width),
        shape(layers, 2, part),
        shape(layers, hidden),
    ] + [shape(layers, width)] * 6
    out_specs = [
        row_spec,
        row_spec,
        pl.BlockSpec((1, 3, cut, part), lambda layer, step: (layer, 0, step, 0)),
        pl.BlockSpec((1, part // steps, width), lambda layer, step: (layer, step, 0)),
        pl.BlockSpec((1, cut, hidden), lambda layer, step: (layer, step, 0)),
        pl.BlockSpec((1, cut, width), lambda layer, step: (layer, step, 0)),
        all_of(layers, 2, part),
        all_of(layers, hidden),
    ] + [all_of(layers, width)] * 6

    def body(*refs):
        sources = refs[: 3 * layers]
        mixed_in, grad_in, small_in = refs[3 * layers : 3 * layers + 3]
        mixed_out, grad_out, qkv, proj, up, down, qv, up_b, *norms = refs[3 * layers + 3 :]
        mixed_out[...] = mixed_in[...].astype(F32)
        grad_out[...] = grad_in[...].astype(F32)
        for number in range(layers):
            attn_in, proj_in, ffn_in = sources[3 * number : 3 * number + 3]

            @pl.when(pl.program_id(0) == number)
            def _():
                qkv[0] = attn_in[...].astype(F32)
                for block in range(width // part):
                    proj[0, :, block * part : (block + 1) * part] = proj_in[block].astype(F32)
                up[0] = ffn_in[0].astype(F32)
                down[0] = ffn_in[1].astype(F32)

        @pl.when((pl.program_id(0) == 0) & (pl.program_id(1) == 0))
        def _():
            values = small_in[...]
            flat = jnp.concatenate([values[n : n + 1] for n in range(own_rows)], axis=1)
            for layer in range(layers):
                for member in range(2):
                    at = (2 * layer + member) * part
                    qv[layer, member : member + 1] = flat[:, at : at + part]
                at = 2 * layers * part + layer * hidden
                up_b[layer : layer + 1] = flat[:, at : at + hidden]
            for member, norm in enumerate(norms):
                norm[...] = values[own_rows + member * layers : own_rows + (member + 1) * layers]

    return pl.pallas_call(
        body,
        grid=(layers, steps),
        out_shape=out_shape,
        in_specs=in_specs,
        out_specs=out_specs,
        compiler_params=pltpu.CompilerParams(vmem_limit_bytes=60 << 20),
    )(*ins)


def local(
    tokens,
    segment_ids,
    cotangent,
    qkv_weight,
    qv_bias,
    proj_weight,
    proj_bias,
    first_gain,
    first_shift,
    up_weight,
    up_bias,
    down_weight,
    down_bias,
    second_gain,
    second_shift,
):
    seq_count, length, width = tokens.shape
    rows = seq_count * length
    layers = qkv_weight.shape[0]
    size = lax.axis_size("tensor")
    chips = lax.axis_size("dp") // 2
    part = qkv_weight.shape[-1]
    qkv_stack = jnp.transpose(qkv_weight, (0, 2, 1, 3))
    low = tokens.reshape(rows, width)
    weights = dict(qkv_w=qkv_stack, proj_w=proj_weight, up_w=up_weight, down_w=down_weight)
    ins = dict(
        low_in_0=low,
        cotangent=cotangent.reshape(rows, width),
        seg_row=segment_ids,
        qv_bias=qv_bias,
        proj_b=proj_bias,
        first_gain=first_gain,
        first_shift=first_shift,
        up_b=up_bias,
        down_b=down_bias,
        second_gain=second_gain,
        second_shift=second_shift,
    )
    for layer in range(layers):
        for name, array in weights.items():
            ins["%s_%d" % (name, layer)] = Layer(array, layer)
    done = forward_kernel(size, chips, 0, ins)
    last, own_rows = backward_kernel(
        size,
        chips,
        1,
        layers,
        dict(
            seg_row=segment_ids,
            log_total_0=done.log_total_0,
            log_total_1=done.log_total_1,
            sums_1=done.sums,
            ffn_share_1=done.ffn_share,
            up_sum_1=done.up_sum,
            inverse_two=done.inverse_two_0,
            inverse_one=done.inverse_one_0,
            first_gain=first_gain,
            second_gain=second_gain,
            proj_w_1=Layer(proj_weight, 1),
            attn_low_1=whole(done.attn_low),
            projected_1=whole(done.projected_1),
            mixed_own=whole(done.mixed_own),
            qkv_w_1=Layer(qkv_stack, 1),
            grad_first_1=whole(done.grad_first),
            unit_two=whole(done.unit_two_0),
            context_in_1=whole(done.context_1),
            low_in_1=whole(done.low_0),
            up_w=Layer(up_weight, 0),
            down_w=Layer(down_weight, 0),
            slope=whole(done.slope_0),
            unit_one=whole(done.unit_one_0),
            act=whole(done.act_0),
            normed_low=whole(done.normed_low_0),
            proj_w_0=Layer(proj_weight, 0),
            qkv_w_0=Layer(qkv_stack, 0),
            projected_0=whole(done.projected_0),
            context_in_0=whole(done.context_0),
            low_in_0=whole(low),
        ),
    )
    ffn_wholes = [last.ffn_whole_0, last.ffn_whole_1]
    attn_wholes = [last.attn_whole_0, last.attn_whole_1]

    mixed, input_grad, qkv, proj, up, down, qv, up_b, *norms = assemble(
        attn_wholes, ffn_wholes, last.mixed, last.grad_low, last.small_total, own_rows, part
    )
    return (
        mixed.reshape(tokens.shape),
        input_grad.reshape(tokens.shape),
        jnp.transpose(qkv, (0, 2, 1, 3)),
        qv,
        proj,
        norms[5],
        norms[3],
        norms[4],
        up,
        up_b,
        down,
        norms[2],
        norms[0],
        norms[1],
    )


def solution(mesh):
    return jax.shard_map(
        local,
        mesh=mesh,
        in_specs=(
            P("dp", None, None),
            P("dp", None),
            P("dp", None, None),
            P(None, None, None, "tensor"),
            P(None, None, "tensor"),
            P(None, "tensor", None),
            P(),
            P(),
            P(),
            P(None, None, "tensor"),
            P(None, "tensor"),
            P(None, "tensor", None),
            P(),
            P(),
            P(),
        ),
        out_specs=(
            P("dp", None, None),
            P("dp", None, None),
            P(None, None, None, "tensor"),
            P(None, None, "tensor"),
            P(None, "tensor", None),
            P(),
            P(),
            P(),
            P(None, None, "tensor"),
            P(None, "tensor"),
            P(None, "tensor", None),
            P(),
            P(),
            P(),
        ),
        check_vma=False,
    )
```
